32 devices in a mesh: section: 2 (over core), expert: 4 (over z), tensor: 4 (over y, x).
Axes of the slice: x: 2, y: 2, z: 4, core: 2. Of those that a mesh axis runs over, the one named last changes fastest.
Arguments:
- boundary: bfloat16 [2, 2, 512, 2048], P('section', None, 'expert'), may hold values from -6 to 6
- seq_lengths: int32 [2, 2, 4, 4], P('section', None, 'expert'), may hold values from 1 to 64, 128 in all within a row
- expert_ids: int32 [2, 2, 512, 8], P('section', None, 'expert'), may hold values from 0 to 15, all different within a row; in each aligned block of 128 rows (0 to 127, 128 to 255, ..., all dimensions but the last counted through in order) at most 96 rows name the same one
- route_weights: float32 [2, 2, 512, 8], P('section', None, 'expert'), may hold values from 0.1 to 0.4
- attn_gain: float32 [2, 2048], P('section'), may hold values from 0.25 to 1.75
- moe_gain: float32 [2, 2048], P('section'), may hold values from 0.25 to 1.75
- query_gain: float32 [2, 128], P('section'), may hold values from 0.25 to 1.75
- key_norm_gain: float32 [2, 128], P('section'), may hold values from 0.25 to 1.75
- w_query: bfloat16 [2, 2048, 4096], P('section', 'expert', 'tensor'), may hold values from -0.125 to 0.125
- key_weight: bfloat16 [2, 2048, 512], P('section', 'expert', 'tensor'), may hold values from -0.125 to 0.125
- value_weight: bfloat16 [2, 2048, 512], P('section', 'expert', 'tensor'), may hold values from -0.125 to 0.125
- w_output: bfloat16 [2, 4096, 2048], P('section', 'tensor', 'expert'), may hold values from -0.5 to 0.5
- w_gate: bfloat16 [2, 16, 768, 2048], P('section', 'expert', 'tensor'), may hold values from -0.125 to 0.125
- w_up: bfloat16 [2, 16, 768, 2048], P('section', 'expert', 'tensor'), may hold values from -0.125 to 0.125
- w_down: bfloat16 [2, 16, 768, 2048], P('section', 'expert', 'tensor'), may hold values from -0.4375 to 0.4375
Outputs:
- ends: bfloat16 [2, 2, 512, 2048], P('section', None, 'expert')
- grad_attn_gain: float32 [2, 2048], P('section')
- grad_moe_gain: float32 [2, 2048], P('section')
- grad_query_gain: float32 [2, 128], P('section')
- grad_key_gain: float32 [2, 128], P('section')
- grad_w_query: float32 [2, 2048, 4096], P('section', 'expert', 'tensor')
- grad_w_key: float32 [2, 2048, 512], P('section', 'expert', 'tensor')
- grad_w_value: float32 [2, 2048, 512], P('section', 'expert', 'tensor')
- grad_w_output: float32 [2, 4096, 2048], P('section', 'tensor', 'expert')
- grad_w_gate: float32 [2, 16, 768, 2048], P('section', 'expert', 'tensor')
- grad_w_up: float32 [2, 16, 768, 2048], P('section', 'expert', 'tensor')
- grad_w_down: float32 [2, 16, 768, 2048], P('section', 'expert', 'tensor')
The draws below stay inside these ranges and needn't reach their ends.
Inputs may be any that keep to these rules, and one draw needn't show every extreme that they name: `expert_ids`: within the 128 rows of one block (one layer, micro-batch and index of the expert axis), no expert is named by more than 96 tokens, a bound that some block reaches. `seq_lengths`: each row sums to 128; the longest sequence of each row has exactly 64 tokens.
All inputs are finite; a program needn't handle non-finite values.
Results may differ from the reference program's by a relative error of at most 0.03.
Values may be sent and summed in bfloat16 or wider, within the bound.
A program may use at most 256 MiB of HBM per device.

```python
import math
import jax
import jax.numpy as jnp
import numpy as np
from jax import lax

MODEL_DIM = 2048
QUERY_HEADS = 32
KEY_VALUE_HEADS = 4
HEAD_DIM = 128
FE = 768
TOPK = 8
MB = 2
NSEQ = 4
MICRO_TOKENS = 128
EXPERTS = 16
TOKENS = 512
SEQ_MOST = 64
CAP = 96
N_SECTION = 2
N_EXPERT = 4


def level_of(rng, shape, cuts, smallest, high):
    factor_of, own = 1.0, jax.random.fold_in(rng, 6)
    for axis_at, blocks in cuts:
        steps = jnp.exp(jax.random.uniform(jax.random.fold_in(own, axis_at), (blocks,), jnp.float32, smallest / len(cuts), high / len(cuts)))
        factor_of = factor_of * jnp.repeat(steps, shape[axis_at] // blocks).reshape([-1 if axis == axis_at else 1 for axis in range(len(shape))])
    return factor_of


def profile(count, total, limit, lean):
    weights = [(1 << 20) // math.isqrt(standing ** lean) + 1 for standing in range(2, count + 1)]
    rest, given = total - limit - (count - 1), [1] * (count - 1)
    while rest > 0:
        movable = [i for i in range(count - 1) if given[i] < limit]
        mass, remaining = sum([weights[i] for i in movable]), rest
        for i in movable:
            more = min(limit - given[i], max(1, remaining * weights[i] // mass), rest)
            given[i] = given[i] + more
            rest = rest - more
    return np.array([limit] + given)


def uneven_parts(own_key, amount, total, most, lean):
    if amount == 2:
        one = jax.random.randint(own_key, (), max(1, total - most), min(most, total - 1) + 1)
        return jnp.stack([one, total - one])
    sizes = jnp.asarray(profile(amount, total, most, lean), jnp.int32)
    twos = (amount - 1) // 2
    source_of, receiver = sizes[1:1 + 2 * twos:2], sizes[2:2 + 2 * twos:2]
    slack = jnp.minimum(source_of - 1, most - receiver)
    moved = jax.random.randint(jax.random.fold_in(own_key, 1), (twos,), 0, 1 << 20) % (slack + 1)
    sizes = sizes.at[1:1 + 2 * twos:2].set(source_of - moved).at[2:2 + 2 * twos:2].set(receiver + moved)
    return sizes[jax.random.permutation(jax.random.fold_in(own_key, 2), amount)]


def shared_out(key, own, number, rows, amount, top, reach, slope):
    order = jax.random.permutation(key, amount)
    crowded, usual = portions_of(amount, rows * top, reach, slope, True), portions_of(amount, rows * top, reach, slope, False)
    places = jnp.arange(amount)

    def named(tallies, turn):
        used = int((tallies > 0).sum())
        fixed = max(1, used // 4)
        moved = fixed + (places - fixed + turn * (used - fixed)) % max(1, amount - fixed)
        return jnp.zeros((amount,), jnp.int32).at[order[jnp.where(places < fixed, places, moved)]].set(jnp.asarray(tallies, jnp.int32))

    tallies = jnp.where(number % 4 == 0, named(crowded, number // 4), named(usual, number - number // 4 - 1))
    mixed = jax.random.permutation(jax.random.fold_in(own, 3), amount)
    donor, sink = mixed[0:amount // 2 * 2:2], mixed[1:amount // 2 * 2:2]
    room = jnp.minimum(tallies[donor] - 1, reach - tallies[sink]) // 2
    room = jnp.where((donor == order[0]) | (sink == order[0]) | (tallies[sink] == 0), 0, jnp.maximum(room, 0))
    moved = jax.random.randint(jax.random.fold_in(own, 4), (amount // 2,), 0, 1 << 20) % (room + 1)
    tallies = tallies.at[donor].add(-moved).at[sink].add(moved)
    items = jnp.searchsorted(jnp.cumsum(tallies), jnp.arange(rows * top), side="right").astype(jnp.int32)
    listing = items.reshape(top, rows).T
    listing = listing[jax.random.permutation(jax.random.fold_in(own, 1), rows)]
    turn = jax.random.randint(jax.random.fold_in(own, 2), (rows, 1), 0, top)
    return jnp.take_along_axis(listing, (jnp.arange(top)[None, :] + turn) % top, axis=1)


def portions_of(number_of, total, reach, lean, full):
    loads = [(1 << 20) // math.isqrt(standing ** lean) + 1 for standing in range(1, number_of + 1)]
    largest = reach if full else min(reach, max(-(-total // number_of), total * loads[0] // sum(loads)))
    least = 1 if total - largest >= number_of - 1 else 0
    counts, rest = [largest] + [least] * (number_of - 1), total - largest - least * (number_of - 1)
    while rest > 0:
        candidates = [i for i in range(1, number_of) if counts[i] < largest] or [i for i in range(1, number_of) if counts[i] < reach]
        whole, budget = sum([loads[i] for i in candidates]), rest
        for i in candidates:
            extra = min(reach - counts[i], max(1, budget * loads[i] // whole), rest)
            counts[i] = counts[i] + extra
            rest = rest - extra
    return np.array(counts)


def bell_draw(own_key, dims, scale, bound, split=(), kind=jnp.bfloat16):
    values = scale * jax.random.normal(own_key, dims, jnp.float32)
    if split:
        values = values * level_of(own_key, dims, split, -0.22, 0.18)
    return jnp.clip(values, -bound, bound).astype(kind)


def setup_inputs(seed: int = 0) -> dict:
    arg_keys = jax.random.split(jax.random.key(seed), 16)
    boundary = bell_draw(arg_keys[0], (N_SECTION, MB, TOKENS, MODEL_DIM), 1.0, 6.0, ((0, 2), (2, 4)))
    seq_lengths = jax.vmap(lambda own: uneven_parts(own, NSEQ, MICRO_TOKENS, SEQ_MOST, 2))(jax.random.split(arg_keys[1], N_SECTION * MB * N_EXPERT)).reshape((N_SECTION, MB, N_EXPERT, NSEQ)).astype(jnp.int32)
    expert_ids_keys = jax.random.split(jax.random.fold_in(arg_keys[2], 1), N_SECTION * MB * TOKENS // MICRO_TOKENS)
    expert_ids_turns = jax.random.permutation(jax.random.fold_in(arg_keys[2], 3), N_SECTION * MB * TOKENS // MICRO_TOKENS)
    expert_ids = jax.vmap(lambda own, number: shared_out(jax.random.fold_in(arg_keys[2], 2), own, number, MICRO_TOKENS, EXPERTS, TOPK, CAP, 2))(expert_ids_keys, expert_ids_turns).reshape((N_SECTION, MB, TOKENS, TOPK))
    route_weights = jnp.clip(jnp.exp(math.log(0.4) - 1.3862944 * jax.random.uniform(arg_keys[3], (N_SECTION, MB, TOKENS, TOPK), jnp.float32) ** level_of(arg_keys[3], (N_SECTION, MB, TOKENS, TOPK), ((0, 2), (2, 4)), -0.2, 0.2)), 0.1, 0.4)
    attn_gain = jnp.clip(1.0 + 0.15 * jax.random.normal(arg_keys[4], (N_SECTION, MODEL_DIM), jnp.float32), 0.25, 1.75)
    moe_gain = jnp.clip(1.0 + 0.15 * jax.random.normal(arg_keys[5], (N_SECTION, MODEL_DIM), jnp.float32), 0.25, 1.75)
    query_gain = jnp.clip(1.0 + 0.15 * jax.random.normal(arg_keys[6], (N_SECTION, HEAD_DIM), jnp.float32), 0.25, 1.75)
    key_norm_gain = jnp.clip(1.0 + 0.15 * jax.random.normal(arg_keys[7], (N_SECTION, HEAD_DIM), jnp.float32), 0.25, 1.75)
    w_query = bell_draw(arg_keys[8], (N_SECTION, MODEL_DIM, QUERY_HEADS * HEAD_DIM), MODEL_DIM ** -0.5, 0.125, ((0, 2), (1, 4), (2, 4)))
    key_weight = bell_draw(arg_keys[9], (N_SECTION, MODEL_DIM, KEY_VALUE_HEADS * HEAD_DIM), MODEL_DIM ** -0.5, 0.125, ((0, 2), (1, 4), (2, 4)))
    value_weight = bell_draw(arg_keys[10], (N_SECTION, MODEL_DIM, KEY_VALUE_HEADS * HEAD_DIM), MODEL_DIM ** -0.5, 0.125, ((0, 2), (1, 4), (2, 4)))
    w_output = bell_draw(arg_keys[11], (N_SECTION, QUERY_HEADS * HEAD_DIM, MODEL_DIM), (max(QUERY_HEADS * HEAD_DIM // 32, 32)) ** -0.5, 0.5, ((0, 2), (1, 4), (2, 4)))
    w_gate = bell_draw(arg_keys[12], (N_SECTION, EXPERTS, FE, MODEL_DIM), MODEL_DIM ** -0.5, 0.125, ((0, 2), (1, 4), (2, 4)))
    w_up = bell_draw(arg_keys[13], (N_SECTION, EXPERTS, FE, MODEL_DIM), MODEL_DIM ** -0.5, 0.125, ((0, 2), (1, 4), (2, 4)))
    w_down = bell_draw(arg_keys[14], (N_SECTION, EXPERTS, FE, MODEL_DIM), (FE // 4) ** -0.5, 0.4375, ((0, 2), (1, 4), (2, 4)))
    return {"boundary": boundary, "seq_lengths": seq_lengths, "expert_ids": expert_ids, "route_weights": route_weights, "attn_gain": attn_gain, "moe_gain": moe_gain, "query_gain": query_gain, "key_norm_gain": key_norm_gain, "w_query": w_query, "key_weight": key_weight, "value_weight": value_weight, "w_output": w_output, "w_gate": w_gate, "w_up": w_up, "w_down": w_down}


EPSILON = 1e-06
THETA = 1000000.0
HIGHEST = lax.Precision.HIGHEST

@jax.custom_vjp
def low(v):
    return lax.optimization_barrier(v.astype(jnp.bfloat16)).astype(jnp.float32)

@jax.custom_vjp
def low_back(v):
    return v

def low_keep(v):
    return (low(v), None)

def low_pass(kept, grad):
    return (grad,)

def back_keep(v):
    return (v, None)

def back_low(kept, grad):
    return (low(grad),)
low.defvjp(low_keep, low_pass)
low_back.defvjp(back_keep, back_low)

def root_mean_scale(value_rows, gain):
    return value_rows * lax.rsqrt(lax.optimization_barrier(jnp.mean(value_rows * value_rows, axis=-1, keepdims=True)) + EPSILON) * gain

def rotate_half(value_rows):
    middle = value_rows.shape[-1] // 2
    return jnp.concatenate([-value_rows[..., middle:], value_rows[..., :middle]], axis=-1)

def rope_tables(places, head_size):
    steps_half = jnp.arange(head_size // 2, dtype=jnp.float32)
    inverse = jnp.exp(steps_half * (-2.0 * math.log(THETA) / head_size))
    angle_table = places.astype(jnp.float32)[:, None] * inverse[None, :]
    angle_table = jnp.concatenate([angle_table, angle_table], axis=-1)
    return (jnp.cos(angle_table), jnp.sin(angle_table))

def block_layout(seq_lengths, row_count):
    seq_ends = jnp.cumsum(seq_lengths).astype(jnp.int32)
    seq_starts = seq_ends - seq_lengths
    places = jnp.arange(row_count, dtype=jnp.int32)
    segment = lax.optimization_barrier(jnp.sum((places[:, None] >= seq_ends[None, :]).astype(jnp.int32), axis=1)).astype(jnp.int32)
    numbers = jnp.arange(seq_lengths.shape[0], dtype=jnp.int32)
    offset = lax.optimization_barrier(jnp.sum(jnp.where(segment[:, None] == numbers[None, :], seq_starts[None, :], 0), axis=1)).astype(jnp.int32)
    return (segment, places - offset)

def route_slots(expert_rows, expert_count, capacity):
    flat_ids = expert_rows.reshape(-1)
    numbers = jnp.arange(expert_count, dtype=jnp.int32)
    onehot = (flat_ids[:, None] == numbers[None, :]).astype(jnp.int32)
    earlier = (jnp.cumsum(onehot, axis=0) - onehot).astype(jnp.int32)
    return (flat_ids * capacity + lax.optimization_barrier(jnp.sum(earlier * onehot, axis=1))).astype(jnp.int32)

def attend(query_rows, heads_key, value_rows, segment):
    score_scale = 1.0 / math.sqrt(query_rows.shape[-1])
    scores = low_back(jnp.einsum('tgjd,sgd->gjts', query_rows, heads_key, precision=HIGHEST) * score_scale)
    places = jnp.arange(segment.shape[0], dtype=jnp.int32)
    allowed = (segment[:, None] == segment[None, :]) & (places[None, :] <= places[:, None])
    scores = jnp.where(allowed, scores, -1e+30)
    weights = low(jax.nn.softmax(scores, axis=-1))
    return jnp.einsum('gjts,sgd->tgjd', weights, value_rows, precision=HIGHEST)

def expert_ffn(rows_in, weight_gate, weight_up, weight_down):
    gate_pre = low_back(jnp.dot(rows_in, weight_gate.T, precision=HIGHEST))
    up_pre = low_back(jnp.dot(rows_in, weight_up.T, precision=HIGHEST))
    hidden = low(jax.nn.silu(gate_pre) * up_pre)
    return low_back(jnp.dot(hidden, weight_down, precision=HIGHEST))

def layer(params, hidden_in, seq_lengths, expert_rows, route_weights):
    attn_gain, moe_gain, query_gain, key_norm_gain, w_query, key_weight, value_weight, w_output, w_gate, w_up, w_down = params
    count_tokens = hidden_in.shape[0]
    segment, places = jax.vmap(lambda length_row: block_layout(length_row, MICRO_TOKENS))(seq_lengths)
    cosine, sine_table = rope_tables(places.reshape(-1), HEAD_DIM)
    normed = low(root_mean_scale(hidden_in, attn_gain))
    query_rows = low_back(jnp.dot(normed, w_query, precision=HIGHEST))
    heads_key = low_back(jnp.dot(normed, key_weight, precision=HIGHEST))
    value_rows = low(low_back(jnp.dot(normed, value_weight, precision=HIGHEST)))
    query_rows = root_mean_scale(query_rows.reshape(count_tokens, QUERY_HEADS, HEAD_DIM), query_gain)
    heads_key = root_mean_scale(heads_key.reshape(count_tokens, KEY_VALUE_HEADS, HEAD_DIM), key_norm_gain)
    query_rows = low(query_rows * cosine[:, None, :] + rotate_half(query_rows) * sine_table[:, None, :])
    heads_key = low(heads_key * cosine[:, None, :] + rotate_half(heads_key) * sine_table[:, None, :])
    query_blocks = query_rows.reshape(N_EXPERT, MICRO_TOKENS, KEY_VALUE_HEADS, QUERY_HEADS // KEY_VALUE_HEADS, HEAD_DIM)
    key_blocks = heads_key.reshape(N_EXPERT, MICRO_TOKENS, KEY_VALUE_HEADS, HEAD_DIM)
    value_blocks = value_rows.reshape(N_EXPERT, MICRO_TOKENS, KEY_VALUE_HEADS, HEAD_DIM)
    attended = lax.map(jax.checkpoint(lambda members: attend(members[0], members[1], members[2], members[3])), (query_blocks, key_blocks, value_blocks, segment))
    mixed_heads = low(low_back(attended.reshape(count_tokens, QUERY_HEADS * HEAD_DIM)))
    after_attn = hidden_in + low_back(jnp.dot(mixed_heads, w_output, precision=HIGHEST))
    moe_in = low(root_mean_scale(after_attn, moe_gain))
    local_slots = jax.vmap(lambda block_ids: route_slots(block_ids, EXPERTS, CAP))(expert_rows.reshape(N_EXPERT, MICRO_TOKENS, TOPK))
    owner_index = jnp.arange(N_EXPERT, dtype=jnp.int32)[:, None]
    slot_spots = (local_slots // CAP * (N_EXPERT * CAP) + owner_index * CAP + local_slots % CAP).reshape(-1).astype(jnp.int32)
    route_count = slot_spots.shape[0]
    slot_table = jnp.full((EXPERTS * N_EXPERT * CAP,), count_tokens, jnp.int32).at[slot_spots].set(jnp.arange(route_count, dtype=jnp.int32) // TOPK)
    padded = jnp.concatenate([moe_in, jnp.zeros((1, moe_in.shape[1]), moe_in.dtype)], axis=0)
    expert_in = padded[slot_table].reshape(EXPERTS, N_EXPERT * CAP, moe_in.shape[1])
    expert_out = lax.map(jax.checkpoint(lambda members: expert_ffn(members[0], members[1], members[2], members[3])), (expert_in, w_gate, w_up, w_down))
    routed = expert_out.reshape(EXPERTS * N_EXPERT * CAP, -1)[slot_spots].reshape(count_tokens, TOPK, -1)
    return after_attn + lax.optimization_barrier(jnp.sum(route_weights[:, :, None] * routed, axis=1))

def reference(boundary, seq_lengths, expert_ids, route_weights, attn_gain, moe_gain, query_gain, key_norm_gain, w_query, key_weight, value_weight, w_output, w_gate, w_up, w_down):
    inputs = boundary[0].astype(jnp.float32)
    cotangent = boundary[1].astype(jnp.float32)
    params = (attn_gain, moe_gain, query_gain, key_norm_gain) + tuple((weight.astype(jnp.float32) for weight in (w_query, key_weight, value_weight, w_output, w_gate, w_up, w_down)))

    def forward(params, inputs):
        finals = []
        for micro_index in range(MB):
            hidden = inputs[micro_index]
            for section_index in range(N_SECTION):
                section_params = tuple((parameter[section_index] for parameter in params))
                hidden = layer(section_params, hidden, seq_lengths[section_index, micro_index], expert_ids[section_index, micro_index], route_weights[section_index, micro_index])
                if section_index + 1 < N_SECTION:
                    hidden = low(low_back(hidden))
            finals.append(hidden)
        return jnp.stack(finals)
    outputs, pullback = jax.vjp(forward, params, inputs)
    grad_params, grad_inputs = pullback(cotangent)
    ends = jnp.stack([grad_inputs, outputs]).astype(jnp.bfloat16)
    return (ends, grad_params[0], grad_params[1], grad_params[2], grad_params[3], grad_params[4], grad_params[5], grad_params[6], grad_params[7], grad_params[8], grad_params[9], grad_params[10])
```

```python
import functools
import math

import jax
import jax.numpy as jnp
from jax import lax
from jax.experimental import pallas as pl
from jax.experimental.pallas import tpu as pltpu
from jax.sharding import PartitionSpec as P

EPSILON = 1e-06
THETA = 1000000.0
LANES = 128
TERM_ROWS = 24
TERM_COLS = 256
MESH = pl.DeviceIdType.MESH
F32 = jnp.float32
BF16 = jnp.bfloat16
VMEM_LIMIT = 60 * 1024 * 1024

ANY = pl.BlockSpec(memory_space=pl.ANY)
VM = pl.BlockSpec(memory_space=pltpu.VMEM)


def partner(index, k, count):
    out, bit = 0, 1
    while bit < count:
        out = out + bit * lax.rem(lax.div(index, bit) + lax.div(k, bit), 2)
        bit *= 2
    return out


def rows_at(start, size):
    return pl.ds(pl.multiple_of(start, size), size)


def remote(src, dst, send_sem, recv_sem, **where):
    return pltpu.make_async_remote_copy(
        src_ref=src,
        dst_ref=dst,
        send_sem=send_sem,
        recv_sem=recv_sem,
        device_id=where,
        device_id_type=MESH,
    )


def greet(peers):
    barrier = pltpu.get_barrier_semaphore()
    for where in peers:
        pl.semaphore_signal(barrier, inc=1, device_id=where, device_id_type=MESH)
    pl.semaphore_wait(barrier, len(peers))


def layer_peers(z, t, nz, nt):
    i32 = jnp.int32
    peers = [{"expert": partner(z, i32(k), nz)} for k in range(1, nz)]
    peers += [{"tensor": partner(t, i32(k), nt)} for k in range(1, nt)]
    return peers


def dot(a, b):
    return lax.dot_general(a, b, (((1,), (0,)), ((), ())), preferred_element_type=F32)


def dot_nt(a, b):
    return lax.dot_general(a, b, (((1,), (1,)), ((), ())), preferred_element_type=F32)


def dot_tn(a, b):
    return lax.dot_general(a, b, (((0,), (0,)), ((), ())), preferred_element_type=F32)


def unit_rows(value):
    factor = lax.rsqrt(jnp.mean(value * value, axis=-1, keepdims=True) + EPSILON)
    return value * factor, factor


def norm_back(grad, gain, unit, factor):
    weighted = grad * gain
    inner = jnp.mean(weighted * unit, axis=-1, keepdims=True)
    return factor * (weighted - unit * inner), jnp.sum(grad * unit, axis=0, keepdims=True)


def expert_gates(gate_rows, first_expert, local_experts, width):
    rows = gate_rows.shape[0]
    lane = lax.broadcasted_iota(jnp.int32, gate_rows.shape, 1)
    column = lax.broadcasted_iota(jnp.int32, (rows, local_experts * width), 1)
    out = None
    for e in range(local_experts):
        one = jnp.sum(jnp.where(lane == first_expert + e, gate_rows, 0.0), axis=1, keepdims=True)
        wide = jnp.broadcast_to(one, column.shape)
        out = wide if out is None else jnp.where(column >= e * width, wide, out)
    return out


def write_terms(terms_ref, row, vector):
    for i in range(vector.shape[1] // TERM_COLS):
        terms_ref[row + i : row + i + 1, :] = vector[:, i * TERM_COLS : (i + 1) * TERM_COLS]


def exchange_sems(nz, nt):
    dma = pltpu.SemaphoreType.DMA
    return [dma((nz,)), dma((nz,)), dma((nz, nt)), dma((nz, nt))] * 2 + [dma((nt,)), dma((nt,))]


def exchange_scratch(nz, nt, rows, block, width):
    return [
        pltpu.VMEM((nz, block, width), BF16),
        pltpu.VMEM((nz, block, width), BF16),
        pltpu.VMEM((block, width), F32),
        pltpu.VMEM((nz, nt, rows, width), BF16),
        pltpu.VMEM((nz, rows, width), BF16),
        pltpu.VMEM((nz, rows, width), BF16),
        pltpu.VMEM((rows, width), F32),
        pltpu.VMEM((block, width), BF16),
    ] + exchange_sems(nz, nt)


def exchange(z, t, nz, nt, rows, own_rows, scratch, ready, work):
    (full, outgoing, part, came_near, passed, came_far, total, _) = scratch[:8]
    (gz_send, gz_recv, gt_send, gt_recv, rz_send, rz_recv, rt_send, rt_recv) = scratch[8:16]
    i32 = jnp.int32
    mine = rows_at(t * rows, rows)

    def far_copy(k):
        return remote(
            full.at[z, mine],
            full.at[z, mine],
            gz_send.at[k],
            gz_recv.at[k],
            expert=partner(z, i32(k), nz),
        )

    def near_copy(k, source, j):
        return remote(
            full.at[source, mine],
            full.at[source, mine],
            gt_send.at[k, j],
            gt_recv.at[k, j],
            tensor=partner(t, i32(j), nt),
        )

    def near_arrival(k, source, j):
        theirs = rows_at(partner(t, i32(j), nt) * rows, rows)
        return remote(
            full.at[source, theirs],
            full.at[source, theirs],
            gt_send.at[k, j],
            gt_recv.at[k, j],
            tensor=partner(t, i32(j), nt),
        )

    def far_arrival(k):
        source = partner(z, i32(k), nz)
        return remote(
            full.at[source, mine],
            full.at[source, mine],
            gz_send.at[k],
            gz_recv.at[k],
            expert=source,
        )

    def part_copy(k, j):
        peer = partner(t, i32(j), nt)
        return remote(
            outgoing.at[k, rows_at(peer * rows, rows)],
            came_near.at[k, j],
            rt_send.at[k, j],
            rt_recv.at[k, j],
            tensor=peer,
        )

    def sum_copy(k):
        return remote(
            passed.at[k],
            came_far.at[k],
            rz_send.at[k],
            rz_recv.at[k],
            expert=partner(z, k, nz),
        )

    full[z, mine] = own_rows
    for k in range(1, nz):
        far_copy(k).start()
    for j in range(1, nt):
        near_copy(0, z, j).start()

    ready()

    def produce(k, source):
        for j in range(1, nt):
            near_arrival(k, source, j).wait_recv()
        part[...] = work(k, source, full[source])
        outgoing[k] = part[...].astype(BF16)
        for j in range(1, nt):
            part_copy(k, j).start()
        return part[mine]

    def collect(k):
        out = passed_own[k]
        for j in range(1, nt):
            part_copy(k, j).wait_recv()
            out = out + came_near[k, j].astype(F32)
        return out

    passed_own = scratch[18]
    passed_own[0] = produce(i32(0), z)
    for k in range(1, nz):
        far_arrival(k).wait_recv()
        for j in range(1, nt):
            near_copy(k, partner(z, i32(k), nz), j).start()

    def step(k, carry):
        passed_own[k] = produce(k, partner(z, k, nz))

        @pl.when(k >= 2)
        def _():
            passed[k - 1] = collect(k - 1).astype(BF16)
            sum_copy(k - 1).start()

        return carry

    lax.fori_loop(1, nz, step, 0)
    passed[nz - 1] = collect(nz - 1).astype(BF16)
    sum_copy(i32(nz - 1)).start()
    total[...] = collect(0)
    for k in range(1, nz):
        sum_copy(i32(k)).wait_recv()
        total[...] += came_far[k].astype(F32)

    def finish():
        for k in range(1, nz):
            far_copy(k).wait_send()
            sum_copy(i32(k)).wait_send()
        for k in range(nz):
            source = partner(z, i32(k), nz)
            for j in range(1, nt):
                near_copy(k, source, j).wait_send()
                part_copy(k, j).wait_send()

    return finish


def spread_rows(t, nt, rows, block_ref, send_sem, recv_sem):
    i32 = jnp.int32
    mine = rows_at(t * rows, rows)
    for j in range(1, nt):
        remote(
            block_ref.at[mine],
            block_ref.at[mine],
            send_sem.at[j],
            recv_sem.at[j],
            tensor=partner(t, i32(j), nt),
        ).start()

    def wait():
        for j in range(1, nt):
            peer = partner(t, i32(j), nt)
            theirs = rows_at(peer * rows, rows)
            copy = remote(
                block_ref.at[theirs],
                block_ref.at[theirs],
                send_sem.at[j],
                recv_sem.at[j],
                tensor=peer,
            )
            copy.wait_send()
            copy.wait_recv()

    return wait


def reduce_rows(t, nt, rows, part, outgoing, came, send_sem, recv_sem):
    i32 = jnp.int32
    outgoing[...] = part[...].astype(BF16)

    def copy(j):
        peer = partner(t, i32(j), nt)
        return remote(
            outgoing.at[rows_at(peer * rows, rows)],
            came.at[j],
            send_sem.at[j],
            recv_sem.at[j],
            tensor=peer,
        )

    for j in range(1, nt):
        copy(j).start()
    total = part[rows_at(t * rows, rows)]
    for j in range(1, nt):
        copy(j).wait_recv()
        total = total + came[j].astype(F32)
    for j in range(1, nt):
        copy(j).wait_send()
    return total


def start_kernel(
    nz, nt, boundary, tabs, gates, gains, wq, wk, wv, wo, wg, wu, wd,
    ends_out, tabs_out, gates_out, gains_out, wq_out, wk_out, wv_out, wo_out, sg_out, su_out, sd_out,
    own_sem, sib_send, sib_recv, gate_send, gate_recv,
    right_send, right_recv, left_send, left_recv, pass_send, pass_recv,
):
    s, z = lax.axis_index("section"), lax.axis_index("expert")
    other = 1 - s
    i32 = jnp.int32
    peers = [{"section": other}]
    for k in range(1, nz):
        zz = partner(z, i32(k), nz)
        peers += [{"expert": zz}, {"section": other, "expert": zz}]

    shard_in, shard_out = (wq, wk, wv, wo), (wq_out, wk_out, wv_out, wo_out)

    def place(a, layer, owner):
        out = shard_out[a]
        if a < 3:
            size = shard_in[a].shape[0]
            return out.at[layer, rows_at(owner * size, size)]
        size = shard_in[a].shape[1]
        return out.at[layer, :, rows_at(owner * size, size)]

    count = len(shard_in)
    own = [pltpu.make_async_copy(shard_in[a], place(a, s, z), own_sem.at[a]) for a in range(count)]
    own += [
        pltpu.make_async_copy(boundary.at[s], ends_out.at[s], own_sem.at[4]),
        pltpu.make_async_copy(tabs.at[s], tabs_out.at[s], own_sem.at[5]),
        pltpu.make_async_copy(gates.at[s], gates_out.at[s, z], own_sem.at[6]),
        pltpu.make_async_copy(gains, gains_out.at[s], own_sem.at[7]),
    ]
    for copy in own:
        copy.start()
    greet(peers)

    def hop(a, owner, step, right, src=None):
        spot = place(a, s, owner)
        sends, recvs = (right_send, right_recv) if right else (left_send, left_recv)
        target = z + 1 if right else z - 1
        return remote(
            spot if src is None else src, spot, sends.at[a, step], recvs.at[a, step], expert=target
        )

    def hand(a, owner, src=None):
        spot = place(a, s, owner)
        return remote(
            spot if src is None else src,
            spot,
            pass_send.at[a, owner],
            pass_recv.at[a, owner],
            section=other,
        )

    def handed(a, owner):
        spot = place(a, other, owner)
        return remote(spot, spot, pass_send.at[a, owner], pass_recv.at[a, owner], section=other)

    for a in range(count):

        @pl.when(z + 1 < nz)
        def _():
            hop(a, z, 1, True, shard_in[a]).start()

        @pl.when(z >= 1)
        def _():
            hop(a, z, 1, False, shard_in[a]).start()

        hand(a, z, shard_in[a]).start()

    sib = [
        remote(boundary.at[other], ends_out.at[s], sib_send.at[0], sib_recv.at[0], section=other),
        remote(tabs.at[other], tabs_out.at[s], sib_send.at[1], sib_recv.at[1], section=other),
        remote(gains, gains_out.at[s], sib_send.at[2], sib_recv.at[2], section=other),
        remote(wg, sg_out, sib_send.at[3], sib_recv.at[3], section=other),
        remote(wu, su_out, sib_send.at[4], sib_recv.at[4], section=other),
        remote(wd, sd_out, sib_send.at[5], sib_recv.at[5], section=other),
    ]
    for copy in sib:
        copy.start()

    def gate_copy(d, k):
        zz = partner(z, i32(k), nz)
        section = s if d == 0 else other
        return remote(
            gates.at[section],
            gates_out.at[s, z],
            gate_send.at[d, k],
            gate_recv.at[d, k],
            section=section,
            expert=zz,
        )

    def gate_arrival(d, k):
        zz = partner(z, i32(k), nz)
        section = s if d == 0 else other
        return remote(
            gates.at[section],
            gates_out.at[section, zz],
            gate_send.at[d, k],
            gate_recv.at[d, k],
            section=section,
            expert=zz,
        )

    for d in range(2):
        for k in range(nz):
            if d or k:
                gate_copy(d, k).start()

    for step in range(1, nz):
        for a in range(count):

            @pl.when(z >= step)
            def _():
                hop(a, z - step, step, True).wait_recv()
                hand(a, z - step).start()

            @pl.when((z >= step) & (z + 1 < nz))
            def _():
                hop(a, z - step, step + 1, True).start()

            @pl.when(z + step < nz)
            def _():
                hop(a, z + step, step, False).wait_recv()
                hand(a, z + step).start()

            @pl.when((z + step < nz) & (z >= 1))
            def _():
                hop(a, z + step, step + 1, False).start()

    for copy in own:
        copy.wait()
    for i, copy in enumerate(sib):
        copy.wait_send()
    sib_in = [
        remote(boundary.at[other], ends_out.at[other], sib_send.at[0], sib_recv.at[0], section=other),
        remote(tabs.at[other], tabs_out.at[other], sib_send.at[1], sib_recv.at[1], section=other),
        remote(gains, gains_out.at[other], sib_send.at[2], sib_recv.at[2], section=other),
    ] + sib[3:]
    for copy in sib_in:
        copy.wait_recv()
    for d in range(2):
        for k in range(nz):
            if d or k:
                gate_copy(d, k).wait_send()
                gate_arrival(d, k).wait_recv()
    for a in range(count):
        for owner in range(nz):
            hand(a, owner).wait_send()
            handed(a, owner).wait_recv()
        for step in range(1, nz):

            @pl.when((z >= step - 1) & (z + 1 < nz))
            def _():
                hop(a, z - (step - 1), step, True).wait_send()

            @pl.when((z + step - 1 < nz) & (z >= 1))
            def _():
                hop(a, z + (step - 1), step, False).wait_send()


def heads_to_rows(value, heads, size):
    return jnp.concatenate([value[:, h * size : (h + 1) * size] for h in range(heads)], axis=0)


def rows_to_heads(value, heads, block):
    return jnp.concatenate([value[h * block : (h + 1) * block] for h in range(heads)], axis=1)


def split_gains(gains, layer, width, size):
    row = gains[layer]
    return (
        row[:, :width],
        row[:, width : 2 * width],
        row[:, 2 * width : 2 * width + size],
        row[:, 2 * width + size :],
    )


def tiled(value, times):
    return jnp.concatenate([value] * times, axis=0)


def half_turn(value):
    return pltpu.roll(value, value.shape[-1] // 2, value.ndim - 1)


def attend_kernel(
    layer, source, nz, nt, heads,
    x_ref, tabs, gains, wq, wk, wv, wo,
    h1_ref, b_ref, a_ref, q_ref, k_ref, v_ref, qr_ref, kr_ref, o_ref,
    wq_s, wk_s, wv_s, wo_s, part, outgoing, came, w_sem, s_sem, r_sem,
):
    z, t = lax.axis_index("expert"), lax.axis_index("tensor")
    loads = [
        pltpu.make_async_copy(src.at[layer], dst, w_sem.at[i])
        for i, (src, dst) in enumerate(((wq, wq_s), (wk, wk_s), (wv, wv_s), (wo, wo_s)))
    ]
    for load in loads:
        load.start()
    i32 = jnp.int32
    greet([{"tensor": partner(t, i32(j), nt)} for j in range(1, nt)])

    block = x_ref.shape[1]
    rows = block // nt
    size = tabs.shape[-1]
    g_attn, g_moe, g_query, g_key = split_gains(gains, layer, x_ref.shape[2], size)
    cos, sin, bias = tabs[layer, 0], tabs[layer, 1], tabs[layer, 2]
    unit, _ = unit_rows(x_ref[source].astype(F32))
    a_ref[...] = (unit * g_attn).astype(BF16)
    loads[0].wait()
    q = dot(a_ref[...], wq_s[...])
    q_ref[...] = q
    loads[1].wait()
    loads[2].wait()
    k = dot(a_ref[...], wk_s[...])
    k_ref[...] = k
    v = dot(a_ref[...], wv_s[...]).astype(BF16)
    v_ref[...] = v
    qn = unit_rows(heads_to_rows(q, heads, size))[0] * g_query
    kn = unit_rows(k)[0] * g_key
    qr = (qn * tiled(cos, heads) + half_turn(qn) * tiled(sin, heads)).astype(BF16)
    kr = (kn * cos + half_turn(kn) * sin).astype(BF16)
    qr_ref[...] = qr
    kr_ref[...] = kr
    scores = dot_nt(qr, kr) * (1.0 / math.sqrt(size)) + tiled(bias, heads)
    peak = jnp.max(scores, axis=-1, keepdims=True)
    weight = jnp.exp(scores - peak)
    probs = weight * (1.0 / jnp.sum(weight, axis=-1, keepdims=True))
    o = dot(probs.astype(BF16), v).astype(BF16)
    o_ref[...] = rows_to_heads(o, heads, block)
    loads[3].wait()
    part[...] = dot(o_ref[...], wo_s[...])
    total = reduce_rows(t, nt, rows, part, outgoing, came, s_sem, r_sem)
    h1 = x_ref[source, rows_at(t * rows, rows)].astype(F32) + total
    h1_ref[...] = h1
    b_ref[...] = (unit_rows(h1)[0] * g_moe).astype(BF16)


def load_experts(layer, s, own, sibling, scratch, sems):
    def copies(refs):
        return [pltpu.make_async_copy(r, d, sems.at[i]) for i, (r, d) in enumerate(zip(refs, scratch))]

    @pl.when(s == layer)
    def _():
        for copy in copies(own):
            copy.start()

    @pl.when(s != layer)
    def _():
        for copy in copies(sibling):
            copy.start()

    return copies(own)


def experts_kernel(
    layer, nz, nt, local_experts,
    b_ref, h1_ref, gates, wg, wu, wd, sg, su, sd,
    y_ref, b_out, g_out, u_out,
    wg_s, wu_s, wd_s, g_s, u_s, w_sem, o_sem, own_part, *scratch,
):
    s, z, t = lax.axis_index("section"), lax.axis_index("expert"), lax.axis_index("tensor")
    rows = b_ref.shape[0]
    loads = load_experts(layer, s, (wg, wu, wd), (sg, su, sd), (wg_s, wu_s, wd_s), w_sem)
    greet(layer_peers(z, t, nz, nt))
    scratch = list(scratch) + [own_part]
    width = wg.shape[0] // local_experts

    def ready():
        for load in loads:
            load.wait()

    def work(k, origin, rows_in):
        gate_pre = dot_nt(rows_in, wg_s[...])
        up_pre = dot_nt(rows_in, wu_s[...])
        g_s[origin] = gate_pre
        u_s[origin] = up_pre
        weight = expert_gates(gates[layer, origin], z * local_experts, local_experts, width)
        hidden = (gate_pre * jax.nn.sigmoid(gate_pre) * up_pre * weight).astype(BF16)
        return dot(hidden, wd_s[...])

    finish = exchange(z, t, nz, nt, rows, b_ref[...], scratch, ready, work)
    full, total, whole = scratch[0], scratch[6], scratch[7]
    saves = [
        pltpu.make_async_copy(full, b_out, o_sem.at[0]),
        pltpu.make_async_copy(g_s, g_out, o_sem.at[1]),
        pltpu.make_async_copy(u_s, u_out, o_sem.at[2]),
    ]
    for save in saves:
        save.start()
    whole[rows_at(t * rows, rows)] = (h1_ref[...] + total[...]).astype(BF16)
    wait = spread_rows(t, nt, rows, whole, scratch[16], scratch[17])
    finish()
    wait()
    y_ref[0] = whole[...]
    for save in saves:
        save.wait()


def experts_back_kernel(
    layer, nz, nt, local_experts,
    dy_ref, h1_ref, gains, gates, g_in, u_in, wg, wu, wd, sg, su, sd,
    dat_ref, dh1_ref, term_ref, dy_out, hid_out, dg_out, du_out,
    wg_s, wu_s, wd_s, g_s, u_s, hid_s, dg_s, du_s, w_sem, g_sem, u_sem, o_sem, own_part, *scratch,
):
    s, z, t = lax.axis_index("section"), lax.axis_index("expert"), lax.axis_index("tensor")
    rows = dy_ref.shape[0]
    loads = load_experts(layer, s, (wd, wg, wu), (sd, sg, su), (wd_s, wg_s, wu_s), w_sem)

    def kept(k):
        origin, slot = partner(z, k, nz), lax.rem(k, 2)
        return (
            pltpu.make_async_copy(g_in.at[origin], g_s.at[slot], g_sem.at[slot]),
            pltpu.make_async_copy(u_in.at[origin], u_s.at[slot], u_sem.at[slot]),
        )

    for load in kept(jnp.int32(0)):
        load.start()
    greet(layer_peers(z, t, nz, nt))
    scratch = list(scratch) + [own_part]
    width = wg.shape[0] // local_experts

    def ready():
        for load in loads:
            load.wait()

    def work(k, origin, rows_in):
        for load in kept(k):
            load.wait()

        @pl.when(k + 1 < nz)
        def _():
            for load in kept(k + 1):
                load.start()

        slot = lax.rem(k, 2)
        gate_pre, up_pre = g_s[slot], u_s[slot]
        weight = expert_gates(gates[layer, origin], z * local_experts, local_experts, width)
        sigmoid = jax.nn.sigmoid(gate_pre)
        silu = gate_pre * sigmoid
        hid_s[origin] = (silu * up_pre * weight).astype(BF16)
        grad_hidden = dot_nt(rows_in, wd_s[...]) * weight
        dg_s[origin] = (grad_hidden * up_pre * sigmoid * (1.0 + gate_pre * (1.0 - sigmoid))).astype(BF16)
        du_s[origin] = (grad_hidden * silu).astype(BF16)
        return dot(dg_s[origin], wg_s[...]) + dot(du_s[origin], wu_s[...])

    finish = exchange(z, t, nz, nt, rows, dy_ref[...], scratch, ready, work)
    full, total, whole = scratch[0], scratch[6], scratch[7]
    saves = [
        pltpu.make_async_copy(full, dy_out, o_sem.at[0]),
        pltpu.make_async_copy(hid_s, hid_out, o_sem.at[1]),
        pltpu.make_async_copy(dg_s, dg_out, o_sem.at[2]),
        pltpu.make_async_copy(du_s, du_out, o_sem.at[3]),
    ]
    for save in saves:
        save.start()
    unit, factor = unit_rows(h1_ref[...])
    width = dy_ref.shape[1]
    back, term = norm_back(total[...], gains[layer, :, width : 2 * width], unit, factor)
    dh1 = dy_ref[...].astype(F32) + back
    dh1_ref[...] = dh1
    term_ref[...] = term
    whole[rows_at(t * rows, rows)] = dh1.astype(BF16)
    wait = spread_rows(t, nt, rows, whole, scratch[16], scratch[17])
    finish()
    wait()
    dat_ref[...] = whole[...]
    for save in saves:
        save.wait()


def attend_back_kernel(
    layer, source, nz, nt, heads,
    x_ref, tabs, gains, dat_ref, dh1_ref, term_moe,
    q_ref, k_ref, v_ref, qr_ref, kr_ref, wq, wk, wv, wo,
    dxr_ref, dx_ref, dqkv_ref, terms_ref,
    wq_s, wk_s, wv_s, wo_s, part, outgoing, came, whole, w_sem, s_sem, r_sem, gs_sem, gr_sem,
):
    z, t = lax.axis_index("expert"), lax.axis_index("tensor")
    loads = [
        pltpu.make_async_copy(src.at[layer], dst, w_sem.at[i])
        for i, (src, dst) in enumerate(((wo, wo_s), (wq, wq_s), (wk, wk_s), (wv, wv_s)))
    ]
    for load in loads:
        load.start()
    i32 = jnp.int32
    greet([{"tensor": partner(t, i32(j), nt)} for j in range(1, nt)])

    block = x_ref.shape[1]
    rows = block // nt
    size = tabs.shape[-1]
    g_attn, _, g_query, g_key = split_gains(gains, layer, x_ref.shape[2], size)
    scale = 1.0 / math.sqrt(size)
    cos, sin, bias = tabs[layer, 0], tabs[layer, 1], tabs[layer, 2]
    cos_all, sin_all = tiled(cos, heads), tiled(sin, heads)
    qr, kr, v = qr_ref[...], kr_ref[...], v_ref[...]
    scores = dot_nt(qr, kr) * scale + tiled(bias, heads)
    peak = jnp.max(scores, axis=-1, keepdims=True)
    weight = jnp.exp(scores - peak)
    probs = weight * (1.0 / jnp.sum(weight, axis=-1, keepdims=True))
    loads[0].wait()
    do = heads_to_rows(dot_nt(dat_ref[...], wo_s[...]).astype(BF16), heads, size)
    dv = dot_tn(probs.astype(BF16), do).astype(BF16)
    dp = dot_nt(do, v)
    ds = (probs * (dp - jnp.sum(probs * dp, axis=-1, keepdims=True))).astype(BF16)
    dqr = dot(ds, kr) * scale
    dkr = dot_tn(ds, qr) * scale
    dqn = dqr * cos_all - half_turn(dqr) * sin_all
    dkn = dkr * cos - half_turn(dkr) * sin
    q_unit, q_factor = unit_rows(heads_to_rows(q_ref[...], heads, size))
    k_unit, k_factor = unit_rows(k_ref[...])
    dq, term_query = norm_back(dqn, g_query, q_unit, q_factor)
    dk, term_key = norm_back(dkn, g_key, k_unit, k_factor)
    dq = rows_to_heads(dq.astype(BF16), heads, block)
    dk = dk.astype(BF16)
    dqkv_ref[:, : heads * size] = dq
    dqkv_ref[:, heads * size : (heads + 1) * size] = dk
    dqkv_ref[:, (heads + 1) * size :] = dv
    for load in loads[1:]:
        load.wait()
    part[...] = dot_nt(dq, wq_s[...]) + dot_nt(dk, wk_s[...]) + dot_nt(dv, wv_s[...])
    total = reduce_rows(t, nt, rows, part, outgoing, came, s_sem, r_sem)
    mine = rows_at(t * rows, rows)
    unit, factor = unit_rows(x_ref[source, mine].astype(F32))
    back, term_attn = norm_back(total, g_attn, unit, factor)
    dx = (dh1_ref[...] + back).astype(BF16)
    dxr_ref[...] = dx
    whole[mine] = dx
    wait = spread_rows(t, nt, rows, whole, gs_sem, gr_sem)
    terms_ref[...] = jnp.zeros_like(terms_ref)
    write_terms(terms_ref, 0, term_moe[...])
    write_terms(terms_ref, 8, term_attn)
    terms_ref[16:17, :size] = term_query
    terms_ref[16:17, size : 2 * size] = term_key
    wait()
    dx_ref[...] = whole[...]


def collect_kernel(
    nz, nt, names,
    *refs,
):
    s, z, t = lax.axis_index("section"), lax.axis_index("expert"), lax.axis_index("tensor")
    count = len(names)
    sets = (refs[:count], refs[count : 2 * count])
    outs = refs[2 * count : 3 * count]
    terms_out = refs[3 * count]
    terms_in, terms_near, send, recv, own_sem, near_send, near_recv = refs[3 * count + 1 :]
    other = 1 - s
    i32 = jnp.int32
    peers = [{"section": other}]
    for k in range(1, nz):
        zz = partner(z, i32(k), nz)
        peers += [{"expert": zz}, {"section": other, "expert": zz}]
    peers += [{"tensor": partner(t, i32(j), nt)} for j in range(1, nt)]
    greet(peers)

    jobs = [(d, k, a) for a in range(count) for k in range(nz) for d in range(2)]
    jobs = [(d, k, a) for d, k, a in jobs if k == 0 or names[a][1] != "near"]

    def source_of(layer, k, a):
        src, kind = sets[layer][a], names[a][1]
        if kind == "slice":
            cols = outs[a].shape[-1]
            return src.at[:, rows_at(partner(z, i32(k), nz) * cols, cols)]
        return src

    def target_of(section, origin, a):
        if names[a][1] == "near":
            return outs[a].at[section]
        if names[a][1] == "terms":
            return terms_in.at[section, origin]
        return outs[a].at[section, origin]

    def copy_of(d, k, a, layer):
        section = s if d == 0 else other
        if d == 0 and k == 0:
            return pltpu.make_async_copy(source_of(layer, k, a), target_of(s, z, a), own_sem.at[a])
        return remote(
            source_of(layer, k, a),
            target_of(s, z, a),
            send.at[a, d, k],
            recv.at[a, d, k],
            section=section,
            expert=partner(z, i32(k), nz),
        )

    def arrival_of(d, k, a):
        section = s if d == 0 else other
        zz = partner(z, i32(k), nz)
        return remote(
            source_of(0, k, a),
            target_of(section, zz, a),
            send.at[a, d, k],
            recv.at[a, d, k],
            section=section,
            expert=zz,
        )

    for d, k, a in jobs:

        @pl.when(s == d)
        def _():
            copy_of(d, k, a, 0).start()

        @pl.when(s != d)
        def _():
            copy_of(d, k, a, 1).start()

    for d, k, a in jobs:
        if d == 0 and k == 0:
            copy_of(d, k, a, 0).wait()
        else:
            copy_of(d, k, a, 0).wait_send()
            arrival_of(d, k, a).wait_recv()

    total = None
    for section in range(2):
        for origin in range(nz):
            one = terms_in[section, origin]
            total = one if total is None else total + one
    terms_near[0] = total

    def near(j):
        return remote(
            terms_near.at[0],
            terms_near.at[j],
            near_send.at[j],
            near_recv.at[j],
            tensor=partner(t, i32(j), nt),
        )

    for j in range(1, nt):
        near(j).start()
    for j in range(1, nt):
        near(j).wait_recv()
        total = total + terms_near[j]
    for j in range(1, nt):
        near(j).wait_send()
    terms_out[...] = total


def shape_of(shape, dtype):
    return jax.ShapeDtypeStruct(tuple(shape), dtype)


def params(collective_id):
    return pltpu.CompilerParams(
        collective_id=collective_id, has_side_effects=True, vmem_limit_bytes=VMEM_LIMIT
    )


def block_tables(lengths, block, size):
    ends = jnp.cumsum(lengths)
    starts = ends - lengths
    places = jnp.arange(block, dtype=jnp.int32)
    segment = jnp.sum((places[:, None] >= ends[None, :]).astype(jnp.int32), axis=1)
    numbers = jnp.arange(lengths.shape[0], dtype=jnp.int32)
    offset = jnp.sum(jnp.where(segment[:, None] == numbers[None, :], starts[None, :], 0), axis=1)
    half = jnp.arange(size // 2, dtype=F32)
    inverse = jnp.exp(half * (-2.0 * math.log(THETA) / size))
    angle = (places - offset).astype(F32)[:, None] * inverse[None, :]
    cos, sin = jnp.cos(angle), jnp.sin(angle)
    allowed = (places[None, :] <= places[:, None]) & (segment[:, None] == segment[None, :])
    bias = jnp.where(allowed, 0.0, -1e30).astype(F32)
    return jnp.stack(
        [
            jnp.concatenate([cos, cos], axis=-1),
            jnp.concatenate([-sin, sin], axis=-1),
            bias,
        ]
    )


def on_device(
    boundary, seq_lengths, expert_ids, route_weights, attn_gain, moe_gain, query_gain, key_norm_gain,
    w_query, key_weight, value_weight, w_output, w_gate, w_up, w_down,
):
    nz, nt = lax.axis_size("expert"), lax.axis_size("tensor")
    micro, block, width = boundary.shape[1:]
    size = query_gain.shape[1]
    heads = w_query.shape[2] // size
    local_experts = w_gate.shape[1]
    hidden = local_experts * w_gate.shape[2]
    experts = local_experts * nz
    rows = block // nt
    q_cols = heads * size
    assert micro == 2 and key_weight.shape[2] == size and experts <= LANES
    dma = pltpu.SemaphoreType.DMA

    tabs = jax.vmap(lambda lengths: block_tables(lengths, block, size))(seq_lengths[0, :, 0])
    lanes = jnp.arange(LANES, dtype=jnp.int32)
    gates = jnp.sum(
        jnp.where(expert_ids[0][..., None] == lanes, route_weights[0][..., None], 0.0), axis=2
    )
    wg, wu, wd = (w[0].reshape(hidden, width) for w in (w_gate, w_up, w_down))
    wq, wk, wv, wo = w_query[0], key_weight[0], value_weight[0], w_output[0]

    gains = jnp.concatenate([attn_gain, moe_gain, query_gain, key_norm_gain], axis=1)

    (edges, tabs_all, gates_all, gains_all, wq_all, wk_all, wv_all, wo_all, sg, su, sd) = pl.pallas_call(
        functools.partial(start_kernel, nz, nt),
        out_shape=(
            shape_of((2, block, width), BF16),
            shape_of((2, 3, block, size), F32),
            shape_of((2, nz, block, LANES), F32),
            shape_of((2,) + gains.shape, F32),
            shape_of((2, width, q_cols), BF16),
            shape_of((2, width, size), BF16),
            shape_of((2, width, size), BF16),
            shape_of((2, q_cols, width), BF16),
            shape_of((hidden, width), BF16),
            shape_of((hidden, width), BF16),
            shape_of((hidden, width), BF16),
        ),
        in_specs=[ANY] * 11,
        out_specs=(ANY,) * 11,
        scratch_shapes=[
            dma((8,)), dma((6,)), dma((6,)), dma((2, nz)), dma((2, nz)),
            dma((4, nz)), dma((4, nz)), dma((4, nz)), dma((4, nz)), dma((4, nz)), dma((4, nz)),
        ],
        compiler_params=params(0),
        name="start",
    )(boundary[0], tabs, gates, gains, wq, wk, wv, wo, wg, wu, wd)

    attn_weights = (wq_all, wk_all, wv_all, wo_all)
    expert_weights = (wg, wu, wd, sg, su, sd)
    attn_scratch = [
        pltpu.VMEM((width, q_cols), BF16),
        pltpu.VMEM((width, size), BF16),
        pltpu.VMEM((width, size), BF16),
        pltpu.VMEM((q_cols, width), BF16),
        pltpu.VMEM((block, width), F32),
        pltpu.VMEM((block, width), BF16),
        pltpu.VMEM((nt, rows, width), BF16),
    ]
    expert_scratch = [pltpu.VMEM((hidden, width), BF16)] * 3 + [pltpu.VMEM((nz, block, hidden), F32)] * 2
    own_part = pltpu.VMEM((nz, rows, width), F32)

    def attend(layer, x, source):
        return pl.pallas_call(
            functools.partial(attend_kernel, layer, source, nz, nt, heads),
            out_shape=(
                shape_of((rows, width), F32),
                shape_of((rows, width), BF16),
                shape_of((block, width), BF16),
                shape_of((block, q_cols), F32),
                shape_of((block, size), F32),
                shape_of((block, size), BF16),
                shape_of((heads * block, size), BF16),
                shape_of((block, size), BF16),
                shape_of((block, q_cols), BF16),
            ),
            in_specs=[VM] * 3 + [ANY] * 4,
            out_specs=(VM,) * 9,
            scratch_shapes=attn_scratch + [dma((4,)), dma((nt,)), dma((nt,))],
            compiler_params=params(1 + layer),
            name=f"attend_{layer}",
        )(x, tabs_all, gains_all, *attn_weights)

    def run_experts(layer, b, h1):
        return pl.pallas_call(
            functools.partial(experts_kernel, layer, nz, nt, local_experts),
            out_shape=(
                shape_of((1, block, width), BF16),
                shape_of((nz, block, width), BF16),
                shape_of((nz, block, hidden), F32),
                shape_of((nz, block, hidden), F32),
            ),
            in_specs=[VM] * 3 + [ANY] * 6,
            out_specs=(VM, ANY, ANY, ANY),
            scratch_shapes=expert_scratch
            + [dma((3,)), dma((3,)), own_part]
            + exchange_scratch(nz, nt, rows, block, width),
            compiler_params=params(3 + layer),
            name=f"experts_{layer}",
        )(b, h1, gates_all, *expert_weights)

    def experts_back(layer, dy, h1, gate_pre, up_pre):
        return pl.pallas_call(
            functools.partial(experts_back_kernel, layer, nz, nt, local_experts),
            out_shape=(
                shape_of((block, width), BF16),
                shape_of((rows, width), F32),
                shape_of((1, width), F32),
                shape_of((nz, block, width), BF16),
                shape_of((nz, block, hidden), BF16),
                shape_of((nz, block, hidden), BF16),
                shape_of((nz, block, hidden), BF16),
            ),
            in_specs=[VM] * 4 + [ANY] * 8,
            out_specs=(VM, VM, VM, ANY, ANY, ANY, ANY),
            scratch_shapes=expert_scratch[:3]
            + [pltpu.VMEM((2, block, hidden), F32)] * 2
            + [pltpu.VMEM((nz, block, hidden), BF16)] * 3
            + [dma((3,)), dma((2,)), dma((2,)), dma((4,)), own_part]
            + exchange_scratch(nz, nt, rows, block, width),
            compiler_params=params(5 + layer),
            name=f"experts_back_{layer}",
        )(dy, h1, gains_all, gates_all, gate_pre, up_pre, *expert_weights)

    def attend_back(layer, x, source, dat, dh1, term_moe, q, k, v, qr, kr):
        return pl.pallas_call(
            functools.partial(attend_back_kernel, layer, source, nz, nt, heads),
            out_shape=(
                shape_of((rows, width), BF16),
                shape_of((block, width), BF16),
                shape_of((block, q_cols + 2 * size), BF16),
                shape_of((TERM_ROWS, TERM_COLS), F32),
            ),
            in_specs=[VM] * 11 + [ANY] * 4,
            out_specs=(VM,) * 4,
            scratch_shapes=attn_scratch
            + [pltpu.VMEM((block, width), BF16)]
            + [dma((4,)), dma((nt,)), dma((nt,)), dma((nt,)), dma((nt,))],
            compiler_params=params(7 + layer),
            name=f"attend_back_{layer}",
        )(x, tabs_all, gains_all, dat, dh1, term_moe, q, k, v, qr, kr, *attn_weights)

    h1_0, b_0, a_0, q_0, k_0, v_0, qr_0, kr_0, o_0 = attend(0, edges, 0)
    x_1, ball_0, gp_0, up_0 = run_experts(0, b_0, h1_0)
    h1_1, b_1, a_1, q_1, k_1, v_1, qr_1, kr_1, o_1 = attend(1, x_1, 0)
    y_1, ball_1, gp_1, up_1 = run_experts(1, b_1, h1_1)

    dy_1 = lax.dynamic_slice_in_dim(edges[1], lax.axis_index("tensor") * rows, rows, 0)
    dat_1, dh1_1, tm_1, dyall_1, hid_1, dg_1, du_1 = experts_back(1, dy_1, h1_1, gp_1, up_1)
    dxr_1, _, dqkv_1, terms_1 = attend_back(
        1, x_1, 0, dat_1, dh1_1, tm_1, q_1, k_1, v_1, qr_1, kr_1
    )
    dat_0, dh1_0, tm_0, dyall_0, hid_0, dg_0, du_0 = experts_back(0, dxr_1, h1_0, gp_0, up_0)
    _, dx_0, dqkv_0, terms_0 = attend_back(
        0, edges, 0, dat_0, dh1_0, tm_0, q_0, k_0, v_0, qr_0, kr_0
    )

    set_0 = (ball_0, dyall_0, hid_0, dg_0, du_0, dx_0, a_0, o_0, dat_0, dqkv_0, terms_0)
    set_1 = (ball_1, dyall_1, hid_1, dg_1, du_1, y_1[0], a_1, o_1, dat_1, dqkv_1, terms_1)
    kinds = ("near",) * 6 + ("slice", "whole", "slice", "whole", "terms")
    names = tuple((str(i), kind) for i, kind in enumerate(kinds))
    out_shapes = []
    for kind, value in zip(kinds, set_0):
        if kind == "near":
            out_shapes.append(shape_of((2,) + value.shape, value.dtype))
        elif kind == "slice":
            out_shapes.append(shape_of((2, nz, block, width // nz), value.dtype))
        elif kind == "whole":
            out_shapes.append(shape_of((2, nz) + value.shape, value.dtype))
        else:
            out_shapes.append(shape_of((8, LANES), F32))
    out_shapes.append(shape_of((TERM_ROWS, TERM_COLS), F32))
    count = len(kinds)
    collected = pl.pallas_call(
        functools.partial(collect_kernel, nz, nt, names),
        out_shape=tuple(out_shapes),
        in_specs=[ANY] * (2 * count),
        out_specs=(ANY,) * count + (VM,),
        scratch_shapes=[
            pltpu.VMEM((2, nz, TERM_ROWS, TERM_COLS), F32),
            pltpu.VMEM((nt, TERM_ROWS, TERM_COLS), F32),
            dma((count, 2, nz)),
            dma((count, 2, nz)),
            dma((count,)),
            dma((nt,)),
            dma((nt,)),
        ],
        compiler_params=params(9),
        name="collect",
    )(*set_0, *set_1)
    (b_all, dy_all, hid, dg, du, ends, a_all, o_all, dat_all, dqkv_all, _, terms) = collected

    def flat(value):
        return value.reshape(-1, value.shape[-1])

    def weight_grad(left, right):
        return lax.dot_general(
            flat(left), flat(right), (((0,), (0,)), ((), ())), preferred_element_type=F32
        )

    def expert_grad(left, right):
        return weight_grad(left, right).reshape(w_gate.shape)

    dqkv_all = flat(dqkv_all)
    a_all = flat(a_all)
    grad_query = weight_grad(a_all, dqkv_all[:, :q_cols])
    grad_key = weight_grad(a_all, dqkv_all[:, q_cols : q_cols + size])
    grad_value = weight_grad(a_all, dqkv_all[:, q_cols + size :])
    return (
        ends[None],
        terms[8:16].reshape(1, width),
        terms[:8].reshape(1, width),
        terms[16:17, :size],
        terms[16:17, size : 2 * size],
        grad_query[None],
        grad_key[None],
        grad_value[None],
        weight_grad(o_all, dat_all)[None],
        expert_grad(dg, b_all),
        expert_grad(du, b_all),
        expert_grad(hid, dy_all),
    )


def solution(mesh):
    return jax.shard_map(
        on_device,
        mesh=mesh,
        in_specs=(
            P("section", None, "expert", None),
            P("section", None, "expert", None),
            P("section", None, "expert", None),
            P("section", None, "expert", None),
            P("section", None),
            P("section", None),
            P("section", None),
            P("section", None),
            P("section", "expert", "tensor"),
            P("section", "expert", "tensor"),
            P("section", "expert", "tensor"),
            P("section", "tensor", "expert"),
            P("section", "expert", "tensor", None),
            P("section", "expert", "tensor", None),
            P("section", "expert", "tensor", None),
        ),
        out_specs=(
            P("section", None, "expert", None),
            P("section", None),
            P("section", None),
            P("section", None),
            P("section", None),
            P("section", "expert", "tensor"),
            P("section", "expert", "tensor"),
            P("section", "expert", "tensor"),
            P("section", "tensor", "expert"),
            P("section", "expert", "tensor", None),
            P("section", "expert", "tensor", None),
            P("section", "expert", "tensor", None),
        ),
        check_vma=False,
    )
```

```python
import functools
import math

import jax
import jax.numpy as jnp
from jax import lax
from jax.experimental import pallas as pl
from jax.experimental.pallas import tpu as pltpu
from jax.sharding import PartitionSpec as P

EPSILON = 1e-06
THETA = 1000000.0
LANES = 128
TERM_ROWS = 24
TERM_COLS = 256
MESH = pl.DeviceIdType.MESH
F32 = jnp.float32
BF16 = jnp.bfloat16
VMEM_LIMIT = 60 * 1024 * 1024

ANY = pl.BlockSpec(memory_space=pl.ANY)
VM = pl.BlockSpec(memory_space=pltpu.VMEM)


def partner(index, k, count):
    out, bit = 0, 1
    while bit < count:
        out = out + bit * lax.rem(lax.div(index, bit) + lax.div(k, bit), 2)
        bit *= 2
    return out


def rows_at(start, size):
    return pl.ds(pl.multiple_of(start, size), size)


def remote(src, dst, send_sem, recv_sem, **where):
    return pltpu.make_async_remote_copy(
        src_ref=src,
        dst_ref=dst,
        send_sem=send_sem,
        recv_sem=recv_sem,
        device_id=where,
        device_id_type=MESH,
    )


def greet(peers):
    barrier = pltpu.get_barrier_semaphore()
    for where in peers:
        pl.semaphore_signal(barrier, inc=1, device_id=where, device_id_type=MESH)
    pl.semaphore_wait(barrier, len(peers))


def layer_peers(z, t, nz, nt):
    i32 = jnp.int32
    peers = [{"expert": partner(z, i32(k), nz)} for k in range(1, nz)]
    peers += [{"tensor": partner(t, i32(k), nt)} for k in range(1, nt)]
    return peers


def dot(a, b):
    return lax.dot_general(a, b, (((1,), (0,)), ((), ())), preferred_element_type=F32)


def dot_nt(a, b):
    return lax.dot_general(a, b, (((1,), (1,)), ((), ())), preferred_element_type=F32)


def dot_tn(a, b):
    return lax.dot_general(a, b, (((0,), (0,)), ((), ())), preferred_element_type=F32)


def unit_rows(value):
    factor = lax.rsqrt(jnp.mean(value * value, axis=-1, keepdims=True) + EPSILON)
    return value * factor, factor


def norm_back(grad, gain, unit, factor):
    weighted = grad * gain
    inner = jnp.mean(weighted * unit, axis=-1, keepdims=True)
    return factor * (weighted - unit * inner), jnp.sum(grad * unit, axis=0, keepdims=True)


def expert_gates(gate_rows, first_expert, local_experts, width):
    rows = gate_rows.shape[0]
    lane = lax.broadcasted_iota(jnp.int32, gate_rows.shape, 1)
    column = lax.broadcasted_iota(jnp.int32, (rows, local_experts * width), 1)
    out = None
    for e in range(local_experts):
        one = jnp.sum(jnp.where(lane == first_expert + e, gate_rows, 0.0), axis=1, keepdims=True)
        wide = jnp.broadcast_to(one, column.shape)
        out = wide if out is None else jnp.where(column >= e * width, wide, out)
    return out


def write_terms(terms_ref, row, vector):
    for i in range(vector.shape[1] // TERM_COLS):
        terms_ref[row + i : row + i + 1, :] = vector[:, i * TERM_COLS : (i + 1) * TERM_COLS]


def exchange_sems(nz, nt):
    dma = pltpu.SemaphoreType.DMA
    return [dma((nz,)), dma((nz,)), dma((nz, nt)), dma((nz, nt))] * 2 + [dma((nt,)), dma((nt,))]


def exchange_scratch(nz, nt, rows, block, width):
    return [
        pltpu.VMEM((nz, block, width), BF16),
        pltpu.VMEM((nz, block, width), BF16),
        pltpu.VMEM((block, width), F32),
        pltpu.VMEM((nz, nt, rows, width), BF16),
        pltpu.VMEM((nz, rows, width), BF16),
        pltpu.VMEM((nz, rows, width), BF16),
        pltpu.VMEM((rows, width), F32),
        pltpu.VMEM((block, width), BF16),
    ] + exchange_sems(nz, nt)


def exchange(z, t, nz, nt, rows, own_rows, scratch, ready, work, moves):
    (full, outgoing, part, came_near, passed, came_far, total, _) = scratch[:8]
    (gz_send, gz_recv, gt_send, gt_recv, rz_send, rz_recv, rt_send, rt_recv) = scratch[8:16]
    i32 = jnp.int32
    mine = rows_at(t * rows, rows)

    def far_copy(k):
        return remote(
            full.at[z, mine],
            full.at[z, mine],
            gz_send.at[k],
            gz_recv.at[k],
            expert=partner(z, i32(k), nz),
        )

    def near_copy(k, source, j):
        return remote(
            full.at[source, mine],
            full.at[source, mine],
            gt_send.at[k, j],
            gt_recv.at[k, j],
            tensor=partner(t, i32(j), nt),
        )

    def near_arrival(k, source, j):
        theirs = rows_at(partner(t, i32(j), nt) * rows, rows)
        return remote(
            full.at[source, theirs],
            full.at[source, theirs],
            gt_send.at[k, j],
            gt_recv.at[k, j],
            tensor=partner(t, i32(j), nt),
        )

    def far_arrival(k):
        source = partner(z, i32(k), nz)
        return remote(
            full.at[source, mine],
            full.at[source, mine],
            gz_send.at[k],
            gz_recv.at[k],
            expert=source,
        )

    def part_copy(k, j):
        peer = partner(t, i32(j), nt)
        return remote(
            outgoing.at[k, rows_at(peer * rows, rows)],
            came_near.at[k, j],
            rt_send.at[k, j],
            rt_recv.at[k, j],
            tensor=peer,
        )

    def sum_copy(k):
        return remote(
            passed.at[k],
            came_far.at[k],
            rz_send.at[k],
            rz_recv.at[k],
            expert=partner(z, k, nz),
        )

    full[z, mine] = own_rows
    for k in range(1, nz):
        far_copy(k).start()
    for j in range(1, nt):
        near_copy(0, z, j).start()
    for move in moves:
        move.start()

    ready()

    def produce(k, source):
        for j in range(1, nt):
            near_arrival(k, source, j).wait_recv()
        part[...] = work(k, source, full[source])
        outgoing[k] = part[...].astype(BF16)
        for j in range(1, nt):
            part_copy(k, j).start()
        return part[mine]

    def collect(k):
        out = passed_own[k]
        for j in range(1, nt):
            part_copy(k, j).wait_recv()
            out = out + came_near[k, j].astype(F32)
        return out

    passed_own = scratch[18]
    passed_own[0] = produce(i32(0), z)
    for k in range(1, nz):
        far_arrival(k).wait_recv()
        for j in range(1, nt):
            near_copy(k, partner(z, i32(k), nz), j).start()

    def step(k, carry):
        passed_own[k] = produce(k, partner(z, k, nz))

        @pl.when(k >= 2)
        def _():
            passed[k - 1] = collect(k - 1).astype(BF16)
            sum_copy(k - 1).start()

        return carry

    lax.fori_loop(1, nz, step, 0)
    for move in moves:
        move.poll(1)
    passed[nz - 1] = collect(nz - 1).astype(BF16)
    sum_copy(i32(nz - 1)).start()
    for move in moves:
        move.poll(2)
    total[...] = collect(0)
    for k in range(1, nz):
        sum_copy(i32(k)).wait_recv()
        total[...] += came_far[k].astype(F32)

    def finish():
        for k in range(1, nz):
            far_copy(k).wait_send()
            sum_copy(i32(k)).wait_send()
        for k in range(nz):
            source = partner(z, i32(k), nz)
            for j in range(1, nt):
                near_copy(k, source, j).wait_send()
                part_copy(k, j).wait_send()

    return finish


def spread_rows(t, nt, rows, block_ref, send_sem, recv_sem):
    i32 = jnp.int32
    mine = rows_at(t * rows, rows)
    for j in range(1, nt):
        remote(
            block_ref.at[mine],
            block_ref.at[mine],
            send_sem.at[j],
            recv_sem.at[j],
            tensor=partner(t, i32(j), nt),
        ).start()

    def wait():
        for j in range(1, nt):
            peer = partner(t, i32(j), nt)
            theirs = rows_at(peer * rows, rows)
            copy = remote(
                block_ref.at[theirs],
                block_ref.at[theirs],
                send_sem.at[j],
                recv_sem.at[j],
                tensor=peer,
            )
            copy.wait_send()
            copy.wait_recv()

    return wait


def reduce_rows(t, nt, rows, part, outgoing, came, send_sem, recv_sem):
    i32 = jnp.int32
    outgoing[...] = part[...].astype(BF16)

    def copy(j):
        peer = partner(t, i32(j), nt)
        return remote(
            outgoing.at[rows_at(peer * rows, rows)],
            came.at[j],
            send_sem.at[j],
            recv_sem.at[j],
            tensor=peer,
        )

    for j in range(1, nt):
        copy(j).start()
    total = part[rows_at(t * rows, rows)]
    for j in range(1, nt):
        copy(j).wait_recv()
        total = total + came[j].astype(F32)
    for j in range(1, nt):
        copy(j).wait_send()
    return total


def all_peers(s, z, t, nz, nt):
    i32 = jnp.int32
    peers = [{"section": 1 - s}]
    for k in range(1, nz):
        zz = partner(z, i32(k), nz)
        peers += [{"expert": zz}, {"section": 1 - s, "expert": zz}]
    return peers + [{"tensor": partner(t, i32(j), nt)} for j in range(1, nt)]


class Relay:
    def __init__(self, layer, spots, nz):
        self.layer, self.spots, self.nz = layer, spots, nz

    def scratch(self, count):
        dma = pltpu.SemaphoreType.DMA
        return [dma((count,))] + [dma((count, self.nz))] * 6

    def bind(self, shards, outs, sems):
        self.s, self.z = lax.axis_index("section"), lax.axis_index("expert")
        self.shards, self.outs, self.sems = shards, outs, sems
        self.source = self.s == self.layer
        self.count = len(shards)
        return self

    def place(self, a, owner):
        dim = self.spots[a]
        size = self.shards[a].shape[dim]
        window = rows_at(owner * size, size)
        return self.outs[a].at[window] if dim == 0 else self.outs[a].at[:, window]

    def home(self, a):
        return pltpu.make_async_copy(self.shards[a], self.place(a, self.z), self.sems[0].at[a])

    def hop(self, a, owner, step, right, own=False):
        spot = self.place(a, owner)
        send, recv = self.sems[1:3] if right else self.sems[3:5]
        return remote(
            self.shards[a] if own else spot,
            spot,
            send.at[a, step],
            recv.at[a, step],
            expert=self.z + 1 if right else self.z - 1,
        )

    def hand(self, a, owner, own=False):
        spot = self.place(a, owner)
        return remote(
            self.shards[a] if own else spot,
            spot,
            self.sems[5].at[a, owner],
            self.sems[6].at[a, owner],
            section=1 - self.s,
        )

    def begin_side(self, a, right):
        @pl.when(self.source & ((self.z + 1 < self.nz) if right else (self.z >= 1)))
        def _():
            self.hop(a, self.z, 1, right, True).start()

    def begin_home(self, a):
        @pl.when(self.source)
        def _():
            self.home(a).start()
            self.hand(a, self.z, True).start()

    def begin(self, a):
        self.begin_side(a, True)
        self.begin_side(a, False)
        self.begin_home(a)

    def step(self, a, k):
        z, nz = self.z, self.nz

        @pl.when(self.source & (z >= k))
        def _():
            self.hop(a, z - k, k, True).wait_recv()

            @pl.when(z + 1 < nz)
            def _():
                self.hop(a, z - k, k + 1, True).start()

            self.hand(a, z - k).start()

        @pl.when(self.source & (z + k < nz))
        def _():
            self.hop(a, z + k, k, False).wait_recv()

            @pl.when(z >= 1)
            def _():
                self.hop(a, z + k, k + 1, False).start()

            self.hand(a, z + k).start()

    def settle(self, a):
        @pl.when(self.source)
        def _():
            self.home(a).wait()

        @pl.when(jnp.logical_not(self.source))
        def _():
            for owner in range(self.nz):
                self.hand(a, owner).wait_recv()

    def end(self, a):
        z, nz = self.z, self.nz

        @pl.when(self.source)
        def _():
            for owner in range(nz):
                self.hand(a, owner).wait_send()
            for step in range(1, nz):

                @pl.when((z >= step - 1) & (z + 1 < nz))
                def _():
                    self.hop(a, z - (step - 1), step, True).wait_send()

                @pl.when((z + step - 1 < nz) & (z >= 1))
                def _():
                    self.hop(a, z + (step - 1), step, False).wait_send()

    def start(self):
        for a in range(self.count):
            self.begin(a)

    def poll(self, turn):
        if turn < self.nz - 1:
            for a in range(self.count):
                self.step(a, turn)

    def finish(self):
        for k in range(min(3, self.nz - 1), self.nz):
            for a in range(self.count):
                self.step(a, k)
        for a in range(self.count):
            self.settle(a)
            self.end(a)


class Gather:
    def __init__(self, layer, nz, sliced=False):
        self.layer, self.nz, self.sliced = layer, nz, sliced

    def scratch(self):
        dma = pltpu.SemaphoreType.DMA
        return [dma((1,)), dma((self.nz,)), dma((2, self.nz))]

    def bind(self, src, out, sems):
        self.s, self.z = lax.axis_index("section"), lax.axis_index("expert")
        self.src, self.out, self.sems = src, out, sems
        return self

    def copy(self, k, local, section=None, origin=None):
        zz = partner(self.z, jnp.int32(k), self.nz)
        src = self.src
        if self.sliced:
            cols = self.out.shape[-1]
            src = src.at[:, rows_at(zz * cols, cols)]
        section = self.s if section is None else section
        spot = self.out.at[section, self.z if origin is None else origin]
        if local:
            return pltpu.make_async_copy(src, spot, self.sems[0].at[0])
        return remote(
            src,
            spot,
            self.sems[1].at[k],
            self.sems[2].at[section, k],
            section=jnp.int32(self.layer),
            expert=zz,
        )

    def start(self):
        for k in range(1, self.nz):
            self.copy(k, False).start()

        @pl.when(self.s == self.layer)
        def _():
            self.copy(0, True).start()

        @pl.when(self.s != self.layer)
        def _():
            self.copy(0, False).start()

    def poll(self, turn):
        pass

    def arrive(self):
        @pl.when(self.s == self.layer)
        def _():
            self.copy(0, True).wait()
            for section in range(2):
                for k in range(self.nz):
                    if k or section != self.layer:
                        zz = partner(self.z, jnp.int32(k), self.nz)
                        self.copy(k, False, section, zz).wait_recv()

    def leave(self):
        for k in range(1, self.nz):
            self.copy(k, False).wait_send()

        @pl.when(self.s != self.layer)
        def _():
            self.copy(0, False).wait_send()

    def finish(self):
        self.arrive()
        self.leave()


class Near:
    def __init__(self, layer, both=False):
        self.layer, self.both = layer, both

    def scratch(self):
        dma = pltpu.SemaphoreType.DMA
        return [dma((1,)), dma((1,)), dma((1,))]

    def bind(self, src, out, sems):
        self.s, self.src, self.out, self.sems = lax.axis_index("section"), src, out, sems
        return self

    def local(self):
        return pltpu.make_async_copy(self.src, self.out.at[self.layer], self.sems[0].at[0])

    def copy(self):
        return remote(
            self.src,
            self.out.at[1 - self.layer] if self.both else self.out,
            self.sems[1].at[0],
            self.sems[2].at[0],
            section=jnp.int32(self.layer),
        )

    def start(self):
        if self.both:

            @pl.when(self.s == self.layer)
            def _():
                self.local().start()

        @pl.when(self.s != self.layer)
        def _():
            self.copy().start()

    def poll(self, turn):
        pass

    def finish(self):
        @pl.when(self.s == self.layer)
        def _():
            if self.both:
                self.local().wait()
            remote(
                self.src,
                self.out.at[1 - self.layer] if self.both else self.out,
                self.sems[1].at[0],
                self.sems[2].at[0],
                section=1 - self.s,
            ).wait_recv()

        @pl.when(self.s != self.layer)
        def _():
            self.copy().wait_send()


def heads_to_rows(value, heads, size):
    return jnp.concatenate([value[:, h * size : (h + 1) * size] for h in range(heads)], axis=0)


def rows_to_heads(value, heads, block):
    return jnp.concatenate([value[h * block : (h + 1) * block] for h in range(heads)], axis=1)


def split_gains(row, width, size):
    return (
        row[:, :width],
        row[:, width : 2 * width],
        row[:, 2 * width : 2 * width + size],
        row[:, 2 * width + size :],
    )


def tiled(value, times):
    return jnp.concatenate([value] * times, axis=0)


def half_turn(value):
    return pltpu.roll(value, value.shape[-1] // 2, value.ndim - 1)


def attend_body(t, nt, heads, x_ref, tables, gains, outs, scratch, wait_qkv, wait_out):
    (h1_ref, b_ref, a_ref, q_ref, k_ref, v_ref, qr_ref, kr_ref, o_ref) = outs
    (wq_s, wk_s, wv_s, wo_s, part, outgoing, came, s_sem, r_sem) = scratch
    block, width = x_ref.shape
    rows = block // nt
    cos, sin, bias = tables
    size = cos.shape[-1]
    g_attn, g_moe, g_query, g_key = split_gains(gains, width, size)
    unit, _ = unit_rows(x_ref[...].astype(F32))
    a_ref[...] = (unit * g_attn).astype(BF16)
    wait_qkv()
    q = dot(a_ref[...], wq_s[...])
    q_ref[...] = q
    k = dot(a_ref[...], wk_s[...])
    k_ref[...] = k
    v = dot(a_ref[...], wv_s[...]).astype(BF16)
    v_ref[...] = v
    qn = unit_rows(heads_to_rows(q, heads, size))[0] * g_query
    kn = unit_rows(k)[0] * g_key
    qr = (qn * tiled(cos, heads) + half_turn(qn) * tiled(sin, heads)).astype(BF16)
    kr = (kn * cos + half_turn(kn) * sin).astype(BF16)
    qr_ref[...] = qr
    kr_ref[...] = kr
    scores = dot_nt(qr, kr) * (1.0 / math.sqrt(size)) + tiled(bias, heads)
    peak = jnp.max(scores, axis=-1, keepdims=True)
    weight = jnp.exp(scores - peak)
    probs = weight * (1.0 / jnp.sum(weight, axis=-1, keepdims=True))
    o = dot(probs.astype(BF16), v).astype(BF16)
    o_ref[...] = rows_to_heads(o, heads, block)
    wait_out()
    part[...] = dot(o_ref[...], wo_s[...])
    total = reduce_rows(t, nt, rows, part, outgoing, came, s_sem, r_sem)
    h1 = x_ref[rows_at(t * rows, rows)].astype(F32) + total
    h1_ref[...] = h1
    b_ref[...] = (unit_rows(h1)[0] * g_moe).astype(BF16)


def start_attend_kernel(nz, nt, heads, relay, ins, outs, scratch):
    s, z, t = lax.axis_index("section"), lax.axis_index("expert"), lax.axis_index("tensor")
    boundary, tabs, gates, gains, wq, wk, wv, wo, wg, wu, wd = ins
    edges, tabs_out, gates_out, gains_out = outs[:4]
    gathered, (sg, su, sd), results = outs[4:8], outs[8:11], outs[11:]
    x_s, tabs_s, gains_s, w_sem, in_sem, own_sem, sib_send, sib_recv, gate_send, gate_recv = scratch[:10]
    relay.bind((wq, wk, wv, wo), gathered, scratch[10:17])
    attn_scratch = scratch[17:]
    other = 1 - s
    i32 = jnp.int32

    own = [
        pltpu.make_async_copy(boundary.at[s], edges.at[s], own_sem.at[0]),
        pltpu.make_async_copy(tabs.at[s], tabs_out.at[s], own_sem.at[1]),
        pltpu.make_async_copy(gains, gains_out.at[s], own_sem.at[2]),
        pltpu.make_async_copy(gates.at[s], gates_out.at[s, z], own_sem.at[3]),
    ]
    for copy in own:
        copy.start()
    greet(all_peers(s, z, t, nz, nt))

    def sibling(i, src, dst):
        return remote(src, dst, sib_send.at[i], sib_recv.at[i], section=other)

    pairs = [
        (boundary.at[other], edges.at[s], edges.at[other]),
        (tabs.at[other], tabs_out.at[s], tabs_out.at[other]),
        (gains, gains_out.at[s], gains_out.at[other]),
        (wg, sg, sg),
        (wu, su, su),
        (wd, sd, sd),
    ]
    for i in range(3):
        sibling(i, *pairs[i][:2]).start()
    for a in range(3):
        relay.begin(a)
    relay.begin_home(3)

    @pl.when(z == 0)
    def _():
        relay.begin_side(3, True)

    @pl.when(z == nz - 1)
    def _():
        relay.begin_side(3, False)

    def gate_copy(d, k, arrival=False):
        zz = partner(z, i32(k), nz)
        section = s if d == 0 else other
        return remote(
            gates.at[section],
            gates_out.at[section, zz] if arrival else gates_out.at[s, z],
            gate_send.at[d, k],
            gate_recv.at[d, k],
            section=section,
            expert=zz,
        )

    turns = [(d, k) for d in range(2) for k in range(nz) if d or k]
    for d, k in turns:
        gate_copy(d, k).start()
    for i in range(3, 6):
        sibling(i, *pairs[i][:2]).start()

    for copy in own:
        copy.wait()
    for i in range(3):
        sibling(i, pairs[i][0], pairs[i][2]).wait_recv()
    loads = [
        pltpu.make_async_copy(edges.at[0], x_s, in_sem.at[0]),
        pltpu.make_async_copy(tabs_out.at[0], tabs_s, in_sem.at[1]),
        pltpu.make_async_copy(gains_out.at[0], gains_s, in_sem.at[2]),
    ]
    for load in loads:
        load.start()
    for load in loads:
        load.wait()

    def bring(a):
        return pltpu.make_async_copy(gathered[a], attn_scratch[a], w_sem.at[a])

    def wait_qkv():
        for k in range(1, nz):
            for a in range(3):
                relay.step(a, k)

            @pl.when((z == k) & (z < nz - 1))
            def _():
                relay.begin_side(3, True)

            @pl.when((z == nz - 1 - k) & (z > 0))
            def _():
                relay.begin_side(3, False)

        for a in range(3):
            relay.settle(a)
            bring(a).start()
        for a in range(3):
            bring(a).wait()

    def wait_out():
        for k in range(1, nz):
            relay.step(3, k)
        relay.settle(3)
        bring(3).start()
        bring(3).wait()

    tables = (tabs_s[0], tabs_s[1], tabs_s[2])
    attend_body(t, nt, heads, x_s, tables, gains_s[...], results, attn_scratch, wait_qkv, wait_out)
    for i in range(6):
        sibling(i, *pairs[i][:2]).wait_send()
    for i in range(3, 6):
        sibling(i, pairs[i][0], pairs[i][2]).wait_recv()
    for d, k in turns:
        gate_copy(d, k).wait_send()
        gate_copy(d, k, True).wait_recv()
    for a in range(4):
        relay.end(a)


def attend_kernel(layer, nz, nt, heads, relay, ins, outs, scratch):
    s, z, t = lax.axis_index("section"), lax.axis_index("expert"), lax.axis_index("tensor")
    x_ref, tabs, gains, wq, wk, wv, wo = ins
    w_sem = scratch[0]
    relay.bind((wo,), outs[:1], scratch[1:8])
    attn_scratch = scratch[8:]
    loads = [
        pltpu.make_async_copy(src, dst, w_sem.at[i])
        for i, (src, dst) in enumerate(zip((wq, wk, wv, outs[0]), attn_scratch))
    ]
    for load in loads[:3]:
        load.start()
    greet(all_peers(s, z, t, nz, nt))
    relay.begin(0)

    def wait_qkv():
        for load in loads[:3]:
            load.wait()

    def wait_out():
        for k in range(1, nz):
            relay.step(0, k)
        relay.settle(0)
        loads[3].start()
        loads[3].wait()

    tables = (tabs[layer, 0], tabs[layer, 1], tabs[layer, 2])
    attend_body(
        t, nt, heads, x_ref, tables, gains[layer], outs[1:], attn_scratch, wait_qkv, wait_out
    )
    relay.end(0)


def load_experts(layer, s, own, sibling, scratch, sems):
    def copies(refs):
        return [pltpu.make_async_copy(r, d, sems.at[i]) for i, (r, d) in enumerate(zip(refs, scratch))]

    @pl.when(s == layer)
    def _():
        for copy in copies(own):
            copy.start()

    @pl.when(s != layer)
    def _():
        for copy in copies(sibling):
            copy.start()

    return copies(own)


def experts_kernel(layer, nz, nt, local_experts, bind, ins, outs, scratch):
    s, z, t = lax.axis_index("section"), lax.axis_index("expert"), lax.axis_index("tensor")
    b_ref, h1_ref, gates, wg, wu, wd, sg, su, sd = ins[:9]
    y_ref, b_out, g_out, u_out = outs[:4]
    wg_s, wu_s, wd_s, g_s, u_s, w_sem, o_sem, own_part = scratch[:8]
    spaces, rest = list(scratch[8:26]) + [own_part], scratch[26:]
    moves = bind(ins[9:], outs[4:], rest)
    rows = b_ref.shape[0]
    loads = load_experts(layer, s, (wg, wu, wd), (sg, su, sd), (wg_s, wu_s, wd_s), w_sem)
    greet(all_peers(s, z, t, nz, nt))
    width = wg.shape[0] // local_experts

    def ready():
        for load in loads:
            load.wait()

    def work(k, origin, rows_in):
        gate_pre = dot_nt(rows_in, wg_s[...])
        up_pre = dot_nt(rows_in, wu_s[...])
        g_s[origin] = gate_pre
        u_s[origin] = up_pre
        weight = expert_gates(gates[layer, origin], z * local_experts, local_experts, width)
        hidden = (gate_pre * jax.nn.sigmoid(gate_pre) * up_pre * weight).astype(BF16)
        return dot(hidden, wd_s[...])

    finish = exchange(z, t, nz, nt, rows, b_ref[...], spaces, ready, work, moves)
    full, total, whole = spaces[0], spaces[6], spaces[7]
    saves = [
        pltpu.make_async_copy(full, b_out, o_sem.at[0]),
        pltpu.make_async_copy(g_s, g_out, o_sem.at[1]),
        pltpu.make_async_copy(u_s, u_out, o_sem.at[2]),
    ]
    for save in saves:
        save.start()
    whole[rows_at(t * rows, rows)] = (h1_ref[...] + total[...]).astype(BF16)
    wait = spread_rows(t, nt, rows, whole, spaces[16], spaces[17])
    finish()
    wait()
    y_ref[...] = whole[...]
    for save in saves:
        save.wait()
    for move in moves:
        move.finish()


def experts_back_kernel(layer, nz, nt, local_experts, bind, ins, outs, scratch):
    s, z, t = lax.axis_index("section"), lax.axis_index("expert"), lax.axis_index("tensor")
    dy_ref, h1_ref, gains, gates, g_in, u_in, wg, wu, wd, sg, su, sd = ins[:12]
    dat_ref, dh1_ref, term_ref, dy_out, hid_out, dg_out, du_out = outs[:7]
    wg_s, wu_s, wd_s, g_s, u_s, hid_s, dg_s, du_s, w_sem, g_sem, u_sem, o_sem, own_part = scratch[:13]
    spaces, rest = list(scratch[13:31]) + [own_part], scratch[31:]
    moves = bind(ins[12:], outs[7:], rest)
    rows, model_width = dy_ref.shape
    loads = load_experts(layer, s, (wd, wg, wu), (sd, sg, su), (wd_s, wg_s, wu_s), w_sem)

    def kept(k):
        origin, slot = partner(z, k, nz), lax.rem(k, 2)
        return (
            pltpu.make_async_copy(g_in.at[origin], g_s.at[slot], g_sem.at[slot]),
            pltpu.make_async_copy(u_in.at[origin], u_s.at[slot], u_sem.at[slot]),
        )

    for load in kept(jnp.int32(0)):
        load.start()
    greet(all_peers(s, z, t, nz, nt))
    width = wg.shape[0] // local_experts

    def ready():
        for load in loads:
            load.wait()

    def work(k, origin, rows_in):
        for load in kept(k):
            load.wait()

        @pl.when(k + 1 < nz)
        def _():
            for load in kept(k + 1):
                load.start()

        slot = lax.rem(k, 2)
        gate_pre, up_pre = g_s[slot], u_s[slot]
        weight = expert_gates(gates[layer, origin], z * local_experts, local_experts, width)
        sigmoid = jax.nn.sigmoid(gate_pre)
        silu = gate_pre * sigmoid
        hid_s[origin] = (silu * up_pre * weight).astype(BF16)
        grad_hidden = dot_nt(rows_in, wd_s[...]) * weight
        dg_s[origin] = (grad_hidden * up_pre * sigmoid * (1.0 + gate_pre * (1.0 - sigmoid))).astype(BF16)
        du_s[origin] = (grad_hidden * silu).astype(BF16)
        return dot(dg_s[origin], wg_s[...]) + dot(du_s[origin], wu_s[...])

    finish = exchange(z, t, nz, nt, rows, dy_ref[...], spaces, ready, work, moves)
    full, total, whole = spaces[0], spaces[6], spaces[7]
    saves = [
        pltpu.make_async_copy(full, dy_out, o_sem.at[0]),
        pltpu.make_async_copy(hid_s, hid_out, o_sem.at[1]),
        pltpu.make_async_copy(dg_s, dg_out, o_sem.at[2]),
        pltpu.make_async_copy(du_s, du_out, o_sem.at[3]),
    ]
    for save in saves:
        save.start()
    unit, factor = unit_rows(h1_ref[...])
    g_moe = gains[layer, :, model_width : 2 * model_width]
    back, term = norm_back(total[...], g_moe, unit, factor)
    dh1 = dy_ref[...].astype(F32) + back
    dh1_ref[...] = dh1
    term_ref[...] = term
    whole[rows_at(t * rows, rows)] = dh1.astype(BF16)
    wait = spread_rows(t, nt, rows, whole, spaces[16], spaces[17])
    finish()
    wait()
    dat_ref[...] = whole[...]
    for save in saves:
        save.wait()
    for move in moves:
        move.finish()


def attend_back_kernel(layer, source, nz, nt, heads, bind, ins, outs, scratch):
    s, z, t = lax.axis_index("section"), lax.axis_index("expert"), lax.axis_index("tensor")
    (x_ref, tabs, gains, dat_ref, dh1_ref, term_moe, q_ref, k_ref, v_ref, qr_ref, kr_ref) = ins[:11]
    wq, wk, wv, wo = ins[11:15]
    dx_ref, dqkv_ref, terms_ref = outs[:3]
    wq_s, wk_s, wv_s, wo_s, part, outgoing, came, s_sem, r_sem, w_sem, gs_sem, gr_sem = scratch[:12]
    if layer == 0:
        whole, terms_near, terms_in, t_sem, near_send, near_recv = scratch[12:18]
        rest, terms_other, moves_in = scratch[18:], ins[15], ins[16:]
        terms_out, moves_out = outs[3], outs[4:]
    else:
        rest, moves_in, moves_out = scratch[12:], ins[15:], outs[3:]
    moves = bind(moves_in, moves_out, rest)
    loads = [
        pltpu.make_async_copy(src, dst, w_sem.at[i])
        for i, (src, dst) in enumerate(((wo, wo_s), (wq, wq_s), (wk, wk_s), (wv, wv_s)))
    ]
    for load in loads:
        load.start()
    greet(all_peers(s, z, t, nz, nt))
    late = ()
    if layer == 0:
        late = moves[-3:]
        moves = moves[:-3]
        late[0].src, late[1].src, late[2].src = dqkv_ref, whole, terms_ref
    for move in moves:
        move.start()

    block = x_ref.shape[1]
    rows = block // nt
    size = tabs.shape[-1]
    g_attn, _, g_query, g_key = split_gains(gains[layer], x_ref.shape[2], size)
    scale = 1.0 / math.sqrt(size)
    cos, sin, bias = tabs[layer, 0], tabs[layer, 1], tabs[layer, 2]
    cos_all, sin_all = tiled(cos, heads), tiled(sin, heads)
    qr, kr, v = qr_ref[...], kr_ref[...], v_ref[...]
    scores = dot_nt(qr, kr) * scale + tiled(bias, heads)
    peak = jnp.max(scores, axis=-1, keepdims=True)
    weight = jnp.exp(scores - peak)
    probs = weight * (1.0 / jnp.sum(weight, axis=-1, keepdims=True))
    loads[0].wait()
    do = heads_to_rows(dot_nt(dat_ref[...], wo_s[...]).astype(BF16), heads, size)
    dv = dot_tn(probs.astype(BF16), do).astype(BF16)
    dp = dot_nt(do, v)
    ds = (probs * (dp - jnp.sum(probs * dp, axis=-1, keepdims=True))).astype(BF16)
    dqr = dot(ds, kr) * scale
    dkr = dot_tn(ds, qr) * scale
    dqn = dqr * cos_all - half_turn(dqr) * sin_all
    dkn = dkr * cos - half_turn(dkr) * sin
    q_unit, q_factor = unit_rows(heads_to_rows(q_ref[...], heads, size))
    k_unit, k_factor = unit_rows(k_ref[...])
    dq, term_query = norm_back(dqn, g_query, q_unit, q_factor)
    dk, term_key = norm_back(dkn, g_key, k_unit, k_factor)
    dq = rows_to_heads(dq.astype(BF16), heads, block)
    dk = dk.astype(BF16)
    dqkv_ref[:, : heads * size] = dq
    dqkv_ref[:, heads * size : (heads + 1) * size] = dk
    dqkv_ref[:, (heads + 1) * size :] = dv
    if layer == 0:
        late[0].start()
    for load in loads[1:]:
        load.wait()
    part[...] = dot_nt(dq, wq_s[...]) + dot_nt(dk, wk_s[...]) + dot_nt(dv, wv_s[...])
    total = reduce_rows(t, nt, rows, part, outgoing, came, s_sem, r_sem)
    mine = rows_at(t * rows, rows)
    unit, factor = unit_rows(x_ref[source, mine].astype(F32))
    back, term_attn = norm_back(total, g_attn, unit, factor)
    dx = (dh1_ref[...] + back).astype(BF16)
    terms_ref[...] = jnp.zeros_like(terms_ref)
    write_terms(terms_ref, 0, term_moe[...])
    write_terms(terms_ref, 8, term_attn)
    terms_ref[16:17, :size] = term_query
    terms_ref[16:17, size : 2 * size] = term_key
    if layer == 1:
        dx_ref[...] = dx
    else:
        late[2].start()
        whole[mine] = dx
        wait = spread_rows(t, nt, rows, whole, gs_sem, gr_sem)
        wait()
        late[1].start()
        late[2].arrive()

        def total_of(ref):
            out = ref[0, 0]
            for section in range(2):
                for origin in range(nz):
                    if section or origin:
                        out = out + ref[section, origin]
            return out

        @pl.when(s == 0)
        def _():
            copy = pltpu.make_async_copy(late[2].out, terms_in, t_sem.at[0])
            copy.start()
            copy.wait()

        @pl.when(s != 0)
        def _():
            copy = pltpu.make_async_copy(terms_other, terms_in, t_sem.at[0])
            copy.start()
            copy.wait()

        terms_near[0] = total_of(terms_in)

        def near(j):
            return remote(
                terms_near.at[0],
                terms_near.at[j],
                near_send.at[j],
                near_recv.at[j],
                tensor=partner(t, jnp.int32(j), nt),
            )

        for j in range(1, nt):
            near(j).start()
        sums = terms_near[0]
        for j in range(1, nt):
            near(j).wait_recv()
            sums = sums + terms_near[j]
        for j in range(1, nt):
            near(j).wait_send()
        terms_out[...] = sums
        late[0].finish()
        late[1].finish()
        late[2].leave()
        dx_ref[...] = dx
    for move in moves:
        move.finish()


def expert_grads_kernel(nz, step, ins, outs, scratch):
    s = lax.axis_index("section")
    own, near = (ins[0:5], ins[5:10]), (ins[10:15], ins[15:20])
    left, right, stage, in_sem, out_sem = scratch

    def loads(layer):
        out = []
        for i in range(5):
            target = left.at[i] if i < 3 else right.at[i - 3]
            out.append(
                (
                    pltpu.make_async_copy(own[layer][i], target.at[pl.ds(0, nz)], in_sem.at[i, 0]),
                    pltpu.make_async_copy(near[layer][i], target.at[pl.ds(nz, nz)], in_sem.at[i, 1]),
                )
            )
        return out

    order = (3, 0, 1, 4, 2)
    for layer in range(2):

        @pl.when(s == layer)
        def _():
            copies = loads(layer)
            for i in order:
                for copy in copies[i]:
                    copy.start()

    waits = loads(0)
    width = right.shape[-1]
    tokens = 2 * nz * right.shape[2]
    cols = left.shape[-1]
    done = set()

    def need(i):
        if i not in done:
            for copy in waits[i]:
                copy.wait()
            done.add(i)

    turn = 0
    for i, r in ((0, 0), (1, 0), (2, 1)):
        need(3 + r)
        need(i)
        for c in range(0, cols, step):
            slot = turn % 2
            if turn >= 2:
                pltpu.make_async_copy(stage.at[slot], outs[0].at[pl.ds(0, step)], out_sem.at[slot]).wait()
            lhs = left[i, :, :, c : c + step].reshape(tokens, step)
            stage[slot] = dot_tn(lhs, right[r].reshape(tokens, width))
            pltpu.make_async_copy(stage.at[slot], outs[i].at[pl.ds(c, step)], out_sem.at[slot]).start()
            turn += 1
    for slot in range(2):
        pltpu.make_async_copy(stage.at[slot], outs[0].at[pl.ds(0, step)], out_sem.at[slot]).wait()


def attend_grads_kernel(q_cols, size, ins, outs, scratch):
    s = lax.axis_index("section")
    spaces, sems = scratch[:4], scratch[4]

    def loads(layer):
        refs = ins[4 * layer : 4 * layer + 4]
        return [pltpu.make_async_copy(r, d, sems.at[i]) for i, (r, d) in enumerate(zip(refs, spaces))]

    for layer in range(2):

        @pl.when(s == layer)
        def _():
            for load in loads(layer):
                load.start()

    waits = loads(0)
    a_s, d_s, o_s, t_s = spaces

    def flat(ref):
        return ref[...].reshape(-1, ref.shape[-1])

    waits[0].wait()
    waits[1].wait()
    grad = dot_tn(flat(a_s), flat(d_s))
    outs[0][...] = grad[:, :q_cols]
    outs[1][...] = grad[:, q_cols : q_cols + size]
    outs[2][...] = grad[:, q_cols + size :]
    waits[2].wait()
    waits[3].wait()
    outs[3][...] = dot_tn(flat(o_s), flat(t_s))


def shape_of(shape, dtype):
    return jax.ShapeDtypeStruct(tuple(shape), dtype)


def like(value, lead=()):
    return shape_of(tuple(lead) + tuple(value.shape), value.dtype)


def call(body, name, number, ins, outs, scratch):
    def kernel(*refs):
        body(refs[: len(ins)], refs[len(ins) : len(ins) + len(outs)], refs[len(ins) + len(outs) :])

    return pl.pallas_call(
        kernel,
        out_shape=tuple(o for o, _ in outs),
        in_specs=[spec for _, spec in ins],
        out_specs=tuple(spec for _, spec in outs),
        scratch_shapes=list(scratch),
        compiler_params=pltpu.CompilerParams(
            collective_id=number, has_side_effects=number is not None, vmem_limit_bytes=VMEM_LIMIT
        ),
        name=name,
    )(*[value for value, _ in ins])


def vm(*values):
    return [(value, VM) for value in values]


def any_place(*values):
    return [(value, ANY) for value in values]


def block_tables(lengths, block, size):
    ends = jnp.cumsum(lengths)
    starts = ends - lengths
    places = jnp.arange(block, dtype=jnp.int32)
    segment = jnp.sum((places[:, None] >= ends[None, :]).astype(jnp.int32), axis=1)
    numbers = jnp.arange(lengths.shape[0], dtype=jnp.int32)
    offset = jnp.sum(jnp.where(segment[:, None] == numbers[None, :], starts[None, :], 0), axis=1)
    half = jnp.arange(size // 2, dtype=F32)
    inverse = jnp.exp(half * (-2.0 * math.log(THETA) / size))
    angle = (places - offset).astype(F32)[:, None] * inverse[None, :]
    cos, sin = jnp.cos(angle), jnp.sin(angle)
    allowed = (places[None, :] <= places[:, None]) & (segment[:, None] == segment[None, :])
    bias = jnp.where(allowed, 0.0, -1e30).astype(F32)
    return jnp.stack(
        [
            jnp.concatenate([cos, cos], axis=-1),
            jnp.concatenate([-sin, sin], axis=-1),
            bias,
        ]
    )


def on_device(
    boundary, seq_lengths, expert_ids, route_weights, attn_gain, moe_gain, query_gain, key_norm_gain,
    w_query, key_weight, value_weight, w_output, w_gate, w_up, w_down,
):
    nz, nt = lax.axis_size("expert"), lax.axis_size("tensor")
    micro, block, width = boundary.shape[1:]
    size = query_gain.shape[1]
    heads = w_query.shape[2] // size
    local_experts = w_gate.shape[1]
    hidden = local_experts * w_gate.shape[2]
    experts = local_experts * nz
    rows = block // nt
    q_cols = heads * size
    assert micro == 2 and key_weight.shape[2] == size and experts <= LANES
    dma = pltpu.SemaphoreType.DMA

    tabs = jax.vmap(lambda lengths: block_tables(lengths, block, size))(seq_lengths[0, :, 0])
    lanes = jnp.arange(LANES, dtype=jnp.int32)
    gates = jnp.sum(
        jnp.where(expert_ids[0][..., None] == lanes, route_weights[0][..., None], 0.0), axis=2
    )
    wg, wu, wd = (w[0].reshape(hidden, width) for w in (w_gate, w_up, w_down))
    wq, wk, wv, wo = w_query[0], key_weight[0], value_weight[0], w_output[0]
    gains = jnp.concatenate([attn_gain, moe_gain, query_gain, key_norm_gain], axis=1)

    spaces = [
        pltpu.VMEM((width, q_cols), BF16),
        pltpu.VMEM((width, size), BF16),
        pltpu.VMEM((width, size), BF16),
        pltpu.VMEM((q_cols, width), BF16),
        pltpu.VMEM((block, width), F32),
        pltpu.VMEM((block, width), BF16),
        pltpu.VMEM((nt, rows, width), BF16),
        dma((nt,)),
        dma((nt,)),
    ]
    gathered = [
        shape_of((width, q_cols), BF16),
        shape_of((width, size), BF16),
        shape_of((width, size), BF16),
        shape_of((q_cols, width), BF16),
    ]
    attend_outs = vm(
        shape_of((rows, width), F32),
        shape_of((rows, width), BF16),
        shape_of((block, width), BF16),
        shape_of((block, q_cols), F32),
        shape_of((block, size), F32),
        shape_of((block, size), BF16),
        shape_of((heads * block, size), BF16),
        shape_of((block, size), BF16),
        shape_of((block, q_cols), BF16),
    )
    own_part = pltpu.VMEM((nz, rows, width), F32)
    expert_scratch = [pltpu.VMEM((hidden, width), BF16)] * 3

    relay = Relay(0, (0, 0, 0, 1), nz)
    started = call(
        functools.partial(start_attend_kernel, nz, nt, heads, relay),
        "start_attend_0",
        0,
        any_place(boundary[0], tabs, gates, gains, wq, wk, wv, wo, wg, wu, wd),
        any_place(
            shape_of((2, block, width), BF16),
            shape_of((2, 3, block, size), F32),
            shape_of((2, nz, block, LANES), F32),
            like(gains, (2,)),
            *gathered,
            *[shape_of((hidden, width), BF16)] * 3,
        )
        + attend_outs,
        [
            pltpu.VMEM((block, width), BF16),
            pltpu.VMEM((3, block, size), F32),
            pltpu.VMEM(gains.shape, F32),
            dma((4,)), dma((3,)), dma((4,)), dma((6,)), dma((6,)), dma((2, nz)), dma((2, nz)),
        ]
        + relay.scratch(4)
        + spaces,
    )
    edges, tabs_all, gates_all, gains_all = started[:4]
    weights_0 = started[4:8]
    expert_weights = (wg, wu, wd) + tuple(started[8:11])
    h1_0, b_0, a_0, q_0, k_0, v_0, qr_0, kr_0, o_0 = started[11:]

    def run_experts(layer, b, h1, move_ins, move_outs, move_scratch, bind):
        return call(
            functools.partial(experts_kernel, layer, nz, nt, local_experts, bind),
            f"experts_{layer}",
            1 + layer,
            vm(b, h1, gates_all) + any_place(*expert_weights, *move_ins),
            vm(shape_of((block, width), BF16))
            + any_place(
                shape_of((nz, block, width), BF16),
                shape_of((nz, block, hidden), F32),
                shape_of((nz, block, hidden), F32),
                *move_outs,
            ),
            expert_scratch
            + [pltpu.VMEM((nz, block, hidden), F32)] * 2
            + [dma((3,)), dma((3,)), own_part]
            + exchange_scratch(nz, nt, rows, block, width)
            + move_scratch,
        )

    def experts_back(layer, dy, h1, gate_pre, up_pre, move_ins, move_outs, move_scratch, bind):
        return call(
            functools.partial(experts_back_kernel, layer, nz, nt, local_experts, bind),
            f"experts_back_{layer}",
            3 + layer,
            vm(dy, h1, gains_all, gates_all)
            + any_place(gate_pre, up_pre, *expert_weights, *move_ins),
            vm(
                shape_of((block, width), BF16),
                shape_of((rows, width), F32),
                shape_of((1, width), F32),
            )
            + any_place(
                shape_of((nz, block, width), BF16),
                shape_of((nz, block, hidden), BF16),
                shape_of((nz, block, hidden), BF16),
                shape_of((nz, block, hidden), BF16),
                *move_outs,
            ),
            expert_scratch
            + [pltpu.VMEM((2, block, hidden), F32)] * 2
            + [pltpu.VMEM((nz, block, hidden), BF16)] * 3
            + [dma((3,)), dma((2,)), dma((2,)), dma((4,)), own_part]
            + exchange_scratch(nz, nt, rows, block, width)
            + move_scratch,
        )

    def binder(kinds):
        def bind(ins, outs, scratch):
            return [
                kind.bind(ins[i] if i < len(ins) else None, outs[i], scratch[3 * i : 3 * i + 3])
                for i, kind in enumerate(kinds)
            ]

        return bind

    def shapes_of(kinds, values):
        out = []
        for kind, value in zip(kinds, values):
            if isinstance(kind, Near):
                out.append(like(value, (2,) if kind.both else ()))
            elif kind.sliced:
                out.append(shape_of((2, nz, block, width // nz), value.dtype))
            else:
                out.append(like(value, (2, nz)))
        return out

    def scratch_of(kinds):
        return [sem for kind in kinds for sem in kind.scratch()]

    qkv = Relay(1, (0, 0, 0), nz)
    ran = run_experts(
        0, b_0, h1_0, (wq, wk, wv), gathered[:3], qkv.scratch(3),
        lambda ins, outs, scratch: [qkv.bind(ins, outs, scratch)],
    )
    x_1, ball_0, gp_0, up_0 = ran[:4]
    qkv_1 = ran[4:]

    relay_1 = Relay(1, (1,), nz)
    attended = call(
        functools.partial(attend_kernel, 1, nz, nt, heads, relay_1),
        "attend_1",
        5,
        vm(x_1, tabs_all, gains_all) + any_place(*qkv_1, wo),
        any_place(gathered[3]) + attend_outs,
        [dma((4,))] + relay_1.scratch(1) + spaces,
    )
    weights_1 = tuple(qkv_1) + (attended[0],)
    h1_1, b_1, a_1, q_1, k_1, v_1, qr_1, kr_1, o_1 = attended[1:]

    kinds = (Gather(0, nz), Gather(0, nz, True), Near(0))
    values = (o_0, a_0, ball_0)
    ran = run_experts(
        1, b_1, h1_1, values, shapes_of(kinds, values), scratch_of(kinds), binder(kinds)
    )
    y_1, ball_1, gp_1, up_1 = ran[:4]
    oall_0, aall_0, bnear_0 = ran[4:]

    dy_1 = lax.dynamic_slice_in_dim(edges[1], lax.axis_index("tensor") * rows, rows, 0)
    kinds = (Gather(1, nz), Gather(1, nz, True), Near(1), Near(1, True))
    values = (o_1, a_1, ball_1, y_1)
    ran = experts_back(
        1, dy_1, h1_1, gp_1, up_1, values, shapes_of(kinds, values), scratch_of(kinds), binder(kinds)
    )
    dat_1, dh1_1, tm_1, dyall_1, hid_1, dg_1, du_1 = ran[:7]
    oall_1, aall_1, bnear_1, ends_1 = ran[7:]

    def attend_back(layer, x, source, dat, dh1, term_moe, kept, weights, kinds, values, late):
        outs = vm(
            shape_of((rows, width), BF16),
            shape_of((block, q_cols + 2 * size), BF16),
            shape_of((TERM_ROWS, TERM_COLS), F32),
        )
        scratch = spaces + [dma((4,)), dma((nt,)), dma((nt,))]
        ins = vm(x, tabs_all, gains_all, dat, dh1, term_moe, *kept) + any_place(*weights)
        shapes = [o for o, _ in outs]
        late_shapes = []
        if late is not None:
            outs += vm(shape_of((TERM_ROWS, TERM_COLS), F32))
            scratch += [
                pltpu.VMEM((block, width), BF16),
                pltpu.VMEM((nt, TERM_ROWS, TERM_COLS), F32),
                pltpu.VMEM((2, nz, TERM_ROWS, TERM_COLS), F32),
                dma((1,)),
                dma((nt,)),
                dma((nt,)),
            ]
            ins += any_place(late)
            last = (Gather(0, nz), Near(0, True), Gather(0, nz))
            late_shapes = shapes_of(last, (shapes[1], shape_of((block, width), BF16), shapes[2]))
            kinds = kinds + last
        return call(
            functools.partial(attend_back_kernel, layer, source, nz, nt, heads, binder(kinds)),
            f"attend_back_{layer}",
            6 + layer,
            ins + any_place(*values),
            outs + any_place(*shapes_of(kinds[: len(values)], values), *late_shapes),
            scratch + scratch_of(kinds),
        )

    kinds = (Gather(1, nz, True), Near(1), Near(1), Near(1), Near(1))
    values = (dat_1, dg_1, du_1, hid_1, dyall_1)
    ran = attend_back(
        1, x_1[None], 0, dat_1, dh1_1, tm_1, (q_1, k_1, v_1, qr_1, kr_1), weights_1, kinds, values, None
    )
    dx_1, dqkv_1, terms_1 = ran[:3]
    datall_1, near_1 = ran[3], ran[4:8]

    kinds = (Gather(1, nz), Gather(1, nz))
    values = (dqkv_1, terms_1)
    ran = experts_back(
        0, dx_1, h1_0, gp_0, up_0, values, shapes_of(kinds, values), scratch_of(kinds), binder(kinds)
    )
    dat_0, dh1_0, tm_0, dyall_0, hid_0, dg_0, du_0 = ran[:7]
    dqkvall_1, termsall_1 = ran[7:]

    kinds = (Gather(0, nz, True), Near(0), Near(0), Near(0), Near(0))
    values = (dat_0, dg_0, du_0, hid_0, dyall_0)
    ran = attend_back(
        0, edges, 0, dat_0, dh1_0, tm_0, (q_0, k_0, v_0, qr_0, kr_0), weights_0, kinds, values, termsall_1
    )
    terms, datall_0, near_0 = ran[3], ran[4], ran[5:9]
    dqkvall_0, ends_0 = ran[9:11]

    step = 256
    flat = shape_of((hidden, width), F32)
    grad_gate, grad_up, grad_down = call(
        functools.partial(expert_grads_kernel, nz, step),
        "expert_grads",
        None,
        any_place(
            dg_0, du_0, hid_0, ball_0, dyall_0,
            dg_1, du_1, hid_1, ball_1, dyall_1,
            *near_0[:3], bnear_0, near_0[3],
            *near_1[:3], bnear_1, near_1[3],
        ),
        any_place(flat, flat, flat),
        [
            pltpu.VMEM((3, 2 * nz, block, hidden), BF16),
            pltpu.VMEM((2, 2 * nz, block, width), BF16),
            pltpu.VMEM((2, step, width), F32),
            dma((5, 2)),
            dma((2,)),
        ],
    )
    operands = (aall_0, dqkvall_0, oall_0, datall_0, aall_1, dqkvall_1, oall_1, datall_1)
    grad_query, grad_key, grad_value, grad_output = call(
        functools.partial(attend_grads_kernel, q_cols, size),
        "attend_grads",
        None,
        any_place(*operands),
        vm(
            shape_of(wq.shape, F32),
            shape_of(wk.shape, F32),
            shape_of(wv.shape, F32),
            shape_of(wo.shape, F32),
        ),
        [pltpu.VMEM(o.shape, o.dtype) for o in operands[:4]] + [dma((4,))],
    )
    ends = jnp.where(lax.axis_index("section") == 0, ends_0, ends_1)
    return (
        ends[None],
        terms[8:16].reshape(1, width),
        terms[:8].reshape(1, width),
        terms[16:17, :size],
        terms[16:17, size : 2 * size],
        grad_query[None],
        grad_key[None],
        grad_value[None],
        grad_output[None],
        grad_gate.reshape(w_gate.shape),
        grad_up.reshape(w_gate.shape),
        grad_down.reshape(w_gate.shape),
    )


def solution(mesh):
    return jax.shard_map(
        on_device,
        mesh=mesh,
        in_specs=(
            P("section", None, "expert", None),
            P("section", None, "expert", None),
            P("section", None, "expert", None),
            P("section", None, "expert", None),
            P("section", None),
            P("section", None),
            P("section", None),
            P("section", None),
            P("section", "expert", "tensor"),
            P("section", "expert", "tensor"),
            P("section", "expert", "tensor"),
            P("section", "tensor", "expert"),
            P("section", "expert", "tensor", None),
            P("section", "expert", "tensor", None),
            P("section", "expert", "tensor", None),
        ),
        out_specs=(
            P("section", None, "expert", None),
            P("section", None),
            P("section", None),
            P("section", None),
            P("section", None),
            P("section", "expert", "tensor"),
            P("section", "expert", "tensor"),
            P("section", "expert", "tensor"),
            P("section", "tensor", "expert"),
            P("section", "expert", "tensor", None),
            P("section", "expert", "tensor", None),
            P("section", "expert", "tensor", None),
        ),
        check_vma=False,
    )
```

```python
import functools
import math

import jax
import jax.numpy as jnp
from jax import lax
from jax.experimental import pallas as pl
from jax.experimental.pallas import tpu as pltpu
from jax.sharding import PartitionSpec as P

EPSILON = 1e-06
THETA = 1000000.0
LANES = 128
TERM_ROWS = 24
TERM_COLS = 256
MESH = pl.DeviceIdType.MESH
F32 = jnp.float32
BF16 = jnp.bfloat16
VMEM_LIMIT = 60 * 1024 * 1024

ANY = pl.BlockSpec(memory_space=pl.ANY)
VM = pl.BlockSpec(memory_space=pltpu.VMEM)
SM = pl.BlockSpec(memory_space=pltpu.SMEM)


def partner(index, k, count):
    out, bit = 0, 1
    while bit < count:
        out = out + bit * lax.rem(lax.div(index, bit) + lax.div(k, bit), 2)
        bit *= 2
    return out


def rows_at(start, size):
    return pl.ds(pl.multiple_of(start, size), size)


def remote(src, dst, send_sem, recv_sem, **where):
    return pltpu.make_async_remote_copy(
        src_ref=src,
        dst_ref=dst,
        send_sem=send_sem,
        recv_sem=recv_sem,
        device_id=where,
        device_id_type=MESH,
    )


def greet(peers):
    barrier = pltpu.get_barrier_semaphore()
    for where in peers:
        pl.semaphore_signal(barrier, inc=1, device_id=where, device_id_type=MESH)
    pl.semaphore_wait(barrier, len(peers))


def layer_peers(z, t, nz, nt):
    i32 = jnp.int32
    peers = [{"expert": partner(z, i32(k), nz)} for k in range(1, nz)]
    peers += [{"tensor": partner(t, i32(k), nt)} for k in range(1, nt)]
    return peers


def dot(a, b):
    return lax.dot_general(a, b, (((1,), (0,)), ((), ())), preferred_element_type=F32)


def dot_nt(a, b):
    return lax.dot_general(a, b, (((1,), (1,)), ((), ())), preferred_element_type=F32)


def dot_tn(a, b):
    return lax.dot_general(a, b, (((0,), (0,)), ((), ())), preferred_element_type=F32)


def unit_rows(value):
    factor = lax.rsqrt(jnp.mean(value * value, axis=-1, keepdims=True) + EPSILON)
    return value * factor, factor


def norm_back(grad, gain, unit, factor):
    weighted = grad * gain
    inner = jnp.mean(weighted * unit, axis=-1, keepdims=True)
    return factor * (weighted - unit * inner), jnp.sum(grad * unit, axis=0, keepdims=True)


def expert_gates(gate_rows, first_expert, local_experts, width):
    rows = gate_rows.shape[0]
    lane = lax.broadcasted_iota(jnp.int32, gate_rows.shape, 1)
    column = lax.broadcasted_iota(jnp.int32, (rows, local_experts * width), 1)
    out = None
    for e in range(local_experts):
        one = jnp.sum(jnp.where(lane == first_expert + e, gate_rows, 0.0), axis=1, keepdims=True)
        wide = jnp.broadcast_to(one, column.shape)
        out = wide if out is None else jnp.where(column >= e * width, wide, out)
    return out


def write_terms(terms_ref, row, vector):
    for i in range(vector.shape[1] // TERM_COLS):
        terms_ref[row + i : row + i + 1, :] = vector[:, i * TERM_COLS : (i + 1) * TERM_COLS]


def exchange_scratch(nz, nt, rows, block, width):
    dma = pltpu.SemaphoreType.DMA
    half = width // 2
    return [
        pltpu.VMEM((nz, block, width), BF16),
        pltpu.VMEM((nz, block, width), BF16),
        pltpu.VMEM((block, width), F32),
        pltpu.VMEM((nz, 2 * rows, half), BF16),
        pltpu.VMEM((nz, 2, rows, half), BF16),
        pltpu.VMEM((nz, 2, rows, half), BF16),
        pltpu.VMEM((nz, 2, rows, half), BF16),
        pltpu.VMEM((nz, rows, width), BF16),
        pltpu.VMEM((nz, rows, width), BF16),
        pltpu.VMEM((nz, rows, width), F32),
        pltpu.VMEM((rows, width), F32),
        pltpu.VMEM((block, width), BF16),
        dma((4, nz)),
        dma((4, nz, 2)),
        dma((6, nz, 2)),
        dma((2, nt)),
    ]


EXCHANGE_SCRATCH = 16


def exchange(z, t, nz, nt, rows, own_rows, scratch, ready, work, moves):
    (full, outgoing, part, from_y, from_x, pairs, came_pairs) = scratch[:7]
    (passed, came_far, own_part, total) = scratch[7:11]
    far_sem, row_sem, part_sem = scratch[12:15]
    assert nt == 4
    i32 = jnp.int32
    width = full.shape[-1]
    half = width // 2
    first, second = pl.ds(0, half), pl.ds(half, half)
    near_x, near_y, across = (partner(t, i32(j), nt) for j in (1, 2, 3))

    def window(index):
        return rows_at(index * rows, rows)

    mine = window(t)
    x_rows, y_rows, across_rows = window(near_x), window(near_y), window(across)
    my_pair = rows_at(lax.div(t, 2) * (2 * rows), 2 * rows)
    y_pair = rows_at(lax.div(near_y, 2) * (2 * rows), 2 * rows)
    in_pair = lax.rem(t, 2)
    pair_mine, pair_x = window(in_pair), window(1 - in_pair)

    def far_copy(k, source):
        spot = full.at[source, mine]
        return remote(spot, spot, far_sem.at[0, k], far_sem.at[1, k], expert=partner(z, i32(k), nz))

    def row_copy(k, source, j, window_of):
        spot = full.at[source, window_of]
        return remote(
            spot, spot, row_sem.at[0, k, j], row_sem.at[1, k, j], tensor=(near_x, near_y)[j]
        )

    def on_copy(k, source, j, window_of):
        spot = full.at[source, window_of, (second, first)[j]]
        return remote(
            spot, spot, row_sem.at[2, k, j], row_sem.at[3, k, j], tensor=(near_x, near_y)[j]
        )

    def send_rows(k, source):
        for j in range(2):
            row_copy(k, source, j, mine).start()

    def pass_rows(k, source):
        row_copy(k, source, 0, x_rows).wait_recv()
        on_copy(k, source, 1, x_rows).start()
        row_copy(k, source, 1, y_rows).wait_recv()
        on_copy(k, source, 0, y_rows).start()

    def wait_rows(k, source):
        for j in range(2):
            on_copy(k, source, j, across_rows).wait_recv()

    def part_copy(k, i):
        src = ((y_pair, first), (across_rows, second), (x_rows, second))[i]
        dst = (from_y.at[k], from_x.at[k, 1], from_x.at[k, 0])[i]
        group, slot = ((0, 0), (2, 1), (2, 0))[i]
        return remote(
            outgoing.at[k, src[0], src[1]],
            dst,
            part_sem.at[group, k, slot],
            part_sem.at[group + 1, k, slot],
            tensor=near_x if i else near_y,
        )

    def pair_copy(k, j):
        return remote(
            pairs.at[k, j],
            came_pairs.at[k, j],
            part_sem.at[4, k, j],
            part_sem.at[5, k, j],
            tensor=(near_x, near_y)[j],
        )

    def sum_copy(k):
        return remote(
            passed.at[k],
            came_far.at[k],
            far_sem.at[2, k],
            far_sem.at[3, k],
            expert=partner(z, k, nz),
        )

    def produce(k, source):
        wait_rows(k, source)
        part[...] = work(k, source, full[source])
        outgoing[k] = part[...].astype(BF16)
        for i in range(3):
            part_copy(k, i).start()
        own_part[k] = part[mine]

    def pair_up(k):
        part_copy(k, 0).wait_recv()
        kept = outgoing[k, x_rows, first].astype(F32)
        pairs[k, 0] = (kept + from_y[k, pair_x].astype(F32)).astype(BF16)
        pair_copy(k, 0).start()
        part_copy(k, 1).wait_recv()
        kept = outgoing[k, y_rows, second].astype(F32)
        pairs[k, 1] = (kept + from_x[k, 1].astype(F32)).astype(BF16)
        pair_copy(k, 1).start()

    def collect(k):
        part_copy(k, 2).wait_recv()
        pair_copy(k, 0).wait_recv()
        pair_copy(k, 1).wait_recv()
        own = own_part[k]
        left = own[:, :half] + from_y[k, pair_mine].astype(F32) + came_pairs[k, 0].astype(F32)
        right = own[:, half:] + from_x[k, 0].astype(F32) + came_pairs[k, 1].astype(F32)
        return left, right

    def collect_own():
        left, right = collect(i32(0))
        total[:, :half] = left
        total[:, half:] = right

    def collect_far(k):
        left, right = collect(k)
        passed[k, :, first] = left.astype(BF16)
        passed[k, :, second] = right.astype(BF16)
        sum_copy(k).start()

    full[z, mine] = own_rows
    for k in range(1, nz):
        far_copy(k, z).start()
    send_rows(0, z)
    ready()
    for k in range(1, nz):
        source = partner(z, i32(k), nz)
        far_copy(k, source).wait_recv()
        send_rows(k, source)
        if k == 1:
            pass_rows(0, z)
    for move in moves:
        move.start()
    pass_rows(1, partner(z, i32(1), nz))

    def step(k, carry):
        @pl.when(k + 1 < nz)
        def _():
            pass_rows(k + 1, partner(z, k + 1, nz))

        turn = lax.rem(k, nz)
        produce(turn, partner(z, turn, nz))

        @pl.when(k >= 2)
        def _():
            pair_up(k - 1)

        @pl.when(k >= 3)
        def _():
            collect_far(k - 2)

        return carry

    lax.fori_loop(1, nz + 1, step, 0)
    for move in moves:
        move.poll(1)
    collect_far(i32(nz - 1))
    pair_up(i32(0))
    for move in moves:
        move.poll(2)
    collect_own()
    for k in range(1, nz):
        sum_copy(i32(k)).wait_recv()
        total[...] += came_far[k].astype(F32)

    def finish():
        for k in range(1, nz):
            far_copy(k, z).wait_send()
            sum_copy(i32(k)).wait_send()
        for k in range(nz):
            source = partner(z, i32(k), nz)
            for j in range(2):
                row_copy(k, source, j, mine).wait_send()
                on_copy(k, source, j, (y_rows, x_rows)[j]).wait_send()
                pair_copy(k, j).wait_send()
            for i in range(3):
                part_copy(k, i).wait_send()

    return finish


def spread_rows(t, nt, rows, block_ref, send_sem, recv_sem):
    i32 = jnp.int32
    mine = rows_at(t * rows, rows)
    for j in range(1, nt):
        remote(
            block_ref.at[mine],
            block_ref.at[mine],
            send_sem.at[j],
            recv_sem.at[j],
            tensor=partner(t, i32(j), nt),
        ).start()

    def wait():
        for j in range(1, nt):
            peer = partner(t, i32(j), nt)
            theirs = rows_at(peer * rows, rows)
            copy = remote(
                block_ref.at[theirs],
                block_ref.at[theirs],
                send_sem.at[j],
                recv_sem.at[j],
                tensor=peer,
            )
            copy.wait_send()
            copy.wait_recv()

    return wait


def reduce_rows(t, nt, rows, part, outgoing, came, send_sem, recv_sem):
    i32 = jnp.int32
    outgoing[...] = part[...].astype(BF16)

    def copy(j):
        peer = partner(t, i32(j), nt)
        return remote(
            outgoing.at[rows_at(peer * rows, rows)],
            came.at[j],
            send_sem.at[j],
            recv_sem.at[j],
            tensor=peer,
        )

    for j in range(1, nt):
        copy(j).start()
    total = part[rows_at(t * rows, rows)]
    for j in range(1, nt):
        copy(j).wait_recv()
        total = total + came[j].astype(F32)
    for j in range(1, nt):
        copy(j).wait_send()
    return total


def all_peers(s, z, t, nz, nt):
    i32 = jnp.int32
    peers = [{"section": 1 - s}]
    for k in range(1, nz):
        zz = partner(z, i32(k), nz)
        peers += [{"expert": zz}, {"section": 1 - s, "expert": zz}]
    return peers + [{"tensor": partner(t, i32(j), nt)} for j in range(1, nt)]


class Relay:
    def __init__(self, layer, spots, nz):
        self.layer, self.spots, self.nz = layer, spots, nz

    def scratch(self, count):
        dma = pltpu.SemaphoreType.DMA
        return [dma((count,))] + [dma((count, self.nz))] * 6

    def bind(self, shards, outs, sems):
        self.s, self.z = lax.axis_index("section"), lax.axis_index("expert")
        self.shards, self.outs, self.sems = shards, outs, sems
        self.source = self.s == self.layer
        self.count = len(shards)
        return self

    def place(self, a, owner):
        dim = self.spots[a]
        size = self.shards[a].shape[dim]
        window = rows_at(owner * size, size)
        return self.outs[a].at[window] if dim == 0 else self.outs[a].at[:, window]

    def home(self, a):
        return pltpu.make_async_copy(self.shards[a], self.place(a, self.z), self.sems[0].at[a])

    def hop(self, a, owner, step, right, own=False):
        spot = self.place(a, owner)
        send, recv = self.sems[1:3] if right else self.sems[3:5]
        return remote(
            self.shards[a] if own else spot,
            spot,
            send.at[a, step],
            recv.at[a, step],
            expert=self.z + 1 if right else self.z - 1,
        )

    def hand(self, a, owner, own=False):
        spot = self.place(a, owner)
        return remote(
            self.shards[a] if own else spot,
            spot,
            self.sems[5].at[a, owner],
            self.sems[6].at[a, owner],
            section=1 - self.s,
        )

    def begin_side(self, a, right):
        @pl.when(self.source & ((self.z + 1 < self.nz) if right else (self.z >= 1)))
        def _():
            self.hop(a, self.z, 1, right, True).start()

    def begin_home(self, a):
        @pl.when(self.source)
        def _():
            self.home(a).start()
            self.hand(a, self.z, True).start()

    def begin(self, a):
        self.begin_side(a, True)
        self.begin_side(a, False)
        self.begin_home(a)

    def step(self, a, k):
        z, nz = self.z, self.nz

        @pl.when(self.source & (z >= k))
        def _():
            self.hop(a, z - k, k, True).wait_recv()

            @pl.when(z + 1 < nz)
            def _():
                self.hop(a, z - k, k + 1, True).start()

            self.hand(a, z - k).start()

        @pl.when(self.source & (z + k < nz))
        def _():
            self.hop(a, z + k, k, False).wait_recv()

            @pl.when(z >= 1)
            def _():
                self.hop(a, z + k, k + 1, False).start()

            self.hand(a, z + k).start()

    def settle(self, a):
        @pl.when(self.source)
        def _():
            self.home(a).wait()

        @pl.when(jnp.logical_not(self.source))
        def _():
            for owner in range(self.nz):
                self.hand(a, owner).wait_recv()

    def end(self, a):
        z, nz = self.z, self.nz

        @pl.when(self.source)
        def _():
            for owner in range(nz):
                self.hand(a, owner).wait_send()
            for step in range(1, nz):

                @pl.when((z >= step - 1) & (z + 1 < nz))
                def _():
                    self.hop(a, z - (step - 1), step, True).wait_send()

                @pl.when((z + step - 1 < nz) & (z >= 1))
                def _():
                    self.hop(a, z + (step - 1), step, False).wait_send()

    def start(self):
        for a in range(self.count):
            self.begin(a)

    def poll(self, turn):
        if turn < self.nz - 1:
            for a in range(self.count):
                self.step(a, turn)

    def finish(self):
        for k in range(min(3, self.nz - 1), self.nz):
            for a in range(self.count):
                self.step(a, k)
        for a in range(self.count):
            self.settle(a)
            self.end(a)


class Gather:
    def __init__(self, layer, nz, sliced=False):
        self.layer, self.nz, self.sliced = layer, nz, sliced

    def scratch(self):
        dma = pltpu.SemaphoreType.DMA
        return [dma((1,)), dma((self.nz,)), dma((2, self.nz))]

    def bind(self, src, out, sems):
        self.s, self.z = lax.axis_index("section"), lax.axis_index("expert")
        self.src, self.out, self.sems = src, out, sems
        return self

    def copy(self, k, local, section=None, origin=None):
        zz = partner(self.z, jnp.int32(k), self.nz)
        src = self.src
        if self.sliced:
            cols = self.out.shape[-1]
            src = src.at[:, rows_at(zz * cols, cols)]
        section = self.s if section is None else section
        spot = self.out.at[section, self.z if origin is None else origin]
        if local:
            return pltpu.make_async_copy(src, spot, self.sems[0].at[0])
        return remote(
            src,
            spot,
            self.sems[1].at[k],
            self.sems[2].at[section, k],
            section=jnp.int32(self.layer),
            expert=zz,
        )

    def start(self):
        for k in range(1, self.nz):
            self.copy(k, False).start()

        @pl.when(self.s == self.layer)
        def _():
            self.copy(0, True).start()

        @pl.when(self.s != self.layer)
        def _():
            self.copy(0, False).start()

    def poll(self, turn):
        pass

    def arrive(self):
        @pl.when(self.s == self.layer)
        def _():
            self.copy(0, True).wait()
            for section in range(2):
                for k in range(self.nz):
                    if k or section != self.layer:
                        zz = partner(self.z, jnp.int32(k), self.nz)
                        self.copy(k, False, section, zz).wait_recv()

    def leave(self):
        for k in range(1, self.nz):
            self.copy(k, False).wait_send()

        @pl.when(self.s != self.layer)
        def _():
            self.copy(0, False).wait_send()

    def finish(self):
        self.arrive()
        self.leave()


class Near:
    def __init__(self, layer, both=False):
        self.layer, self.both = layer, both

    def scratch(self):
        dma = pltpu.SemaphoreType.DMA
        return [dma((1,)), dma((1,)), dma((1,))]

    def bind(self, src, out, sems):
        self.s, self.src, self.out, self.sems = lax.axis_index("section"), src, out, sems
        return self

    def local(self):
        return pltpu.make_async_copy(self.src, self.out.at[self.layer], self.sems[0].at[0])

    def copy(self):
        return remote(
            self.src,
            self.out.at[1 - self.layer] if self.both else self.out,
            self.sems[1].at[0],
            self.sems[2].at[0],
            section=jnp.int32(self.layer),
        )

    def start(self):
        if self.both:

            @pl.when(self.s == self.layer)
            def _():
                self.local().start()

        @pl.when(self.s != self.layer)
        def _():
            self.copy().start()

    def poll(self, turn):
        pass

    def finish(self):
        @pl.when(self.s == self.layer)
        def _():
            if self.both:
                self.local().wait()
            remote(
                self.src,
                self.out.at[1 - self.layer] if self.both else self.out,
                self.sems[1].at[0],
                self.sems[2].at[0],
                section=1 - self.s,
            ).wait_recv()

        @pl.when(self.s != self.layer)
        def _():
            self.copy().wait_send()


def heads_to_rows(value, heads, size):
    return jnp.concatenate([value[:, h * size : (h + 1) * size] for h in range(heads)], axis=0)


def rows_to_heads(value, heads, block):
    return jnp.concatenate([value[h * block : (h + 1) * block] for h in range(heads)], axis=1)


def split_gains(row, width, size):
    return (
        row[:, :width],
        row[:, width : 2 * width],
        row[:, 2 * width : 2 * width + size],
        row[:, 2 * width + size :],
    )


def tiled(value, times):
    return jnp.concatenate([value] * times, axis=0)


def half_turn(value):
    return pltpu.roll(value, value.shape[-1] // 2, value.ndim - 1)


def attend_body(t, nt, heads, x_ref, tables, gains, outs, scratch, wait_qkv, wait_out):
    (h1_ref, b_ref, a_ref, q_ref, k_ref, v_ref, qr_ref, kr_ref, o_ref) = outs
    (wq_s, wk_s, wv_s, wo_s, part, outgoing, came, s_sem, r_sem) = scratch
    block, width = x_ref.shape
    rows = block // nt
    cos, sin, bias = tables
    size = cos.shape[-1]
    g_attn, g_moe, g_query, g_key = split_gains(gains, width, size)
    unit, _ = unit_rows(x_ref[...].astype(F32))
    a_ref[...] = (unit * g_attn).astype(BF16)
    wait_qkv()
    q = dot(a_ref[...], wq_s[...])
    q_ref[...] = q
    k = dot(a_ref[...], wk_s[...])
    k_ref[...] = k
    v = dot(a_ref[...], wv_s[...]).astype(BF16)
    v_ref[...] = v
    qn = unit_rows(heads_to_rows(q, heads, size))[0] * g_query
    kn = unit_rows(k)[0] * g_key
    qr = (qn * tiled(cos, heads) + half_turn(qn) * tiled(sin, heads)).astype(BF16)
    kr = (kn * cos + half_turn(kn) * sin).astype(BF16)
    qr_ref[...] = qr
    kr_ref[...] = kr
    scores = dot_nt(qr, kr) * (1.0 / math.sqrt(size)) + tiled(bias, heads)
    peak = jnp.max(scores, axis=-1, keepdims=True)
    weight = jnp.exp(scores - peak)
    probs = weight * (1.0 / jnp.sum(weight, axis=-1, keepdims=True))
    o = dot(probs.astype(BF16), v).astype(BF16)
    o_ref[...] = rows_to_heads(o, heads, block)
    wait_out()
    part[...] = dot(o_ref[...], wo_s[...])
    total = reduce_rows(t, nt, rows, part, outgoing, came, s_sem, r_sem)
    h1 = x_ref[rows_at(t * rows, rows)].astype(F32) + total
    h1_ref[...] = h1
    b_ref[...] = (unit_rows(h1)[0] * g_moe).astype(BF16)


def fill_tables(tabs, lengths, m):
    block, size = tabs.shape[2:]
    row = lax.broadcasted_iota(jnp.int32, (block, size), 0)
    lane = lax.broadcasted_iota(jnp.int32, (block, size), 1)
    begin, segment, segment_of_lane = (jnp.zeros((block, size), jnp.int32) for _ in range(3))
    end = jnp.int32(0)
    for n in range(lengths.shape[1]):
        end = end + lengths[m, n]
        begin = jnp.where(row >= end, end, begin)
        segment = segment + jnp.where(row >= end, 1, 0)
        segment_of_lane = segment_of_lane + jnp.where(lane >= end, 1, 0)
    half = size // 2
    position = jnp.where(lane >= half, lane - half, lane).astype(F32)
    inverse = jnp.exp(position * (-2.0 * math.log(THETA) / size))
    angle = (row - begin).astype(F32) * inverse
    sin = jnp.sin(angle)
    tabs[m, 0] = jnp.cos(angle)
    tabs[m, 1] = jnp.where(lane >= half, sin, -sin)
    tabs[m, 2] = jnp.where((lane <= row) & (segment == segment_of_lane), 0.0, -1e30)


def fill_gates(gates, ids, route_weights, m):
    expert_of, weight_of = ids[m], route_weights[m]
    lane = lax.broadcasted_iota(jnp.int32, gates.shape[1:], 1)
    out = jnp.zeros(gates.shape[1:], F32)
    for c in range(expert_of.shape[1]):
        out = out + jnp.where(lane == expert_of[:, c : c + 1], weight_of[:, c : c + 1], 0.0)
    gates[m] = out


def start_attend_kernel(nz, nt, heads, relay, ins, outs, scratch):
    s, z, t = lax.axis_index("section"), lax.axis_index("expert"), lax.axis_index("tensor")
    lengths, ids, route_weights, boundary, gains, wq, wk, wv, wo, wg, wu, wd = ins
    edges, tabs_out, gates_out, gains_out = outs[:4]
    gathered, (sg, su, sd), results = outs[4:8], outs[8:11], outs[11:]
    x_s, tabs_s, gains_s, tabs, gates = scratch[:5]
    w_sem, in_sem, own_sem, sib_send, sib_recv, gate_send, gate_recv = scratch[5:12]
    relay.bind((wq, wk, wv, wo), gathered, scratch[12:19])
    attn_scratch = scratch[19:]
    other = 1 - s
    i32 = jnp.int32

    own = [
        pltpu.make_async_copy(boundary.at[s], edges.at[s], own_sem.at[0]),
        pltpu.make_async_copy(tabs.at[s], tabs_out.at[s], own_sem.at[1]),
        pltpu.make_async_copy(gains, gains_out.at[s], own_sem.at[2]),
        pltpu.make_async_copy(gates.at[s], gates_out.at[s, z], own_sem.at[3]),
    ]
    own[0].start()
    own[2].start()
    greet(all_peers(s, z, t, nz, nt))

    def sibling(i, src, dst):
        return remote(src, dst, sib_send.at[i], sib_recv.at[i], section=other)

    pairs = [
        (boundary.at[other], edges.at[s], edges.at[other]),
        (tabs.at[other], tabs_out.at[s], tabs_out.at[other]),
        (gains, gains_out.at[s], gains_out.at[other]),
        (wg, sg, sg),
        (wu, su, su),
        (wd, sd, sd),
    ]
    for i in (0, 2):
        sibling(i, *pairs[i][:2]).start()
    for a in range(3):
        relay.begin(a)
    relay.begin_home(3)

    @pl.when(z == 0)
    def _():
        relay.begin_side(3, True)

    @pl.when(z == nz - 1)
    def _():
        relay.begin_side(3, False)

    def gate_copy(d, k, arrival=False):
        zz = partner(z, i32(k), nz)
        section = s if d == 0 else other
        return remote(
            gates.at[section],
            gates_out.at[section, zz] if arrival else gates_out.at[s, z],
            gate_send.at[d, k],
            gate_recv.at[d, k],
            section=section,
            expert=zz,
        )

    for m in range(2):
        fill_tables(tabs, lengths, m)
    sibling(1, *pairs[1][:2]).start()
    own[1].start()
    for m in range(2):
        fill_gates(gates, ids, route_weights, m)
    own[3].start()
    turns = [(d, k) for d in range(2) for k in range(nz) if d or k]
    for d, k in turns:
        gate_copy(d, k).start()
    for i in range(3, 6):
        sibling(i, *pairs[i][:2]).start()

    for copy in own:
        copy.wait()
    for i in range(3):
        sibling(i, pairs[i][0], pairs[i][2]).wait_recv()
    loads = [
        pltpu.make_async_copy(edges.at[0], x_s, in_sem.at[0]),
        pltpu.make_async_copy(tabs_out.at[0], tabs_s, in_sem.at[1]),
        pltpu.make_async_copy(gains_out.at[0], gains_s, in_sem.at[2]),
    ]
    for load in loads:
        load.start()
    for load in loads:
        load.wait()

    def bring(a):
        return pltpu.make_async_copy(gathered[a], attn_scratch[a], w_sem.at[a])

    def wait_qkv():
        for k in range(1, nz):
            for a in range(3):
                relay.step(a, k)

            @pl.when((z == k) & (z < nz - 1))
            def _():
                relay.begin_side(3, True)

            @pl.when((z == nz - 1 - k) & (z > 0))
            def _():
                relay.begin_side(3, False)

        for a in range(3):
            relay.settle(a)
            bring(a).start()
        for a in range(3):
            bring(a).wait()

    def wait_out():
        for k in range(1, nz):
            relay.step(3, k)
        relay.settle(3)
        bring(3).start()
        bring(3).wait()

    tables = (tabs_s[0], tabs_s[1], tabs_s[2])
    attend_body(t, nt, heads, x_s, tables, gains_s[...], results, attn_scratch, wait_qkv, wait_out)
    for i in range(6):
        sibling(i, *pairs[i][:2]).wait_send()
    for i in range(3, 6):
        sibling(i, pairs[i][0], pairs[i][2]).wait_recv()
    for d, k in turns:
        gate_copy(d, k).wait_send()
        gate_copy(d, k, True).wait_recv()
    for a in range(4):
        relay.end(a)


def attend_kernel(layer, nz, nt, heads, bind, ins, outs, scratch):
    s, z, t = lax.axis_index("section"), lax.axis_index("expert"), lax.axis_index("tensor")
    x_ref, tabs, gains, wq, wk, wv, wo = ins[:7]
    w_sem, attn_scratch, rest = scratch[0], scratch[1:10], scratch[10:]
    moves = bind(ins[7:], outs[9:], rest)
    loads = [
        pltpu.make_async_copy(src, dst, w_sem.at[i])
        for i, (src, dst) in enumerate(zip((wq, wk, wv, wo), attn_scratch))
    ]
    for load in loads:
        load.start()
    greet(all_peers(s, z, t, nz, nt))
    for move in moves:
        move.start()

    def wait_qkv():
        for load in loads[:3]:
            load.wait()

    tables = (tabs[layer, 0], tabs[layer, 1], tabs[layer, 2])
    attend_body(
        t, nt, heads, x_ref, tables, gains[layer], outs[:9], attn_scratch, wait_qkv, loads[3].wait
    )
    for move in moves:
        move.finish()


def load_experts(layer, s, own, sibling, scratch, sems):
    def copies(refs):
        return [pltpu.make_async_copy(r, d, sems.at[i]) for i, (r, d) in enumerate(zip(refs, scratch))]

    @pl.when(s == layer)
    def _():
        for copy in copies(own):
            copy.start()

    @pl.when(s != layer)
    def _():
        for copy in copies(sibling):
            copy.start()

    return copies(own)


def experts_kernel(layer, nz, nt, local_experts, bind, ins, outs, scratch):
    s, z, t = lax.axis_index("section"), lax.axis_index("expert"), lax.axis_index("tensor")
    b_ref, h1_ref, gates, wg, wu, wd, sg, su, sd = ins[:9]
    y_ref, b_out, g_out, u_out = outs[:4]
    wg_s, wu_s, wd_s, g_s, u_s, w_sem, o_sem = scratch[:7]
    spaces, rest = scratch[7 : 7 + EXCHANGE_SCRATCH], scratch[7 + EXCHANGE_SCRATCH :]
    moves = bind(ins[9:], outs[4:], rest)
    rows = b_ref.shape[0]
    loads = load_experts(layer, s, (wg, wu, wd), (sg, su, sd), (wg_s, wu_s, wd_s), w_sem)
    greet(all_peers(s, z, t, nz, nt))
    width = wg.shape[0] // local_experts

    def ready():
        for load in loads:
            load.wait()

    def work(k, origin, rows_in):
        gate_pre = dot_nt(rows_in, wg_s[...])
        up_pre = dot_nt(rows_in, wu_s[...])
        g_s[origin] = gate_pre
        u_s[origin] = up_pre
        weight = expert_gates(gates[layer, origin], z * local_experts, local_experts, width)
        hidden = (gate_pre * jax.nn.sigmoid(gate_pre) * up_pre * weight).astype(BF16)
        return dot(hidden, wd_s[...])

    finish = exchange(z, t, nz, nt, rows, b_ref[...], spaces, ready, work, moves)
    full, total, whole, spread_sem = spaces[0], spaces[10], spaces[11], spaces[15]
    saves = [
        pltpu.make_async_copy(full, b_out, o_sem.at[0]),
        pltpu.make_async_copy(g_s, g_out, o_sem.at[1]),
        pltpu.make_async_copy(u_s, u_out, o_sem.at[2]),
    ]
    for save in saves:
        save.start()
    whole[rows_at(t * rows, rows)] = (h1_ref[...] + total[...]).astype(BF16)
    wait = spread_rows(t, nt, rows, whole, spread_sem.at[0], spread_sem.at[1])
    finish()
    wait()
    y_ref[...] = whole[...]
    for save in saves:
        save.wait()
    for move in moves:
        move.finish()


def experts_back_kernel(layer, nz, nt, local_experts, bind, ins, outs, scratch):
    s, z, t = lax.axis_index("section"), lax.axis_index("expert"), lax.axis_index("tensor")
    dy_ref, h1_ref, gains, gates, g_in, u_in, wg, wu, wd, sg, su, sd = ins[:12]
    dat_ref, dh1_ref, term_ref, dy_out, hid_out, dg_out, du_out = outs[:7]
    wg_s, wu_s, wd_s, g_s, u_s, hid_s, dg_s, du_s, w_sem, g_sem, u_sem, o_sem = scratch[:12]
    spaces, rest = scratch[12 : 12 + EXCHANGE_SCRATCH], scratch[12 + EXCHANGE_SCRATCH :]
    moves = bind(ins[12:], outs[7:], rest)
    rows, model_width = dy_ref.shape
    loads = load_experts(layer, s, (wd, wg, wu), (sd, sg, su), (wd_s, wg_s, wu_s), w_sem)

    def kept(k):
        origin, slot = partner(z, lax.rem(k + 1, nz), nz), lax.rem(k, 2)
        return (
            pltpu.make_async_copy(g_in.at[origin], g_s.at[slot], g_sem.at[slot]),
            pltpu.make_async_copy(u_in.at[origin], u_s.at[slot], u_sem.at[slot]),
        )

    for load in kept(jnp.int32(0)):
        load.start()
    greet(all_peers(s, z, t, nz, nt))
    width = wg.shape[0] // local_experts

    def ready():
        for load in loads:
            load.wait()

    def work(k, origin, rows_in):
        turn = lax.rem(k + nz - 1, nz)
        for load in kept(turn):
            load.wait()

        @pl.when(turn + 1 < nz)
        def _():
            for load in kept(turn + 1):
                load.start()

        slot = lax.rem(turn, 2)
        gate_pre, up_pre = g_s[slot], u_s[slot]
        weight = expert_gates(gates[layer, origin], z * local_experts, local_experts, width)
        sigmoid = jax.nn.sigmoid(gate_pre)
        silu = gate_pre * sigmoid
        hid_s[origin] = (silu * up_pre * weight).astype(BF16)
        grad_hidden = dot_nt(rows_in, wd_s[...]) * weight
        dg_s[origin] = (grad_hidden * up_pre * sigmoid * (1.0 + gate_pre * (1.0 - sigmoid))).astype(BF16)
        du_s[origin] = (grad_hidden * silu).astype(BF16)
        return dot(dg_s[origin], wg_s[...]) + dot(du_s[origin], wu_s[...])

    finish = exchange(z, t, nz, nt, rows, dy_ref[...], spaces, ready, work, moves)
    full, total, whole, spread_sem = spaces[0], spaces[10], spaces[11], spaces[15]
    saves = [
        pltpu.make_async_copy(full, dy_out, o_sem.at[0]),
        pltpu.make_async_copy(hid_s, hid_out, o_sem.at[1]),
        pltpu.make_async_copy(dg_s, dg_out, o_sem.at[2]),
        pltpu.make_async_copy(du_s, du_out, o_sem.at[3]),
    ]
    for save in saves:
        save.start()
    unit, factor = unit_rows(h1_ref[...])
    g_moe = gains[layer, :, model_width : 2 * model_width]
    back, term = norm_back(total[...], g_moe, unit, factor)
    dh1 = dy_ref[...].astype(F32) + back
    dh1_ref[...] = dh1
    term_ref[...] = term
    whole[rows_at(t * rows, rows)] = dh1.astype(BF16)
    wait = spread_rows(t, nt, rows, whole, spread_sem.at[0], spread_sem.at[1])
    finish()
    wait()
    dat_ref[...] = whole[...]
    for save in saves:
        save.wait()
    for move in moves:
        move.finish()


def attend_back_kernel(layer, source, nz, nt, heads, bind, ins, outs, scratch):
    s, z, t = lax.axis_index("section"), lax.axis_index("expert"), lax.axis_index("tensor")
    (x_ref, tabs, gains, dat_ref, dh1_ref, term_moe, q_ref, k_ref, v_ref, qr_ref, kr_ref) = ins[:11]
    wq, wk, wv, wo = ins[11:15]
    dx_ref, dqkv_ref, terms_ref = outs[:3]
    wq_s, wk_s, wv_s, wo_s, part, outgoing, came, s_sem, r_sem, w_sem, gs_sem, gr_sem = scratch[:12]
    if layer == 0:
        whole, terms_near, terms_in, t_sem, near_send, near_recv = scratch[12:18]
        rest, terms_other, moves_in = scratch[18:], ins[15], ins[16:]
        terms_out, moves_out = outs[3], outs[4:]
    else:
        rest, moves_in, moves_out = scratch[12:], ins[15:], outs[3:]
    moves = bind(moves_in, moves_out, rest)
    loads = [
        pltpu.make_async_copy(src, dst, w_sem.at[i])
        for i, (src, dst) in enumerate(((wo, wo_s), (wq, wq_s), (wk, wk_s), (wv, wv_s)))
    ]
    for load in loads:
        load.start()
    greet(all_peers(s, z, t, nz, nt))
    late = ()
    if layer == 0:
        late = moves[-3:]
        moves = moves[:-3]
        late[0].src, late[1].src, late[2].src = dqkv_ref, whole, terms_ref
    for move in moves:
        move.start()

    block = x_ref.shape[1]
    rows = block // nt
    size = tabs.shape[-1]
    g_attn, _, g_query, g_key = split_gains(gains[layer], x_ref.shape[2], size)
    scale = 1.0 / math.sqrt(size)
    cos, sin, bias = tabs[layer, 0], tabs[layer, 1], tabs[layer, 2]
    cos_all, sin_all = tiled(cos, heads), tiled(sin, heads)
    qr, kr, v = qr_ref[...], kr_ref[...], v_ref[...]
    scores = dot_nt(qr, kr) * scale + tiled(bias, heads)
    peak = jnp.max(scores, axis=-1, keepdims=True)
    weight = jnp.exp(scores - peak)
    probs = weight * (1.0 / jnp.sum(weight, axis=-1, keepdims=True))
    loads[0].wait()
    do = heads_to_rows(dot_nt(dat_ref[...], wo_s[...]).astype(BF16), heads, size)
    dv = dot_tn(probs.astype(BF16), do).astype(BF16)
    dp = dot_nt(do, v)
    ds = (probs * (dp - jnp.sum(probs * dp, axis=-1, keepdims=True))).astype(BF16)
    dqr = dot(ds, kr) * scale
    dkr = dot_tn(ds, qr) * scale
    dqn = dqr * cos_all - half_turn(dqr) * sin_all
    dkn = dkr * cos - half_turn(dkr) * sin
    q_unit, q_factor = unit_rows(heads_to_rows(q_ref[...], heads, size))
    k_unit, k_factor = unit_rows(k_ref[...])
    dq, term_query = norm_back(dqn, g_query, q_unit, q_factor)
    dk, term_key = norm_back(dkn, g_key, k_unit, k_factor)
    dq = rows_to_heads(dq.astype(BF16), heads, block)
    dk = dk.astype(BF16)
    dqkv_ref[:, : heads * size] = dq
    dqkv_ref[:, heads * size : (heads + 1) * size] = dk
    dqkv_ref[:, (heads + 1) * size :] = dv
    if layer == 0:
        late[0].start()
    for load in loads[1:]:
        load.wait()
    part[...] = dot_nt(dq, wq_s[...]) + dot_nt(dk, wk_s[...]) + dot_nt(dv, wv_s[...])
    total = reduce_rows(t, nt, rows, part, outgoing, came, s_sem, r_sem)
    mine = rows_at(t * rows, rows)
    unit, factor = unit_rows(x_ref[source, mine].astype(F32))
    back, term_attn = norm_back(total, g_attn, unit, factor)
    dx = (dh1_ref[...] + back).astype(BF16)
    terms_ref[...] = jnp.zeros_like(terms_ref)
    write_terms(terms_ref, 0, term_moe[...])
    write_terms(terms_ref, 8, term_attn)
    terms_ref[16:17, :size] = term_query
    terms_ref[16:17, size : 2 * size] = term_key
    if layer == 1:
        dx_ref[...] = dx
    else:
        late[2].start()
        whole[mine] = dx
        wait = spread_rows(t, nt, rows, whole, gs_sem, gr_sem)
        wait()
        late[1].start()
        late[2].arrive()

        def total_of(ref):
            out = ref[0, 0]
            for section in range(2):
                for origin in range(nz):
                    if section or origin:
                        out = out + ref[section, origin]
            return out

        @pl.when(s == 0)
        def _():
            copy = pltpu.make_async_copy(late[2].out, terms_in, t_sem.at[0])
            copy.start()
            copy.wait()

        @pl.when(s != 0)
        def _():
            copy = pltpu.make_async_copy(terms_other, terms_in, t_sem.at[0])
            copy.start()
            copy.wait()

        terms_near[0] = total_of(terms_in)

        def near(j):
            return remote(
                terms_near.at[0],
                terms_near.at[j],
                near_send.at[j],
                near_recv.at[j],
                tensor=partner(t, jnp.int32(j), nt),
            )

        for j in range(1, nt):
            near(j).start()
        sums = terms_near[0]
        for j in range(1, nt):
            near(j).wait_recv()
            sums = sums + terms_near[j]
        for j in range(1, nt):
            near(j).wait_send()
        terms_out[...] = sums
        late[0].finish()
        late[1].finish()
        late[2].leave()
        dx_ref[...] = dx
    for move in moves:
        move.finish()


def expert_grads_kernel(nz, step, ins, outs, scratch):
    s = lax.axis_index("section")
    own, near = (ins[0:5], ins[5:10]), (ins[10:15], ins[15:20])
    left, right, stage, in_sem, out_sem = scratch

    def loads(layer):
        out = []
        for i in range(5):
            target = left.at[i] if i < 3 else right.at[i - 3]
            out.append(
                (
                    pltpu.make_async_copy(own[layer][i], target.at[pl.ds(0, nz)], in_sem.at[i, 0]),
                    pltpu.make_async_copy(near[layer][i], target.at[pl.ds(nz, nz)], in_sem.at[i, 1]),
                )
            )
        return out

    order = (3, 0, 1, 4, 2)
    for layer in range(2):

        @pl.when(s == layer)
        def _():
            copies = loads(layer)
            for i in order:
                for copy in copies[i]:
                    copy.start()

    waits = loads(0)
    width = right.shape[-1]
    tokens = 2 * nz * right.shape[2]
    cols = left.shape[-1]
    done = set()

    def need(i):
        if i not in done:
            for copy in waits[i]:
                copy.wait()
            done.add(i)

    turn = 0
    for i, r in ((0, 0), (1, 0), (2, 1)):
        need(3 + r)
        need(i)
        for c in range(0, cols, step):
            slot = turn % 2
            if turn >= 2:
                pltpu.make_async_copy(stage.at[slot], outs[0].at[pl.ds(0, step)], out_sem.at[slot]).wait()
            lhs = left[i, :, :, c : c + step].reshape(tokens, step)
            stage[slot] = dot_tn(lhs, right[r].reshape(tokens, width))
            pltpu.make_async_copy(stage.at[slot], outs[i].at[pl.ds(c, step)], out_sem.at[slot]).start()
            turn += 1
    for slot in range(2):
        pltpu.make_async_copy(stage.at[slot], outs[0].at[pl.ds(0, step)], out_sem.at[slot]).wait()


def attend_grads_kernel(nz, q_cols, size, ins, outs, scratch):
    s, z = lax.axis_index("section"), lax.axis_index("expert")
    spaces, sems, d_sem = scratch[:4], scratch[4], scratch[5]
    a_s, o_s, t_s, d_s = spaces
    early, blocks, late = ins[:3], ins[3 : 3 + nz], ins[3 + nz :]

    def loads(refs):
        return [pltpu.make_async_copy(r, d, sems.at[i]) for i, (r, d) in enumerate(zip(refs, spaces))]

    def parts(layer):
        out = []
        for k in range(nz):
            spot = partner(z, jnp.int32(k), nz)
            src = blocks[k] if layer == 0 else late[3].at[:, spot]
            out.append(pltpu.make_async_copy(src, d_s.at[:, spot], d_sem.at[k]))
        return out

    for layer, refs in enumerate((early, late[:3])):

        @pl.when(s == layer)
        def _():
            for load in loads(refs) + parts(layer):
                load.start()

    waits = loads(early)

    def flat(ref):
        return ref[...].reshape(-1, ref.shape[-1])

    waits[1].wait()
    waits[2].wait()
    outs[3][...] = dot_tn(flat(o_s), flat(t_s))
    waits[0].wait()
    for load in parts(0):
        load.wait()
    grad = dot_tn(flat(a_s), flat(d_s))
    outs[0][...] = grad[:, :q_cols]
    outs[1][...] = grad[:, q_cols : q_cols + size]
    outs[2][...] = grad[:, q_cols + size :]


def shape_of(shape, dtype):
    return jax.ShapeDtypeStruct(tuple(shape), dtype)


def like(value, lead=()):
    return shape_of(tuple(lead) + tuple(value.shape), value.dtype)


def call(body, name, number, ins, outs, scratch):
    def kernel(*refs):
        body(refs[: len(ins)], refs[len(ins) : len(ins) + len(outs)], refs[len(ins) + len(outs) :])

    return pl.pallas_call(
        kernel,
        out_shape=tuple(o for o, _ in outs),
        in_specs=[spec for _, spec in ins],
        out_specs=tuple(spec for _, spec in outs),
        scratch_shapes=list(scratch),
        compiler_params=pltpu.CompilerParams(
            collective_id=number, has_side_effects=number is not None, vmem_limit_bytes=VMEM_LIMIT
        ),
        name=name,
    )(*[value for value, _ in ins])


def vm(*values):
    return [(value, VM) for value in values]


def any_place(*values):
    return [(value, ANY) for value in values]


def on_device(
    boundary, seq_lengths, expert_ids, route_weights, attn_gain, moe_gain, query_gain, key_norm_gain,
    w_query, key_weight, value_weight, w_output, w_gate, w_up, w_down,
):
    nz, nt = lax.axis_size("expert"), lax.axis_size("tensor")
    micro, block, width = boundary.shape[1:]
    size = query_gain.shape[1]
    heads = w_query.shape[2] // size
    local_experts = w_gate.shape[1]
    hidden = local_experts * w_gate.shape[2]
    experts = local_experts * nz
    rows = block // nt
    q_cols = heads * size
    assert micro == 2 and key_weight.shape[2] == size == block and experts <= LANES
    dma = pltpu.SemaphoreType.DMA

    wg, wu, wd = (w[0].reshape(hidden, width) for w in (w_gate, w_up, w_down))
    wq, wk, wv, wo = w_query[0], key_weight[0], value_weight[0], w_output[0]
    gains = jnp.concatenate([attn_gain, moe_gain, query_gain, key_norm_gain], axis=1)

    spaces = [
        pltpu.VMEM((width, q_cols), BF16),
        pltpu.VMEM((width, size), BF16),
        pltpu.VMEM((width, size), BF16),
        pltpu.VMEM((q_cols, width), BF16),
        pltpu.VMEM((block, width), F32),
        pltpu.VMEM((block, width), BF16),
        pltpu.VMEM((nt, rows, width), BF16),
        dma((nt,)),
        dma((nt,)),
    ]
    gathered = [
        shape_of((width, q_cols), BF16),
        shape_of((width, size), BF16),
        shape_of((width, size), BF16),
        shape_of((q_cols, width), BF16),
    ]
    attend_outs = vm(
        shape_of((rows, width), F32),
        shape_of((rows, width), BF16),
        shape_of((block, width), BF16),
        shape_of((block, q_cols), F32),
        shape_of((block, size), F32),
        shape_of((block, size), BF16),
        shape_of((heads * block, size), BF16),
        shape_of((block, size), BF16),
        shape_of((block, q_cols), BF16),
    )
    expert_scratch = [pltpu.VMEM((hidden, width), BF16)] * 3

    def binder(kinds):
        def bind(ins, outs, scratch):
            return [
                kind.bind(ins[i] if i < len(ins) else None, outs[i], scratch[3 * i : 3 * i + 3])
                for i, kind in enumerate(kinds)
            ]

        return bind

    def shapes_of(kinds, values):
        out = []
        for kind, value in zip(kinds, values):
            if isinstance(kind, Near):
                out.append(like(value, (2,) if kind.both else ()))
            elif kind.sliced:
                out.append(shape_of((2, nz, block, width // nz), value.dtype))
            else:
                out.append(like(value, (2, nz)))
        return out

    def scratch_of(kinds):
        return [sem for kind in kinds for sem in kind.scratch()]

    relay = Relay(0, (0, 0, 0, 1), nz)
    started = call(
        functools.partial(start_attend_kernel, nz, nt, heads, relay),
        "start_attend_0",
        0,
        [(seq_lengths[0, :, 0], SM)]
        + vm(expert_ids[0], route_weights[0])
        + any_place(boundary[0], gains, wq, wk, wv, wo, wg, wu, wd),
        any_place(
            shape_of((2, block, width), BF16),
            shape_of((2, 3, block, size), F32),
            shape_of((2, nz, block, LANES), F32),
            like(gains, (2,)),
            *gathered,
            *[shape_of((hidden, width), BF16)] * 3,
        )
        + attend_outs,
        [
            pltpu.VMEM((block, width), BF16),
            pltpu.VMEM((3, block, size), F32),
            pltpu.VMEM(gains.shape, F32),
            pltpu.VMEM((2, 3, block, size), F32),
            pltpu.VMEM((2, block, LANES), F32),
            dma((4,)), dma((3,)), dma((4,)), dma((6,)), dma((6,)), dma((2, nz)), dma((2, nz)),
        ]
        + relay.scratch(4)
        + spaces,
    )
    edges, tabs_all, gates_all, gains_all = started[:4]
    weights_0 = started[4:8]
    expert_weights = (wg, wu, wd) + tuple(started[8:11])
    h1_0, b_0, a_0, q_0, k_0, v_0, qr_0, kr_0, o_0 = started[11:]

    def run_experts(layer, b, h1, move_ins, move_outs, move_scratch, bind):
        return call(
            functools.partial(experts_kernel, layer, nz, nt, local_experts, bind),
            f"experts_{layer}",
            1 + layer,
            vm(b, h1, gates_all) + any_place(*expert_weights, *move_ins),
            vm(shape_of((block, width), BF16))
            + any_place(
                shape_of((nz, block, width), BF16),
                shape_of((nz, block, hidden), F32),
                shape_of((nz, block, hidden), F32),
                *move_outs,
            ),
            expert_scratch
            + [pltpu.VMEM((nz, block, hidden), F32)] * 2
            + [dma((3,)), dma((3,))]
            + exchange_scratch(nz, nt, rows, block, width)
            + move_scratch,
        )

    def experts_back(layer, dy, h1, gate_pre, up_pre, move_ins, move_outs, move_scratch, bind):
        return call(
            functools.partial(experts_back_kernel, layer, nz, nt, local_experts, bind),
            f"experts_back_{layer}",
            3 + layer,
            vm(dy, h1, gains_all, gates_all)
            + any_place(gate_pre, up_pre, *expert_weights, *move_ins),
            vm(
                shape_of((block, width), BF16),
                shape_of((rows, width), F32),
                shape_of((1, width), F32),
            )
            + any_place(
                shape_of((nz, block, width), BF16),
                shape_of((nz, block, hidden), BF16),
                shape_of((nz, block, hidden), BF16),
                shape_of((nz, block, hidden), BF16),
                *move_outs,
            ),
            expert_scratch
            + [pltpu.VMEM((2, block, hidden), F32)] * 2
            + [pltpu.VMEM((nz, block, hidden), BF16)] * 3
            + [dma((3,)), dma((2,)), dma((2,)), dma((4,))]
            + exchange_scratch(nz, nt, rows, block, width)
            + move_scratch,
        )

    relay_1 = Relay(1, (0, 0, 0, 1), nz)
    ran = run_experts(
        0, b_0, h1_0, (wq, wk, wv, wo), gathered, relay_1.scratch(4),
        lambda ins, outs, scratch: [relay_1.bind(ins, outs, scratch)],
    )
    x_1, ball_0, gp_0, up_0 = ran[:4]
    weights_1 = tuple(ran[4:])

    kinds = (Gather(0, nz, True),)
    values = (a_0,)
    attended = call(
        functools.partial(attend_kernel, 1, nz, nt, heads, binder(kinds)),
        "attend_1",
        5,
        vm(x_1, tabs_all, gains_all) + any_place(*weights_1, *values),
        attend_outs + any_place(*shapes_of(kinds, values)),
        [dma((4,))] + spaces + scratch_of(kinds),
    )
    h1_1, b_1, a_1, q_1, k_1, v_1, qr_1, kr_1, o_1 = attended[:9]
    aall_0 = attended[9]

    kinds = (Gather(0, nz), Near(0))
    values = (o_0, ball_0)
    ran = run_experts(
        1, b_1, h1_1, values, shapes_of(kinds, values), scratch_of(kinds), binder(kinds)
    )
    y_1, ball_1, gp_1, up_1 = ran[:4]
    oall_0, bnear_0 = ran[4:]

    dy_1 = lax.dynamic_slice_in_dim(edges[1], lax.axis_index("tensor") * rows, rows, 0)
    kinds = (Gather(1, nz), Near(1), Near(1, True))
    values = (o_1, ball_1, y_1)
    ran = experts_back(
        1, dy_1, h1_1, gp_1, up_1, values, shapes_of(kinds, values), scratch_of(kinds), binder(kinds)
    )
    dat_1, dh1_1, tm_1, dyall_1, hid_1, dg_1, du_1 = ran[:7]
    oall_1, bnear_1, ends_1 = ran[7:]

    def attend_back(layer, x, source, dat, dh1, term_moe, kept, weights, kinds, values, late):
        outs = vm(
            shape_of((rows, width), BF16),
            shape_of((block, q_cols + 2 * size), BF16),
            shape_of((TERM_ROWS, TERM_COLS), F32),
        )
        scratch = spaces + [dma((4,)), dma((nt,)), dma((nt,))]
        ins = vm(x, tabs_all, gains_all, dat, dh1, term_moe, *kept) + any_place(*weights)
        shapes = [o for o, _ in outs]
        late_shapes = []
        if late is not None:
            outs += vm(shape_of((TERM_ROWS, TERM_COLS), F32))
            scratch += [
                pltpu.VMEM((block, width), BF16),
                pltpu.VMEM((nt, TERM_ROWS, TERM_COLS), F32),
                pltpu.VMEM((2, nz, TERM_ROWS, TERM_COLS), F32),
                dma((1,)),
                dma((nt,)),
                dma((nt,)),
            ]
            ins += any_place(late)
            last = (Near(0, True), Near(0, True), Gather(0, nz))
            late_shapes = shapes_of(last, (shapes[1], shape_of((block, width), BF16), shapes[2]))
            kinds = kinds + last
        return call(
            functools.partial(attend_back_kernel, layer, source, nz, nt, heads, binder(kinds)),
            f"attend_back_{layer}",
            6 + layer,
            ins + any_place(*values),
            outs + any_place(*shapes_of(kinds[: len(values)], values), *late_shapes),
            scratch + scratch_of(kinds),
        )

    kinds = (Gather(1, nz, True), Near(1), Near(1), Near(1), Near(1), Gather(1, nz, True))
    values = (dat_1, dg_1, du_1, hid_1, dyall_1, a_1)
    ran = attend_back(
        1, x_1[None], 0, dat_1, dh1_1, tm_1, (q_1, k_1, v_1, qr_1, kr_1), weights_1, kinds, values, None
    )
    dx_1, dqkv_1, terms_1 = ran[:3]
    datall_1, near_1, aall_1 = ran[3], ran[4:8], ran[8]

    kinds = (Gather(1, nz), Gather(1, nz))
    values = (dqkv_1, terms_1)
    ran = experts_back(
        0, dx_1, h1_0, gp_0, up_0, values, shapes_of(kinds, values), scratch_of(kinds), binder(kinds)
    )
    dat_0, dh1_0, tm_0, dyall_0, hid_0, dg_0, du_0 = ran[:7]
    dqkvall_1, termsall_1 = ran[7:]

    kinds = (Gather(0, nz, True), Near(0), Near(0), Near(0), Near(0))
    values = (dat_0, dg_0, du_0, hid_0, dyall_0)
    ran = attend_back(
        0, edges, 0, dat_0, dh1_0, tm_0, (q_0, k_0, v_0, qr_0, kr_0), weights_0, kinds, values, termsall_1
    )
    terms, datall_0, near_0 = ran[3], ran[4], ran[5:9]
    dqkv_both, ends_0 = ran[9:11]
    dqkv_0 = [dqkv_both]
    for k in range(1, nz):
        pairs = [(place, place ^ k) for place in range(nz)]
        dqkv_0.append(lax.ppermute(dqkv_both, ("section", "expert"), pairs))

    step = 256
    flat = shape_of((hidden, width), F32)
    grad_gate, grad_up, grad_down = call(
        functools.partial(expert_grads_kernel, nz, step),
        "expert_grads",
        None,
        any_place(
            dg_0, du_0, hid_0, ball_0, dyall_0,
            dg_1, du_1, hid_1, ball_1, dyall_1,
            *near_0[:3], bnear_0, near_0[3],
            *near_1[:3], bnear_1, near_1[3],
        ),
        any_place(flat, flat, flat),
        [
            pltpu.VMEM((3, 2 * nz, block, hidden), BF16),
            pltpu.VMEM((2, 2 * nz, block, width), BF16),
            pltpu.VMEM((2, step, width), F32),
            dma((5, 2)),
            dma((2,)),
        ],
    )
    operands = (aall_0, oall_0, datall_0, *dqkv_0, aall_1, oall_1, datall_1, dqkvall_1)
    grad_query, grad_key, grad_value, grad_output = call(
        functools.partial(attend_grads_kernel, nz, q_cols, size),
        "attend_grads",
        None,
        any_place(*operands),
        vm(
            shape_of(wq.shape, F32),
            shape_of(wk.shape, F32),
            shape_of(wv.shape, F32),
            shape_of(wo.shape, F32),
        ),
        [pltpu.VMEM(o.shape, o.dtype) for o in operands[-4:]] + [dma((3,)), dma((nz,))],
    )
    ends = jnp.where(lax.axis_index("section") == 0, ends_0, ends_1)
    return (
        ends[None],
        terms[8:16].reshape(1, width),
        terms[:8].reshape(1, width),
        terms[16:17, :size],
        terms[16:17, size : 2 * size],
        grad_query[None],
        grad_key[None],
        grad_value[None],
        grad_output[None],
        grad_gate.reshape(w_gate.shape),
        grad_up.reshape(w_gate.shape),
        grad_down.reshape(w_gate.shape),
    )


def solution(mesh):
    return jax.shard_map(
        on_device,
        mesh=mesh,
        in_specs=(
            P("section", None, "expert", None),
            P("section", None, "expert", None),
            P("section", None, "expert", None),
            P("section", None, "expert", None),
            P("section", None),
            P("section", None),
            P("section", None),
            P("section", None),
            P("section", "expert", "tensor"),
            P("section", "expert", "tensor"),
            P("section", "expert", "tensor"),
            P("section", "tensor", "expert"),
            P("section", "expert", "tensor", None),
            P("section", "expert", "tensor", None),
            P("section", "expert", "tensor", None),
        ),
        out_specs=(
            P("section", None, "expert", None),
            P("section", None),
            P("section", None),
            P("section", None),
            P("section", None),
            P("section", "expert", "tensor"),
            P("section", "expert", "tensor"),
            P("section", "expert", "tensor"),
            P("section", "tensor", "expert"),
            P("section", "expert", "tensor", None),
            P("section", "expert", "tensor", None),
            P("section", "expert", "tensor", None),
        ),
        check_vma=False,
    )
```

```python
import functools
import math

import jax
import jax.numpy as jnp
from jax import lax
from jax.experimental import pallas as pl
from jax.experimental.pallas import tpu as pltpu
from jax.sharding import PartitionSpec as P

EPSILON = 1e-06
THETA = 1000000.0
LANES = 128
TERM_ROWS = 24
TERM_COLS = 256
MESH = pl.DeviceIdType.MESH
F32 = jnp.float32
BF16 = jnp.bfloat16
VMEM_LIMIT = 62 * 1024 * 1024

ANY = pl.BlockSpec(memory_space=pl.ANY)
VM = pl.BlockSpec(memory_space=pltpu.VMEM)
SM = pl.BlockSpec(memory_space=pltpu.SMEM)


def partner(index, k, count):
    out, bit = 0, 1
    while bit < count:
        out = out + bit * lax.rem(lax.div(index, bit) + lax.div(k, bit), 2)
        bit *= 2
    return out


def rows_at(start, size):
    return pl.ds(pl.multiple_of(start, size), size)


def remote(src, dst, send_sem, recv_sem, **where):
    return pltpu.make_async_remote_copy(
        src_ref=src,
        dst_ref=dst,
        send_sem=send_sem,
        recv_sem=recv_sem,
        device_id=where,
        device_id_type=MESH,
    )


def greet(peers):
    barrier = pltpu.get_barrier_semaphore()
    for where in peers:
        pl.semaphore_signal(barrier, inc=1, device_id=where, device_id_type=MESH)
    pl.semaphore_wait(barrier, len(peers))


def layer_peers(z, t, nz, nt):
    i32 = jnp.int32
    peers = [{"expert": partner(z, i32(k), nz)} for k in range(1, nz)]
    peers += [{"tensor": partner(t, i32(k), nt)} for k in range(1, nt)]
    return peers


def dot(a, b):
    return lax.dot_general(a, b, (((1,), (0,)), ((), ())), preferred_element_type=F32)


def dot_nt(a, b):
    return lax.dot_general(a, b, (((1,), (1,)), ((), ())), preferred_element_type=F32)


def dot_tn(a, b):
    return lax.dot_general(a, b, (((0,), (0,)), ((), ())), preferred_element_type=F32)


def unit_rows(value):
    factor = lax.rsqrt(jnp.mean(value * value, axis=-1, keepdims=True) + EPSILON)
    return value * factor, factor


def norm_back(grad, gain, unit, factor):
    weighted = grad * gain
    inner = jnp.mean(weighted * unit, axis=-1, keepdims=True)
    return factor * (weighted - unit * inner), jnp.sum(grad * unit, axis=0, keepdims=True)


def expert_gates(gate_rows, first_expert, local_experts, width):
    rows = gate_rows.shape[0]
    lane = lax.broadcasted_iota(jnp.int32, gate_rows.shape, 1)
    column = lax.broadcasted_iota(jnp.int32, (rows, local_experts * width), 1)
    out = None
    for e in range(local_experts):
        one = jnp.sum(jnp.where(lane == first_expert + e, gate_rows, 0.0), axis=1, keepdims=True)
        wide = jnp.broadcast_to(one, column.shape)
        out = wide if out is None else jnp.where(column >= e * width, wide, out)
    return out


def write_terms(terms_ref, row, vector):
    for i in range(vector.shape[1] // TERM_COLS):
        terms_ref[row + i : row + i + 1, :] = vector[:, i * TERM_COLS : (i + 1) * TERM_COLS]


class Square:
    def __init__(self, nz, nt, rows, width):
        assert nt == 4
        self.z, self.t = lax.axis_index("expert"), lax.axis_index("tensor")
        self.nz, self.rows = nz, rows
        half = width // 2
        self.half, self.first, self.second = half, pl.ds(0, half), pl.ds(half, half)
        near_x, near_y, across = (partner(self.t, jnp.int32(j), nt) for j in (1, 2, 3))
        self.near = (near_x, near_y)
        self.mine, self.x_rows, self.y_rows, self.across_rows = (
            self.window(i) for i in (self.t, near_x, near_y, across)
        )
        self.y_pair = rows_at(lax.div(near_y, 2) * (2 * rows), 2 * rows)
        in_pair = lax.rem(self.t, 2)
        self.pair_mine, self.pair_x = self.window(in_pair), self.window(1 - in_pair)

    def window(self, index):
        return rows_at(index * self.rows, self.rows)


class RowGather:
    @staticmethod
    def scratch(nz):
        return [pltpu.SemaphoreType.DMA((2, nz)), pltpu.SemaphoreType.DMA((4, nz, 2))]

    def __init__(self, square, full, sems):
        self.sq, self.full = square, full
        self.far_sem, self.row_sem = sems

    def far_copy(self, k, source, src=None):
        sq = self.sq
        spot = self.full.at[source, sq.mine]
        return remote(
            spot if src is None else src,
            spot,
            self.far_sem.at[0, k],
            self.far_sem.at[1, k],
            expert=partner(sq.z, jnp.int32(k), sq.nz),
        )

    def row_copy(self, k, source, j, window, src=None):
        spot = self.full.at[source, window]
        return remote(
            spot if src is None else src,
            spot,
            self.row_sem.at[0, k, j],
            self.row_sem.at[1, k, j],
            tensor=self.sq.near[j],
        )

    def on_copy(self, k, source, j, window):
        spot = self.full.at[source, window, (self.sq.second, self.sq.first)[j]]
        return remote(
            spot, spot, self.row_sem.at[2, k, j], self.row_sem.at[3, k, j], tensor=self.sq.near[j]
        )

    def send(self, k, source, src=None):
        for j in range(2):
            self.row_copy(k, source, j, self.sq.mine, src).start()

    def hand_on(self, k, source):
        self.row_copy(k, source, 0, self.sq.x_rows).wait_recv()
        self.on_copy(k, source, 1, self.sq.x_rows).start()
        self.row_copy(k, source, 1, self.sq.y_rows).wait_recv()
        self.on_copy(k, source, 0, self.sq.y_rows).start()

    def arrive(self, k, source):
        for j in range(2):
            self.on_copy(k, source, j, self.sq.across_rows).wait_recv()

    def leave(self, k, source):
        for j in range(2):
            self.row_copy(k, source, j, self.sq.mine).wait_send()
            self.on_copy(k, source, j, (self.sq.y_rows, self.sq.x_rows)[j]).wait_send()


class RowSum:
    @staticmethod
    def scratch(nz, rows, block, width):
        half = width // 2
        dma = pltpu.SemaphoreType.DMA
        return [
            pltpu.VMEM((nz, block, width), BF16),
            pltpu.VMEM((nz, 2 * rows, half), BF16),
            pltpu.VMEM((nz, 2, rows, half), BF16),
            pltpu.VMEM((nz, 2, rows, half), BF16),
            pltpu.VMEM((nz, 2, rows, half), BF16),
            pltpu.VMEM((nz, rows, width), BF16),
            pltpu.VMEM((nz, rows, width), BF16),
            pltpu.VMEM((rows, width), F32),
            dma((2, nz)),
            dma((6, nz, 2)),
        ]

    count = 10

    def __init__(self, square, scratch, own=None):
        self.sq, self.own = square, own
        (self.outgoing, self.from_y, self.from_x, self.pairs, self.came_pairs) = scratch[:5]
        (self.passed, self.came_far, self.total, self.far_sem, self.part_sem) = scratch[5:]

    def part_copy(self, k, i):
        sq = self.sq
        window, cols = ((sq.y_pair, sq.first), (sq.across_rows, sq.second), (sq.x_rows, sq.second))[i]
        dst = (self.from_y.at[k], self.from_x.at[k, 1], self.from_x.at[k, 0])[i]
        group, slot = ((0, 0), (2, 1), (2, 0))[i]
        return remote(
            self.outgoing.at[k, window, cols],
            dst,
            self.part_sem.at[group, k, slot],
            self.part_sem.at[group + 1, k, slot],
            tensor=sq.near[0] if i else sq.near[1],
        )

    def pair_copy(self, k, j):
        return remote(
            self.pairs.at[k, j],
            self.came_pairs.at[k, j],
            self.part_sem.at[4, k, j],
            self.part_sem.at[5, k, j],
            tensor=self.sq.near[j],
        )

    def sum_copy(self, k):
        return remote(
            self.passed.at[k],
            self.came_far.at[k],
            self.far_sem.at[0, k],
            self.far_sem.at[1, k],
            expert=partner(self.sq.z, k, self.sq.nz),
        )

    def send(self, k):
        for i in range(3):
            self.part_copy(k, i).start()

    def pair_up(self, k):
        sq = self.sq
        self.part_copy(k, 0).wait_recv()
        kept = self.outgoing[k, sq.x_rows, sq.first].astype(F32)
        self.pairs[k, 0] = (kept + self.from_y[k, sq.pair_x].astype(F32)).astype(BF16)
        self.pair_copy(k, 0).start()
        self.part_copy(k, 1).wait_recv()
        kept = self.outgoing[k, sq.y_rows, sq.second].astype(F32)
        self.pairs[k, 1] = (kept + self.from_x[k, 1].astype(F32)).astype(BF16)
        self.pair_copy(k, 1).start()

    def collect(self, k):
        sq = self.sq
        self.part_copy(k, 2).wait_recv()
        self.pair_copy(k, 0).wait_recv()
        self.pair_copy(k, 1).wait_recv()
        own = self.outgoing[k, sq.mine].astype(F32) if self.own is None else self.own[k]
        left = own[:, : sq.half] + self.from_y[k, sq.pair_mine].astype(F32)
        right = own[:, sq.half :] + self.from_x[k, 0].astype(F32)
        return (
            left + self.came_pairs[k, 0].astype(F32),
            right + self.came_pairs[k, 1].astype(F32),
        )

    def collect_own(self):
        left, right = self.collect(jnp.int32(0))
        self.total[:, : self.sq.half] = left
        self.total[:, self.sq.half :] = right

    def collect_far(self, k):
        left, right = self.collect(k)
        self.passed[k, :, self.sq.first] = left.astype(BF16)
        self.passed[k, :, self.sq.second] = right.astype(BF16)
        self.sum_copy(k).start()

    def add_far(self):
        for k in range(1, self.sq.nz):
            self.sum_copy(jnp.int32(k)).wait_recv()
            self.total[...] += self.came_far[k].astype(F32)

    def leave(self, far=True):
        for k in range(self.sq.nz):
            if k and far:
                self.sum_copy(jnp.int32(k)).wait_send()
            for j in range(2):
                self.pair_copy(k, j).wait_send()
            for i in range(3):
                self.part_copy(k, i).wait_send()


def exchange_scratch(nz, nt, rows, block, width):
    return (
        [
            pltpu.VMEM((nz, block, width), BF16),
            ("part", pltpu.VMEM((block, width), F32)),
            ("own", pltpu.VMEM((nz, rows, width), F32)),
            pltpu.VMEM((block, width), BF16),
            pltpu.SemaphoreType.DMA((2, nt)),
        ]
        + RowGather.scratch(nz)
        + RowSum.scratch(nz, rows, block, width)
    )


EXCHANGE_SCRATCH = 7 + RowSum.count


def exchange(nz, nt, own_rows, scratch, ready, work, at):
    full, part, own_part = scratch[:3]
    sq = Square(nz, nt, own_rows.shape[0], full.shape[-1])
    z = sq.z
    gather = RowGather(sq, full, scratch[5:7])
    sums = RowSum(sq, scratch[7 : 7 + RowSum.count], own_part)
    i32 = jnp.int32

    def produce(k, source):
        gather.arrive(k, source)
        part[...] = work(k, source, full[source])
        sums.outgoing[k] = part[...].astype(BF16)
        sums.send(k)
        own_part[k] = part[sq.mine]

    full[z, sq.mine] = own_rows
    for k in range(1, nz):
        gather.far_copy(k, z).start()
    gather.send(0, z)
    at("begin")
    ready()
    for k in range(1, nz):
        source = partner(z, i32(k), nz)
        gather.far_copy(k, source).wait_recv()
        gather.send(k, source)
        if k == 1:
            gather.hand_on(0, z)
    at("arrived")
    gather.hand_on(1, partner(z, i32(1), nz))

    def step(k, carry):
        @pl.when(k + 1 < nz)
        def _():
            gather.hand_on(k + 1, partner(z, k + 1, nz))

        turn = lax.rem(k, nz)
        produce(turn, partner(z, turn, nz))

        @pl.when(k >= 2)
        def _():
            sums.pair_up(k - 1)

        @pl.when(k >= 3)
        def _():
            sums.collect_far(k - 2)

        @pl.when(k == 2)
        def _():
            at("second")

        return carry

    lax.fori_loop(1, nz + 1, step, 0)
    at("looped")
    sums.collect_far(i32(nz - 1))
    sums.pair_up(i32(0))
    sums.collect_own()
    at("collected")
    sums.add_far()

    def finish():
        for k in range(nz):
            source = partner(z, i32(k), nz)
            if k:
                gather.far_copy(k, z).wait_send()
            gather.leave(k, source)
        sums.leave()

    return sums.total, finish


def spread_rows(t, nt, rows, block_ref, send_sem, recv_sem):
    i32 = jnp.int32
    mine = rows_at(t * rows, rows)
    for j in range(1, nt):
        remote(
            block_ref.at[mine],
            block_ref.at[mine],
            send_sem.at[j],
            recv_sem.at[j],
            tensor=partner(t, i32(j), nt),
        ).start()

    def wait():
        for j in range(1, nt):
            peer = partner(t, i32(j), nt)
            theirs = rows_at(peer * rows, rows)
            copy = remote(
                block_ref.at[theirs],
                block_ref.at[theirs],
                send_sem.at[j],
                recv_sem.at[j],
                tensor=peer,
            )
            copy.wait_send()
            copy.wait_recv()

    return wait


def reduce_rows(t, nt, rows, part, outgoing, came, send_sem, recv_sem):
    i32 = jnp.int32
    outgoing[...] = part[...].astype(BF16)

    def copy(j):
        peer = partner(t, i32(j), nt)
        return remote(
            outgoing.at[rows_at(peer * rows, rows)],
            came.at[j],
            send_sem.at[j],
            recv_sem.at[j],
            tensor=peer,
        )

    for j in range(1, nt):
        copy(j).start()
    total = part[rows_at(t * rows, rows)]
    for j in range(1, nt):
        copy(j).wait_recv()
        total = total + came[j].astype(F32)
    for j in range(1, nt):
        copy(j).wait_send()
    return total


def all_peers(s, z, t, nz, nt):
    i32 = jnp.int32
    peers = [{"section": 1 - s}]
    for k in range(1, nz):
        zz = partner(z, i32(k), nz)
        peers += [{"expert": zz}, {"section": 1 - s, "expert": zz}]
    return peers + [{"tensor": partner(t, i32(j), nt)} for j in range(1, nt)]


class Relay:
    def __init__(self, layer, spots, nz):
        self.layer, self.spots, self.nz = layer, spots, nz

    def scratch(self, count=4):
        dma = pltpu.SemaphoreType.DMA
        return [dma((count,))] + [dma((count, self.nz))] * 6

    def bind(self, shards, outs, sems):
        self.s, self.z = lax.axis_index("section"), lax.axis_index("expert")
        self.shards, self.outs, self.sems = shards, outs, sems
        self.source = self.hands = self.s == self.layer
        self.count = len(shards)
        return self

    def place(self, a, owner):
        dim = self.spots[a]
        size = self.shards[a].shape[dim]
        window = rows_at(owner * size, size)
        return self.outs[a].at[window] if dim == 0 else self.outs[a].at[:, window]

    def home(self, a):
        return pltpu.make_async_copy(self.shards[a], self.place(a, self.z), self.sems[0].at[a])

    def hop(self, a, owner, step, right, own=False):
        spot = self.place(a, owner)
        send, recv = self.sems[1:3] if right else self.sems[3:5]
        return remote(
            self.shards[a] if own else spot,
            spot,
            send.at[a, step],
            recv.at[a, step],
            expert=self.z + 1 if right else self.z - 1,
        )

    def hand(self, a, owner, own=False):
        spot = self.place(a, owner)
        return remote(
            self.shards[a] if own else spot,
            spot,
            self.sems[5].at[a, owner],
            self.sems[6].at[a, owner],
            section=1 - self.s,
        )

    def begin_side(self, a, right):
        @pl.when(self.source & ((self.z + 1 < self.nz) if right else (self.z >= 1)))
        def _():
            self.hop(a, self.z, 1, right, True).start()

    def begin_home(self, a):
        @pl.when(self.source)
        def _():
            self.home(a).start()

        @pl.when(self.hands)
        def _():
            self.hand(a, self.z, True).start()

    def begin(self, a):
        self.begin_side(a, True)
        self.begin_side(a, False)
        self.begin_home(a)

    def step(self, a, k):
        z, nz = self.z, self.nz

        @pl.when(self.source & (z >= k))
        def _():
            self.hop(a, z - k, k, True).wait_recv()

            @pl.when(z + 1 < nz)
            def _():
                self.hop(a, z - k, k + 1, True).start()

            @pl.when(self.hands)
            def _():
                self.hand(a, z - k).start()

        @pl.when(self.source & (z + k < nz))
        def _():
            self.hop(a, z + k, k, False).wait_recv()

            @pl.when(z >= 1)
            def _():
                self.hop(a, z + k, k + 1, False).start()

            @pl.when(self.hands)
            def _():
                self.hand(a, z + k).start()

    def settle(self, a):
        @pl.when(self.source)
        def _():
            self.home(a).wait()

        @pl.when(jnp.logical_not(self.source))
        def _():
            for owner in range(self.nz):
                self.hand(a, owner).wait_recv()

    def end(self, a):
        z, nz = self.z, self.nz

        @pl.when(self.hands)
        def _():
            for owner in range(nz):
                self.hand(a, owner).wait_send()

        @pl.when(self.source)
        def _():
            for step in range(1, nz):

                @pl.when((z >= step - 1) & (z + 1 < nz))
                def _():
                    self.hop(a, z - (step - 1), step, True).wait_send()

                @pl.when((z + step - 1 < nz) & (z >= 1))
                def _():
                    self.hop(a, z + (step - 1), step, False).wait_send()

    def start(self):
        for a in range(self.count):
            self.begin(a)

    def poll(self, turn):
        if turn < min(3, self.nz - 1):
            for a in range(self.count):
                self.step(a, turn)

    def finish(self):
        for k in range(min(3, self.nz - 1), self.nz):
            for a in range(self.count):
                self.step(a, k)
        for a in range(self.count):
            self.settle(a)
            self.end(a)


class Line(Relay):
    def __init__(self, layer, nz):
        super().__init__(layer, None, nz)

    def scratch(self):
        return super().scratch(1)

    def bind(self, ins, outs, sems):
        super().bind(ins, outs, sems)
        self.source, self.hands = self.s >= 0, self.s != self.layer
        return self

    def place(self, a, owner, section=None):
        return self.outs[a].at[self.s if section is None else section, owner]

    def settle(self, a):
        self.home(a).wait()

        @pl.when(self.s == self.layer)
        def _():
            for owner in range(self.nz):
                spot = self.place(a, owner, 1 - self.layer)
                remote(
                    spot, spot, self.sems[5].at[a, owner], self.sems[6].at[a, owner], section=1 - self.s
                ).wait_recv()


class Slice:
    def __init__(self, layer, nz, nt):
        self.layer, self.nz, self.nt = layer, nz, nt

    def scratch(self):
        dma = pltpu.SemaphoreType.DMA
        return [dma((2,)), dma((self.nz,)), dma((2, self.nz)), dma((2, self.nt))]

    def bind(self, ins, outs, sems):
        self.s, self.z, self.t = (lax.axis_index(a) for a in ("section", "expert", "tensor"))
        self.src, (self.out, self.rows_out), self.sems = ins[0], outs, sems
        rows, self.cols = self.rows_out.shape[2:]
        self.rows = rows
        self.mine = rows_at(self.t * rows, rows)
        self.receives = self.s == self.layer
        return self

    def far(self, k, local, section=None, origin=None):
        zz = partner(self.z, jnp.int32(k), self.nz)
        src = self.src.at[self.mine, rows_at(zz * self.cols, self.cols)]
        section = self.s if section is None else section
        spot = self.rows_out.at[section, self.z if origin is None else origin]
        if local:
            return pltpu.make_async_copy(src, spot, self.sems[0].at[0])
        return remote(
            src,
            spot,
            self.sems[1].at[k],
            self.sems[2].at[section, k],
            section=jnp.int32(self.layer),
            expert=zz,
        )

    def near(self, j, window):
        return remote(
            self.rows_out,
            self.out.at[:, :, window],
            self.sems[3].at[0, j],
            self.sems[3].at[1, j],
            tensor=partner(self.t, jnp.int32(j), self.nt),
        )

    def home(self):
        return pltpu.make_async_copy(self.rows_out, self.out.at[:, :, self.mine], self.sems[0].at[1])

    def start(self):
        for k in range(1, self.nz):
            self.far(k, False).start()

        @pl.when(self.receives)
        def _():
            self.far(0, True).start()

        @pl.when(jnp.logical_not(self.receives))
        def _():
            self.far(0, False).start()

    def poll(self, turn):
        if turn != 1:
            return

        @pl.when(self.receives)
        def _():
            self.far(0, True).wait()
            for section in range(2):
                for k in range(self.nz):
                    if k or section != self.layer:
                        zz = partner(self.z, jnp.int32(k), self.nz)
                        self.far(k, False, section, zz).wait_recv()
            self.home().start()
            for j in range(1, self.nt):
                self.near(j, self.mine).start()

    def finish(self):
        for k in range(1, self.nz):
            self.far(k, False).wait_send()

        @pl.when(jnp.logical_not(self.receives))
        def _():
            self.far(0, False).wait_send()

        @pl.when(self.receives)
        def _():
            self.home().wait()
            for j in range(1, self.nt):
                theirs = partner(self.t, jnp.int32(j), self.nt) * self.rows
                self.near(j, rows_at(theirs, self.rows)).wait_recv()
                self.near(j, self.mine).wait_send()


class Gather:
    def __init__(self, layer, nz):
        self.layer, self.nz = layer, nz

    def scratch(self):
        dma = pltpu.SemaphoreType.DMA
        return [dma((1,)), dma((self.nz,)), dma((2, self.nz))]

    def bind(self, ins, outs, sems):
        self.s, self.z = lax.axis_index("section"), lax.axis_index("expert")
        self.src, self.out, self.sems = (ins or (None,))[0], outs[0], sems
        return self

    def copy(self, k, local, section=None, origin=None):
        zz = partner(self.z, jnp.int32(k), self.nz)
        src = self.src
        section = self.s if section is None else section
        spot = self.out.at[section, self.z if origin is None else origin]
        if local:
            return pltpu.make_async_copy(src, spot, self.sems[0].at[0])
        return remote(
            src,
            spot,
            self.sems[1].at[k],
            self.sems[2].at[section, k],
            section=jnp.int32(self.layer),
            expert=zz,
        )

    def start(self):
        for k in range(1, self.nz):
            self.copy(k, False).start()

        @pl.when(self.s == self.layer)
        def _():
            self.copy(0, True).start()

        @pl.when(self.s != self.layer)
        def _():
            self.copy(0, False).start()

    def poll(self, turn):
        pass

    def arrive(self):
        @pl.when(self.s == self.layer)
        def _():
            self.copy(0, True).wait()
            for section in range(2):
                for k in range(self.nz):
                    if k or section != self.layer:
                        zz = partner(self.z, jnp.int32(k), self.nz)
                        self.copy(k, False, section, zz).wait_recv()

    def leave(self):
        for k in range(1, self.nz):
            self.copy(k, False).wait_send()

        @pl.when(self.s != self.layer)
        def _():
            self.copy(0, False).wait_send()

    def finish(self):
        self.arrive()
        self.leave()


class Near:
    def __init__(self, layer, both=False):
        self.layer, self.both = layer, both

    def scratch(self):
        dma = pltpu.SemaphoreType.DMA
        return [dma((1,)), dma((1,)), dma((1,))]

    def bind(self, ins, outs, sems):
        self.s, self.sems = lax.axis_index("section"), sems
        self.src, self.out = (ins or (None,))[0], outs[0]
        return self

    def local(self):
        return pltpu.make_async_copy(self.src, self.out.at[self.layer], self.sems[0].at[0])

    def copy(self):
        return remote(
            self.src,
            self.out.at[1 - self.layer] if self.both else self.out,
            self.sems[1].at[0],
            self.sems[2].at[0],
            section=jnp.int32(self.layer),
        )

    def start(self):
        if self.both:

            @pl.when(self.s == self.layer)
            def _():
                self.local().start()

        @pl.when(self.s != self.layer)
        def _():
            self.copy().start()

    def poll(self, turn):
        pass

    def finish(self):
        @pl.when(self.s == self.layer)
        def _():
            if self.both:
                self.local().wait()
            remote(
                self.src,
                self.out.at[1 - self.layer] if self.both else self.out,
                self.sems[1].at[0],
                self.sems[2].at[0],
                section=1 - self.s,
            ).wait_recv()

        @pl.when(self.s != self.layer)
        def _():
            self.copy().wait_send()


class RowsFar:
    def __init__(self, slot, nz, nt):
        self.slot, self.nz, self.nt = slot, nz, nt

    def scratch(self):
        return [pltpu.SemaphoreType.DMA((1,)), pltpu.SemaphoreType.DMA((2, self.nz))]

    def bind(self, ins, outs, sems):
        self.z, self.t = lax.axis_index("expert"), lax.axis_index("tensor")
        self.src, self.out, self.sems = ins[0], outs[0], sems
        return self

    def copy(self, k, origin):
        rows = self.out.shape[1]
        src = self.src.at[self.slot, rows_at(self.t * rows, rows)]
        if k == 0:
            return pltpu.make_async_copy(src, self.out.at[origin], self.sems[0].at[0])
        return remote(
            src,
            self.out.at[origin],
            self.sems[1].at[0, k],
            self.sems[1].at[1, k],
            expert=partner(self.z, jnp.int32(k), self.nz),
        )

    def start(self):
        for k in range(self.nz):
            self.copy(k, self.z).start()

    def poll(self, turn):
        pass

    def finish(self):
        self.copy(0, self.z).wait()
        for k in range(1, self.nz):
            self.copy(k, self.z).wait_send()
            self.copy(k, partner(self.z, jnp.int32(k), self.nz)).wait_recv()


class Spread:
    def __init__(self, nz, nt):
        self.nz, self.nt = nz, nt

    def scratch(self):
        return [pltpu.SemaphoreType.DMA((1,))] + RowGather.scratch(self.nz)

    def bind(self, ins, outs, sems):
        self.src, self.out, self.sems = ins[0], outs[0], sems
        self.sq = Square(self.nz, self.nt, *self.src.shape[1:])
        self.gather = RowGather(self.sq, self.out, sems[1:])
        return self

    def local(self):
        return pltpu.make_async_copy(self.src, self.out.at[:, self.sq.mine], self.sems[0].at[0])

    def start(self):
        self.local().start()
        for k in range(self.nz):
            self.gather.send(k, k, self.src.at[k])

    def poll(self, turn):
        if turn == 1:
            for k in range(self.nz):
                self.gather.hand_on(k, k)

    def finish(self):
        self.local().wait()
        for k in range(self.nz):
            self.gather.arrive(k, k)
            self.gather.leave(k, k)


class SumNear:
    def __init__(self, nz, nt, rows, block, width):
        self.nz, self.nt = nz, nt
        self.shape = rows, block, width

    def scratch(self):
        return [pltpu.SemaphoreType.DMA((2,))] + RowSum.scratch(self.nz, *self.shape)

    def bind(self, ins, outs, scratch):
        self.src, self.out, self.sems = ins[0], outs[0], scratch[0]
        self.sq = Square(self.nz, self.nt, self.shape[0], self.shape[2])
        self.sums = RowSum(self.sq, scratch[1:])
        return self

    def start(self):
        load = pltpu.make_async_copy(self.src, self.sums.outgoing, self.sems.at[0])
        load.start()
        load.wait()
        for k in range(self.nz):
            self.sums.send(k)

    def poll(self, turn):
        if turn == 1:
            for k in range(self.nz):
                self.sums.pair_up(jnp.int32(k))
        if turn == 2:
            for k in range(self.nz):
                left, right = self.sums.collect(jnp.int32(k))
                self.sums.passed[k, :, self.sq.first] = left.astype(BF16)
                self.sums.passed[k, :, self.sq.second] = right.astype(BF16)
            self.save().start()

    def save(self):
        return pltpu.make_async_copy(self.sums.passed, self.out, self.sems.at[1])

    def finish(self):
        self.save().wait()
        self.sums.leave(False)


class SumFar:
    def __init__(self, nz, rows, width):
        self.nz, self.shape = nz, (rows, width)

    def scratch(self):
        dma = pltpu.SemaphoreType.DMA
        return [
            pltpu.VMEM((self.nz,) + self.shape, BF16),
            pltpu.VMEM(self.shape, BF16),
            dma((2,)),
            dma((2, self.nz)),
        ]

    def bind(self, ins, outs, scratch):
        self.z = lax.axis_index("expert")
        self.src, self.rows_ref = ins
        self.out = outs[0]
        self.came, self.result, self.sems, self.far_sem = scratch
        return self

    def copy(self, k):
        if k == 0:
            return pltpu.make_async_copy(self.src.at[0], self.came.at[0], self.sems.at[0])
        return remote(
            self.src.at[k],
            self.came.at[k],
            self.far_sem.at[0, k],
            self.far_sem.at[1, k],
            expert=partner(self.z, jnp.int32(k), self.nz),
        )

    def save(self):
        return pltpu.make_async_copy(self.result, self.out, self.sems.at[1])

    def start(self):
        for k in range(self.nz):
            self.copy(k).start()

    def poll(self, turn):
        if turn == 2:
            self.copy(0).wait()
            total = self.rows_ref[...] + self.came[0].astype(F32)
            for k in range(1, self.nz):
                self.copy(k).wait_recv()
                total = total + self.came[k].astype(F32)
            self.result[...] = total.astype(BF16)
            self.save().start()

    def finish(self):
        self.save().wait()
        for k in range(1, self.nz):
            self.copy(k).wait_send()


class SpreadNear:
    def __init__(self, layer, nt, block, width):
        self.nt, self.shape, self.near = nt, (block, width), Near(layer, True)

    def scratch(self):
        dma = pltpu.SemaphoreType.DMA
        return [pltpu.VMEM(self.shape, BF16), dma((1,)), dma((2, self.nt))] + self.near.scratch()

    def bind(self, ins, outs, scratch):
        self.t = lax.axis_index("tensor")
        self.src = ins[0]
        self.whole, self.load_sem, self.spread_sem = scratch[:3]
        self.near.bind([self.whole], outs, scratch[3:])
        self.rows = self.src.shape[0]
        return self

    def start(self):
        load = pltpu.make_async_copy(
            self.src, self.whole.at[rows_at(self.t * self.rows, self.rows)], self.load_sem.at[0]
        )
        load.start()
        load.wait()
        self.wait = spread_rows(
            self.t, self.nt, self.rows, self.whole, self.spread_sem.at[0], self.spread_sem.at[1]
        )

    def poll(self, turn):
        if turn == 1:
            self.wait()
            self.near.start()

    def finish(self):
        self.near.finish()


def heads_to_rows(value, heads, size):
    return jnp.concatenate([value[:, h * size : (h + 1) * size] for h in range(heads)], axis=0)


def rows_to_heads(value, heads, block):
    return jnp.concatenate([value[h * block : (h + 1) * block] for h in range(heads)], axis=1)


def split_gains(row, width, size):
    return (
        row[:, :width],
        row[:, width : 2 * width],
        row[:, 2 * width : 2 * width + size],
        row[:, 2 * width + size :],
    )


def tiled(value, times):
    return jnp.concatenate([value] * times, axis=0)


def half_turn(value):
    return pltpu.roll(value, value.shape[-1] // 2, value.ndim - 1)


def attend_body(t, nt, heads, x_ref, tables, gains, outs, scratch, wait_qkv, wait_out):
    (h1_ref, b_ref, a_ref, q_ref, k_ref, v_ref, qr_ref, kr_ref, o_ref) = outs
    (wq_s, wk_s, wv_s, wo_s, part, outgoing, came, s_sem, r_sem) = scratch
    block, width = x_ref.shape
    rows = block // nt
    cos, sin, bias = tables
    size = cos.shape[-1]
    g_attn, g_moe, g_query, g_key = split_gains(gains, width, size)
    unit, _ = unit_rows(x_ref[...].astype(F32))
    a_ref[...] = (unit * g_attn).astype(BF16)
    wait_qkv()
    q = dot(a_ref[...], wq_s[...])
    q_ref[...] = q
    k = dot(a_ref[...], wk_s[...])
    k_ref[...] = k
    v = dot(a_ref[...], wv_s[...]).astype(BF16)
    v_ref[...] = v
    qn = unit_rows(heads_to_rows(q, heads, size))[0] * g_query
    kn = unit_rows(k)[0] * g_key
    qr = (qn * tiled(cos, heads) + half_turn(qn) * tiled(sin, heads)).astype(BF16)
    kr = (kn * cos + half_turn(kn) * sin).astype(BF16)
    qr_ref[...] = qr
    kr_ref[...] = kr
    scores = dot_nt(qr, kr) * (1.0 / math.sqrt(size)) + tiled(bias, heads)
    peak = jnp.max(scores, axis=-1, keepdims=True)
    weight = jnp.exp(scores - peak)
    probs = weight * (1.0 / jnp.sum(weight, axis=-1, keepdims=True))
    o = dot(probs.astype(BF16), v).astype(BF16)
    o_ref[...] = rows_to_heads(o, heads, block)
    wait_out()
    part[...] = dot(o_ref[...], wo_s[...])
    total = reduce_rows(t, nt, rows, part, outgoing, came, s_sem, r_sem)
    h1 = x_ref[rows_at(t * rows, rows)].astype(F32) + total
    h1_ref[...] = h1
    b_ref[...] = (unit_rows(h1)[0] * g_moe).astype(BF16)


def fill_tables(tabs, lengths, m):
    block, size = tabs.shape[2:]
    row = lax.broadcasted_iota(jnp.int32, (block, size), 0)
    lane = lax.broadcasted_iota(jnp.int32, (block, size), 1)
    begin, segment, segment_of_lane = (jnp.zeros((block, size), jnp.int32) for _ in range(3))
    end = jnp.int32(0)
    for n in range(lengths.shape[1]):
        end = end + lengths[m, n]
        begin = jnp.where(row >= end, end, begin)
        segment = segment + jnp.where(row >= end, 1, 0)
        segment_of_lane = segment_of_lane + jnp.where(lane >= end, 1, 0)
    half = size // 2
    position = jnp.where(lane >= half, lane - half, lane).astype(F32)
    inverse = jnp.exp(position * (-2.0 * math.log(THETA) / size))
    angle = (row - begin).astype(F32) * inverse
    sin = jnp.sin(angle)
    tabs[m, 0] = jnp.cos(angle)
    tabs[m, 1] = jnp.where(lane >= half, sin, -sin)
    tabs[m, 2] = jnp.where((lane <= row) & (segment == segment_of_lane), 0.0, -1e30)


def fill_gates(gates, ids, route_weights, m):
    expert_of, weight_of = ids[m], route_weights[m]
    lane = lax.broadcasted_iota(jnp.int32, gates.shape[1:], 1)
    out = jnp.zeros(gates.shape[1:], F32)
    for c in range(expert_of.shape[1]):
        out = out + jnp.where(lane == expert_of[:, c : c + 1], weight_of[:, c : c + 1], 0.0)
    gates[m] = out


def start_attend_kernel(nz, nt, heads, relay, hello, at, ins, outs, scratch):
    s, z, t = lax.axis_index("section"), lax.axis_index("expert"), lax.axis_index("tensor")
    lengths, ids, route_weights, boundary, gains, wq, wk, wv, wo, wg, wu, wd = ins
    edges, tabs_out, gates_out, gains_out = outs[:4]
    gathered, (sg, su, sd), results = outs[4:8], outs[8:11], outs[11:]
    x_s, tabs_s, gains_s, tabs, gates = scratch[:5]
    w_sem, in_sem, own_sem, sib_send, sib_recv, gate_send, gate_recv = scratch[5:12]
    relay.bind((wq, wk, wv, wo), gathered, scratch[12:19])
    attn_scratch = scratch[19:]
    other = 1 - s
    i32 = jnp.int32

    own = [
        pltpu.make_async_copy(boundary.at[s], edges.at[s], own_sem.at[0]),
        pltpu.make_async_copy(tabs.at[s], tabs_out.at[s], own_sem.at[1]),
        pltpu.make_async_copy(gains, gains_out.at[s], own_sem.at[2]),
        pltpu.make_async_copy(gates.at[s], gates_out.at[s, z], own_sem.at[3]),
    ]
    own[0].start()
    own[2].start()
    hello(all_peers(s, z, t, nz, nt))

    def sibling(i, src, dst):
        return remote(src, dst, sib_send.at[i], sib_recv.at[i], section=other)

    pairs = [
        (boundary.at[other], edges.at[s], edges.at[other]),
        (tabs.at[other], tabs_out.at[s], tabs_out.at[other]),
        (gains, gains_out.at[s], gains_out.at[other]),
        (wg, sg, sg),
        (wu, su, su),
        (wd, sd, sd),
    ]
    for i in (0, 2):
        sibling(i, *pairs[i][:2]).start()
    for a in range(3):
        relay.begin(a)
    relay.begin_home(3)

    def gate_copy(d, k, arrival=False):
        zz = partner(z, i32(k), nz)
        section = s if d == 0 else other
        return remote(
            gates.at[section],
            gates_out.at[section, zz] if arrival else gates_out.at[s, z],
            gate_send.at[d, k],
            gate_recv.at[d, k],
            section=section,
            expert=zz,
        )

    for m in range(2):
        fill_tables(tabs, lengths, m)
    sibling(1, *pairs[1][:2]).start()
    own[1].start()
    for m in range(2):
        fill_gates(gates, ids, route_weights, m)
    own[3].start()
    turns = [(d, k) for d in range(2) for k in range(nz) if d or k]
    for d, k in turns:
        gate_copy(d, k).start()
    for i in range(3, 6):
        sibling(i, *pairs[i][:2]).start()

    for copy in own:
        copy.wait()
    for i in range(3):
        sibling(i, pairs[i][0], pairs[i][2]).wait_recv()
    loads = [
        pltpu.make_async_copy(edges.at[0], x_s, in_sem.at[0]),
        pltpu.make_async_copy(tabs_out.at[0], tabs_s, in_sem.at[1]),
        pltpu.make_async_copy(gains_out.at[0], gains_s, in_sem.at[2]),
    ]
    for load in loads:
        load.start()
    for load in loads:
        load.wait()

    def bring(a):
        return pltpu.make_async_copy(gathered[a], attn_scratch[a], w_sem.at[a])

    def wait_qkv():
        for k in range(1, nz):
            for a in range(3):
                relay.step(a, k)

            @pl.when((z == k) | ((z == 0) & (k == 1)))
            def _():
                relay.begin_side(3, True)

            @pl.when((z == nz - 1 - k) | ((z == nz - 1) & (k == 1)))
            def _():
                relay.begin_side(3, False)

        for a in range(3):
            relay.settle(a)
            bring(a).start()
        for a in range(3):
            bring(a).wait()

    def wait_out():
        for k in range(1, nz):
            relay.step(3, k)
        at("shards")
        relay.settle(3)
        bring(3).start()
        bring(3).wait()

    tables = (tabs_s[0], tabs_s[1], tabs_s[2])
    attend_body(t, nt, heads, x_s, tables, gains_s[...], results, attn_scratch, wait_qkv, wait_out)
    for i in range(6):
        sibling(i, *pairs[i][:2]).wait_send()
    for i in range(3, 6):
        sibling(i, pairs[i][0], pairs[i][2]).wait_recv()
    for d, k in turns:
        gate_copy(d, k).wait_send()
        gate_copy(d, k, True).wait_recv()
    for a in range(4):
        relay.end(a)
    at("end")


def attend_kernel(layer, nz, nt, heads, hello, at, ins, outs, scratch):
    s, z, t = lax.axis_index("section"), lax.axis_index("expert"), lax.axis_index("tensor")
    x_ref, tabs, gains, wq, wk, wv, wo = ins
    w_sem, tabs_s, gains_s, attn_scratch = scratch[0], scratch[1], scratch[2], scratch[3:]
    loads = [
        pltpu.make_async_copy(src, dst, w_sem.at[i])
        for i, (src, dst) in enumerate(zip((wq, wk, wv, wo), attn_scratch))
    ]
    small = [
        pltpu.make_async_copy(tabs.at[layer], tabs_s, w_sem.at[4]),
        pltpu.make_async_copy(gains.at[layer], gains_s, w_sem.at[5]),
    ]
    for load in small:
        load.start()
    hello(all_peers(s, z, t, nz, nt))
    at("begin")
    for load in small:
        load.wait()

    def wait_qkv():
        at("qkv")
        for load in loads[:3]:
            load.start()
        for load in loads[:3]:
            load.wait()

    def wait_out():
        at("out")
        loads[3].start()
        loads[3].wait()

    tables = (tabs_s[0], tabs_s[1], tabs_s[2])
    attend_body(t, nt, heads, x_ref, tables, gains_s[...], outs, attn_scratch, wait_qkv, wait_out)
    at("end")


def load_experts(layer, s, own, sibling, scratch, sems):
    def copies(refs):
        return [pltpu.make_async_copy(r, d, sems.at[i]) for i, (r, d) in enumerate(zip(refs, scratch))]

    @pl.when(s == layer)
    def _():
        for copy in copies(own):
            copy.start()

    @pl.when(s != layer)
    def _():
        for copy in copies(sibling):
            copy.start()

    return copies(own)


def experts_kernel(layer, nz, nt, local_experts, hello, at, ins, outs, scratch):
    s, z, t = lax.axis_index("section"), lax.axis_index("expert"), lax.axis_index("tensor")
    b_ref, h1_ref, gates, wg, wu, wd, sg, su, sd = ins
    y_ref, b_out, g_out, u_out = outs
    wg_s, wu_s, wd_s, g_s, u_s, gates_s, w_sem, o_sem = scratch[:8]
    spaces = scratch[8:]
    rows = b_ref.shape[0]
    loads = load_experts(layer, s, (wg, wu, wd), (sg, su, sd), (wg_s, wu_s, wd_s), w_sem)
    loads.append(pltpu.make_async_copy(gates.at[layer], gates_s, w_sem.at[3]))
    loads[3].start()
    hello(all_peers(s, z, t, nz, nt))
    width = wg.shape[0] // local_experts

    def ready():
        for load in loads:
            load.wait()

    def work(k, origin, rows_in):
        gate_pre = dot_nt(rows_in, wg_s[...])
        up_pre = dot_nt(rows_in, wu_s[...])
        g_s[origin] = gate_pre
        u_s[origin] = up_pre
        weight = expert_gates(gates_s[origin], z * local_experts, local_experts, width)
        hidden = (gate_pre * jax.nn.sigmoid(gate_pre) * up_pre * weight).astype(BF16)
        return dot(hidden, wd_s[...])

    total, finish = exchange(nz, nt, b_ref[...], spaces, ready, work, at)
    full, whole, spread_sem = spaces[0], spaces[3], spaces[4]
    saves = [
        pltpu.make_async_copy(full, b_out, o_sem.at[0]),
        pltpu.make_async_copy(g_s, g_out, o_sem.at[1]),
        pltpu.make_async_copy(u_s, u_out, o_sem.at[2]),
    ]
    for save in saves:
        save.start()
    whole[rows_at(t * rows, rows)] = (h1_ref[...] + total[...]).astype(BF16)
    wait = spread_rows(t, nt, rows, whole, spread_sem.at[0], spread_sem.at[1])
    at("spread")
    finish()
    wait()
    y_ref[...] = whole[...]
    for save in saves:
        save.wait()
    at("end")


def experts_back_kernel(layer, nz, nt, local_experts, hello, at, ins, outs, scratch):
    s, z, t = lax.axis_index("section"), lax.axis_index("expert"), lax.axis_index("tensor")
    dy_ref, h1_ref, gains, gates, g_in, u_in, wg, wu, wd, sg, su, sd = ins
    dat_ref, dh1_ref, term_ref, dy_out, hid_out, dg_out, du_out = outs
    wg_s, wu_s, wd_s, g_s, u_s, hid_s, dg_s, du_s, w_sem, g_sem, u_sem, o_sem = scratch[:12]
    gates_s, scratch = scratch[12], scratch[:12] + scratch[13:]
    spaces = scratch[12:]
    rows, model_width = dy_ref.shape
    loads = load_experts(layer, s, (wd, wg, wu), (sd, sg, su), (wd_s, wg_s, wu_s), w_sem)
    loads.append(pltpu.make_async_copy(gates.at[layer], gates_s, w_sem.at[3]))
    loads[3].start()

    def kept(k):
        origin, slot = partner(z, lax.rem(k + 1, nz), nz), lax.rem(k, 2)
        return (
            pltpu.make_async_copy(g_in.at[origin], g_s.at[slot], g_sem.at[slot]),
            pltpu.make_async_copy(u_in.at[origin], u_s.at[slot], u_sem.at[slot]),
        )

    for load in kept(jnp.int32(0)):
        load.start()
    hello(all_peers(s, z, t, nz, nt))
    width = wg.shape[0] // local_experts

    def ready():
        for load in loads:
            load.wait()

    def work(k, origin, rows_in):
        turn = lax.rem(k + nz - 1, nz)
        for load in kept(turn):
            load.wait()

        @pl.when(turn + 1 < nz)
        def _():
            for load in kept(turn + 1):
                load.start()

        slot = lax.rem(turn, 2)
        gate_pre, up_pre = g_s[slot], u_s[slot]
        weight = expert_gates(gates_s[origin], z * local_experts, local_experts, width)
        sigmoid = jax.nn.sigmoid(gate_pre)
        silu = gate_pre * sigmoid
        hid_s[origin] = (silu * up_pre * weight).astype(BF16)
        grad_hidden = dot_nt(rows_in, wd_s[...]) * weight
        dg_s[origin] = (grad_hidden * up_pre * sigmoid * (1.0 + gate_pre * (1.0 - sigmoid))).astype(BF16)
        du_s[origin] = (grad_hidden * silu).astype(BF16)
        return dot(dg_s[origin], wg_s[...]) + dot(du_s[origin], wu_s[...])

    total, finish = exchange(nz, nt, dy_ref[...], spaces, ready, work, at)
    full, whole, spread_sem = spaces[0], spaces[3], spaces[4]
    saves = [
        pltpu.make_async_copy(full, dy_out, o_sem.at[0]),
        pltpu.make_async_copy(hid_s, hid_out, o_sem.at[1]),
        pltpu.make_async_copy(dg_s, dg_out, o_sem.at[2]),
        pltpu.make_async_copy(du_s, du_out, o_sem.at[3]),
    ]
    for save in saves:
        save.start()
    unit, factor = unit_rows(h1_ref[...])
    g_moe = gains[layer, :, model_width : 2 * model_width]
    back, term = norm_back(total[...], g_moe, unit, factor)
    dh1 = dy_ref[...].astype(F32) + back
    dh1_ref[...] = dh1
    term_ref[...] = term
    whole[rows_at(t * rows, rows)] = dh1.astype(BF16)
    wait = spread_rows(t, nt, rows, whole, spread_sem.at[0], spread_sem.at[1])
    at("spread")
    finish()
    wait()
    dat_ref[...] = whole[...]
    for save in saves:
        save.wait()
    at("end")


def experts_both_kernel(layer, nz, nt, local_experts, hello, at, ins, outs, scratch):
    s, z, t = lax.axis_index("section"), lax.axis_index("expert"), lax.axis_index("tensor")
    b_ref, h1_ref, dy_ref, gains, gates, dy_all, wg, wu, wd, sg, su, sd = ins
    dat_ref, dh1_ref, term_ref, b_out, y_out, hid_out, dg_out, du_out = outs
    wg_s, wu_s, wd_s, dy_s, y_s, hid_s, dg_s, du_s, w_sem, dy_sem, y_sem, o_sem = scratch[:12]
    gates_s, scratch = scratch[12], scratch[:12] + scratch[13:]
    spaces = scratch[12:]
    rows, model_width = b_ref.shape
    loads = load_experts(layer, s, (wg, wu, wd), (sg, su, sd), (wg_s, wu_s, wd_s), w_sem)
    loads.append(pltpu.make_async_copy(gates.at[layer], gates_s, w_sem.at[3]))
    loads[3].start()

    def cotangent(turn):
        origin, slot = partner(z, lax.rem(turn + 1, nz), nz), lax.rem(turn, 2)
        return pltpu.make_async_copy(dy_all.at[origin], dy_s.at[slot], dy_sem.at[slot])

    def store(turn):
        k, slot = lax.rem(turn + 1, nz), lax.rem(turn, 2)
        return pltpu.make_async_copy(y_s.at[slot], y_out.at[k], y_sem.at[slot])

    cotangent(jnp.int32(0)).start()
    hello(all_peers(s, z, t, nz, nt))
    width = wg.shape[0] // local_experts

    def ready():
        for load in loads:
            load.wait()

    def work(k, origin, rows_in):
        turn = lax.rem(k + nz - 1, nz)
        slot = lax.rem(turn, 2)
        cotangent(turn).wait()

        @pl.when(turn + 1 < nz)
        def _():
            cotangent(turn + 1).start()

        @pl.when(turn >= 2)
        def _():
            store(turn - 2).wait()

        gate_pre = dot_nt(rows_in, wg_s[...])
        up_pre = dot_nt(rows_in, wu_s[...])
        weight = expert_gates(gates_s[origin], z * local_experts, local_experts, width)
        sigmoid = jax.nn.sigmoid(gate_pre)
        silu = gate_pre * sigmoid
        hid_s[origin] = (silu * up_pre * weight).astype(BF16)
        grad_hidden = dot_nt(dy_s[slot], wd_s[...]) * weight
        dg_s[origin] = (grad_hidden * up_pre * sigmoid * (1.0 + gate_pre * (1.0 - sigmoid))).astype(BF16)
        du_s[origin] = (grad_hidden * silu).astype(BF16)
        y_s[slot] = dot(hid_s[origin], wd_s[...]).astype(BF16)
        store(turn).start()
        return dot(dg_s[origin], wg_s[...]) + dot(du_s[origin], wu_s[...])

    total, finish = exchange(nz, nt, b_ref[...], spaces, ready, work, at)
    full, whole, spread_sem = spaces[0], spaces[3], spaces[4]
    saves = [
        pltpu.make_async_copy(full, b_out, o_sem.at[0]),
        pltpu.make_async_copy(hid_s, hid_out, o_sem.at[1]),
        pltpu.make_async_copy(dg_s, dg_out, o_sem.at[2]),
        pltpu.make_async_copy(du_s, du_out, o_sem.at[3]),
    ]
    for save in saves:
        save.start()
    unit, factor = unit_rows(h1_ref[...])
    g_moe = gains[layer, :, model_width : 2 * model_width]
    back, term = norm_back(total[...], g_moe, unit, factor)
    dh1 = dy_ref[...].astype(F32) + back
    dh1_ref[...] = dh1
    term_ref[...] = term
    whole[rows_at(t * rows, rows)] = dh1.astype(BF16)
    wait = spread_rows(t, nt, rows, whole, spread_sem.at[0], spread_sem.at[1])
    at("spread")
    finish()
    wait()
    dat_ref[...] = whole[...]
    for save in saves:
        save.wait()
    store(jnp.int32(nz - 2)).wait()
    store(jnp.int32(nz - 1)).wait()
    at("end")


def attend_back_kernel(layer, source, nz, nt, heads, hello, at, ins, outs, scratch):
    s, z, t = lax.axis_index("section"), lax.axis_index("expert"), lax.axis_index("tensor")
    (x_ref, tabs, gains, dat_ref, dh1_ref, term_moe, q_ref, k_ref, v_ref, qr_ref, kr_ref) = ins[:11]
    wq, wk, wv, wo = ins[11:15]
    dx_ref, dqkv_ref, terms_ref = outs[:3]
    wq_s, wk_s, wv_s, wo_s, part, outgoing, came, s_sem, r_sem, w_sem, gs_sem, gr_sem = scratch[:12]
    x_s, scratch = scratch[12], scratch[13:]
    if layer == 0:
        whole, terms_near, terms_in, t_sem, near_send, near_recv = scratch
        terms_other, terms_out = ins[15], outs[3]
    block, model_width = dat_ref.shape
    rows = block // nt
    mine = rows_at(t * rows, rows)
    x_copy = pltpu.make_async_copy(
        x_ref.at[mine] if source is None else x_ref.at[source, mine], x_s, w_sem.at[4]
    )
    x_copy.start()
    loads = [
        pltpu.make_async_copy(src, dst, w_sem.at[i])
        for i, (src, dst) in enumerate(((wo, wo_s), (wq, wq_s), (wk, wk_s), (wv, wv_s)))
    ]
    for load in loads:
        load.start()
    hello(all_peers(s, z, t, nz, nt))
    if layer == 0:
        late = [at.moves[name] for name in ("dqkv_0", "dx_0", "terms_0")]
        late[0].src, late[1].src, late[2].src = dqkv_ref, whole, terms_ref
    at("begin")

    size = tabs.shape[-1]
    g_attn, _, g_query, g_key = split_gains(gains[layer], model_width, size)
    scale = 1.0 / math.sqrt(size)
    cos, sin, bias = tabs[layer, 0], tabs[layer, 1], tabs[layer, 2]
    cos_all, sin_all = tiled(cos, heads), tiled(sin, heads)
    qr, kr, v = qr_ref[...], kr_ref[...], v_ref[...]
    scores = dot_nt(qr, kr) * scale + tiled(bias, heads)
    peak = jnp.max(scores, axis=-1, keepdims=True)
    weight = jnp.exp(scores - peak)
    probs = weight * (1.0 / jnp.sum(weight, axis=-1, keepdims=True))
    loads[0].wait()
    do = heads_to_rows(dot_nt(dat_ref[...], wo_s[...]).astype(BF16), heads, size)
    dv = dot_tn(probs.astype(BF16), do).astype(BF16)
    dp = dot_nt(do, v)
    ds = (probs * (dp - jnp.sum(probs * dp, axis=-1, keepdims=True))).astype(BF16)
    dqr = dot(ds, kr) * scale
    dkr = dot_tn(ds, qr) * scale
    dqn = dqr * cos_all - half_turn(dqr) * sin_all
    dkn = dkr * cos - half_turn(dkr) * sin
    q_unit, q_factor = unit_rows(heads_to_rows(q_ref[...], heads, size))
    k_unit, k_factor = unit_rows(k_ref[...])
    dq, term_query = norm_back(dqn, g_query, q_unit, q_factor)
    dk, term_key = norm_back(dkn, g_key, k_unit, k_factor)
    dq = rows_to_heads(dq.astype(BF16), heads, block)
    dk = dk.astype(BF16)
    dqkv_ref[:, : heads * size] = dq
    dqkv_ref[:, heads * size : (heads + 1) * size] = dk
    dqkv_ref[:, (heads + 1) * size :] = dv
    if layer == 0:
        late[0].start()
    at("dqkv")
    for load in loads[1:]:
        load.wait()
    part[...] = dot_nt(dq, wq_s[...]) + dot_nt(dk, wk_s[...]) + dot_nt(dv, wv_s[...])
    total = reduce_rows(t, nt, rows, part, outgoing, came, s_sem, r_sem)
    at("reduced")
    x_copy.wait()
    unit, factor = unit_rows(x_s[...].astype(F32))
    back, term_attn = norm_back(total, g_attn, unit, factor)
    dx = (dh1_ref[...] + back).astype(BF16)
    terms_ref[...] = jnp.zeros_like(terms_ref)
    write_terms(terms_ref, 0, term_moe[...])
    write_terms(terms_ref, 8, term_attn)
    terms_ref[16:17, :size] = term_query
    terms_ref[16:17, size : 2 * size] = term_key
    at("terms")
    if layer == 1:
        dx_ref[...] = dx
    else:
        late[2].start()
        whole[mine] = dx
        wait = spread_rows(t, nt, rows, whole, gs_sem, gr_sem)
        wait()
        late[1].start()
        late[2].arrive()

        def total_of(ref):
            out = ref[0, 0]
            for section in range(2):
                for origin in range(nz):
                    if section or origin:
                        out = out + ref[section, origin]
            return out

        @pl.when(s == 0)
        def _():
            copy = pltpu.make_async_copy(late[2].out, terms_in, t_sem.at[0])
            copy.start()
            copy.wait()

        @pl.when(s != 0)
        def _():
            copy = pltpu.make_async_copy(terms_other, terms_in, t_sem.at[0])
            copy.start()
            copy.wait()

        terms_near[0] = total_of(terms_in)

        def near(j):
            return remote(
                terms_near.at[0],
                terms_near.at[j],
                near_send.at[j],
                near_recv.at[j],
                tensor=partner(t, jnp.int32(j), nt),
            )

        for j in range(1, nt):
            near(j).start()
        sums = terms_near[0]
        for j in range(1, nt):
            near(j).wait_recv()
            sums = sums + terms_near[j]
        for j in range(1, nt):
            near(j).wait_send()
        terms_out[...] = sums
        late[0].finish()
        late[1].finish()
        late[2].leave()
        dx_ref[...] = dx
    at("end")


def expert_grads_kernel(nz, step, ins, outs, scratch):
    s = lax.axis_index("section")
    own, near = (ins[0:5], ins[5:10]), (ins[10:15], ins[15:20])
    left, right, stage, in_sem, out_sem = scratch

    def loads(layer):
        out = []
        for i in range(5):
            target = left.at[i] if i < 3 else right.at[i - 3]
            out.append(
                (
                    pltpu.make_async_copy(own[layer][i], target.at[pl.ds(0, nz)], in_sem.at[i, 0]),
                    pltpu.make_async_copy(near[layer][i], target.at[pl.ds(nz, nz)], in_sem.at[i, 1]),
                )
            )
        return out

    order = (3, 0, 1, 4, 2)
    for layer in range(2):

        @pl.when(s == layer)
        def _():
            copies = loads(layer)
            for i in order:
                for copy in copies[i]:
                    copy.start()

    waits = loads(0)
    width = right.shape[-1]
    tokens = 2 * nz * right.shape[2]
    cols = left.shape[-1]
    done = set()

    def need(i):
        if i not in done:
            for copy in waits[i]:
                copy.wait()
            done.add(i)

    turn = 0
    for i, r in ((0, 0), (1, 0), (2, 1)):
        need(3 + r)
        need(i)
        for c in range(0, cols, step):
            slot = turn % 2
            if turn >= 2:
                pltpu.make_async_copy(stage.at[slot], outs[0].at[pl.ds(0, step)], out_sem.at[slot]).wait()
            lhs = left[i, :, :, c : c + step].reshape(tokens, step)
            stage[slot] = dot_tn(lhs, right[r].reshape(tokens, width))
            pltpu.make_async_copy(stage.at[slot], outs[i].at[pl.ds(c, step)], out_sem.at[slot]).start()
            turn += 1
    for slot in range(2):
        pltpu.make_async_copy(stage.at[slot], outs[0].at[pl.ds(0, step)], out_sem.at[slot]).wait()


def attend_grads_kernel(q_cols, size, ins, outs, scratch):
    s = lax.axis_index("section")
    spaces, sems = scratch[:4], scratch[4]
    a_s, o_s, t_s, d_s = spaces

    def loads(layer):
        refs = ins[4 * layer : 4 * layer + 4]
        return [pltpu.make_async_copy(r, d, sems.at[i]) for i, (r, d) in enumerate(zip(refs, spaces))]

    for layer in range(2):

        @pl.when(s == layer)
        def _():
            for load in loads(layer):
                load.start()

    waits = loads(0)

    def flat(ref):
        return ref[...].reshape(-1, ref.shape[-1])

    waits[0].wait()
    waits[3].wait()
    grad = dot_tn(flat(a_s), flat(d_s))
    outs[0][...] = grad[:, :q_cols]
    outs[1][...] = grad[:, q_cols : q_cols + size]
    outs[2][...] = grad[:, q_cols + size :]
    waits[1].wait()
    waits[2].wait()
    outs[3][...] = dot_tn(flat(o_s), flat(t_s))


def shape_of(shape, dtype):
    return jax.ShapeDtypeStruct(tuple(shape), dtype)


def like(value, lead=()):
    return shape_of(tuple(lead) + tuple(value.shape), value.dtype)


def call(body, name, number, ins, outs, scratch):
    def kernel(*refs):
        body(refs[: len(ins)], refs[len(ins) : len(ins) + len(outs)], refs[len(ins) + len(outs) :])

    return pl.pallas_call(
        kernel,
        out_shape=tuple(shape_of(o.shape, o.dtype) for o, _ in outs),
        in_specs=[spec for _, spec in ins],
        out_specs=tuple(spec for _, spec in outs),
        scratch_shapes=list(scratch),
        compiler_params=pltpu.CompilerParams(
            collective_id=number, has_side_effects=number is not None, vmem_limit_bytes=VMEM_LIMIT
        ),
        name=name,
    )(*[value for value, _ in ins])


class Slot:
    def __init__(self, shape):
        self.shape, self.dtype, self.value = tuple(shape.shape), shape.dtype, None


class At:
    def __init__(self, stage, plan, moves):
        self.stage, self.plan, self.moves = stage, plan, moves

    def __call__(self, point):
        for name, act in self.plan.get((self.stage, point), ()):
            act(self.moves[name])


USUAL = {
    "second": None,
    "looped": 1, "out": 1, "dqkv": 1,
    "collected": 2, "reduced": 2,
    "spread": 3, "terms": 3,
}


class Group:
    def __init__(self, name, number, fused):
        self.name, self.number, self.fused = name, number, fused
        self.stages, self.moves, self.plan = [], {}, {}

    def stage(self, name, body, ins, outs, scratch):
        slots = [Slot(shape) for shape, _ in outs]
        self.stages.append((name, body, ins, list(zip(slots, [spec for _, spec in outs])), scratch))
        return slots

    def move(self, name, stage, move, ins, outs, plan, start="begin", manual=False):
        slots = [Slot(shape) for shape in outs]
        self.moves[name] = (stage, move, ins, [(slot, ANY) for slot in slots])
        if not self.fused:
            plan = []
            if not manual:
                plan = [(stage, start, lambda m: m.start()), (stage, "end", lambda m: m.finish())]
                for point, turn in USUAL.items():
                    if turn:
                        plan.append((stage, point, lambda m, turn=turn: m.poll(turn)))
        for at_stage, point, act in plan:
            self.plan.setdefault((at_stage, point), []).append((name, act))
        return slots

    def run(self):
        if self.fused:
            self.launch(self.name, self.number, self.stages, list(self.moves))
            return
        for i, stage in enumerate(self.stages):
            names = [name for name, entry in self.moves.items() if entry[0] == stage[0]]
            self.launch(stage[0], self.number + i, [stage], names)

    def launch(self, name, number, stages, names):
        moves = [self.moves[n] for n in names]
        outs = [pair for stage in stages for pair in stage[3]] + [p for m in moves for p in m[3]]
        out_at = {id(slot): i for i, (slot, _) in enumerate(outs)}
        ins, in_at, scratch, scratch_at = [], {}, [], {}

        def place(pairs):
            where = []
            for value, spec in pairs:
                if id(value) in out_at:
                    where.append(("out", out_at[id(value)]))
                    continue
                key = (id(value), id(spec))
                if key not in in_at:
                    in_at[key] = len(ins)
                    ins.append((value.value if isinstance(value, Slot) else value, spec))
                where.append(("in", in_at[key]))
            return where

        def reserve(items):
            where = []
            for item in items:
                key, space = item if isinstance(item, tuple) else (None, item)
                if key is not None and key in scratch_at:
                    where.append(scratch_at[key])
                    continue
                scratch.append(space)
                where.append(len(scratch) - 1)
                if key is not None:
                    scratch_at[key] = len(scratch) - 1
            return where

        stage_at = [(place(st[2]), [out_at[id(o)] for o, _ in st[3]], reserve(st[4])) for st in stages]
        move_at = [
            (place(m[2]), [out_at[id(o)] for o, _ in m[3]], reserve(m[1].scratch())) for m in moves
        ]

        def body(in_refs, out_refs, scratch_refs):
            def pick(places):
                where, results, spaces = places
                refs = [(out_refs if kind == "out" else in_refs)[i] for kind, i in where]
                return refs, [out_refs[i] for i in results], [scratch_refs[i] for i in spaces]

            bound = {n: m[1].bind(*pick(at)) for n, m, at in zip(names, moves, move_at)}
            for i, stage in enumerate(stages):
                hello = greet if i == 0 else lambda peers: None
                stage[1](hello, At(stage[0], self.plan, bound), *pick(stage_at[i]))

        results = call(body, name, number, ins, outs, scratch)
        for (slot, _), value in zip(outs, results):
            slot.value = value


def vm(*values):
    return [(value, VM) for value in values]


def any_place(*values):
    return [(value, ANY) for value in values]


def on_device(
    boundary, seq_lengths, expert_ids, route_weights, attn_gain, moe_gain, query_gain, key_norm_gain,
    w_query, key_weight, value_weight, w_output, w_gate, w_up, w_down,
):
    nz, nt = lax.axis_size("expert"), lax.axis_size("tensor")
    micro, block, width = boundary.shape[1:]
    size = query_gain.shape[1]
    heads = w_query.shape[2] // size
    local_experts = w_gate.shape[1]
    hidden = local_experts * w_gate.shape[2]
    experts = local_experts * nz
    rows = block // nt
    q_cols = heads * size
    assert micro == 2 and key_weight.shape[2] == size == block and experts <= LANES
    dma = pltpu.SemaphoreType.DMA

    wg, wu, wd = (w[0].reshape(hidden, width) for w in (w_gate, w_up, w_down))
    wq, wk, wv, wo = w_query[0], key_weight[0], value_weight[0], w_output[0]
    gains = jnp.concatenate([attn_gain, moe_gain, query_gain, key_norm_gain], axis=1)

    def attend_spaces(own):
        return [
            ("wq", pltpu.VMEM((width, q_cols), BF16)),
            ("wk", pltpu.VMEM((width, size), BF16)),
            ("wv", pltpu.VMEM((width, size), BF16)),
            ("wo", pltpu.VMEM((q_cols, width), BF16)),
            ("part", pltpu.VMEM((block, width), F32)),
            pltpu.VMEM((block, width), BF16),
            pltpu.VMEM((nt, rows, width), BF16),
            dma((nt,)),
            dma((nt,)),
        ]

    gathered = [
        shape_of((width, q_cols), BF16),
        shape_of((width, size), BF16),
        shape_of((width, size), BF16),
        shape_of((q_cols, width), BF16),
    ]
    attend_outs = vm(
        shape_of((rows, width), F32),
        shape_of((rows, width), BF16),
        shape_of((block, width), BF16),
        shape_of((block, q_cols), F32),
        shape_of((block, size), F32),
        shape_of((block, size), BF16),
        shape_of((heads * block, size), BF16),
        shape_of((block, size), BF16),
        shape_of((block, q_cols), BF16),
    )
    expert_scratch = [("wg", pltpu.VMEM((hidden, width), BF16)), ("wu", pltpu.VMEM((hidden, width), BF16))]
    expert_scratch += [("wd", pltpu.VMEM((hidden, width), BF16))]
    hid_scratch = [(n, pltpu.VMEM((nz, block, hidden), BF16)) for n in ("hid", "dg", "du")]
    all_tokens = shape_of((nz, block, width), BF16)
    all_hidden = shape_of((nz, block, hidden), BF16)
    cols = width // nz
    sliced = [shape_of((2, nz, block, cols), BF16), shape_of((2, nz, rows, cols), BF16)]

    def start(move):
        move.start()

    def finish(move):
        move.finish()

    def poll(turn):
        return lambda move: move.poll(turn)

    def steps(arrays, k):
        return lambda move: [move.step(a, k) for a in arrays]

    def begins(*arrays):
        return lambda move: [move.begin(a) for a in arrays]

    def settles(*arrays):
        return lambda move: [move.settle(a) for a in arrays]

    def ends_of(move):
        for a in range(4):
            move.end(a)

    fused = nz <= 4
    fore = Group("forward", 0, fused)
    relay = Relay(0, (0, 0, 0, 1), nz)
    started = fore.stage(
        "attend_0",
        functools.partial(start_attend_kernel, nz, nt, heads, relay),
        [(seq_lengths[0, :, 0], SM)]
        + vm(expert_ids[0], route_weights[0])
        + any_place(boundary[0], gains, wq, wk, wv, wo, wg, wu, wd),
        any_place(
            shape_of((2, block, width), BF16),
            shape_of((2, 3, block, size), F32),
            shape_of((2, nz, block, LANES), F32),
            like(gains, (2,)),
            *gathered,
            *[shape_of((hidden, width), BF16)] * 3,
        )
        + attend_outs,
        [
            pltpu.VMEM((block, width), BF16),
            pltpu.VMEM((3, block, size), F32),
            pltpu.VMEM(gains.shape, F32),
            pltpu.VMEM((2, 3, block, size), F32),
            pltpu.VMEM((2, block, LANES), F32),
            dma((4,)), dma((3,)), dma((5,)), dma((6,)), dma((6,)), dma((2, nz)), dma((2, nz)),
        ]
        + relay.scratch(4)
        + attend_spaces(0),
    )
    edges, tabs_all, gates_all, gains_all = started[:4]
    weights_0 = started[4:8]
    expert_weights = (wg, wu, wd) + tuple(started[8:11])
    h1_0, b_0, a_0, q_0, k_0, v_0, qr_0, kr_0, o_0 = started[11:]

    x_1, ball_0, gp_0, up_0 = fore.stage(
        "experts_0",
        functools.partial(experts_kernel, 0, nz, nt, local_experts),
        vm(b_0, h1_0) + any_place(gates_all, *expert_weights),
        vm(shape_of((block, width), BF16))
        + any_place(
            all_tokens,
            shape_of((nz, block, hidden), F32),
            shape_of((nz, block, hidden), F32),
        ),
        expert_scratch
        + [pltpu.VMEM((nz, block, hidden), F32)] * 2
        + [pltpu.VMEM((nz, block, LANES), F32), dma((4,)), dma((3,))]
        + exchange_scratch(nz, nt, rows, block, width),
    )

    weights_1 = fore.move(
        "weights_1", "experts_0", Relay(1, (0, 0, 0, 1), nz), any_place(wq, wk, wv, wo), gathered,
        [
            ("attend_0", "shards", begins(0, 1, 2)),
            ("experts_0", "begin", steps((0, 1, 2), 1)),
            ("experts_0", "begin", begins(3)),
            ("experts_0", "second", steps((0, 1, 2), 2)),
            ("experts_0", "looped", steps((3,), 1)),
            ("experts_0", "collected", steps((0, 1, 2), 3)),
            ("experts_0", "spread", steps((3,), 2)),
            ("attend_1", "qkv", settles(0, 1, 2)),
            ("attend_1", "out", steps((3,), 3)),
            ("attend_1", "out", settles(3)),
            ("attend_1", "end", ends_of),
        ],
    )

    (dy_rows,) = fore.move(
        "dy_rows", "attend_0", RowsFar(1, nz, nt), any_place(edges), [shape_of((nz, rows, width), BF16)],
        [("experts_0", "looped", start), ("attend_1", "begin", finish)],
        "shards",
    )
    (dyall_1,) = fore.move(
        "dy_all", "experts_0", Spread(nz, nt), any_place(dy_rows), [all_tokens],
        [("attend_1", "begin", start), ("attend_1", "out", poll(1)), ("attend_1", "end", finish)],
    )

    h1_1, b_1, a_1, q_1, k_1, v_1, qr_1, kr_1, o_1 = fore.stage(
        "attend_1",
        functools.partial(attend_kernel, 1, nz, nt, heads),
        vm(x_1) + any_place(tabs_all, gains_all, *weights_1),
        attend_outs,
        [dma((6,)), pltpu.VMEM((3, block, size), F32), pltpu.VMEM(gains.shape, F32)] + attend_spaces(1),
    )
    aall_0, _ = fore.move(
        "a_0", "attend_1", Slice(0, nz, nt), any_place(a_0), sliced,
        [("attend_1", "begin", start), ("attend_1", "out", poll(1)), ("attend_1", "end", finish)],
    )
    fore.run()

    back = Group("backward", 8, fused)
    dy_1 = lax.dynamic_slice_in_dim(edges.value[1], lax.axis_index("tensor") * rows, rows, 0)
    dat_1, dh1_1, tm_1, ball_1, yparts_1, hid_1, dg_1, du_1 = back.stage(
        "both_1",
        functools.partial(experts_both_kernel, 1, nz, nt, local_experts),
        vm(b_1, h1_1, dy_1, gains_all) + any_place(gates_all, dyall_1, *expert_weights),
        vm(
            shape_of((block, width), BF16),
            shape_of((rows, width), F32),
            shape_of((1, width), F32),
        )
        + any_place(all_tokens, all_tokens, all_hidden, all_hidden, all_hidden),
        expert_scratch
        + [pltpu.VMEM((2, block, width), BF16)] * 2
        + hid_scratch
        + [dma((4,)), dma((2,)), dma((2,)), dma((4,)), ("gates", pltpu.VMEM((nz, block, LANES), F32))]
        + exchange_scratch(nz, nt, rows, block, width),
    )

    def attend_back(layer, x, source, dat, dh1, term_moe, kept, weights, others=None):
        outs = vm(
            shape_of((rows, width), BF16),
            shape_of((block, q_cols + 2 * size), BF16),
            shape_of((TERM_ROWS, TERM_COLS), F32),
        )
        scratch = attend_spaces(layer) + [dma((5,)), dma((nt,)), dma((nt,))]
        scratch += [pltpu.VMEM((rows, width), BF16)]
        ins = any_place(x) + vm(tabs_all, gains_all, dat, dh1, term_moe, *kept) + any_place(*weights)
        if others is not None:
            outs += vm(shape_of((TERM_ROWS, TERM_COLS), F32))
            scratch += [
                pltpu.VMEM((block, width), BF16),
                pltpu.VMEM((nt, TERM_ROWS, TERM_COLS), F32),
                pltpu.VMEM((2, nz, TERM_ROWS, TERM_COLS), F32),
                dma((1,)),
                dma((nt,)),
                dma((nt,)),
            ]
            ins += any_place(others)
        return back.stage(
            f"attend_back_{layer}",
            functools.partial(attend_back_kernel, layer, source, nz, nt, heads),
            ins,
            outs,
            scratch,
        )

    last = ("attend_back_0", "end", finish)
    kept_1, kept_0 = (q_1, k_1, v_1, qr_1, kr_1), (q_0, k_0, v_0, qr_0, kr_0)
    dx_1, dqkv_1, terms_1 = attend_back(1, x_1, None, dat_1, dh1_1, tm_1, kept_1, weights_1)
    dat_0, dh1_0, tm_0, dyall_0, hid_0, dg_0, du_0 = back.stage(
        "experts_back_0",
        functools.partial(experts_back_kernel, 0, nz, nt, local_experts),
        vm(dx_1, h1_0, gains_all) + any_place(gates_all, gp_0, up_0, *expert_weights),
        vm(
            shape_of((block, width), BF16),
            shape_of((rows, width), F32),
            shape_of((1, width), F32),
        )
        + any_place(all_tokens, all_hidden, all_hidden, all_hidden),
        expert_scratch
        + [pltpu.VMEM((2, block, hidden), F32)] * 2
        + hid_scratch
        + [dma((4,)), dma((2,)), dma((2,)), dma((4,)), ("gates", pltpu.VMEM((nz, block, LANES), F32))]
        + exchange_scratch(nz, nt, rows, block, width),
    )

    def gather(name, stage, layer, value, begin, end=last):
        return back.move(
            name, stage, Gather(layer, nz), any_place(value), [like(value, (2, nz))],
            [begin + (start,), end], begin[1],
        )

    def near(name, stage, layer, value):
        return back.move(
            name, stage, Near(layer), any_place(value), [like(value)], [(stage, "begin", start), last]
        )

    def columns(name, stage, layer, value, begin, middle):
        return back.move(
            name, stage, Slice(layer, nz, nt), any_place(value), sliced,
            [begin + (start,), middle + (poll(1),), last], begin[1] if begin[0] == stage else "begin",
        )

    (bnear_0,) = near("b_0", "both_1", 0, ball_0)
    (oall_0,) = gather("o_0", "both_1", 0, o_0, ("both_1", "arrived"))
    aall_1, _ = columns(
        "a_1", "both_1", 1, a_1, ("both_1", "looped"), ("attend_back_1", "dqkv")
    )
    (oall_1,) = gather("o_1", "attend_back_1", 1, o_1, ("attend_back_1", "begin"))
    near_1 = [
        near(f"near_1_{i}", "attend_back_1", 1, value)[0]
        for i, value in enumerate((dg_1, du_1, hid_1, ball_1, dyall_1))
    ]
    datall_1, _ = columns(
        "dat_1", "attend_back_1", 1, dat_1, ("attend_back_1", "begin"), ("attend_back_1", "reduced")
    )
    (ysums_1,) = back.move(
        "y_near", "attend_back_1", SumNear(nz, nt, rows, block, width), any_place(yparts_1),
        [shape_of((nz, rows, width), BF16)],
        [
            ("attend_back_1", "begin", start),
            ("attend_back_1", "dqkv", poll(1)),
            ("attend_back_1", "end", poll(2)),
            ("attend_back_1", "end", finish),
        ],
    )
    (dqkvall_1,) = gather("dqkv_1", "experts_back_0", 1, dqkv_1, ("experts_back_0", "arrived"))
    (termsall_1,) = gather(
        "terms_1", "experts_back_0", 1, terms_1, ("experts_back_0", "begin"),
        ("attend_back_0", "begin", finish),
    )
    (yrows_1,) = back.move(
        "y_far", "experts_back_0", SumFar(nz, rows, width), any_place(ysums_1) + vm(h1_1),
        [shape_of((rows, width), BF16)],
        [
            ("experts_back_0", "arrived", start),
            ("experts_back_0", "spread", poll(2)),
            ("experts_back_0", "end", finish),
        ],
    )
    _, dqkv_0, terms_0, terms = attend_back(
        0, edges, 0, dat_0, dh1_0, tm_0, kept_0, weights_0, termsall_1
    )
    datall_0, _ = columns(
        "dat_0", "attend_back_0", 0, dat_0, ("attend_back_0", "begin"), ("attend_back_0", "reduced")
    )
    near_0 = [bnear_0] + [
        near(f"near_0_{i}", "attend_back_0", 0, value)[0]
        for i, value in enumerate((dyall_0, dg_0, du_0, hid_0))
    ]
    (ends_1,) = back.move(
        "y_spread", "attend_back_0", SpreadNear(1, nt, block, width), any_place(yrows_1),
        [shape_of((2, block, width), BF16)],
        [("attend_back_0", "begin", start), ("attend_back_0", "dqkv", poll(1)), last],
    )
    hand = [("dqkv_0", Gather(0, nz), like(dqkv_0, (2, nz)))]
    hand += [("dx_0", Near(0, True), shape_of((2, block, width), BF16))]
    hand += [("terms_0", Gather(0, nz), like(terms_0, (2, nz)))]
    dqkvall_0, ends_0, _ = (
        back.move(name, "attend_back_0", move, [], [shape], [], manual=True)[0]
        for name, move, shape in hand
    )
    back.run()

    step = 256
    flat = shape_of((hidden, width), F32)
    grad_gate, grad_up, grad_down = call(
        functools.partial(expert_grads_kernel, nz, step),
        "expert_grads",
        None,
        any_place(
            *(
                slot.value
                for slot in (
                    dg_0, du_0, hid_0, ball_0, dyall_0,
                    dg_1, du_1, hid_1, ball_1, dyall_1,
                    *near_0[2:], *near_0[:2],
                    *near_1,
                )
            )
        ),
        any_place(flat, flat, flat),
        [
            pltpu.VMEM((3, 2 * nz, block, hidden), BF16),
            pltpu.VMEM((2, 2 * nz, block, width), BF16),
            pltpu.VMEM((2, step, width), F32),
            dma((5, 2)),
            dma((2,)),
        ],
    )
    operands = (aall_0, oall_0, datall_0, dqkvall_0, aall_1, oall_1, datall_1, dqkvall_1)
    operands = tuple(slot.value for slot in operands)
    terms = terms.value
    grad_query, grad_key, grad_value, grad_output = call(
        functools.partial(attend_grads_kernel, q_cols, size),
        "attend_grads",
        None,
        any_place(*operands),
        vm(
            shape_of(wq.shape, F32),
            shape_of(wk.shape, F32),
            shape_of(wv.shape, F32),
            shape_of(wo.shape, F32),
        ),
        [pltpu.VMEM(o.shape, o.dtype) for o in operands[:4]] + [dma((4,))],
    )
    ends = jnp.where(lax.axis_index("section") == 0, ends_0.value, ends_1.value)
    return (
        ends[None],
        terms[8:16].reshape(1, width),
        terms[:8].reshape(1, width),
        terms[16:17, :size],
        terms[16:17, size : 2 * size],
        grad_query[None],
        grad_key[None],
        grad_value[None],
        grad_output[None],
        grad_gate.reshape(w_gate.shape),
        grad_up.reshape(w_gate.shape),
        grad_down.reshape(w_gate.shape),
    )


def solution(mesh):
    return jax.shard_map(
        on_device,
        mesh=mesh,
        in_specs=(
            P("section", None, "expert", None),
            P("section", None, "expert", None),
            P("section", None, "expert", None),
            P("section", None, "expert", None),
            P("section", None),
            P("section", None),
            P("section", None),
            P("section", None),
            P("section", "expert", "tensor"),
            P("section", "expert", "tensor"),
            P("section", "expert", "tensor"),
            P("section", "tensor", "expert"),
            P("section", "expert", "tensor", None),
            P("section", "expert", "tensor", None),
            P("section", "expert", "tensor", None),
        ),
        out_specs=(
            P("section", None, "expert", None),
            P("section", None),
            P("section", None),
            P("section", None),
            P("section", None),
            P("section", "expert", "tensor"),
            P("section", "expert", "tensor"),
            P("section", "expert", "tensor"),
            P("section", "tensor", "expert"),
            P("section", "expert", "tensor", None),
            P("section", "expert", "tensor", None),
            P("section", "expert", "tensor", None),
        ),
        check_vma=False,
    )
```

```python
import functools
import math

import jax
import jax.numpy as jnp
from jax import lax
from jax.experimental import pallas as pl
from jax.experimental.pallas import tpu as pltpu
from jax.sharding import PartitionSpec as P

EPSILON = 1e-06
THETA = 1000000.0
LANES = 128
TERM_ROWS = 24
TERM_COLS = 256
MESH = pl.DeviceIdType.MESH
SECTION, EXPERT, TENSOR = "section", "expert", "tensor"
F32 = jnp.float32
BF16 = jnp.bfloat16
VMEM_LIMIT = 62 * 1024 * 1024

ANY = pl.BlockSpec(memory_space=pl.ANY)
VM = pl.BlockSpec(memory_space=pltpu.VMEM)
SM = pl.BlockSpec(memory_space=pltpu.SMEM)

(
    BEGIN, END, SPREAD, ARRIVED, SECOND, LOOPED, COLLECTED, TABLES, QKV, SHARDS, SENT, OUT, REDUCED, DQKV, TERMS, TAIL,
) = range(0, 16)
(
    ATTEND_0, EXPERTS_0, ATTEND_1, BOTH_1, ATTEND_BACK_1, EXPERTS_BACK_0, ATTEND_BACK_0,
) = range(0, 7)
(
    MOVE_WEIGHTS_1, MOVE_DY_ROWS, MOVE_DY_ALL, MOVE_B_0, MOVE_O_0, MOVE_A_0, MOVE_A_1, MOVE_O_1, MOVE_DAT_1, MOVE_Y_NEAR, MOVE_DQKV_1, MOVE_TERMS_1, MOVE_Y_FAR, MOVE_DAT_0, MOVE_Y_SPREAD, MOVE_DQKV_0, MOVE_DX_0, MOVE_TERMS_0,
) = range(0, 18)
NEAR_0, NEAR_1 = 40, 50
(
    SHARED_PART, SHARED_OWN, SHARED_GATES, SHARED_WG, SHARED_WU, SHARED_WD, SHARED_WQ, SHARED_WK, SHARED_WV, SHARED_WO, SHARED_HID, SHARED_DG, SHARED_DU,
) = range(0, 13)


def partner(index, k, count):
    out, bit = 0, 1
    while bit < count:
        out = out + bit * lax.rem(lax.div(index, bit) + lax.div(k, bit), 2)
        bit *= 2
    return out


def rows_at(start, size):
    return pl.ds(pl.multiple_of(start, size), size)


def remote(src, dst, send_sem, recv_sem, **where):
    return pltpu.make_async_remote_copy(
        src_ref=src,
        dst_ref=dst,
        send_sem=send_sem,
        recv_sem=recv_sem,
        device_id=where,
        device_id_type=MESH,
    )


def greet(peers):
    barrier = pltpu.get_barrier_semaphore()
    for where in peers:
        pl.semaphore_signal(barrier, inc=1, device_id=where, device_id_type=MESH)
    pl.semaphore_wait(barrier, len(peers))


def layer_peers(z, t, nz, nt):
    i32 = jnp.int32
    peers = [{"expert": partner(z, i32(k), nz)} for k in range(1, nz)]
    peers += [{TENSOR: partner(t, i32(k), nt)} for k in range(1, nt)]
    return peers


def dot(a, b):
    return lax.dot_general(a, b, (((1,), (0,)), ((), ())), preferred_element_type=F32)


def dot_nt(a, b):
    return lax.dot_general(a, b, (((1,), (1,)), ((), ())), preferred_element_type=F32)


def dot_tn(a, b):
    return lax.dot_general(a, b, (((0,), (0,)), ((), ())), preferred_element_type=F32)


def unit_rows(value):
    factor = lax.rsqrt(jnp.mean(value * value, axis=-1, keepdims=True) + EPSILON)
    return value * factor, factor


def norm_back(grad, gain, unit, factor):
    weighted = grad * gain
    inner = jnp.mean(weighted * unit, axis=-1, keepdims=True)
    return factor * (weighted - unit * inner), jnp.sum(grad * unit, axis=0, keepdims=True)


def expert_gates(gate_rows, first_expert, local_experts, width):
    rows = gate_rows.shape[0]
    lane = lax.broadcasted_iota(jnp.int32, gate_rows.shape, 1)
    column = lax.broadcasted_iota(jnp.int32, (rows, local_experts * width), 1)
    out = None
    for e in range(local_experts):
        one = jnp.sum(jnp.where(lane == first_expert + e, gate_rows, 0.0), axis=1, keepdims=True)
        wide = jnp.broadcast_to(one, column.shape)
        out = wide if out is None else jnp.where(column >= e * width, wide, out)
    return out


def write_terms(terms_ref, row, vector):
    for i in range(vector.shape[1] // TERM_COLS):
        terms_ref[row + i : row + i + 1, :] = vector[:, i * TERM_COLS : (i + 1) * TERM_COLS]


class Square:
    def __init__(self, nz, nt, rows, width):
        assert nt == 4
        self.z, self.t = lax.axis_index(EXPERT), lax.axis_index(TENSOR)
        self.nz, self.rows = nz, rows
        half = width // 2
        self.half, self.first, self.second = half, pl.ds(0, half), pl.ds(half, half)
        near_x, near_y, across = (partner(self.t, jnp.int32(j), nt) for j in (1, 2, 3))
        self.near = (near_x, near_y)
        self.mine, self.x_rows, self.y_rows, self.across_rows = (
            self.window(i) for i in (self.t, near_x, near_y, across)
        )
        self.y_pair = rows_at(lax.div(near_y, 2) * (2 * rows), 2 * rows)
        in_pair = lax.rem(self.t, 2)
        self.pair_mine, self.pair_x = self.window(in_pair), self.window(1 - in_pair)

    def window(self, index):
        return rows_at(index * self.rows, self.rows)


class RowGather:
    @staticmethod
    def scratch(nz):
        return [pltpu.SemaphoreType.DMA((2, nz)), pltpu.SemaphoreType.DMA((4, nz, 2))]

    def __init__(self, square, full, sems):
        self.sq, self.full = square, full
        self.far_sem, self.row_sem = sems

    def far_copy(self, k, source, src=None):
        sq = self.sq
        spot = self.full.at[source, sq.mine]
        return remote(
            spot if src is None else src,
            spot,
            self.far_sem.at[0, k],
            self.far_sem.at[1, k],
            expert=partner(sq.z, jnp.int32(k), sq.nz),
        )

    def row_copy(self, k, source, j, window, src=None):
        spot = self.full.at[source, window]
        return remote(
            spot if src is None else src,
            spot,
            self.row_sem.at[0, k, j],
            self.row_sem.at[1, k, j],
            tensor=self.sq.near[j],
        )

    def on_copy(self, k, source, j, window):
        spot = self.full.at[source, window, (self.sq.second, self.sq.first)[j]]
        return remote(
            spot, spot, self.row_sem.at[2, k, j], self.row_sem.at[3, k, j], tensor=self.sq.near[j]
        )

    def send(self, k, source, src=None):
        for j in range(2):
            self.row_copy(k, source, j, self.sq.mine, src).start()

    def hand_on(self, k, source):
        self.row_copy(k, source, 0, self.sq.x_rows).wait_recv()
        self.on_copy(k, source, 1, self.sq.x_rows).start()
        self.row_copy(k, source, 1, self.sq.y_rows).wait_recv()
        self.on_copy(k, source, 0, self.sq.y_rows).start()

    def arrive(self, k, source):
        for j in range(2):
            self.on_copy(k, source, j, self.sq.across_rows).wait_recv()

    def leave(self, k, source):
        for j in range(2):
            self.row_copy(k, source, j, self.sq.mine).wait_send()
            self.on_copy(k, source, j, (self.sq.y_rows, self.sq.x_rows)[j]).wait_send()


class RowSum:
    @staticmethod
    def scratch(nz, rows, block, width):
        half = width // 2
        dma = pltpu.SemaphoreType.DMA
        return [
            pltpu.VMEM((nz, block, width), BF16),
            pltpu.VMEM((nz, 2 * rows, half), BF16),
            pltpu.VMEM((nz, 2, rows, half), BF16),
            pltpu.VMEM((nz, 2, rows, half), BF16),
            pltpu.VMEM((nz, 2, rows, half), BF16),
            pltpu.VMEM((nz, rows, width), BF16),
            pltpu.VMEM((nz, rows, width), BF16),
            pltpu.VMEM((rows, width), F32),
            dma((2, nz)),
            dma((6, nz, 2)),
        ]

    count = 10

    def __init__(self, square, scratch, own=None):
        self.sq, self.own = square, own
        (self.outgoing, self.from_y, self.from_x, self.pairs, self.came_pairs) = scratch[:5]
        (self.passed, self.came_far, self.total, self.far_sem, self.part_sem) = scratch[5:]

    def part_copy(self, k, i):
        sq = self.sq
        window, cols = ((sq.y_pair, sq.first), (sq.across_rows, sq.second), (sq.x_rows, sq.second))[i]
        dst = (self.from_y.at[k], self.from_x.at[k, 1], self.from_x.at[k, 0])[i]
        group, slot = ((0, 0), (2, 1), (2, 0))[i]
        return remote(
            self.outgoing.at[k, window, cols],
            dst,
            self.part_sem.at[group, k, slot],
            self.part_sem.at[group + 1, k, slot],
            tensor=sq.near[0] if i else sq.near[1],
        )

    def pair_copy(self, k, j):
        return remote(
            self.pairs.at[k, j],
            self.came_pairs.at[k, j],
            self.part_sem.at[4, k, j],
            self.part_sem.at[5, k, j],
            tensor=self.sq.near[j],
        )

    def sum_copy(self, k):
        return remote(
            self.passed.at[k],
            self.came_far.at[k],
            self.far_sem.at[0, k],
            self.far_sem.at[1, k],
            expert=partner(self.sq.z, k, self.sq.nz),
        )

    def send(self, k):
        for i in range(3):
            self.part_copy(k, i).start()

    def pair_up(self, k):
        sq = self.sq
        self.part_copy(k, 0).wait_recv()
        kept = self.outgoing[k, sq.x_rows, sq.first].astype(F32)
        self.pairs[k, 0] = (kept + self.from_y[k, sq.pair_x].astype(F32)).astype(BF16)
        self.pair_copy(k, 0).start()
        self.part_copy(k, 1).wait_recv()
        kept = self.outgoing[k, sq.y_rows, sq.second].astype(F32)
        self.pairs[k, 1] = (kept + self.from_x[k, 1].astype(F32)).astype(BF16)
        self.pair_copy(k, 1).start()

    def collect(self, k):
        sq = self.sq
        self.part_copy(k, 2).wait_recv()
        self.pair_copy(k, 0).wait_recv()
        self.pair_copy(k, 1).wait_recv()
        own = self.outgoing[k, sq.mine].astype(F32) if self.own is None else self.own[k]
        left = own[:, : sq.half] + self.from_y[k, sq.pair_mine].astype(F32)
        right = own[:, sq.half :] + self.from_x[k, 0].astype(F32)
        return (
            left + self.came_pairs[k, 0].astype(F32),
            right + self.came_pairs[k, 1].astype(F32),
        )

    def collect_own(self):
        left, right = self.collect(jnp.int32(0))
        self.total[:, : self.sq.half] = left
        self.total[:, self.sq.half :] = right

    def collect_far(self, k):
        left, right = self.collect(k)
        self.passed[k, :, self.sq.first] = left.astype(BF16)
        self.passed[k, :, self.sq.second] = right.astype(BF16)
        self.sum_copy(k).start()

    def add_far(self):
        for k in range(1, self.sq.nz):
            self.sum_copy(jnp.int32(k)).wait_recv()
            self.total[...] += self.came_far[k].astype(F32)

    def leave(self, far=True):
        for k in range(self.sq.nz):
            if k and far:
                self.sum_copy(jnp.int32(k)).wait_send()
            for j in range(2):
                self.pair_copy(k, j).wait_send()
            for i in range(3):
                self.part_copy(k, i).wait_send()


def exchange_scratch(nz, nt, rows, block, width):
    return (
        [
            pltpu.VMEM((nz, block, width), BF16),
            (SHARED_PART, pltpu.VMEM((block, width), F32)),
            (SHARED_OWN, pltpu.VMEM((nz, rows, width), F32)),
            pltpu.VMEM((block, width), BF16),
            pltpu.SemaphoreType.DMA((2, nt)),
        ]
        + RowGather.scratch(nz)
        + RowSum.scratch(nz, rows, block, width)
    )


EXCHANGE_SCRATCH = 7 + RowSum.count


def exchange(nz, nt, own_rows, scratch, ready, work, at):
    full, part, own_part = scratch[:3]
    sq = Square(nz, nt, own_rows.shape[0], full.shape[-1])
    z = sq.z
    gather = RowGather(sq, full, scratch[5:7])
    sums = RowSum(sq, scratch[7 : 7 + RowSum.count], own_part)
    i32 = jnp.int32

    def produce(k, source):
        gather.arrive(k, source)
        part[...] = work(k, source, full[source])
        sums.outgoing[k] = part[...].astype(BF16)
        sums.send(k)
        own_part[k] = part[sq.mine]

    full[z, sq.mine] = own_rows
    for k in range(1, nz):
        gather.far_copy(k, z).start()
    gather.send(0, z)
    at(BEGIN)
    ready()
    for k in range(1, nz):
        source = partner(z, i32(k), nz)
        gather.far_copy(k, source).wait_recv()
        gather.send(k, source)
        if k == 1:
            gather.hand_on(0, z)
    at(ARRIVED)
    gather.hand_on(1, partner(z, i32(1), nz))

    def step(k, carry):
        @pl.when(k + 1 < nz)
        def _():
            gather.hand_on(k + 1, partner(z, k + 1, nz))

        turn = lax.rem(k, nz)
        produce(turn, partner(z, turn, nz))

        @pl.when(k >= 2)
        def _():
            sums.pair_up(k - 1)

        @pl.when(k >= 3)
        def _():
            sums.collect_far(k - 2)

        @pl.when(k == 2)
        def _():
            at(SECOND)

        return carry

    lax.fori_loop(1, nz + 1, step, 0)
    at(LOOPED)
    sums.collect_far(i32(nz - 1))
    sums.pair_up(i32(0))
    sums.collect_own()
    at(COLLECTED)
    sums.add_far()

    def finish():
        for k in range(nz):
            source = partner(z, i32(k), nz)
            if k:
                gather.far_copy(k, z).wait_send()
            gather.leave(k, source)
        sums.leave()

    return sums.total, finish


def spread_rows(t, nt, rows, block_ref, send_sem, recv_sem):
    i32 = jnp.int32
    mine = rows_at(t * rows, rows)
    for j in range(1, nt):
        remote(
            block_ref.at[mine],
            block_ref.at[mine],
            send_sem.at[j],
            recv_sem.at[j],
            tensor=partner(t, i32(j), nt),
        ).start()

    def wait():
        for j in range(1, nt):
            peer = partner(t, i32(j), nt)
            theirs = rows_at(peer * rows, rows)
            copy = remote(
                block_ref.at[theirs],
                block_ref.at[theirs],
                send_sem.at[j],
                recv_sem.at[j],
                tensor=peer,
            )
            copy.wait_send()
            copy.wait_recv()

    return wait


def reduce_rows(t, nt, rows, part, outgoing, came, send_sem, recv_sem, at):
    i32 = jnp.int32
    outgoing[...] = part[...].astype(BF16)

    def copy(j):
        peer = partner(t, i32(j), nt)
        return remote(
            outgoing.at[rows_at(peer * rows, rows)],
            came.at[j],
            send_sem.at[j],
            recv_sem.at[j],
            tensor=peer,
        )

    for j in range(1, nt):
        copy(j).start()
    at(SENT)
    total = part[rows_at(t * rows, rows)]
    for j in range(1, nt):
        copy(j).wait_recv()
        total = total + came[j].astype(F32)
    for j in range(1, nt):
        copy(j).wait_send()
    return total


def all_peers(s, z, t, nz, nt):
    i32 = jnp.int32
    peers = [{SECTION: 1 - s}]
    for k in range(1, nz):
        zz = partner(z, i32(k), nz)
        peers += [{EXPERT: zz}, {SECTION: 1 - s, EXPERT: zz}]
    return peers + [{TENSOR: partner(t, i32(j), nt)} for j in range(1, nt)]


class Relay:
    def __init__(self, layer, spots, nz):
        self.layer, self.spots, self.nz = layer, spots, nz

    def scratch(self, count=4):
        dma = pltpu.SemaphoreType.DMA
        return [dma((count,))] + [dma((count, self.nz))] * 6

    def bind(self, shards, outs, sems):
        self.s, self.z = lax.axis_index(SECTION), lax.axis_index(EXPERT)
        self.shards, self.outs, self.sems = shards, outs, sems
        self.source = self.hands = self.s == self.layer
        self.count = len(shards)
        return self

    def place(self, a, owner):
        dim = self.spots[a]
        size = self.shards[a].shape[dim]
        window = rows_at(owner * size, size)
        return self.outs[a].at[window] if dim == 0 else self.outs[a].at[:, window]

    def home(self, a):
        return pltpu.make_async_copy(self.shards[a], self.place(a, self.z), self.sems[0].at[a])

    def hop(self, a, owner, step, right, own=False):
        spot = self.place(a, owner)
        send, recv = self.sems[1:3] if right else self.sems[3:5]
        return remote(
            self.shards[a] if own else spot,
            spot,
            send.at[a, step],
            recv.at[a, step],
            expert=self.z + 1 if right else self.z - 1,
        )

    def hand(self, a, owner, own=False):
        spot = self.place(a, owner)
        return remote(
            self.shards[a] if own else spot,
            spot,
            self.sems[5].at[a, owner],
            self.sems[6].at[a, owner],
            section=1 - self.s,
        )

    def begin_side(self, a, right):
        @pl.when(self.source & ((self.z + 1 < self.nz) if right else (self.z >= 1)))
        def _():
            self.hop(a, self.z, 1, right, True).start()

    def begin_home(self, a):
        @pl.when(self.source)
        def _():
            self.home(a).start()

        @pl.when(self.hands)
        def _():
            self.hand(a, self.z, True).start()

    def begin(self, a):
        self.begin_side(a, True)
        self.begin_side(a, False)
        self.begin_home(a)

    def step(self, a, k):
        z, nz = self.z, self.nz

        @pl.when(self.source & (z >= k))
        def _():
            self.hop(a, z - k, k, True).wait_recv()

            @pl.when(z + 1 < nz)
            def _():
                self.hop(a, z - k, k + 1, True).start()

            @pl.when(self.hands)
            def _():
                self.hand(a, z - k).start()

        @pl.when(self.source & (z + k < nz))
        def _():
            self.hop(a, z + k, k, False).wait_recv()

            @pl.when(z >= 1)
            def _():
                self.hop(a, z + k, k + 1, False).start()

            @pl.when(self.hands)
            def _():
                self.hand(a, z + k).start()

    def settle(self, a):
        @pl.when(self.source)
        def _():
            self.home(a).wait()

        @pl.when(jnp.logical_not(self.source))
        def _():
            for owner in range(self.nz):
                self.hand(a, owner).wait_recv()

    def end(self, a):
        z, nz = self.z, self.nz

        @pl.when(self.hands)
        def _():
            for owner in range(nz):
                self.hand(a, owner).wait_send()

        @pl.when(self.source)
        def _():
            for step in range(1, nz):

                @pl.when((z >= step - 1) & (z + 1 < nz))
                def _():
                    self.hop(a, z - (step - 1), step, True).wait_send()

                @pl.when((z + step - 1 < nz) & (z >= 1))
                def _():
                    self.hop(a, z + (step - 1), step, False).wait_send()

    def start(self):
        for a in range(self.count):
            self.begin(a)

    def poll(self, turn):
        if turn < min(3, self.nz - 1):
            for a in range(self.count):
                self.step(a, turn)

    def finish(self):
        for k in range(min(3, self.nz - 1), self.nz):
            for a in range(self.count):
                self.step(a, k)
        for a in range(self.count):
            self.settle(a)
            self.end(a)


class Line(Relay):
    def __init__(self, layer, nz):
        super().__init__(layer, None, nz)

    def scratch(self):
        return super().scratch(1)

    def bind(self, ins, outs, sems):
        super().bind(ins, outs, sems)
        self.source, self.hands = self.s >= 0, self.s != self.layer
        return self

    def place(self, a, owner, section=None):
        return self.outs[a].at[self.s if section is None else section, owner]

    def settle(self, a):
        self.home(a).wait()

        @pl.when(self.s == self.layer)
        def _():
            for owner in range(self.nz):
                spot = self.place(a, owner, 1 - self.layer)
                remote(
                    spot, spot, self.sems[5].at[a, owner], self.sems[6].at[a, owner], section=1 - self.s
                ).wait_recv()


class Slice:
    def __init__(self, layer, nz, nt):
        self.layer, self.nz, self.nt = layer, nz, nt

    def scratch(self):
        dma = pltpu.SemaphoreType.DMA
        return [dma((2,)), dma((self.nz,)), dma((2, self.nz)), dma((2, self.nt))]

    def bind(self, ins, outs, sems):
        self.s, self.z, self.t = (lax.axis_index(a) for a in (SECTION, EXPERT, TENSOR))
        self.src, (self.out, self.rows_out), self.sems = ins[0], outs, sems
        rows, self.cols = self.rows_out.shape[2:]
        self.rows = rows
        self.mine = rows_at(self.t * rows, rows)
        self.receives = self.s == self.layer
        return self

    def far(self, k, local, section=None, origin=None):
        zz = partner(self.z, jnp.int32(k), self.nz)
        src = self.src.at[self.mine, rows_at(zz * self.cols, self.cols)]
        section = self.s if section is None else section
        spot = self.rows_out.at[section, self.z if origin is None else origin]
        if local:
            return pltpu.make_async_copy(src, spot, self.sems[0].at[0])
        return remote(
            src,
            spot,
            self.sems[1].at[k],
            self.sems[2].at[section, k],
            section=jnp.int32(self.layer),
            expert=zz,
        )

    def near(self, j, window):
        return remote(
            self.rows_out,
            self.out.at[:, :, window],
            self.sems[3].at[0, j],
            self.sems[3].at[1, j],
            tensor=partner(self.t, jnp.int32(j), self.nt),
        )

    def home(self):
        return pltpu.make_async_copy(self.rows_out, self.out.at[:, :, self.mine], self.sems[0].at[1])

    def start(self):
        for k in range(1, self.nz):
            self.far(k, False).start()

        @pl.when(self.receives)
        def _():
            self.far(0, True).start()

        @pl.when(jnp.logical_not(self.receives))
        def _():
            self.far(0, False).start()

    def poll(self, turn):
        if turn != 1:
            return

        @pl.when(self.receives)
        def _():
            self.far(0, True).wait()
            for section in range(2):
                for k in range(self.nz):
                    if k or section != self.layer:
                        zz = partner(self.z, jnp.int32(k), self.nz)
                        self.far(k, False, section, zz).wait_recv()
            self.home().start()
            for j in range(1, self.nt):
                self.near(j, self.mine).start()

    def finish(self):
        for k in range(1, self.nz):
            self.far(k, False).wait_send()

        @pl.when(jnp.logical_not(self.receives))
        def _():
            self.far(0, False).wait_send()

        @pl.when(self.receives)
        def _():
            self.home().wait()
            for j in range(1, self.nt):
                theirs = partner(self.t, jnp.int32(j), self.nt) * self.rows
                self.near(j, rows_at(theirs, self.rows)).wait_recv()
                self.near(j, self.mine).wait_send()


class Gather:
    def __init__(self, layer, nz):
        self.layer, self.nz = layer, nz

    def scratch(self):
        dma = pltpu.SemaphoreType.DMA
        return [dma((1,)), dma((self.nz,)), dma((2, self.nz))]

    def bind(self, ins, outs, sems):
        self.s, self.z = lax.axis_index(SECTION), lax.axis_index(EXPERT)
        self.src, self.out, self.sems = (ins or (None,))[0], outs[0], sems
        return self

    def copy(self, k, local, section=None, origin=None):
        zz = partner(self.z, jnp.int32(k), self.nz)
        src = self.src
        section = self.s if section is None else section
        spot = self.out.at[section, self.z if origin is None else origin]
        if local:
            return pltpu.make_async_copy(src, spot, self.sems[0].at[0])
        return remote(
            src,
            spot,
            self.sems[1].at[k],
            self.sems[2].at[section, k],
            section=jnp.int32(self.layer),
            expert=zz,
        )

    def start(self):
        for k in range(1, self.nz):
            self.copy(k, False).start()

        @pl.when(self.s == self.layer)
        def _():
            self.copy(0, True).start()

        @pl.when(self.s != self.layer)
        def _():
            self.copy(0, False).start()

    def poll(self, turn):
        pass

    def arrive(self):
        @pl.when(self.s == self.layer)
        def _():
            self.copy(0, True).wait()
            for section in range(2):
                for k in range(self.nz):
                    if k or section != self.layer:
                        zz = partner(self.z, jnp.int32(k), self.nz)
                        self.copy(k, False, section, zz).wait_recv()

    def leave(self):
        for k in range(1, self.nz):
            self.copy(k, False).wait_send()

        @pl.when(self.s != self.layer)
        def _():
            self.copy(0, False).wait_send()

    def finish(self):
        self.arrive()
        self.leave()


class Near:
    def __init__(self, layer, both=False):
        self.layer, self.both = layer, both

    def scratch(self):
        dma = pltpu.SemaphoreType.DMA
        return [dma((1,)), dma((1,)), dma((1,))]

    def bind(self, ins, outs, sems):
        self.s, self.sems = lax.axis_index(SECTION), sems
        self.src, self.out = (ins or (None,))[0], outs[0]
        return self

    def local(self):
        return pltpu.make_async_copy(self.src, self.out.at[self.layer], self.sems[0].at[0])

    def copy(self):
        return remote(
            self.src,
            self.out.at[1 - self.layer] if self.both else self.out,
            self.sems[1].at[0],
            self.sems[2].at[0],
            section=jnp.int32(self.layer),
        )

    def start(self):
        if self.both:

            @pl.when(self.s == self.layer)
            def _():
                self.local().start()

        @pl.when(self.s != self.layer)
        def _():
            self.copy().start()

    def poll(self, turn):
        pass

    def finish(self):
        @pl.when(self.s == self.layer)
        def _():
            if self.both:
                self.local().wait()
            remote(
                self.src,
                self.out.at[1 - self.layer] if self.both else self.out,
                self.sems[1].at[0],
                self.sems[2].at[0],
                section=1 - self.s,
            ).wait_recv()

        @pl.when(self.s != self.layer)
        def _():
            self.copy().wait_send()


class RowsFar:
    def __init__(self, slot, nz, nt):
        self.slot, self.nz, self.nt = slot, nz, nt

    def scratch(self):
        return [pltpu.SemaphoreType.DMA((1,)), pltpu.SemaphoreType.DMA((2, self.nz))]

    def bind(self, ins, outs, sems):
        self.z, self.t = lax.axis_index(EXPERT), lax.axis_index(TENSOR)
        self.src, self.out, self.sems = ins[0], outs[0], sems
        return self

    def copy(self, k, origin):
        rows = self.out.shape[1]
        src = self.src.at[self.slot, rows_at(self.t * rows, rows)]
        if k == 0:
            return pltpu.make_async_copy(src, self.out.at[origin], self.sems[0].at[0])
        return remote(
            src,
            self.out.at[origin],
            self.sems[1].at[0, k],
            self.sems[1].at[1, k],
            expert=partner(self.z, jnp.int32(k), self.nz),
        )

    def start(self):
        for k in range(self.nz):
            self.copy(k, self.z).start()

    def poll(self, turn):
        pass

    def finish(self):
        self.copy(0, self.z).wait()
        for k in range(1, self.nz):
            self.copy(k, self.z).wait_send()
            self.copy(k, partner(self.z, jnp.int32(k), self.nz)).wait_recv()


class Spread:
    def __init__(self, nz, nt):
        self.nz, self.nt = nz, nt

    def scratch(self):
        return [pltpu.SemaphoreType.DMA((1,))] + RowGather.scratch(self.nz)

    def bind(self, ins, outs, sems):
        self.src, self.out, self.sems = ins[0], outs[0], sems
        self.sq = Square(self.nz, self.nt, *self.src.shape[1:])
        self.gather = RowGather(self.sq, self.out, sems[1:])
        return self

    def local(self):
        return pltpu.make_async_copy(self.src, self.out.at[:, self.sq.mine], self.sems[0].at[0])

    def start(self):
        self.local().start()
        for k in range(self.nz):
            self.gather.send(k, k, self.src.at[k])

    def poll(self, turn):
        if turn == 1:
            for k in range(self.nz):
                self.gather.hand_on(k, k)

    def finish(self):
        self.local().wait()
        for k in range(self.nz):
            self.gather.arrive(k, k)
            self.gather.leave(k, k)


class SumNear:
    def __init__(self, nz, nt, rows, block, width):
        self.nz, self.nt = nz, nt
        self.shape = rows, block, width

    def scratch(self):
        rows, block, width = self.shape
        half = width // 2
        return [
            pltpu.SemaphoreType.DMA((2,)),
            pltpu.SemaphoreType.DMA((2, 5)),
            pltpu.VMEM((self.nz, block, width), BF16),
            pltpu.VMEM((self.nz, 2 * rows, half), BF16),
            pltpu.VMEM((2, self.nz, rows, half), BF16),
            pltpu.VMEM((2, self.nz, rows, half), BF16),
            pltpu.VMEM((2, self.nz, rows, half), BF16),
            pltpu.VMEM((self.nz, rows, width), BF16),
        ]

    def bind(self, ins, outs, scratch):
        self.src, self.out = ins[0], outs[0]
        self.sems, self.sem = scratch[:2]
        self.parts, self.from_y, self.from_x, self.pairs, self.came, self.result = scratch[2:]
        self.sq = Square(self.nz, self.nt, self.shape[0], self.shape[2])
        return self

    def load(self):
        return pltpu.make_async_copy(self.src, self.parts, self.sems.at[0])

    def save(self):
        return pltpu.make_async_copy(self.result, self.out, self.sems.at[1])

    def copy(self, i):
        sq = self.sq
        if i < 3:
            window, cols = ((sq.y_pair, sq.first), (sq.across_rows, sq.second), (sq.x_rows, sq.second))[i]
            src = self.src.at[:, window, cols]
            dst = (self.from_y, self.from_x.at[1], self.from_x.at[0])[i]
        else:
            src, dst = self.pairs.at[i - 3], self.came.at[i - 3]
        peer = sq.near[(1, 0, 0, 0, 1)[i]]
        return remote(src, dst, self.sem.at[0, i], self.sem.at[1, i], tensor=peer)

    def start(self):
        self.load().start()
        for i in range(3):
            self.copy(i).start()

    def poll(self, turn):
        sq = self.sq
        if turn == 1:
            self.load().wait()
            self.copy(0).wait_recv()
            kept = self.parts[:, sq.x_rows, sq.first].astype(F32)
            self.pairs[0] = (kept + self.from_y[:, sq.pair_x].astype(F32)).astype(BF16)
            self.copy(3).start()
            self.copy(1).wait_recv()
            kept = self.parts[:, sq.y_rows, sq.second].astype(F32)
            self.pairs[1] = (kept + self.from_x[1].astype(F32)).astype(BF16)
            self.copy(4).start()
        if turn == 2:
            for i in (2, 3, 4):
                self.copy(i).wait_recv()
            left = self.parts[:, sq.mine, sq.first].astype(F32)
            left = left + self.from_y[:, sq.pair_mine].astype(F32) + self.came[0].astype(F32)
            right = self.parts[:, sq.mine, sq.second].astype(F32)
            right = right + self.from_x[0].astype(F32) + self.came[1].astype(F32)
            self.result[:, :, sq.first] = left.astype(BF16)
            self.result[:, :, sq.second] = right.astype(BF16)
            self.save().start()

    def finish(self):
        self.save().wait()
        for i in range(5):
            self.copy(i).wait_send()


class SumFar:
    def __init__(self, nz, rows, width):
        self.nz, self.shape = nz, (rows, width)

    def scratch(self):
        dma = pltpu.SemaphoreType.DMA
        return [
            pltpu.VMEM((self.nz,) + self.shape, BF16),
            pltpu.VMEM(self.shape, BF16),
            dma((2,)),
            dma((2, self.nz)),
        ]

    def bind(self, ins, outs, scratch):
        self.z = lax.axis_index(EXPERT)
        self.src, self.rows_ref = ins
        self.out = outs[0]
        self.came, self.result, self.sems, self.far_sem = scratch
        return self

    def copy(self, k):
        if k == 0:
            return pltpu.make_async_copy(self.src.at[0], self.came.at[0], self.sems.at[0])
        return remote(
            self.src.at[k],
            self.came.at[k],
            self.far_sem.at[0, k],
            self.far_sem.at[1, k],
            expert=partner(self.z, jnp.int32(k), self.nz),
        )

    def save(self):
        return pltpu.make_async_copy(self.result, self.out, self.sems.at[1])

    def start(self):
        for k in range(self.nz):
            self.copy(k).start()

    def poll(self, turn):
        if turn == 2:
            self.copy(0).wait()
            total = self.rows_ref[...] + self.came[0].astype(F32)
            for k in range(1, self.nz):
                self.copy(k).wait_recv()
                total = total + self.came[k].astype(F32)
            self.result[...] = total.astype(BF16)
            self.save().start()

    def finish(self):
        self.save().wait()
        for k in range(1, self.nz):
            self.copy(k).wait_send()


class SpreadNear:
    def __init__(self, layer, nt, block, width):
        self.nt, self.shape, self.near = nt, (block, width), Near(layer, True)

    def scratch(self):
        dma = pltpu.SemaphoreType.DMA
        return [pltpu.VMEM(self.shape, BF16), dma((1,)), dma((2, self.nt))] + self.near.scratch()

    def bind(self, ins, outs, scratch):
        self.t = lax.axis_index(TENSOR)
        self.src = ins[0]
        self.whole, self.load_sem, self.spread_sem = scratch[:3]
        self.near.bind([self.whole], outs, scratch[3:])
        self.rows = self.src.shape[0]
        return self

    def start(self):
        load = pltpu.make_async_copy(
            self.src, self.whole.at[rows_at(self.t * self.rows, self.rows)], self.load_sem.at[0]
        )
        load.start()
        load.wait()
        self.wait = spread_rows(
            self.t, self.nt, self.rows, self.whole, self.spread_sem.at[0], self.spread_sem.at[1]
        )

    def poll(self, turn):
        if turn == 1:
            self.wait()
            self.near.start()

    def finish(self):
        self.near.finish()


def heads_to_rows(value, heads, size):
    return jnp.concatenate([value[:, h * size : (h + 1) * size] for h in range(heads)], axis=0)


def rows_to_heads(value, heads, block):
    return jnp.concatenate([value[h * block : (h + 1) * block] for h in range(heads)], axis=1)


def split_gains(row, width, size):
    return (
        row[:, :width],
        row[:, width : 2 * width],
        row[:, 2 * width : 2 * width + size],
        row[:, 2 * width + size :],
    )


def tiled(value, times):
    return jnp.concatenate([value] * times, axis=0)


def half_turn(value):
    return pltpu.roll(value, value.shape[-1] // 2, value.ndim - 1)


def attend_body(t, nt, heads, x_ref, tables, gains, outs, scratch, wait_qkv, wait_out, at):
    (h1_ref, b_ref, a_ref, q_ref, k_ref, v_ref, qr_ref, kr_ref, o_ref) = outs
    (wq_s, wk_s, wv_s, wo_s, part, outgoing, came, s_sem, r_sem) = scratch
    block, width = x_ref.shape
    rows = block // nt
    cos, sin, bias = tables
    size = cos.shape[-1]
    g_attn, g_moe, g_query, g_key = split_gains(gains, width, size)
    unit, _ = unit_rows(x_ref[...].astype(F32))
    a_ref[...] = (unit * g_attn).astype(BF16)
    wait_qkv()
    q = dot(a_ref[...], wq_s[...])
    q_ref[...] = q
    k = dot(a_ref[...], wk_s[...])
    k_ref[...] = k
    v = dot(a_ref[...], wv_s[...]).astype(BF16)
    v_ref[...] = v
    qn = unit_rows(heads_to_rows(q, heads, size))[0] * g_query
    kn = unit_rows(k)[0] * g_key
    qr = (qn * tiled(cos, heads) + half_turn(qn) * tiled(sin, heads)).astype(BF16)
    kr = (kn * cos + half_turn(kn) * sin).astype(BF16)
    qr_ref[...] = qr
    kr_ref[...] = kr
    scores = dot_nt(qr, kr) * (1.0 / math.sqrt(size)) + tiled(bias, heads)
    peak = jnp.max(scores, axis=-1, keepdims=True)
    weight = jnp.exp(scores - peak)
    probs = weight * (1.0 / jnp.sum(weight, axis=-1, keepdims=True))
    o = dot(probs.astype(BF16), v).astype(BF16)
    o_ref[...] = rows_to_heads(o, heads, block)
    wait_out()
    part[...] = dot(o_ref[...], wo_s[...])
    total = reduce_rows(t, nt, rows, part, outgoing, came, s_sem, r_sem, at)
    h1 = x_ref[rows_at(t * rows, rows)].astype(F32) + total
    h1_ref[...] = h1
    b_ref[...] = (unit_rows(h1)[0] * g_moe).astype(BF16)


def fill_tables(tabs, lengths, m):
    block, size = tabs.shape[2:]
    row = lax.broadcasted_iota(jnp.int32, (block, size), 0)
    lane = lax.broadcasted_iota(jnp.int32, (block, size), 1)
    begin, segment, segment_of_lane = (jnp.zeros((block, size), jnp.int32) for _ in range(3))
    end = jnp.int32(0)
    for n in range(lengths.shape[1]):
        end = end + lengths[m, n]
        begin = jnp.where(row >= end, end, begin)
        segment = segment + jnp.where(row >= end, 1, 0)
        segment_of_lane = segment_of_lane + jnp.where(lane >= end, 1, 0)
    half = size // 2
    position = jnp.where(lane >= half, lane - half, lane).astype(F32)
    inverse = jnp.exp(position * (-2.0 * math.log(THETA) / size))
    angle = (row - begin).astype(F32) * inverse
    sin = jnp.sin(angle)
    tabs[m, 0] = jnp.cos(angle)
    tabs[m, 1] = jnp.where(lane >= half, sin, -sin)
    tabs[m, 2] = jnp.where((lane <= row) & (segment == segment_of_lane), 0.0, -1e30)


def fill_gates(gates, ids, route_weights, m):
    expert_of, weight_of = ids[m], route_weights[m]
    lane = lax.broadcasted_iota(jnp.int32, gates.shape[1:], 1)
    out = jnp.zeros(gates.shape[1:], F32)
    for c in range(expert_of.shape[1]):
        out = out + jnp.where(lane == expert_of[:, c : c + 1], weight_of[:, c : c + 1], 0.0)
    gates[m] = out


def start_attend_kernel(nz, nt, heads, relay, hello, at, ins, outs, scratch):
    s, z, t = lax.axis_index(SECTION), lax.axis_index(EXPERT), lax.axis_index(TENSOR)
    lengths, ids, route_weights, boundary, gains, wq, wk, wv, wo, wg, wu, wd = ins
    edges, tabs_out, gates_out, gains_out = outs[:4]
    gathered, (sg, su, sd), results = outs[4:8], outs[8:11], outs[11:]
    x_s, tabs_s, gains_s, tabs, gates = scratch[:5]
    w_sem, in_sem, own_sem, sib_send, sib_recv, gate_send, gate_recv = scratch[5:12]
    relay.bind((wq, wk, wv, wo), gathered, scratch[12:19])
    attn_scratch = scratch[19:]
    other = 1 - s
    i32 = jnp.int32

    own = [
        pltpu.make_async_copy(boundary.at[s], edges.at[s], own_sem.at[0]),
        pltpu.make_async_copy(tabs.at[s], tabs_out.at[s], own_sem.at[1]),
        pltpu.make_async_copy(gains, gains_out.at[s], own_sem.at[2]),
        pltpu.make_async_copy(gates.at[s], gates_out.at[s, z], own_sem.at[3]),
    ]
    own[0].start()
    own[2].start()
    hello(all_peers(s, z, t, nz, nt))

    def sibling(i, src, dst):
        return remote(src, dst, sib_send.at[i], sib_recv.at[i], section=other)

    pairs = [
        (boundary.at[other], edges.at[s], edges.at[other]),
        (tabs.at[other], tabs_out.at[s], tabs_out.at[other]),
        (gains, gains_out.at[s], gains_out.at[other]),
        (wg, sg, sg),
        (wu, su, su),
        (wd, sd, sd),
    ]
    for i in (0, 2):
        sibling(i, *pairs[i][:2]).start()
    for a in range(3):
        relay.begin(a)
    relay.begin_home(3)

    def gate_copy(d, k, arrival=False):
        zz = partner(z, i32(k), nz)
        section = s if d == 0 else other
        return remote(
            gates.at[section],
            gates_out.at[section, zz] if arrival else gates_out.at[s, z],
            gate_send.at[d, k],
            gate_recv.at[d, k],
            section=section,
            expert=zz,
        )

    for m in range(2):
        fill_tables(tabs, lengths, m)
    sibling(1, *pairs[1][:2]).start()
    own[1].start()
    for m in range(2):
        fill_gates(gates, ids, route_weights, m)
    own[3].start()
    turns = [(d, k) for d in range(2) for k in range(nz) if d or k]
    for d, k in turns:
        gate_copy(d, k).start()
    for i in range(3, 6):
        sibling(i, *pairs[i][:2]).start()

    for copy in own:
        copy.wait()
    for i in range(3):
        sibling(i, pairs[i][0], pairs[i][2]).wait_recv()
    at(TABLES)
    loads = [
        pltpu.make_async_copy(edges.at[0], x_s, in_sem.at[0]),
        pltpu.make_async_copy(tabs_out.at[0], tabs_s, in_sem.at[1]),
        pltpu.make_async_copy(gains_out.at[0], gains_s, in_sem.at[2]),
    ]
    for load in loads:
        load.start()
    for load in loads:
        load.wait()

    def bring(a):
        return pltpu.make_async_copy(gathered[a], attn_scratch[a], w_sem.at[a])

    def wait_qkv():
        for k in range(1, nz):
            for a in range(3):
                relay.step(a, k)

            @pl.when((z == k) | ((z == 0) & (k == 1)))
            def _():
                relay.begin_side(3, True)

            @pl.when((z == nz - 1 - k) | ((z == nz - 1) & (k == 1)))
            def _():
                relay.begin_side(3, False)

        for a in range(3):
            relay.settle(a)
            bring(a).start()
        for a in range(3):
            bring(a).wait()
        at(QKV)

    def wait_out():
        for k in range(1, nz):
            relay.step(3, k)
        at(SHARDS)
        relay.settle(3)
        bring(3).start()
        bring(3).wait()

    tables = (tabs_s[0], tabs_s[1], tabs_s[2])
    attend_body(t, nt, heads, x_s, tables, gains_s[...], results, attn_scratch, wait_qkv, wait_out, at)
    for i in range(6):
        sibling(i, *pairs[i][:2]).wait_send()
    for i in range(3, 6):
        sibling(i, pairs[i][0], pairs[i][2]).wait_recv()
    for d, k in turns:
        gate_copy(d, k).wait_send()
        gate_copy(d, k, True).wait_recv()
    for a in range(4):
        relay.end(a)
    at(END)


def attend_kernel(layer, nz, nt, heads, hello, at, ins, outs, scratch):
    s, z, t = lax.axis_index(SECTION), lax.axis_index(EXPERT), lax.axis_index(TENSOR)
    x_ref, tabs, gains, wq, wk, wv, wo = ins
    w_sem, tabs_s, gains_s, attn_scratch = scratch[0], scratch[1], scratch[2], scratch[3:]
    loads = [
        pltpu.make_async_copy(src, dst, w_sem.at[i])
        for i, (src, dst) in enumerate(zip((wq, wk, wv, wo), attn_scratch))
    ]
    small = [
        pltpu.make_async_copy(tabs.at[layer], tabs_s, w_sem.at[4]),
        pltpu.make_async_copy(gains.at[layer], gains_s, w_sem.at[5]),
    ]
    for load in small:
        load.start()
    hello(all_peers(s, z, t, nz, nt))
    at(BEGIN)
    for load in small:
        load.wait()

    def wait_qkv():
        at(QKV)
        for load in loads[:3]:
            load.start()
        for load in loads[:3]:
            load.wait()

    def wait_out():
        at(OUT)
        loads[3].start()
        loads[3].wait()

    tables = (tabs_s[0], tabs_s[1], tabs_s[2])
    attend_body(t, nt, heads, x_ref, tables, gains_s[...], outs, attn_scratch, wait_qkv, wait_out, at)
    at(END)


def load_experts(layer, s, own, sibling, scratch, sems):
    def copies(refs):
        return [pltpu.make_async_copy(r, d, sems.at[i]) for i, (r, d) in enumerate(zip(refs, scratch))]

    @pl.when(s == layer)
    def _():
        for copy in copies(own):
            copy.start()

    @pl.when(s != layer)
    def _():
        for copy in copies(sibling):
            copy.start()

    return copies(own)


def experts_kernel(layer, nz, nt, local_experts, hello, at, ins, outs, scratch):
    s, z, t = lax.axis_index(SECTION), lax.axis_index(EXPERT), lax.axis_index(TENSOR)
    b_ref, h1_ref, gates, wg, wu, wd, sg, su, sd = ins
    y_ref, b_out, g_out, u_out = outs
    wg_s, wu_s, wd_s, g_s, u_s, gates_s, w_sem, o_sem = scratch[:8]
    spaces = scratch[8:]
    rows = b_ref.shape[0]
    loads = load_experts(layer, s, (wg, wu, wd), (sg, su, sd), (wg_s, wu_s, wd_s), w_sem)
    loads.append(pltpu.make_async_copy(gates.at[layer], gates_s, w_sem.at[3]))
    loads[3].start()
    hello(all_peers(s, z, t, nz, nt))
    width = wg.shape[0] // local_experts

    def ready():
        for load in loads:
            load.wait()

    def work(k, origin, rows_in):
        gate_pre = dot_nt(rows_in, wg_s[...])
        up_pre = dot_nt(rows_in, wu_s[...])
        g_s[origin] = gate_pre
        u_s[origin] = up_pre
        weight = expert_gates(gates_s[origin], z * local_experts, local_experts, width)
        hidden = (gate_pre * jax.nn.sigmoid(gate_pre) * up_pre * weight).astype(BF16)
        return dot(hidden, wd_s[...])

    total, finish = exchange(nz, nt, b_ref[...], spaces, ready, work, at)
    full, whole, spread_sem = spaces[0], spaces[3], spaces[4]
    saves = [
        pltpu.make_async_copy(full, b_out, o_sem.at[0]),
        pltpu.make_async_copy(g_s, g_out, o_sem.at[1]),
        pltpu.make_async_copy(u_s, u_out, o_sem.at[2]),
    ]
    for save in saves:
        save.start()
    whole[rows_at(t * rows, rows)] = (h1_ref[...] + total[...]).astype(BF16)
    wait = spread_rows(t, nt, rows, whole, spread_sem.at[0], spread_sem.at[1])
    at(SPREAD)
    finish()
    wait()
    y_ref[...] = whole[...]
    for save in saves:
        save.wait()
    at(END)


def experts_back_kernel(layer, nz, nt, local_experts, hello, at, ins, outs, scratch):
    s, z, t = lax.axis_index(SECTION), lax.axis_index(EXPERT), lax.axis_index(TENSOR)
    dy_ref, h1_ref, gains, gates, g_in, u_in, wg, wu, wd, sg, su, sd = ins
    dat_ref, dh1_ref, term_ref, dy_out, hid_out, dg_out, du_out = outs
    wg_s, wu_s, wd_s, g_s, u_s, hid_s, dg_s, du_s, w_sem, g_sem, u_sem, o_sem = scratch[:12]
    gates_s, scratch = scratch[12], scratch[:12] + scratch[13:]
    spaces = scratch[12:]
    rows, model_width = dy_ref.shape
    loads = load_experts(layer, s, (wd, wg, wu), (sd, sg, su), (wd_s, wg_s, wu_s), w_sem)
    loads.append(pltpu.make_async_copy(gates.at[layer], gates_s, w_sem.at[3]))
    loads[3].start()

    def kept(k):
        origin, slot = partner(z, lax.rem(k + 1, nz), nz), lax.rem(k, 2)
        return (
            pltpu.make_async_copy(g_in.at[origin], g_s.at[slot], g_sem.at[slot]),
            pltpu.make_async_copy(u_in.at[origin], u_s.at[slot], u_sem.at[slot]),
        )

    for load in kept(jnp.int32(0)):
        load.start()
    hello(all_peers(s, z, t, nz, nt))
    width = wg.shape[0] // local_experts

    def ready():
        for load in loads:
            load.wait()

    def work(k, origin, rows_in):
        turn = lax.rem(k + nz - 1, nz)
        for load in kept(turn):
            load.wait()

        @pl.when(turn + 1 < nz)
        def _():
            for load in kept(turn + 1):
                load.start()

        slot = lax.rem(turn, 2)
        gate_pre, up_pre = g_s[slot], u_s[slot]
        weight = expert_gates(gates_s[origin], z * local_experts, local_experts, width)
        sigmoid = jax.nn.sigmoid(gate_pre)
        silu = gate_pre * sigmoid
        hid_s[origin] = (silu * up_pre * weight).astype(BF16)
        grad_hidden = dot_nt(rows_in, wd_s[...]) * weight
        dg_s[origin] = (grad_hidden * up_pre * sigmoid * (1.0 + gate_pre * (1.0 - sigmoid))).astype(BF16)
        du_s[origin] = (grad_hidden * silu).astype(BF16)
        return dot(dg_s[origin], wg_s[...]) + dot(du_s[origin], wu_s[...])

    total, finish = exchange(nz, nt, dy_ref[...], spaces, ready, work, at)
    full, whole, spread_sem = spaces[0], spaces[3], spaces[4]
    saves = [
        pltpu.make_async_copy(full, dy_out, o_sem.at[0]),
        pltpu.make_async_copy(hid_s, hid_out, o_sem.at[1]),
        pltpu.make_async_copy(dg_s, dg_out, o_sem.at[2]),
        pltpu.make_async_copy(du_s, du_out, o_sem.at[3]),
    ]
    for save in saves:
        save.start()
    unit, factor = unit_rows(h1_ref[...])
    g_moe = gains[layer, :, model_width : 2 * model_width]
    back, term = norm_back(total[...], g_moe, unit, factor)
    dh1 = dy_ref[...].astype(F32) + back
    dh1_ref[...] = dh1
    term_ref[...] = term
    mine = rows_at(t * rows, rows)
    whole[mine] = dh1.astype(BF16)
    dat_ref[mine] = dh1.astype(BF16)
    wait = spread_rows(t, nt, rows, whole, spread_sem.at[0], spread_sem.at[1])
    at(SPREAD)
    finish()
    wait()
    for j in range(1, nt):
        theirs = rows_at(partner(t, jnp.int32(j), nt) * rows, rows)
        dat_ref[theirs] = whole[theirs]
    for save in saves:
        save.wait()
    at(END)


def experts_both_kernel(layer, nz, nt, local_experts, hello, at, ins, outs, scratch):
    s, z, t = lax.axis_index(SECTION), lax.axis_index(EXPERT), lax.axis_index(TENSOR)
    b_ref, h1_ref, dy_ref, gains, gates, dy_all, wg, wu, wd, sg, su, sd = ins
    dat_ref, dh1_ref, term_ref, b_out, y_out, hid_out, dg_out, du_out = outs
    wg_s, wu_s, wd_s, dy_s, y_s, hid_s, dg_s, du_s, w_sem, dy_sem, y_sem, o_sem = scratch[:12]
    gates_s, scratch = scratch[12], scratch[:12] + scratch[13:]
    spaces = scratch[12:]
    rows, model_width = b_ref.shape
    loads = load_experts(layer, s, (wg, wu, wd), (sg, su, sd), (wg_s, wu_s, wd_s), w_sem)
    loads.append(pltpu.make_async_copy(gates.at[layer], gates_s, w_sem.at[3]))
    loads[3].start()

    def cotangent(turn):
        origin, slot = partner(z, lax.rem(turn + 1, nz), nz), lax.rem(turn, 2)
        return pltpu.make_async_copy(dy_all.at[origin], dy_s.at[slot], dy_sem.at[slot])

    def store(turn):
        k, slot = lax.rem(turn + 1, nz), lax.rem(turn, 2)
        return pltpu.make_async_copy(y_s.at[slot], y_out.at[k], y_sem.at[slot])

    cotangent(jnp.int32(0)).start()
    hello(all_peers(s, z, t, nz, nt))
    width = wg.shape[0] // local_experts

    def ready():
        for load in loads:
            load.wait()

    def work(k, origin, rows_in):
        turn = lax.rem(k + nz - 1, nz)
        slot = lax.rem(turn, 2)
        cotangent(turn).wait()

        @pl.when(turn + 1 < nz)
        def _():
            cotangent(turn + 1).start()

        @pl.when(turn >= 2)
        def _():
            store(turn - 2).wait()

        gate_pre = dot_nt(rows_in, wg_s[...])
        up_pre = dot_nt(rows_in, wu_s[...])
        weight = expert_gates(gates_s[origin], z * local_experts, local_experts, width)
        sigmoid = jax.nn.sigmoid(gate_pre)
        silu = gate_pre * sigmoid
        hid_s[origin] = (silu * up_pre * weight).astype(BF16)
        grad_hidden = dot_nt(dy_s[slot], wd_s[...]) * weight
        dg_s[origin] = (grad_hidden * up_pre * sigmoid * (1.0 + gate_pre * (1.0 - sigmoid))).astype(BF16)
        du_s[origin] = (grad_hidden * silu).astype(BF16)
        y_s[slot] = dot(hid_s[origin], wd_s[...]).astype(BF16)
        store(turn).start()
        return dot(dg_s[origin], wg_s[...]) + dot(du_s[origin], wu_s[...])

    total, finish = exchange(nz, nt, b_ref[...], spaces, ready, work, at)
    full, whole, spread_sem = spaces[0], spaces[3], spaces[4]
    saves = [
        pltpu.make_async_copy(full, b_out, o_sem.at[0]),
        pltpu.make_async_copy(hid_s, hid_out, o_sem.at[1]),
        pltpu.make_async_copy(dg_s, dg_out, o_sem.at[2]),
        pltpu.make_async_copy(du_s, du_out, o_sem.at[3]),
    ]
    for save in saves:
        save.start()
    unit, factor = unit_rows(h1_ref[...])
    g_moe = gains[layer, :, model_width : 2 * model_width]
    back, term = norm_back(total[...], g_moe, unit, factor)
    dh1 = dy_ref[...].astype(F32) + back
    dh1_ref[...] = dh1
    term_ref[...] = term
    mine = rows_at(t * rows, rows)
    whole[mine] = dh1.astype(BF16)
    dat_ref[mine] = dh1.astype(BF16)
    wait = spread_rows(t, nt, rows, whole, spread_sem.at[0], spread_sem.at[1])
    at(SPREAD)
    finish()
    wait()
    for j in range(1, nt):
        theirs = rows_at(partner(t, jnp.int32(j), nt) * rows, rows)
        dat_ref[theirs] = whole[theirs]
    for save in saves:
        save.wait()
    store(jnp.int32(nz - 2)).wait()
    store(jnp.int32(nz - 1)).wait()
    at(END)


def attend_back_kernel(layer, source, nz, nt, heads, hello, at, ins, outs, scratch):
    s, z, t = lax.axis_index(SECTION), lax.axis_index(EXPERT), lax.axis_index(TENSOR)
    (x_ref, tabs, gains, dat_ref, dh1_ref, term_moe, q_ref, k_ref, v_ref, qr_ref, kr_ref) = ins[:11]
    wq, wk, wv, wo = ins[11:15]
    dx_ref, dqkv_ref, terms_ref = outs[:3]
    wq_s, wk_s, wv_s, wo_s, part, outgoing, came, s_sem, r_sem, w_sem, gs_sem, gr_sem = scratch[:12]
    x_s, scratch = scratch[12], scratch[13:]
    if layer == 0:
        whole, terms_near, terms_in, t_sem, near_send, near_recv = scratch
        terms_other, terms_out = ins[15], outs[3]
    block, model_width = dat_ref.shape
    rows = block // nt
    mine = rows_at(t * rows, rows)
    x_copy = pltpu.make_async_copy(
        x_ref.at[mine] if source is None else x_ref.at[source, mine], x_s, w_sem.at[4]
    )
    x_copy.start()
    loads = [
        pltpu.make_async_copy(src, dst, w_sem.at[i])
        for i, (src, dst) in enumerate(((wo, wo_s), (wq, wq_s), (wk, wk_s), (wv, wv_s)))
    ]
    for load in loads:
        load.start()
    hello(all_peers(s, z, t, nz, nt))
    if layer == 0:
        late = [at.moves[name] for name in (MOVE_DQKV_0, MOVE_DX_0, MOVE_TERMS_0)]
        late[0].src, late[1].src, late[2].src = dqkv_ref, whole, terms_ref
    at(BEGIN)

    size = tabs.shape[-1]
    g_attn, _, g_query, g_key = split_gains(gains[layer], model_width, size)
    scale = 1.0 / math.sqrt(size)
    cos, sin, bias = tabs[layer, 0], tabs[layer, 1], tabs[layer, 2]
    cos_all, sin_all = tiled(cos, heads), tiled(sin, heads)
    qr, kr, v = qr_ref[...], kr_ref[...], v_ref[...]
    scores = dot_nt(qr, kr) * scale + tiled(bias, heads)
    peak = jnp.max(scores, axis=-1, keepdims=True)
    weight = jnp.exp(scores - peak)
    probs = weight * (1.0 / jnp.sum(weight, axis=-1, keepdims=True))
    loads[0].wait()
    do = heads_to_rows(dot_nt(dat_ref[...], wo_s[...]).astype(BF16), heads, size)
    dv = dot_tn(probs.astype(BF16), do).astype(BF16)
    dp = dot_nt(do, v)
    ds = (probs * (dp - jnp.sum(probs * dp, axis=-1, keepdims=True))).astype(BF16)
    dqr = dot(ds, kr) * scale
    dkr = dot_tn(ds, qr) * scale
    dqn = dqr * cos_all - half_turn(dqr) * sin_all
    dkn = dkr * cos - half_turn(dkr) * sin
    q_unit, q_factor = unit_rows(heads_to_rows(q_ref[...], heads, size))
    k_unit, k_factor = unit_rows(k_ref[...])
    dq, term_query = norm_back(dqn, g_query, q_unit, q_factor)
    dk, term_key = norm_back(dkn, g_key, k_unit, k_factor)
    dq = rows_to_heads(dq.astype(BF16), heads, block)
    dk = dk.astype(BF16)
    dqkv_ref[:, : heads * size] = dq
    dqkv_ref[:, heads * size : (heads + 1) * size] = dk
    dqkv_ref[:, (heads + 1) * size :] = dv
    if layer == 0:
        late[0].start()
    at(DQKV)
    for load in loads[1:]:
        load.wait()
    part[...] = dot_nt(dq, wq_s[...]) + dot_nt(dk, wk_s[...]) + dot_nt(dv, wv_s[...])
    total = reduce_rows(t, nt, rows, part, outgoing, came, s_sem, r_sem, at)
    at(REDUCED)
    x_copy.wait()
    unit, factor = unit_rows(x_s[...].astype(F32))
    back, term_attn = norm_back(total, g_attn, unit, factor)
    dx = (dh1_ref[...] + back).astype(BF16)
    terms_ref[...] = jnp.zeros_like(terms_ref)
    write_terms(terms_ref, 0, term_moe[...])
    write_terms(terms_ref, 8, term_attn)
    terms_ref[16:17, :size] = term_query
    terms_ref[16:17, size : 2 * size] = term_key
    at(TERMS)
    if layer == 1:
        dx_ref[...] = dx
    else:
        late[2].start()
        whole[mine] = dx
        wait = spread_rows(t, nt, rows, whole, gs_sem, gr_sem)
        wait()
        late[1].start()
        late[2].arrive()

        def total_of(ref):
            out = ref[0, 0]
            for section in range(2):
                for origin in range(nz):
                    if section or origin:
                        out = out + ref[section, origin]
            return out

        @pl.when(s == 0)
        def _():
            copy = pltpu.make_async_copy(late[2].out, terms_in, t_sem.at[0])
            copy.start()
            copy.wait()

        @pl.when(s != 0)
        def _():
            copy = pltpu.make_async_copy(terms_other, terms_in, t_sem.at[0])
            copy.start()
            copy.wait()

        terms_near[0] = total_of(terms_in)

        def near(j):
            return remote(
                terms_near.at[0],
                terms_near.at[j],
                near_send.at[j],
                near_recv.at[j],
                tensor=partner(t, jnp.int32(j), nt),
            )

        for j in range(1, nt):
            near(j).start()
        sums = terms_near[0]
        for j in range(1, nt):
            near(j).wait_recv()
            sums = sums + terms_near[j]
        for j in range(1, nt):
            near(j).wait_send()
        terms_out[...] = sums
        at(TAIL)
        late[0].finish()
        late[1].finish()
        late[2].leave()
        dx_ref[...] = dx
    at(END)


def expert_grads_kernel(nz, step, ins, outs, scratch):
    s = lax.axis_index(SECTION)
    own, near = (ins[0:5], ins[5:10]), (ins[10:15], ins[15:20])
    left, right, stage, in_sem, out_sem = scratch

    def loads(layer):
        out = []
        for i in range(5):
            target = left.at[i] if i < 3 else right.at[i - 3]
            out.append(
                (
                    pltpu.make_async_copy(own[layer][i], target.at[pl.ds(0, nz)], in_sem.at[i, 0]),
                    pltpu.make_async_copy(near[layer][i], target.at[pl.ds(nz, nz)], in_sem.at[i, 1]),
                )
            )
        return out

    order = (3, 0, 1, 4, 2)
    for layer in range(2):

        @pl.when(s == layer)
        def _():
            copies = loads(layer)
            for i in order:
                for copy in copies[i]:
                    copy.start()

    waits = loads(0)
    width = right.shape[-1]
    tokens = 2 * nz * right.shape[2]
    cols = left.shape[-1]
    done = set()

    def need(i):
        if i not in done:
            for copy in waits[i]:
                copy.wait()
            done.add(i)

    turn = 0
    for i, r in ((0, 0), (1, 0), (2, 1)):
        need(3 + r)
        need(i)
        for c in range(0, cols, step):
            slot = turn % 2
            if turn >= 2:
                pltpu.make_async_copy(stage.at[slot], outs[0].at[pl.ds(0, step)], out_sem.at[slot]).wait()
            lhs = left[i, :, :, c : c + step].reshape(tokens, step)
            stage[slot] = dot_tn(lhs, right[r].reshape(tokens, width))
            pltpu.make_async_copy(stage.at[slot], outs[i].at[pl.ds(c, step)], out_sem.at[slot]).start()
            turn += 1
    for slot in range(2):
        pltpu.make_async_copy(stage.at[slot], outs[0].at[pl.ds(0, step)], out_sem.at[slot]).wait()


def attend_grads_kernel(q_cols, size, ins, outs, scratch):
    s = lax.axis_index(SECTION)
    spaces, sems = scratch[:4], scratch[4]
    a_s, o_s, t_s, d_s = spaces

    def loads(layer):
        refs = ins[4 * layer : 4 * layer + 4]
        return [pltpu.make_async_copy(r, d, sems.at[i]) for i, (r, d) in enumerate(zip(refs, spaces))]

    for layer in range(2):

        @pl.when(s == layer)
        def _():
            for load in loads(layer):
                load.start()

    waits = loads(0)

    def flat(ref):
        return ref[...].reshape(-1, ref.shape[-1])

    waits[0].wait()
    waits[3].wait()
    grad = dot_tn(flat(a_s), flat(d_s))
    outs[0][...] = grad[:, :q_cols]
    outs[1][...] = grad[:, q_cols : q_cols + size]
    outs[2][...] = grad[:, q_cols + size :]
    waits[1].wait()
    waits[2].wait()
    outs[3][...] = dot_tn(flat(o_s), flat(t_s))


def shape_of(shape, dtype):
    return jax.ShapeDtypeStruct(tuple(shape), dtype)


def like(value, lead=()):
    return shape_of(tuple(lead) + tuple(value.shape), value.dtype)


def call(body, name, number, ins, outs, scratch):
    def kernel(*refs):
        body(refs[: len(ins)], refs[len(ins) : len(ins) + len(outs)], refs[len(ins) + len(outs) :])

    return pl.pallas_call(
        kernel,
        out_shape=tuple(shape_of(o.shape, o.dtype) for o, _ in outs),
        in_specs=[spec for _, spec in ins],
        out_specs=tuple(spec for _, spec in outs),
        scratch_shapes=list(scratch),
        compiler_params=pltpu.CompilerParams(
            collective_id=number, has_side_effects=number is not None, vmem_limit_bytes=VMEM_LIMIT
        ),
        name=name,
    )(*[value for value, _ in ins])


class Slot:
    def __init__(self, shape):
        self.shape, self.dtype, self.value = tuple(shape.shape), shape.dtype, None


class At:
    def __init__(self, stage, plan, moves):
        self.stage, self.plan, self.moves = stage, plan, moves

    def __call__(self, point):
        for name, act in self.plan.get((self.stage, point), ()):
            act(self.moves[name])


USUAL = {
    SECOND: None,
    LOOPED: 1, OUT: 1, DQKV: 1,
    COLLECTED: 2, REDUCED: 2,
    SPREAD: 3, TERMS: 3,
}


class Group:
    def __init__(self, name, number, fused):
        self.name, self.number, self.fused = name, number, fused
        self.stages, self.moves, self.plan = [], {}, {}

    def stage(self, name, body, ins, outs, scratch):
        slots = [Slot(shape) for shape, _ in outs]
        self.stages.append((name, body, ins, list(zip(slots, [spec for _, spec in outs])), scratch))
        return slots

    def move(self, name, stage, move, ins, outs, plan, start=BEGIN, manual=False):
        slots = [Slot(shape) for shape in outs]
        self.moves[name] = (stage, move, ins, [(slot, ANY) for slot in slots])
        if not self.fused:
            plan = []
            if not manual:
                plan = [(stage, start, lambda m: m.start()), (stage, END, lambda m: m.finish())]
                for point, turn in USUAL.items():
                    if turn:
                        plan.append((stage, point, lambda m, turn=turn: m.poll(turn)))
        for at_stage, point, act in plan:
            self.plan.setdefault((at_stage, point), []).append((name, act))
        return slots

    def run(self):
        if self.fused:
            self.launch(self.name, self.number, self.stages, list(self.moves))
            return
        for i, stage in enumerate(self.stages):
            names = [name for name, entry in self.moves.items() if entry[0] == stage[0]]
            self.launch(self.name + str(i), self.number + i, [stage], names)

    def launch(self, name, number, stages, names):
        moves = [self.moves[n] for n in names]
        outs = [pair for stage in stages for pair in stage[3]] + [p for m in moves for p in m[3]]
        out_at = {id(slot): i for i, (slot, _) in enumerate(outs)}
        ins, in_at, scratch, scratch_at = [], {}, [], {}

        def place(pairs):
            where = []
            for value, spec in pairs:
                if id(value) in out_at:
                    where.append((True, out_at[id(value)]))
                    continue
                key = (id(value), id(spec))
                if key not in in_at:
                    in_at[key] = len(ins)
                    ins.append((value.value if isinstance(value, Slot) else value, spec))
                where.append((False, in_at[key]))
            return where

        def reserve(items):
            where = []
            for item in items:
                key, space = item if isinstance(item, tuple) else (None, item)
                if key is not None and key in scratch_at:
                    where.append(scratch_at[key])
                    continue
                scratch.append(space)
                where.append(len(scratch) - 1)
                if key is not None:
                    scratch_at[key] = len(scratch) - 1
            return where

        stage_at = [(place(st[2]), [out_at[id(o)] for o, _ in st[3]], reserve(st[4])) for st in stages]
        move_at = [
            (place(m[2]), [out_at[id(o)] for o, _ in m[3]], reserve(m[1].scratch())) for m in moves
        ]

        def body(in_refs, out_refs, scratch_refs):
            def pick(places):
                where, results, spaces = places
                refs = [(out_refs if made else in_refs)[i] for made, i in where]
                return refs, [out_refs[i] for i in results], [scratch_refs[i] for i in spaces]

            bound = {n: m[1].bind(*pick(at)) for n, m, at in zip(names, moves, move_at)}
            for i, stage in enumerate(stages):
                hello = greet if i == 0 else lambda peers: None
                stage[1](hello, At(stage[0], self.plan, bound), *pick(stage_at[i]))

        results = call(body, name, number, ins, outs, scratch)
        for (slot, _), value in zip(outs, results):
            slot.value = value


def vm(*values):
    return [(value, VM) for value in values]


def any_place(*values):
    return [(value, ANY) for value in values]


def on_device(
    boundary, seq_lengths, expert_ids, route_weights, attn_gain, moe_gain, query_gain, key_norm_gain,
    w_query, key_weight, value_weight, w_output, w_gate, w_up, w_down,
):
    nz, nt = lax.axis_size("expert"), lax.axis_size("tensor")
    micro, block, width = boundary.shape[1:]
    size = query_gain.shape[1]
    heads = w_query.shape[2] // size
    local_experts = w_gate.shape[1]
    hidden = local_experts * w_gate.shape[2]
    experts = local_experts * nz
    rows = block // nt
    q_cols = heads * size
    assert micro == 2 and key_weight.shape[2] == size == block and experts <= LANES
    dma = pltpu.SemaphoreType.DMA

    wg, wu, wd = (w[0].reshape(hidden, width) for w in (w_gate, w_up, w_down))
    wq, wk, wv, wo = w_query[0], key_weight[0], value_weight[0], w_output[0]
    gains = jnp.concatenate([attn_gain, moe_gain, query_gain, key_norm_gain], axis=1)

    def attend_spaces(own):
        return [
            (SHARED_WQ, pltpu.VMEM((width, q_cols), BF16)),
            (SHARED_WK, pltpu.VMEM((width, size), BF16)),
            (SHARED_WV, pltpu.VMEM((width, size), BF16)),
            (SHARED_WO, pltpu.VMEM((q_cols, width), BF16)),
            (SHARED_PART, pltpu.VMEM((block, width), F32)),
            pltpu.VMEM((block, width), BF16),
            pltpu.VMEM((nt, rows, width), BF16),
            dma((nt,)),
            dma((nt,)),
        ]

    gathered = [
        shape_of((width, q_cols), BF16),
        shape_of((width, size), BF16),
        shape_of((width, size), BF16),
        shape_of((q_cols, width), BF16),
    ]
    attend_outs = vm(
        shape_of((rows, width), F32),
        shape_of((rows, width), BF16),
        shape_of((block, width), BF16),
        shape_of((block, q_cols), F32),
        shape_of((block, size), F32),
        shape_of((block, size), BF16),
        shape_of((heads * block, size), BF16),
        shape_of((block, size), BF16),
        shape_of((block, q_cols), BF16),
    )
    expert_scratch = [(SHARED_WG, pltpu.VMEM((hidden, width), BF16)), (SHARED_WU, pltpu.VMEM((hidden, width), BF16))]
    expert_scratch += [(SHARED_WD, pltpu.VMEM((hidden, width), BF16))]
    hid_scratch = [(n, pltpu.VMEM((nz, block, hidden), BF16)) for n in (SHARED_HID, SHARED_DG, SHARED_DU)]
    all_tokens = shape_of((nz, block, width), BF16)
    all_hidden = shape_of((nz, block, hidden), BF16)
    cols = width // nz
    sliced = [shape_of((2, nz, block, cols), BF16), shape_of((2, nz, rows, cols), BF16)]

    def start(move):
        move.start()

    def finish(move):
        move.finish()

    def poll(turn):
        return lambda move: move.poll(turn)

    def steps(arrays, k):
        return lambda move: [move.step(a, k) for a in arrays]

    def begins(*arrays):
        return lambda move: [move.begin(a) for a in arrays]

    def settles(*arrays):
        return lambda move: [move.settle(a) for a in arrays]

    def ends_of(move):
        for a in range(4):
            move.end(a)

    fused = nz <= 4
    fore = Group("forward", 0, fused)
    relay = Relay(0, (0, 0, 0, 1), nz)
    started = fore.stage(
        ATTEND_0,
        functools.partial(start_attend_kernel, nz, nt, heads, relay),
        [(seq_lengths[0, :, 0], SM)]
        + vm(expert_ids[0], route_weights[0])
        + any_place(boundary[0], gains, wq, wk, wv, wo, wg, wu, wd),
        any_place(
            shape_of((2, block, width), BF16),
            shape_of((2, 3, block, size), F32),
            shape_of((2, nz, block, LANES), F32),
            like(gains, (2,)),
            *gathered,
            *[shape_of((hidden, width), BF16)] * 3,
        )
        + attend_outs,
        [
            pltpu.VMEM((block, width), BF16),
            pltpu.VMEM((3, block, size), F32),
            pltpu.VMEM(gains.shape, F32),
            pltpu.VMEM((2, 3, block, size), F32),
            pltpu.VMEM((2, block, LANES), F32),
            dma((4,)), dma((3,)), dma((5,)), dma((6,)), dma((6,)), dma((2, nz)), dma((2, nz)),
        ]
        + relay.scratch(4)
        + attend_spaces(0),
    )
    edges, tabs_all, gates_all, gains_all = started[:4]
    weights_0 = started[4:8]
    expert_weights = (wg, wu, wd) + tuple(started[8:11])
    h1_0, b_0, a_0, q_0, k_0, v_0, qr_0, kr_0, o_0 = started[11:]

    x_1, ball_0, gp_0, up_0 = fore.stage(
        EXPERTS_0,
        functools.partial(experts_kernel, 0, nz, nt, local_experts),
        vm(b_0, h1_0) + any_place(gates_all, *expert_weights),
        vm(shape_of((block, width), BF16))
        + any_place(
            all_tokens,
            shape_of((nz, block, hidden), F32),
            shape_of((nz, block, hidden), F32),
        ),
        expert_scratch
        + [pltpu.VMEM((nz, block, hidden), F32)] * 2
        + [pltpu.VMEM((nz, block, LANES), F32), dma((4,)), dma((3,))]
        + exchange_scratch(nz, nt, rows, block, width),
    )

    weights_1 = fore.move(
        MOVE_WEIGHTS_1, EXPERTS_0, Relay(1, (0, 0, 0, 1), nz), any_place(wq, wk, wv, wo), gathered,
        [
            (ATTEND_0, SHARDS, begins(0, 1, 2)),
            (ATTEND_0, SENT, steps((0, 1, 2), 1)),
            (ATTEND_0, SENT, begins(3)),
            (EXPERTS_0, ARRIVED, steps((0, 1, 2), 2)),
            (EXPERTS_0, ARRIVED, steps((3,), 1)),
            (EXPERTS_0, LOOPED, steps((0, 1, 2), 3)),
            (EXPERTS_0, LOOPED, steps((3,), 2)),
            (ATTEND_1, QKV, settles(0, 1, 2)),
            (ATTEND_1, OUT, steps((3,), 3)),
            (ATTEND_1, OUT, settles(3)),
            (ATTEND_1, END, ends_of),
        ],
    )

    (dy_rows,) = fore.move(
        MOVE_DY_ROWS, ATTEND_0, RowsFar(1, nz, nt), any_place(edges), [shape_of((nz, rows, width), BF16)],
        [(ATTEND_0, TABLES, start), (ATTEND_0, QKV, finish)],
        SHARDS,
    )
    (dyall_1,) = fore.move(
        MOVE_DY_ALL, EXPERTS_0, Spread(nz, nt), any_place(dy_rows), [all_tokens],
        [(ATTEND_0, QKV, start), (ATTEND_0, SHARDS, poll(1)), (EXPERTS_0, END, finish)],
    )

    h1_1, b_1, a_1, q_1, k_1, v_1, qr_1, kr_1, o_1 = fore.stage(
        ATTEND_1,
        functools.partial(attend_kernel, 1, nz, nt, heads),
        vm(x_1) + any_place(tabs_all, gains_all, *weights_1),
        attend_outs,
        [dma((6,)), pltpu.VMEM((3, block, size), F32), pltpu.VMEM(gains.shape, F32)] + attend_spaces(1),
    )
    fore.run()

    back = Group("backward", 8, fused)
    dy_1 = lax.dynamic_slice_in_dim(edges.value[1], lax.axis_index(TENSOR) * rows, rows, 0)
    dat_1, dh1_1, tm_1, ball_1, yparts_1, hid_1, dg_1, du_1 = back.stage(
        BOTH_1,
        functools.partial(experts_both_kernel, 1, nz, nt, local_experts),
        vm(b_1, h1_1, dy_1, gains_all) + any_place(gates_all, dyall_1, *expert_weights),
        vm(
            shape_of((block, width), BF16),
            shape_of((rows, width), F32),
            shape_of((1, width), F32),
        )
        + any_place(all_tokens, all_tokens, all_hidden, all_hidden, all_hidden),
        expert_scratch
        + [pltpu.VMEM((2, block, width), BF16)] * 2
        + hid_scratch
        + [dma((4,)), dma((2,)), dma((2,)), dma((4,)), (SHARED_GATES, pltpu.VMEM((nz, block, LANES), F32))]
        + exchange_scratch(nz, nt, rows, block, width),
    )

    def attend_back(layer, x, source, dat, dh1, term_moe, kept, weights, others=None):
        outs = vm(
            shape_of((rows, width), BF16),
            shape_of((block, q_cols + 2 * size), BF16),
            shape_of((TERM_ROWS, TERM_COLS), F32),
        )
        scratch = attend_spaces(layer) + [dma((5,)), dma((nt,)), dma((nt,))]
        scratch += [pltpu.VMEM((rows, width), BF16)]
        ins = any_place(x) + vm(tabs_all, gains_all, dat, dh1, term_moe, *kept) + any_place(*weights)
        if others is not None:
            outs += vm(shape_of((TERM_ROWS, TERM_COLS), F32))
            scratch += [
                pltpu.VMEM((block, width), BF16),
                pltpu.VMEM((nt, TERM_ROWS, TERM_COLS), F32),
                pltpu.VMEM((2, nz, TERM_ROWS, TERM_COLS), F32),
                dma((1,)),
                dma((nt,)),
                dma((nt,)),
            ]
            ins += any_place(others)
        return back.stage(
            ATTEND_BACK_1 if layer else ATTEND_BACK_0,
            functools.partial(attend_back_kernel, layer, source, nz, nt, heads),
            ins,
            outs,
            scratch,
        )

    last = (ATTEND_BACK_0, END, finish)
    kept_1, kept_0 = (q_1, k_1, v_1, qr_1, kr_1), (q_0, k_0, v_0, qr_0, kr_0)
    dx_1, dqkv_1, terms_1 = attend_back(1, x_1, None, dat_1, dh1_1, tm_1, kept_1, weights_1)
    dat_0, dh1_0, tm_0, dyall_0, hid_0, dg_0, du_0 = back.stage(
        EXPERTS_BACK_0,
        functools.partial(experts_back_kernel, 0, nz, nt, local_experts),
        vm(dx_1, h1_0, gains_all) + any_place(gates_all, gp_0, up_0, *expert_weights),
        vm(
            shape_of((block, width), BF16),
            shape_of((rows, width), F32),
            shape_of((1, width), F32),
        )
        + any_place(all_tokens, all_hidden, all_hidden, all_hidden),
        expert_scratch
        + [pltpu.VMEM((2, block, hidden), F32)] * 2
        + hid_scratch
        + [dma((4,)), dma((2,)), dma((2,)), dma((4,)), (SHARED_GATES, pltpu.VMEM((nz, block, LANES), F32))]
        + exchange_scratch(nz, nt, rows, block, width),
    )

    def gather(name, stage, layer, value, begin, end=last):
        return back.move(
            name, stage, Gather(layer, nz), any_place(value), [like(value, (2, nz))],
            [begin + (start,), end], begin[1],
        )

    def line(name, stage, layer, value, begin, *points):
        plan = [begin + (start,)]
        plan += [point + (steps((0,), k + 1),) for k, point in enumerate(points)]
        plan += [(ATTEND_BACK_0, END, settles(0)), (ATTEND_BACK_0, END, lambda m: m.end(0))]
        return back.move(
            name, stage, Line(layer, nz), any_place(value), [like(value, (2, nz))], plan, begin[1]
        )

    def near(name, stage, layer, value):
        return back.move(
            name, stage, Near(layer), any_place(value), [like(value)], [(stage, BEGIN, start), last]
        )

    def columns(name, stage, layer, value, begin, middle):
        return back.move(
            name, stage, Slice(layer, nz, nt), any_place(value), sliced,
            [begin + (start,), middle + (poll(1),), last], begin[1] if begin[0] == stage else BEGIN,
        )

    (bnear_0,) = near(MOVE_B_0, BOTH_1, 0, ball_0)
    (oall_0,) = gather(MOVE_O_0, BOTH_1, 0, o_0, (BOTH_1, ARRIVED))
    aall_0, _ = columns(
        MOVE_A_0, BOTH_1, 0, a_0, (ATTEND_BACK_1, BEGIN), (EXPERTS_BACK_0, BEGIN)
    )
    aall_1, _ = columns(
        MOVE_A_1, BOTH_1, 1, a_1, (ATTEND_BACK_1, BEGIN), (EXPERTS_BACK_0, BEGIN)
    )
    (oall_1,) = gather(MOVE_O_1, ATTEND_BACK_1, 1, o_1, (ATTEND_BACK_1, BEGIN))
    near_1 = [
        near(NEAR_1 + i, ATTEND_BACK_1, 1, value)[0]
        for i, value in enumerate((dg_1, du_1, hid_1, ball_1, dyall_1))
    ]
    datall_1, _ = columns(
        MOVE_DAT_1, ATTEND_BACK_1, 1, dat_1, (BOTH_1, SPREAD), (ATTEND_BACK_1, DQKV)
    )
    (ysums_1,) = back.move(
        MOVE_Y_NEAR, ATTEND_BACK_1, SumNear(nz, nt, rows, block, width), any_place(yparts_1),
        [shape_of((nz, rows, width), BF16)],
        [
            (ATTEND_BACK_1, BEGIN, start),
            (EXPERTS_BACK_0, BEGIN, poll(1)),
            (EXPERTS_BACK_0, LOOPED, poll(2)),
            (EXPERTS_BACK_0, COLLECTED, finish),
        ],
    )
    (dqkvall_1,) = gather(MOVE_DQKV_1, EXPERTS_BACK_0, 1, dqkv_1, (EXPERTS_BACK_0, ARRIVED))
    (termsall_1,) = gather(
        MOVE_TERMS_1, EXPERTS_BACK_0, 1, terms_1, (EXPERTS_BACK_0, BEGIN),
        (ATTEND_BACK_0, BEGIN, finish),
    )
    (yrows_1,) = back.move(
        MOVE_Y_FAR, EXPERTS_BACK_0, SumFar(nz, rows, width), any_place(ysums_1) + vm(h1_1),
        [shape_of((rows, width), BF16)],
        [
            (EXPERTS_BACK_0, SPREAD, start),
            (ATTEND_BACK_0, SENT, poll(2)),
            (ATTEND_BACK_0, SENT, finish),
        ],
    )
    _, dqkv_0, terms_0, terms = attend_back(
        0, edges, 0, dat_0, dh1_0, tm_0, kept_0, weights_0, termsall_1
    )
    datall_0, _ = columns(
        MOVE_DAT_0, ATTEND_BACK_0, 0, dat_0, (EXPERTS_BACK_0, SPREAD), (ATTEND_BACK_0, DQKV)
    )
    near_0 = [bnear_0] + [
        near(NEAR_0 + i, ATTEND_BACK_0, 0, value)[0]
        for i, value in enumerate((dyall_0, dg_0, du_0, hid_0))
    ]
    (ends_1,) = back.move(
        MOVE_Y_SPREAD, ATTEND_BACK_0, SpreadNear(1, nt, block, width), any_place(yrows_1),
        [shape_of((2, block, width), BF16)],
        [(ATTEND_BACK_0, TERMS, start), (ATTEND_BACK_0, TAIL, poll(1)), last],
    )
    hand = [(MOVE_DQKV_0, Gather(0, nz), like(dqkv_0, (2, nz)))]
    hand += [(MOVE_DX_0, Near(0, True), shape_of((2, block, width), BF16))]
    hand += [(MOVE_TERMS_0, Gather(0, nz), like(terms_0, (2, nz)))]
    dqkvall_0, ends_0, _ = (
        back.move(name, ATTEND_BACK_0, move, [], [shape], [], manual=True)[0]
        for name, move, shape in hand
    )
    back.run()

    step = 256
    flat = shape_of((hidden, width), F32)
    grad_gate, grad_up, grad_down = call(
        functools.partial(expert_grads_kernel, nz, step),
        "expert_grads",
        None,
        any_place(
            *(
                slot.value
                for slot in (
                    dg_0, du_0, hid_0, ball_0, dyall_0,
                    dg_1, du_1, hid_1, ball_1, dyall_1,
                    *near_0[2:], *near_0[:2],
                    *near_1,
                )
            )
        ),
        any_place(flat, flat, flat),
        [
            pltpu.VMEM((3, 2 * nz, block, hidden), BF16),
            pltpu.VMEM((2, 2 * nz, block, width), BF16),
            pltpu.VMEM((2, step, width), F32),
            dma((5, 2)),
            dma((2,)),
        ],
    )
    operands = (aall_0, oall_0, datall_0, dqkvall_0, aall_1, oall_1, datall_1, dqkvall_1)
    operands = tuple(slot.value for slot in operands)
    terms = terms.value
    grad_query, grad_key, grad_value, grad_output = call(
        functools.partial(attend_grads_kernel, q_cols, size),
        "attend_grads",
        None,
        any_place(*operands),
        vm(
            shape_of(wq.shape, F32),
            shape_of(wk.shape, F32),
            shape_of(wv.shape, F32),
            shape_of(wo.shape, F32),
        ),
        [pltpu.VMEM(o.shape, o.dtype) for o in operands[:4]] + [dma((4,))],
    )
    ends = jnp.where(lax.axis_index(SECTION) == 0, ends_0.value, ends_1.value)
    return (
        ends[None],
        terms[8:16].reshape(1, width),
        terms[:8].reshape(1, width),
        terms[16:17, :size],
        terms[16:17, size : 2 * size],
        grad_query[None],
        grad_key[None],
        grad_value[None],
        grad_output[None],
        grad_gate.reshape(w_gate.shape),
        grad_up.reshape(w_gate.shape),
        grad_down.reshape(w_gate.shape),
    )


def solution(mesh):
    return jax.shard_map(
        on_device,
        mesh=mesh,
        in_specs=(
            P(SECTION, None, EXPERT, None),
            P(SECTION, None, EXPERT, None),
            P(SECTION, None, EXPERT, None),
            P(SECTION, None, EXPERT, None),
            P(SECTION, None),
            P(SECTION, None),
            P(SECTION, None),
            P(SECTION, None),
            P(SECTION, EXPERT, TENSOR),
            P(SECTION, EXPERT, TENSOR),
            P(SECTION, EXPERT, TENSOR),
            P(SECTION, TENSOR, EXPERT),
            P(SECTION, EXPERT, TENSOR, None),
            P(SECTION, EXPERT, TENSOR, None),
            P(SECTION, EXPERT, TENSOR, None),
        ),
        out_specs=(
            P(SECTION, None, EXPERT, None),
            P(SECTION, None),
            P(SECTION, None),
            P(SECTION, None),
            P(SECTION, None),
            P(SECTION, EXPERT, TENSOR),
            P(SECTION, EXPERT, TENSOR),
            P(SECTION, EXPERT, TENSOR),
            P(SECTION, TENSOR, EXPERT),
            P(SECTION, EXPERT, TENSOR, None),
            P(SECTION, EXPERT, TENSOR, None),
            P(SECTION, EXPERT, TENSOR, None),
        ),
        check_vma=False,
    )
```

```python
import functools
import math

import jax
import jax.numpy as jnp
from jax import lax
from jax.experimental import pallas as pl
from jax.experimental.pallas import tpu as pltpu
from jax.sharding import PartitionSpec as P

EPSILON = 1e-06
THETA = 1000000.0
LANES = 128
TERM_ROWS = 24
TERM_COLS = 256
MESH = pl.DeviceIdType.MESH
SECTION, EXPERT, TENSOR = "section", "expert", "tensor"
F32 = jnp.float32
BF16 = jnp.bfloat16
VMEM_LIMIT = 62 * 1024 * 1024

ANY = pl.BlockSpec(memory_space=pl.ANY)
VM = pl.BlockSpec(memory_space=pltpu.VMEM)
SM = pl.BlockSpec(memory_space=pltpu.SMEM)

(
    BEGIN, END, SPREAD, ARRIVED, SECOND, LOOPED, COLLECTED, TABLES, QKV, SHARDS, SENT, OUT, REDUCED, DQKV, TERMS, TAIL,
) = range(0, 16)
(
    ATTEND_0, EXPERTS_0, ATTEND_1, BOTH_1, ATTEND_BACK_1, EXPERTS_BACK_0, ATTEND_BACK_0,
) = range(0, 7)
(
    MOVE_WEIGHTS_1, MOVE_DY_ROWS, MOVE_DY_ALL, MOVE_B_0, MOVE_O_0, MOVE_A_0, MOVE_A_1, MOVE_O_1, MOVE_DAT_1, MOVE_Y_NEAR, MOVE_DQKV_1, MOVE_TERMS_1, MOVE_Y_FAR, MOVE_DAT_0, MOVE_Y_SPREAD, MOVE_DQKV_0, MOVE_DX_0, MOVE_TERMS_0,
) = range(0, 18)
NEAR_0, NEAR_1 = 40, 50
(
    SHARED_PART, SHARED_OWN, SHARED_GATES, SHARED_WG, SHARED_WU, SHARED_WD, SHARED_WQ, SHARED_WK, SHARED_WV, SHARED_WO, SHARED_HID, SHARED_DG, SHARED_DU,
) = range(0, 13)


def partner(index, k, count):
    out, bit = 0, 1
    while bit < count:
        out = out + bit * lax.rem(lax.div(index, bit) + lax.div(k, bit), 2)
        bit *= 2
    return out


def rows_at(start, size):
    return pl.ds(pl.multiple_of(start, size), size)


def remote(src, dst, send_sem, recv_sem, **where):
    return pltpu.make_async_remote_copy(
        src_ref=src,
        dst_ref=dst,
        send_sem=send_sem,
        recv_sem=recv_sem,
        device_id=where,
        device_id_type=MESH,
    )


def greet(peers):
    barrier = pltpu.get_barrier_semaphore()
    for where in peers:
        pl.semaphore_signal(barrier, inc=1, device_id=where, device_id_type=MESH)
    pl.semaphore_wait(barrier, len(peers))


def layer_peers(z, t, nz, nt):
    i32 = jnp.int32
    peers = [{"expert": partner(z, i32(k), nz)} for k in range(1, nz)]
    peers += [{TENSOR: partner(t, i32(k), nt)} for k in range(1, nt)]
    return peers


def dot(a, b):
    return lax.dot_general(a, b, (((1,), (0,)), ((), ())), preferred_element_type=F32)


def dot_nt(a, b):
    return lax.dot_general(a, b, (((1,), (1,)), ((), ())), preferred_element_type=F32)


def dot_tn(a, b):
    return lax.dot_general(a, b, (((0,), (0,)), ((), ())), preferred_element_type=F32)


def unit_rows(value):
    factor = lax.rsqrt(jnp.mean(value * value, axis=-1, keepdims=True) + EPSILON)
    return value * factor, factor


def norm_back(grad, gain, unit, factor):
    weighted = grad * gain
    inner = jnp.mean(weighted * unit, axis=-1, keepdims=True)
    return factor * (weighted - unit * inner), jnp.sum(grad * unit, axis=0, keepdims=True)


def expert_gates(gate_rows, first_expert, local_experts, width):
    rows = gate_rows.shape[0]
    lane = lax.broadcasted_iota(jnp.int32, gate_rows.shape, 1)
    column = lax.broadcasted_iota(jnp.int32, (rows, local_experts * width), 1)
    out = None
    for e in range(local_experts):
        one = jnp.sum(jnp.where(lane == first_expert + e, gate_rows, 0.0), axis=1, keepdims=True)
        wide = jnp.broadcast_to(one, column.shape)
        out = wide if out is None else jnp.where(column >= e * width, wide, out)
    return out


def write_terms(terms_ref, row, vector):
    for i in range(vector.shape[1] // TERM_COLS):
        terms_ref[row + i : row + i + 1, :] = vector[:, i * TERM_COLS : (i + 1) * TERM_COLS]


class Square:
    def __init__(self, nz, nt, rows, width):
        assert nt == 4
        self.z, self.t = lax.axis_index(EXPERT), lax.axis_index(TENSOR)
        self.nz, self.rows = nz, rows
        half = width // 2
        self.half, self.first, self.second = half, pl.ds(0, half), pl.ds(half, half)
        near_x, near_y, across = (partner(self.t, jnp.int32(j), nt) for j in (1, 2, 3))
        self.near = (near_x, near_y)
        self.mine, self.x_rows, self.y_rows, self.across_rows = (
            self.window(i) for i in (self.t, near_x, near_y, across)
        )
        self.y_pair = rows_at(lax.div(near_y, 2) * (2 * rows), 2 * rows)
        in_pair = lax.rem(self.t, 2)
        self.pair_mine, self.pair_x = self.window(in_pair), self.window(1 - in_pair)

    def window(self, index):
        return rows_at(index * self.rows, self.rows)


class RowGather:
    @staticmethod
    def scratch(nz):
        return [pltpu.SemaphoreType.DMA((2, nz)), pltpu.SemaphoreType.DMA((4, nz, 2))]

    def __init__(self, square, full, sems):
        self.sq, self.full = square, full
        self.far_sem, self.row_sem = sems

    def far_copy(self, k, source, src=None):
        sq = self.sq
        spot = self.full.at[source, sq.mine]
        return remote(
            spot if src is None else src,
            spot,
            self.far_sem.at[0, k],
            self.far_sem.at[1, k],
            expert=partner(sq.z, jnp.int32(k), sq.nz),
        )

    def row_copy(self, k, source, j, window, src=None):
        spot = self.full.at[source, window]
        return remote(
            spot if src is None else src,
            spot,
            self.row_sem.at[0, k, j],
            self.row_sem.at[1, k, j],
            tensor=self.sq.near[j],
        )

    def on_copy(self, k, source, j, window):
        spot = self.full.at[source, window, (self.sq.second, self.sq.first)[j]]
        return remote(
            spot, spot, self.row_sem.at[2, k, j], self.row_sem.at[3, k, j], tensor=self.sq.near[j]
        )

    def send(self, k, source, src=None):
        for j in range(2):
            self.row_copy(k, source, j, self.sq.mine, src).start()

    def hand_on(self, k, source):
        self.row_copy(k, source, 0, self.sq.x_rows).wait_recv()
        self.on_copy(k, source, 1, self.sq.x_rows).start()
        self.row_copy(k, source, 1, self.sq.y_rows).wait_recv()
        self.on_copy(k, source, 0, self.sq.y_rows).start()

    def arrive(self, k, source):
        for j in range(2):
            self.on_copy(k, source, j, self.sq.across_rows).wait_recv()

    def leave(self, k, source):
        for j in range(2):
            self.row_copy(k, source, j, self.sq.mine).wait_send()
            self.on_copy(k, source, j, (self.sq.y_rows, self.sq.x_rows)[j]).wait_send()


class RowSum:
    @staticmethod
    def scratch(nz, rows, block, width):
        half = width // 2
        dma = pltpu.SemaphoreType.DMA
        return [
            pltpu.VMEM((nz, block, width), BF16),
            pltpu.VMEM((nz, 2 * rows, half), BF16),
            pltpu.VMEM((nz, 2, rows, half), BF16),
            pltpu.VMEM((nz, 2, rows, half), BF16),
            pltpu.VMEM((nz, 2, rows, half), BF16),
            pltpu.VMEM((nz, rows, width), BF16),
            pltpu.VMEM((nz, rows, width), BF16),
            pltpu.VMEM((rows, width), F32),
            dma((2, nz)),
            dma((6, nz, 2)),
        ]

    count = 10

    def __init__(self, square, scratch, own=None):
        self.sq, self.own = square, own
        (self.outgoing, self.from_y, self.from_x, self.pairs, self.came_pairs) = scratch[:5]
        (self.passed, self.came_far, self.total, self.far_sem, self.part_sem) = scratch[5:]

    def part_copy(self, k, i):
        sq = self.sq
        window, cols = ((sq.y_pair, sq.first), (sq.across_rows, sq.second), (sq.x_rows, sq.second))[i]
        dst = (self.from_y.at[k], self.from_x.at[k, 1], self.from_x.at[k, 0])[i]
        group, slot = ((0, 0), (2, 1), (2, 0))[i]
        return remote(
            self.outgoing.at[k, window, cols],
            dst,
            self.part_sem.at[group, k, slot],
            self.part_sem.at[group + 1, k, slot],
            tensor=sq.near[0] if i else sq.near[1],
        )

    def pair_copy(self, k, j):
        return remote(
            self.pairs.at[k, j],
            self.came_pairs.at[k, j],
            self.part_sem.at[4, k, j],
            self.part_sem.at[5, k, j],
            tensor=self.sq.near[j],
        )

    def sum_copy(self, k):
        return remote(
            self.passed.at[k],
            self.came_far.at[k],
            self.far_sem.at[0, k],
            self.far_sem.at[1, k],
            expert=partner(self.sq.z, k, self.sq.nz),
        )

    def send(self, k):
        for i in range(3):
            self.part_copy(k, i).start()

    def pair_up(self, k):
        sq = self.sq
        self.part_copy(k, 0).wait_recv()
        kept = self.outgoing[k, sq.x_rows, sq.first].astype(F32)
        self.pairs[k, 0] = (kept + self.from_y[k, sq.pair_x].astype(F32)).astype(BF16)
        self.pair_copy(k, 0).start()
        self.part_copy(k, 1).wait_recv()
        kept = self.outgoing[k, sq.y_rows, sq.second].astype(F32)
        self.pairs[k, 1] = (kept + self.from_x[k, 1].astype(F32)).astype(BF16)
        self.pair_copy(k, 1).start()

    def collect(self, k):
        sq = self.sq
        self.part_copy(k, 2).wait_recv()
        self.pair_copy(k, 0).wait_recv()
        self.pair_copy(k, 1).wait_recv()
        own = self.outgoing[k, sq.mine].astype(F32) if self.own is None else self.own[k]
        left = own[:, : sq.half] + self.from_y[k, sq.pair_mine].astype(F32)
        right = own[:, sq.half :] + self.from_x[k, 0].astype(F32)
        return (
            left + self.came_pairs[k, 0].astype(F32),
            right + self.came_pairs[k, 1].astype(F32),
        )

    def collect_own(self):
        left, right = self.collect(jnp.int32(0))
        self.total[:, : self.sq.half] = left
        self.total[:, self.sq.half :] = right

    def collect_far(self, k):
        left, right = self.collect(k)
        self.passed[k, :, self.sq.first] = left.astype(BF16)
        self.passed[k, :, self.sq.second] = right.astype(BF16)
        self.sum_copy(k).start()

    def add_far(self):
        for k in range(1, self.sq.nz):
            self.sum_copy(jnp.int32(k)).wait_recv()
            self.total[...] += self.came_far[k].astype(F32)

    def leave(self, far=True):
        for k in range(self.sq.nz):
            if k and far:
                self.sum_copy(jnp.int32(k)).wait_send()
            for j in range(2):
                self.pair_copy(k, j).wait_send()
            for i in range(3):
                self.part_copy(k, i).wait_send()


def exchange_scratch(nz, nt, rows, block, width):
    return (
        [
            pltpu.VMEM((nz, block, width), BF16),
            (SHARED_PART, pltpu.VMEM((block, width), F32)),
            (SHARED_OWN, pltpu.VMEM((nz, rows, width), F32)),
            pltpu.VMEM((block, width), BF16),
            pltpu.SemaphoreType.DMA((2, nt)),
        ]
        + RowGather.scratch(nz)
        + RowSum.scratch(nz, rows, block, width)
    )


EXCHANGE_SCRATCH = 7 + RowSum.count


def exchange(nz, nt, own_rows, scratch, ready, work, at):
    full, part, own_part = scratch[:3]
    sq = Square(nz, nt, own_rows.shape[0], full.shape[-1])
    z = sq.z
    gather = RowGather(sq, full, scratch[5:7])
    sums = RowSum(sq, scratch[7 : 7 + RowSum.count], own_part)
    i32 = jnp.int32

    def produce(k, source):
        gather.arrive(k, source)
        part[...] = work(k, source, full[source])
        sums.outgoing[k] = part[...].astype(BF16)
        sums.send(k)
        own_part[k] = part[sq.mine]

    full[z, sq.mine] = own_rows
    for k in range(1, nz):
        gather.far_copy(k, z).start()
    gather.send(0, z)
    at(BEGIN)
    ready()
    for k in range(1, nz):
        source = partner(z, i32(k), nz)
        gather.far_copy(k, source).wait_recv()
        gather.send(k, source)
        if k == 1:
            gather.hand_on(0, z)
    at(ARRIVED)
    gather.hand_on(1, partner(z, i32(1), nz))

    def step(k, carry):
        @pl.when(k + 1 < nz)
        def _():
            gather.hand_on(k + 1, partner(z, k + 1, nz))

        turn = lax.rem(k, nz)
        produce(turn, partner(z, turn, nz))

        @pl.when(k >= 2)
        def _():
            sums.pair_up(k - 1)

        @pl.when(k >= 3)
        def _():
            sums.collect_far(k - 2)

        @pl.when(k == 2)
        def _():
            at(SECOND)

        return carry

    lax.fori_loop(1, nz + 1, step, 0)
    at(LOOPED)
    sums.collect_far(i32(nz - 1))
    sums.pair_up(i32(0))
    sums.collect_own()
    at(COLLECTED)
    sums.add_far()

    def finish():
        for k in range(nz):
            source = partner(z, i32(k), nz)
            if k:
                gather.far_copy(k, z).wait_send()
            gather.leave(k, source)
        sums.leave()

    return sums.total, finish


def spread_rows(t, nt, rows, block_ref, send_sem, recv_sem):
    i32 = jnp.int32
    mine = rows_at(t * rows, rows)
    for j in range(1, nt):
        remote(
            block_ref.at[mine],
            block_ref.at[mine],
            send_sem.at[j],
            recv_sem.at[j],
            tensor=partner(t, i32(j), nt),
        ).start()

    def wait():
        for j in range(1, nt):
            peer = partner(t, i32(j), nt)
            theirs = rows_at(peer * rows, rows)
            copy = remote(
                block_ref.at[theirs],
                block_ref.at[theirs],
                send_sem.at[j],
                recv_sem.at[j],
                tensor=peer,
            )
            copy.wait_send()
            copy.wait_recv()

    return wait


def reduce_rows(t, nt, rows, part, outgoing, came, send_sem, recv_sem, at):
    i32 = jnp.int32
    outgoing[...] = part[...].astype(BF16)

    def copy(j):
        peer = partner(t, i32(j), nt)
        return remote(
            outgoing.at[rows_at(peer * rows, rows)],
            came.at[j],
            send_sem.at[j],
            recv_sem.at[j],
            tensor=peer,
        )

    for j in range(1, nt):
        copy(j).start()
    at(SENT)
    total = part[rows_at(t * rows, rows)]
    for j in range(1, nt):
        copy(j).wait_recv()
        total = total + came[j].astype(F32)
    for j in range(1, nt):
        copy(j).wait_send()
    return total


def all_peers(s, z, t, nz, nt):
    i32 = jnp.int32
    peers = [{SECTION: 1 - s}]
    for k in range(1, nz):
        zz = partner(z, i32(k), nz)
        peers += [{EXPERT: zz}, {SECTION: 1 - s, EXPERT: zz}]
    return peers + [{TENSOR: partner(t, i32(j), nt)} for j in range(1, nt)]


class Relay:
    def __init__(self, layer, spots, nz):
        self.layer, self.spots, self.nz = layer, spots, nz

    def scratch(self, count=4):
        dma = pltpu.SemaphoreType.DMA
        return [dma((count,))] + [dma((count, self.nz))] * 6

    def bind(self, shards, outs, sems):
        self.s, self.z = lax.axis_index(SECTION), lax.axis_index(EXPERT)
        self.shards, self.outs, self.sems = shards, outs, sems
        self.source = self.hands = self.s == self.layer
        self.count = len(shards)
        return self

    def place(self, a, owner):
        dim = self.spots[a]
        size = self.shards[a].shape[dim]
        window = rows_at(owner * size, size)
        return self.outs[a].at[window] if dim == 0 else self.outs[a].at[:, window]

    def home(self, a):
        return pltpu.make_async_copy(self.shards[a], self.place(a, self.z), self.sems[0].at[a])

    def hop(self, a, owner, step, right, own=False):
        spot = self.place(a, owner)
        send, recv = self.sems[1:3] if right else self.sems[3:5]
        return remote(
            self.shards[a] if own else spot,
            spot,
            send.at[a, step],
            recv.at[a, step],
            expert=self.z + 1 if right else self.z - 1,
        )

    def hand(self, a, owner, own=False):
        spot = self.place(a, owner)
        return remote(
            self.shards[a] if own else spot,
            spot,
            self.sems[5].at[a, owner],
            self.sems[6].at[a, owner],
            section=1 - self.s,
        )

    def begin_side(self, a, right):
        @pl.when(self.source & ((self.z + 1 < self.nz) if right else (self.z >= 1)))
        def _():
            self.hop(a, self.z, 1, right, True).start()

    def begin_home(self, a):
        @pl.when(self.source)
        def _():
            self.home(a).start()

        @pl.when(self.hands)
        def _():
            self.hand(a, self.z, True).start()

    def begin(self, a):
        self.begin_side(a, True)
        self.begin_side(a, False)
        self.begin_home(a)

    def step(self, a, k):
        z, nz = self.z, self.nz

        @pl.when(self.source & (z >= k))
        def _():
            self.hop(a, z - k, k, True).wait_recv()

            @pl.when(z + 1 < nz)
            def _():
                self.hop(a, z - k, k + 1, True).start()

            @pl.when(self.hands)
            def _():
                self.hand(a, z - k).start()

        @pl.when(self.source & (z + k < nz))
        def _():
            self.hop(a, z + k, k, False).wait_recv()

            @pl.when(z >= 1)
            def _():
                self.hop(a, z + k, k + 1, False).start()

            @pl.when(self.hands)
            def _():
                self.hand(a, z + k).start()

    def settle(self, a):
        @pl.when(self.source)
        def _():
            self.home(a).wait()

        @pl.when(jnp.logical_not(self.source))
        def _():
            for owner in range(self.nz):
                self.hand(a, owner).wait_recv()

    def end(self, a):
        z, nz = self.z, self.nz

        @pl.when(self.hands)
        def _():
            for owner in range(nz):
                self.hand(a, owner).wait_send()

        @pl.when(self.source)
        def _():
            for step in range(1, nz):

                @pl.when((z >= step - 1) & (z + 1 < nz))
                def _():
                    self.hop(a, z - (step - 1), step, True).wait_send()

                @pl.when((z + step - 1 < nz) & (z >= 1))
                def _():
                    self.hop(a, z + (step - 1), step, False).wait_send()

    def start(self):
        for a in range(self.count):
            self.begin(a)

    def poll(self, turn):
        if turn < min(3, self.nz - 1):
            for a in range(self.count):
                self.step(a, turn)

    def finish(self):
        for k in range(min(3, self.nz - 1), self.nz):
            for a in range(self.count):
                self.step(a, k)
        for a in range(self.count):
            self.settle(a)
            self.end(a)


class Line(Relay):
    def __init__(self, layer, nz):
        super().__init__(layer, None, nz)

    def scratch(self):
        return super().scratch(1)

    def bind(self, ins, outs, sems):
        super().bind(ins, outs, sems)
        self.source, self.hands = self.s >= 0, self.s != self.layer
        return self

    def place(self, a, owner, section=None):
        return self.outs[a].at[self.s if section is None else section, owner]

    def settle(self, a):
        self.home(a).wait()

        @pl.when(self.s == self.layer)
        def _():
            for owner in range(self.nz):
                spot = self.place(a, owner, 1 - self.layer)
                remote(
                    spot, spot, self.sems[5].at[a, owner], self.sems[6].at[a, owner], section=1 - self.s
                ).wait_recv()


class Slice:
    def __init__(self, layer, nz, nt):
        self.layer, self.nz, self.nt = layer, nz, nt

    def scratch(self):
        dma = pltpu.SemaphoreType.DMA
        return [dma((2,)), dma((self.nz,)), dma((2, self.nz)), dma((2, self.nt))]

    def bind(self, ins, outs, sems):
        self.s, self.z, self.t = (lax.axis_index(a) for a in (SECTION, EXPERT, TENSOR))
        self.src, (self.out, self.rows_out), self.sems = ins[0], outs, sems
        rows, self.cols = self.rows_out.shape[2:]
        self.rows = rows
        self.mine = rows_at(self.t * rows, rows)
        self.receives = self.s == self.layer
        return self

    def far(self, k, local, section=None, origin=None):
        zz = partner(self.z, jnp.int32(k), self.nz)
        src = self.src.at[self.mine, rows_at(zz * self.cols, self.cols)]
        section = self.s if section is None else section
        spot = self.rows_out.at[section, self.z if origin is None else origin]
        if local:
            return pltpu.make_async_copy(src, spot, self.sems[0].at[0])
        return remote(
            src,
            spot,
            self.sems[1].at[k],
            self.sems[2].at[section, k],
            section=jnp.int32(self.layer),
            expert=zz,
        )

    def near(self, j, window):
        return remote(
            self.rows_out,
            self.out.at[:, :, window],
            self.sems[3].at[0, j],
            self.sems[3].at[1, j],
            tensor=partner(self.t, jnp.int32(j), self.nt),
        )

    def home(self):
        return pltpu.make_async_copy(self.rows_out, self.out.at[:, :, self.mine], self.sems[0].at[1])

    def start(self):
        for k in range(1, self.nz):
            self.far(k, False).start()

        @pl.when(self.receives)
        def _():
            self.far(0, True).start()

        @pl.when(jnp.logical_not(self.receives))
        def _():
            self.far(0, False).start()

    def poll(self, turn):
        if turn != 1:
            return

        @pl.when(self.receives)
        def _():
            self.far(0, True).wait()
            for section in range(2):
                for k in range(self.nz):
                    if k or section != self.layer:
                        zz = partner(self.z, jnp.int32(k), self.nz)
                        self.far(k, False, section, zz).wait_recv()
            self.home().start()
            for j in range(1, self.nt):
                self.near(j, self.mine).start()

    def finish(self):
        for k in range(1, self.nz):
            self.far(k, False).wait_send()

        @pl.when(jnp.logical_not(self.receives))
        def _():
            self.far(0, False).wait_send()

        @pl.when(self.receives)
        def _():
            self.home().wait()
            for j in range(1, self.nt):
                theirs = partner(self.t, jnp.int32(j), self.nt) * self.rows
                self.near(j, rows_at(theirs, self.rows)).wait_recv()
                self.near(j, self.mine).wait_send()


class Gather:
    def __init__(self, layer, nz):
        self.layer, self.nz = layer, nz

    def scratch(self):
        dma = pltpu.SemaphoreType.DMA
        return [dma((1,)), dma((self.nz,)), dma((2, self.nz))]

    def bind(self, ins, outs, sems):
        self.s, self.z = lax.axis_index(SECTION), lax.axis_index(EXPERT)
        self.src, self.out, self.sems = (ins or (None,))[0], outs[0], sems
        return self

    def copy(self, k, local, section=None, origin=None):
        zz = partner(self.z, jnp.int32(k), self.nz)
        src = self.src
        section = self.s if section is None else section
        spot = self.out.at[section, self.z if origin is None else origin]
        if local:
            return pltpu.make_async_copy(src, spot, self.sems[0].at[0])
        return remote(
            src,
            spot,
            self.sems[1].at[k],
            self.sems[2].at[section, k],
            section=jnp.int32(self.layer),
            expert=zz,
        )

    def start(self):
        for k in range(1, self.nz):
            self.copy(k, False).start()

        @pl.when(self.s == self.layer)
        def _():
            self.copy(0, True).start()

        @pl.when(self.s != self.layer)
        def _():
            self.copy(0, False).start()

    def poll(self, turn):
        pass

    def arrive(self):
        @pl.when(self.s == self.layer)
        def _():
            self.copy(0, True).wait()
            for section in range(2):
                for k in range(self.nz):
                    if k or section != self.layer:
                        zz = partner(self.z, jnp.int32(k), self.nz)
                        self.copy(k, False, section, zz).wait_recv()

    def leave(self):
        for k in range(1, self.nz):
            self.copy(k, False).wait_send()

        @pl.when(self.s != self.layer)
        def _():
            self.copy(0, False).wait_send()

    def finish(self):
        self.arrive()
        self.leave()


class Near:
    def __init__(self, layer, both=False):
        self.layer, self.both = layer, both

    def scratch(self):
        dma = pltpu.SemaphoreType.DMA
        return [dma((1,)), dma((1,)), dma((1,))]

    def bind(self, ins, outs, sems):
        self.s, self.sems = lax.axis_index(SECTION), sems
        self.src, self.out = (ins or (None,))[0], outs[0]
        return self

    def local(self):
        return pltpu.make_async_copy(self.src, self.out.at[self.layer], self.sems[0].at[0])

    def copy(self):
        return remote(
            self.src,
            self.out.at[1 - self.layer] if self.both else self.out,
            self.sems[1].at[0],
            self.sems[2].at[0],
            section=jnp.int32(self.layer),
        )

    def start(self):
        if self.both:

            @pl.when(self.s == self.layer)
            def _():
                self.local().start()

        @pl.when(self.s != self.layer)
        def _():
            self.copy().start()

    def poll(self, turn):
        pass

    def finish(self):
        @pl.when(self.s == self.layer)
        def _():
            if self.both:
                self.local().wait()
            remote(
                self.src,
                self.out.at[1 - self.layer] if self.both else self.out,
                self.sems[1].at[0],
                self.sems[2].at[0],
                section=1 - self.s,
            ).wait_recv()

        @pl.when(self.s != self.layer)
        def _():
            self.copy().wait_send()


class RowsFar:
    def __init__(self, slot, nz, nt):
        self.slot, self.nz, self.nt = slot, nz, nt

    def scratch(self):
        return [pltpu.SemaphoreType.DMA((1,)), pltpu.SemaphoreType.DMA((2, self.nz))]

    def bind(self, ins, outs, sems):
        self.z, self.t = lax.axis_index(EXPERT), lax.axis_index(TENSOR)
        self.src, self.out, self.sems = ins[0], outs[0], sems
        return self

    def copy(self, k, origin):
        rows = self.out.shape[1]
        src = self.src.at[self.slot, rows_at(self.t * rows, rows)]
        if k == 0:
            return pltpu.make_async_copy(src, self.out.at[origin], self.sems[0].at[0])
        return remote(
            src,
            self.out.at[origin],
            self.sems[1].at[0, k],
            self.sems[1].at[1, k],
            expert=partner(self.z, jnp.int32(k), self.nz),
        )

    def start(self):
        for k in range(self.nz):
            self.copy(k, self.z).start()

    def poll(self, turn):
        pass

    def finish(self):
        self.copy(0, self.z).wait()
        for k in range(1, self.nz):
            self.copy(k, self.z).wait_send()
            self.copy(k, partner(self.z, jnp.int32(k), self.nz)).wait_recv()


class Spread:
    def __init__(self, nz, nt):
        self.nz, self.nt = nz, nt

    def scratch(self):
        return [pltpu.SemaphoreType.DMA((1,))] + RowGather.scratch(self.nz)

    def bind(self, ins, outs, sems):
        self.src, self.out, self.sems = ins[0], outs[0], sems
        self.sq = Square(self.nz, self.nt, *self.src.shape[1:])
        self.gather = RowGather(self.sq, self.out, sems[1:])
        return self

    def local(self):
        return pltpu.make_async_copy(self.src, self.out.at[:, self.sq.mine], self.sems[0].at[0])

    def start(self):
        self.local().start()
        for k in range(self.nz):
            self.gather.send(k, k, self.src.at[k])

    def poll(self, turn):
        if turn == 1:
            for k in range(self.nz):
                self.gather.hand_on(k, k)

    def finish(self):
        self.local().wait()
        for k in range(self.nz):
            self.gather.arrive(k, k)
            self.gather.leave(k, k)


class SumNear:
    def __init__(self, nz, nt, rows, block, width):
        self.nz, self.nt = nz, nt
        self.shape = rows, block, width

    def scratch(self):
        rows, block, width = self.shape
        half = width // 2
        return [
            pltpu.SemaphoreType.DMA((2,)),
            pltpu.SemaphoreType.DMA((2, 5)),
            pltpu.VMEM((self.nz, block, width), BF16),
            pltpu.VMEM((self.nz, 2 * rows, half), BF16),
            pltpu.VMEM((2, self.nz, rows, half), BF16),
            pltpu.VMEM((2, self.nz, rows, half), BF16),
            pltpu.VMEM((2, self.nz, rows, half), BF16),
            pltpu.VMEM((self.nz, rows, width), BF16),
        ]

    def bind(self, ins, outs, scratch):
        self.src, self.out = ins[0], outs[0]
        self.sems, self.sem = scratch[:2]
        self.parts, self.from_y, self.from_x, self.pairs, self.came, self.result = scratch[2:]
        self.sq = Square(self.nz, self.nt, self.shape[0], self.shape[2])
        return self

    def load(self):
        return pltpu.make_async_copy(self.src, self.parts, self.sems.at[0])

    def save(self):
        return pltpu.make_async_copy(self.result, self.out, self.sems.at[1])

    def copy(self, i):
        sq = self.sq
        if i < 3:
            window, cols = ((sq.y_pair, sq.first), (sq.across_rows, sq.second), (sq.x_rows, sq.second))[i]
            src = self.src.at[:, window, cols]
            dst = (self.from_y, self.from_x.at[1], self.from_x.at[0])[i]
        else:
            src, dst = self.pairs.at[i - 3], self.came.at[i - 3]
        peer = sq.near[(1, 0, 0, 0, 1)[i]]
        return remote(src, dst, self.sem.at[0, i], self.sem.at[1, i], tensor=peer)

    def start(self):
        self.load().start()
        for i in range(3):
            self.copy(i).start()

    def poll(self, turn):
        sq = self.sq
        if turn == 1:
            self.load().wait()
            self.copy(0).wait_recv()
            kept = self.parts[:, sq.x_rows, sq.first].astype(F32)
            self.pairs[0] = (kept + self.from_y[:, sq.pair_x].astype(F32)).astype(BF16)
            self.copy(3).start()
            self.copy(1).wait_recv()
            kept = self.parts[:, sq.y_rows, sq.second].astype(F32)
            self.pairs[1] = (kept + self.from_x[1].astype(F32)).astype(BF16)
            self.copy(4).start()
        if turn == 2:
            for i in (2, 3, 4):
                self.copy(i).wait_recv()
            left = self.parts[:, sq.mine, sq.first].astype(F32)
            left = left + self.from_y[:, sq.pair_mine].astype(F32) + self.came[0].astype(F32)
            right = self.parts[:, sq.mine, sq.second].astype(F32)
            right = right + self.from_x[0].astype(F32) + self.came[1].astype(F32)
            self.result[:, :, sq.first] = left.astype(BF16)
            self.result[:, :, sq.second] = right.astype(BF16)
            self.save().start()

    def finish(self):
        self.save().wait()
        for i in range(5):
            self.copy(i).wait_send()


class SumFar:
    def __init__(self, nz, rows, width):
        self.nz, self.shape = nz, (rows, width)

    def scratch(self):
        dma = pltpu.SemaphoreType.DMA
        return [
            pltpu.VMEM((self.nz,) + self.shape, BF16),
            pltpu.VMEM(self.shape, BF16),
            dma((2,)),
            dma((2, self.nz)),
        ]

    def bind(self, ins, outs, scratch):
        self.z = lax.axis_index(EXPERT)
        self.src, self.rows_ref = ins
        self.out = outs[0]
        self.came, self.result, self.sems, self.far_sem = scratch
        return self

    def copy(self, k):
        if k == 0:
            return pltpu.make_async_copy(self.src.at[0], self.came.at[0], self.sems.at[0])
        return remote(
            self.src.at[k],
            self.came.at[k],
            self.far_sem.at[0, k],
            self.far_sem.at[1, k],
            expert=partner(self.z, jnp.int32(k), self.nz),
        )

    def save(self):
        return pltpu.make_async_copy(self.result, self.out, self.sems.at[1])

    def start(self):
        for k in range(self.nz):
            self.copy(k).start()

    def poll(self, turn):
        if turn == 2:
            self.copy(0).wait()
            total = self.rows_ref[...] + self.came[0].astype(F32)
            for k in range(1, self.nz):
                self.copy(k).wait_recv()
                total = total + self.came[k].astype(F32)
            self.result[...] = total.astype(BF16)
            self.save().start()

    def finish(self):
        self.save().wait()
        for k in range(1, self.nz):
            self.copy(k).wait_send()


class SpreadNear:
    def __init__(self, layer, nt, block, width):
        self.nt, self.shape, self.near = nt, (block, width), Near(layer, True)

    def scratch(self):
        dma = pltpu.SemaphoreType.DMA
        return [pltpu.VMEM(self.shape, BF16), dma((1,)), dma((2, self.nt))] + self.near.scratch()

    def bind(self, ins, outs, scratch):
        self.t = lax.axis_index(TENSOR)
        self.src = ins[0]
        self.whole, self.load_sem, self.spread_sem = scratch[:3]
        self.near.bind([self.whole], outs, scratch[3:])
        self.rows = self.src.shape[0]
        return self

    def start(self):
        load = pltpu.make_async_copy(
            self.src, self.whole.at[rows_at(self.t * self.rows, self.rows)], self.load_sem.at[0]
        )
        load.start()
        load.wait()
        self.wait = spread_rows(
            self.t, self.nt, self.rows, self.whole, self.spread_sem.at[0], self.spread_sem.at[1]
        )

    def poll(self, turn):
        if turn == 1:
            self.wait()
            self.near.start()

    def finish(self):
        self.near.finish()


def heads_to_rows(value, heads, size):
    return jnp.concatenate([value[:, h * size : (h + 1) * size] for h in range(heads)], axis=0)


def rows_to_heads(value, heads, block):
    return jnp.concatenate([value[h * block : (h + 1) * block] for h in range(heads)], axis=1)


def split_gains(row, width, size):
    return (
        row[:, :width],
        row[:, width : 2 * width],
        row[:, 2 * width : 2 * width + size],
        row[:, 2 * width + size :],
    )


def tiled(value, times):
    return jnp.concatenate([value] * times, axis=0)


def half_turn(value):
    return pltpu.roll(value, value.shape[-1] // 2, value.ndim - 1)


def attend_body(t, nt, heads, x_ref, tables, gains, outs, scratch, wait_qkv, wait_out, at):
    (h1_ref, b_ref, a_ref, q_ref, k_ref, v_ref, qr_ref, kr_ref, o_ref) = outs
    (wq_s, wk_s, wv_s, wo_s, part, outgoing, came, s_sem, r_sem) = scratch
    block, width = x_ref.shape
    rows = block // nt
    cos, sin, bias = tables
    size = cos.shape[-1]
    g_attn, g_moe, g_query, g_key = split_gains(gains, width, size)
    unit, _ = unit_rows(x_ref[...].astype(F32))
    a_ref[...] = (unit * g_attn).astype(BF16)
    wait_qkv()
    q = dot(a_ref[...], wq_s[...])
    q_ref[...] = q
    k = dot(a_ref[...], wk_s[...])
    k_ref[...] = k
    v = dot(a_ref[...], wv_s[...]).astype(BF16)
    v_ref[...] = v
    qn = unit_rows(heads_to_rows(q, heads, size))[0] * g_query
    kn = unit_rows(k)[0] * g_key
    qr = (qn * tiled(cos, heads) + half_turn(qn) * tiled(sin, heads)).astype(BF16)
    kr = (kn * cos + half_turn(kn) * sin).astype(BF16)
    qr_ref[...] = qr
    kr_ref[...] = kr
    scores = dot_nt(qr, kr) * (1.0 / math.sqrt(size)) + tiled(bias, heads)
    peak = jnp.max(scores, axis=-1, keepdims=True)
    weight = jnp.exp(scores - peak)
    probs = weight * (1.0 / jnp.sum(weight, axis=-1, keepdims=True))
    o = dot(probs.astype(BF16), v).astype(BF16)
    o_ref[...] = rows_to_heads(o, heads, block)
    wait_out()
    part[...] = dot(o_ref[...], wo_s[...])
    total = reduce_rows(t, nt, rows, part, outgoing, came, s_sem, r_sem, at)
    h1 = x_ref[rows_at(t * rows, rows)].astype(F32) + total
    h1_ref[...] = h1
    b_ref[...] = (unit_rows(h1)[0] * g_moe).astype(BF16)


def fill_tables(tabs, lengths, m):
    block, size = tabs.shape[2:]
    row = lax.broadcasted_iota(jnp.int32, (block, size), 0)
    lane = lax.broadcasted_iota(jnp.int32, (block, size), 1)
    begin, segment, segment_of_lane = (jnp.zeros((block, size), jnp.int32) for _ in range(3))
    end = jnp.int32(0)
    for n in range(lengths.shape[1]):
        end = end + lengths[m, n]
        begin = jnp.where(row >= end, end, begin)
        segment = segment + jnp.where(row >= end, 1, 0)
        segment_of_lane = segment_of_lane + jnp.where(lane >= end, 1, 0)
    half = size // 2
    position = jnp.where(lane >= half, lane - half, lane).astype(F32)
    inverse = jnp.exp(position * (-2.0 * math.log(THETA) / size))
    angle = (row - begin).astype(F32) * inverse
    sin = jnp.sin(angle)
    tabs[m, 0] = jnp.cos(angle)
    tabs[m, 1] = jnp.where(lane >= half, sin, -sin)
    tabs[m, 2] = jnp.where((lane <= row) & (segment == segment_of_lane), 0.0, -1e30)


def fill_gates(gates, ids, route_weights, m):
    expert_of, weight_of = ids[m], route_weights[m]
    lane = lax.broadcasted_iota(jnp.int32, gates.shape[1:], 1)
    out = jnp.zeros(gates.shape[1:], F32)
    for c in range(expert_of.shape[1]):
        out = out + jnp.where(lane == expert_of[:, c : c + 1], weight_of[:, c : c + 1], 0.0)
    gates[m] = out


def start_attend_kernel(nz, nt, heads, relay, hello, at, ins, outs, scratch):
    s, z, t = lax.axis_index(SECTION), lax.axis_index(EXPERT), lax.axis_index(TENSOR)
    lengths, ids, route_weights, g_attn, g_moe, g_query, g_key, boundary, wq, wk, wv, wo, wg, wu, wd = ins
    edges, tabs_out, gates_out, gains_out = outs[:4]
    gathered, (sg, su, sd), results = outs[4:8], outs[8:11], outs[11:]
    x_s, tabs_s, gains_s, gains, tabs, gates = scratch[:6]
    w_sem, in_sem, own_sem, sib_send, sib_recv, gate_send, gate_recv = scratch[6:13]
    relay.bind((wq, wk, wv, wo), gathered, scratch[13:20])
    attn_scratch = scratch[20:]
    column = 0
    for gain in (g_attn, g_moe, g_query, g_key):
        gains[:, column : column + gain.shape[1]] = gain[...]
        column += gain.shape[1]
    other = 1 - s
    i32 = jnp.int32

    own = [
        pltpu.make_async_copy(boundary.at[s], edges.at[s], own_sem.at[0]),
        pltpu.make_async_copy(tabs.at[s], tabs_out.at[s], own_sem.at[1]),
        pltpu.make_async_copy(gains, gains_out.at[s], own_sem.at[2]),
        pltpu.make_async_copy(gates.at[s], gates_out.at[s, z], own_sem.at[3]),
    ]
    own[0].start()
    own[2].start()
    hello(all_peers(s, z, t, nz, nt))

    def sibling(i, src, dst):
        return remote(src, dst, sib_send.at[i], sib_recv.at[i], section=other)

    pairs = [
        (boundary.at[other], edges.at[s], edges.at[other]),
        (tabs.at[other], tabs_out.at[s], tabs_out.at[other]),
        (gains, gains_out.at[s], gains_out.at[other]),
        (wg, sg, sg),
        (wu, su, su),
        (wd, sd, sd),
    ]
    for i in (0, 2):
        sibling(i, *pairs[i][:2]).start()
    for a in range(3):
        relay.begin(a)
    relay.begin_home(3)

    def gate_copy(d, k, arrival=False):
        zz = partner(z, i32(k), nz)
        section = s if d == 0 else other
        return remote(
            gates.at[section],
            gates_out.at[section, zz] if arrival else gates_out.at[s, z],
            gate_send.at[d, k],
            gate_recv.at[d, k],
            section=section,
            expert=zz,
        )

    for m in range(2):
        fill_tables(tabs, lengths, m)
    sibling(1, *pairs[1][:2]).start()
    own[1].start()
    for m in range(2):
        fill_gates(gates, ids, route_weights, m)
    own[3].start()
    turns = [(d, k) for d in range(2) for k in range(nz) if d or k]
    for d, k in turns:
        gate_copy(d, k).start()
    for i in range(3, 6):
        sibling(i, *pairs[i][:2]).start()

    for copy in own:
        copy.wait()
    for i in range(3):
        sibling(i, pairs[i][0], pairs[i][2]).wait_recv()
    at(TABLES)
    loads = [
        pltpu.make_async_copy(edges.at[0], x_s, in_sem.at[0]),
        pltpu.make_async_copy(tabs_out.at[0], tabs_s, in_sem.at[1]),
        pltpu.make_async_copy(gains_out.at[0], gains_s, in_sem.at[2]),
    ]
    for load in loads:
        load.start()
    for load in loads:
        load.wait()

    def bring(a):
        return pltpu.make_async_copy(gathered[a], attn_scratch[a], w_sem.at[a])

    def wait_qkv():
        for k in range(1, nz):
            for a in range(3):
                relay.step(a, k)

            @pl.when((z == k) | ((z == 0) & (k == 1)))
            def _():
                relay.begin_side(3, True)

            @pl.when((z == nz - 1 - k) | ((z == nz - 1) & (k == 1)))
            def _():
                relay.begin_side(3, False)

        for a in range(3):
            relay.settle(a)
            bring(a).start()
        for a in range(3):
            bring(a).wait()
        at(QKV)

    def wait_out():
        for k in range(1, nz):
            relay.step(3, k)
        at(SHARDS)
        relay.settle(3)
        bring(3).start()
        bring(3).wait()

    tables = (tabs_s[0], tabs_s[1], tabs_s[2])
    attend_body(t, nt, heads, x_s, tables, gains_s[...], results, attn_scratch, wait_qkv, wait_out, at)
    for i in range(6):
        sibling(i, *pairs[i][:2]).wait_send()
    for i in range(3, 6):
        sibling(i, pairs[i][0], pairs[i][2]).wait_recv()
    for d, k in turns:
        gate_copy(d, k).wait_send()
        gate_copy(d, k, True).wait_recv()
    for a in range(4):
        relay.end(a)
    at(END)


def attend_kernel(layer, nz, nt, heads, hello, at, ins, outs, scratch):
    s, z, t = lax.axis_index(SECTION), lax.axis_index(EXPERT), lax.axis_index(TENSOR)
    x_ref, tabs, gains, wq, wk, wv, wo = ins
    w_sem, tabs_s, gains_s, attn_scratch = scratch[0], scratch[1], scratch[2], scratch[3:]
    loads = [
        pltpu.make_async_copy(src, dst, w_sem.at[i])
        for i, (src, dst) in enumerate(zip((wq, wk, wv, wo), attn_scratch))
    ]
    small = [
        pltpu.make_async_copy(tabs.at[layer], tabs_s, w_sem.at[4]),
        pltpu.make_async_copy(gains.at[layer], gains_s, w_sem.at[5]),
    ]
    for load in small:
        load.start()
    hello(all_peers(s, z, t, nz, nt))
    at(BEGIN)
    for load in small:
        load.wait()

    def wait_qkv():
        at(QKV)
        for load in loads[:3]:
            load.start()
        for load in loads[:3]:
            load.wait()

    def wait_out():
        at(OUT)
        loads[3].start()
        loads[3].wait()

    tables = (tabs_s[0], tabs_s[1], tabs_s[2])
    attend_body(t, nt, heads, x_ref, tables, gains_s[...], outs, attn_scratch, wait_qkv, wait_out, at)
    at(END)


def load_experts(layer, s, own, sibling, scratch, sems):
    def copies(refs):
        return [pltpu.make_async_copy(r, d, sems.at[i]) for i, (r, d) in enumerate(zip(refs, scratch))]

    @pl.when(s == layer)
    def _():
        for copy in copies(own):
            copy.start()

    @pl.when(s != layer)
    def _():
        for copy in copies(sibling):
            copy.start()

    return copies(own)


def experts_kernel(layer, nz, nt, local_experts, hello, at, ins, outs, scratch):
    s, z, t = lax.axis_index(SECTION), lax.axis_index(EXPERT), lax.axis_index(TENSOR)
    b_ref, h1_ref, gates, wg, wu, wd, sg, su, sd = ins
    y_ref, b_out, g_out, u_out = outs
    wg_s, wu_s, wd_s, g_s, u_s, gates_s, w_sem, o_sem = scratch[:8]
    spaces = scratch[8:]
    rows = b_ref.shape[0]
    loads = load_experts(layer, s, (wg, wu, wd), (sg, su, sd), (wg_s, wu_s, wd_s), w_sem)
    loads.append(pltpu.make_async_copy(gates.at[layer], gates_s, w_sem.at[3]))
    loads[3].start()
    hello(all_peers(s, z, t, nz, nt))
    width = wg.shape[0] // local_experts

    def ready():
        for load in loads:
            load.wait()

    def work(k, origin, rows_in):
        gate_pre = dot_nt(rows_in, wg_s[...])
        up_pre = dot_nt(rows_in, wu_s[...])
        g_s[origin] = gate_pre
        u_s[origin] = up_pre
        weight = expert_gates(gates_s[origin], z * local_experts, local_experts, width)
        hidden = (gate_pre * jax.nn.sigmoid(gate_pre) * up_pre * weight).astype(BF16)
        return dot(hidden, wd_s[...])

    total, finish = exchange(nz, nt, b_ref[...], spaces, ready, work, at)
    full, whole, spread_sem = spaces[0], spaces[3], spaces[4]
    saves = [
        pltpu.make_async_copy(full, b_out, o_sem.at[0]),
        pltpu.make_async_copy(g_s, g_out, o_sem.at[1]),
        pltpu.make_async_copy(u_s, u_out, o_sem.at[2]),
    ]
    for save in saves:
        save.start()
    whole[rows_at(t * rows, rows)] = (h1_ref[...] + total[...]).astype(BF16)
    wait = spread_rows(t, nt, rows, whole, spread_sem.at[0], spread_sem.at[1])
    at(SPREAD)
    finish()
    wait()
    y_ref[...] = whole[...]
    for save in saves:
        save.wait()
    at(END)


def experts_back_kernel(layer, nz, nt, local_experts, hello, at, ins, outs, scratch):
    s, z, t = lax.axis_index(SECTION), lax.axis_index(EXPERT), lax.axis_index(TENSOR)
    dy_ref, h1_ref, gains, gates, g_in, u_in, wg, wu, wd, sg, su, sd = ins
    dat_ref, dh1_ref, term_ref, dy_out, hid_out, dg_out, du_out = outs
    wg_s, wu_s, wd_s, g_s, u_s, hid_s, dg_s, du_s, w_sem, g_sem, u_sem, o_sem = scratch[:12]
    gates_s, scratch = scratch[12], scratch[:12] + scratch[13:]
    spaces = scratch[12:]
    rows, model_width = dy_ref.shape
    loads = load_experts(layer, s, (wd, wg, wu), (sd, sg, su), (wd_s, wg_s, wu_s), w_sem)
    loads.append(pltpu.make_async_copy(gates.at[layer], gates_s, w_sem.at[3]))
    loads[3].start()

    def kept(k):
        origin, slot = partner(z, lax.rem(k + 1, nz), nz), lax.rem(k, 2)
        return (
            pltpu.make_async_copy(g_in.at[origin], g_s.at[slot], g_sem.at[slot]),
            pltpu.make_async_copy(u_in.at[origin], u_s.at[slot], u_sem.at[slot]),
        )

    for load in kept(jnp.int32(0)):
        load.start()
    hello(all_peers(s, z, t, nz, nt))
    width = wg.shape[0] // local_experts

    def ready():
        for load in loads:
            load.wait()

    def work(k, origin, rows_in):
        turn = lax.rem(k + nz - 1, nz)
        for load in kept(turn):
            load.wait()

        @pl.when(turn + 1 < nz)
        def _():
            for load in kept(turn + 1):
                load.start()

        slot = lax.rem(turn, 2)
        gate_pre, up_pre = g_s[slot], u_s[slot]
        weight = expert_gates(gates_s[origin], z * local_experts, local_experts, width)
        sigmoid = jax.nn.sigmoid(gate_pre)
        silu = gate_pre * sigmoid
        hid_s[origin] = (silu * up_pre * weight).astype(BF16)
        grad_hidden = dot_nt(rows_in, wd_s[...]) * weight
        dg_s[origin] = (grad_hidden * up_pre * sigmoid * (1.0 + gate_pre * (1.0 - sigmoid))).astype(BF16)
        du_s[origin] = (grad_hidden * silu).astype(BF16)
        return dot(dg_s[origin], wg_s[...]) + dot(du_s[origin], wu_s[...])

    total, finish = exchange(nz, nt, dy_ref[...], spaces, ready, work, at)
    full, whole, spread_sem = spaces[0], spaces[3], spaces[4]
    saves = [
        pltpu.make_async_copy(full, dy_out, o_sem.at[0]),
        pltpu.make_async_copy(hid_s, hid_out, o_sem.at[1]),
        pltpu.make_async_copy(dg_s, dg_out, o_sem.at[2]),
        pltpu.make_async_copy(du_s, du_out, o_sem.at[3]),
    ]
    for save in saves:
        save.start()
    unit, factor = unit_rows(h1_ref[...])
    g_moe = gains[layer, :, model_width : 2 * model_width]
    back, term = norm_back(total[...], g_moe, unit, factor)
    dh1 = dy_ref[...].astype(F32) + back
    dh1_ref[...] = dh1
    term_ref[...] = term
    mine = rows_at(t * rows, rows)
    whole[mine] = dh1.astype(BF16)
    dat_ref[mine] = dh1.astype(BF16)
    wait = spread_rows(t, nt, rows, whole, spread_sem.at[0], spread_sem.at[1])
    at(SPREAD)
    finish()
    wait()
    for j in range(1, nt):
        theirs = rows_at(partner(t, jnp.int32(j), nt) * rows, rows)
        dat_ref[theirs] = whole[theirs]
    for save in saves:
        save.wait()
    at(END)


def experts_both_kernel(layer, nz, nt, local_experts, hello, at, ins, outs, scratch):
    s, z, t = lax.axis_index(SECTION), lax.axis_index(EXPERT), lax.axis_index(TENSOR)
    b_ref, h1_ref, gains, edges, gates, dy_all, wg, wu, wd, sg, su, sd = ins
    dat_ref, dh1_ref, term_ref, b_out, y_out, hid_out, dg_out, du_out = outs
    wg_s, wu_s, wd_s, dy_s, y_s, hid_s, dg_s, du_s, w_sem, dy_sem, y_sem, o_sem = scratch[:12]
    gates_s, dy_ref, scratch = scratch[12], scratch[13], scratch[:12] + scratch[14:]
    spaces = scratch[12:]
    rows, model_width = b_ref.shape
    loads = load_experts(layer, s, (wg, wu, wd), (sg, su, sd), (wg_s, wu_s, wd_s), w_sem)
    loads.append(pltpu.make_async_copy(gates.at[layer], gates_s, w_sem.at[3]))
    loads[3].start()
    own_rows = edges.at[layer, rows_at(t * rows, rows)]
    loads.append(pltpu.make_async_copy(own_rows, dy_ref, w_sem.at[4]))
    loads[4].start()

    def cotangent(turn):
        origin, slot = partner(z, lax.rem(turn + 1, nz), nz), lax.rem(turn, 2)
        return pltpu.make_async_copy(dy_all.at[origin], dy_s.at[slot], dy_sem.at[slot])

    def store(turn):
        k, slot = lax.rem(turn + 1, nz), lax.rem(turn, 2)
        return pltpu.make_async_copy(y_s.at[slot], y_out.at[k], y_sem.at[slot])

    cotangent(jnp.int32(0)).start()
    hello(all_peers(s, z, t, nz, nt))
    width = wg.shape[0] // local_experts

    def ready():
        for load in loads:
            load.wait()

    def work(k, origin, rows_in):
        turn = lax.rem(k + nz - 1, nz)
        slot = lax.rem(turn, 2)
        cotangent(turn).wait()

        @pl.when(turn + 1 < nz)
        def _():
            cotangent(turn + 1).start()

        @pl.when(turn >= 2)
        def _():
            store(turn - 2).wait()

        gate_pre = dot_nt(rows_in, wg_s[...])
        up_pre = dot_nt(rows_in, wu_s[...])
        weight = expert_gates(gates_s[origin], z * local_experts, local_experts, width)
        sigmoid = jax.nn.sigmoid(gate_pre)
        silu = gate_pre * sigmoid
        hid_s[origin] = (silu * up_pre * weight).astype(BF16)
        grad_hidden = dot_nt(dy_s[slot], wd_s[...]) * weight
        dg_s[origin] = (grad_hidden * up_pre * sigmoid * (1.0 + gate_pre * (1.0 - sigmoid))).astype(BF16)
        du_s[origin] = (grad_hidden * silu).astype(BF16)
        y_s[slot] = dot(hid_s[origin], wd_s[...]).astype(BF16)
        store(turn).start()
        return dot(dg_s[origin], wg_s[...]) + dot(du_s[origin], wu_s[...])

    total, finish = exchange(nz, nt, b_ref[...], spaces, ready, work, at)
    full, whole, spread_sem = spaces[0], spaces[3], spaces[4]
    saves = [
        pltpu.make_async_copy(full, b_out, o_sem.at[0]),
        pltpu.make_async_copy(hid_s, hid_out, o_sem.at[1]),
        pltpu.make_async_copy(dg_s, dg_out, o_sem.at[2]),
        pltpu.make_async_copy(du_s, du_out, o_sem.at[3]),
    ]
    for save in saves:
        save.start()
    unit, factor = unit_rows(h1_ref[...])
    g_moe = gains[layer, :, model_width : 2 * model_width]
    back, term = norm_back(total[...], g_moe, unit, factor)
    dh1 = dy_ref[...].astype(F32) + back
    dh1_ref[...] = dh1
    term_ref[...] = term
    mine = rows_at(t * rows, rows)
    whole[mine] = dh1.astype(BF16)
    dat_ref[mine] = dh1.astype(BF16)
    wait = spread_rows(t, nt, rows, whole, spread_sem.at[0], spread_sem.at[1])
    at(SPREAD)
    finish()
    wait()
    for j in range(1, nt):
        theirs = rows_at(partner(t, jnp.int32(j), nt) * rows, rows)
        dat_ref[theirs] = whole[theirs]
    for save in saves:
        save.wait()
    store(jnp.int32(nz - 2)).wait()
    store(jnp.int32(nz - 1)).wait()
    at(END)


def attend_back_kernel(layer, source, nz, nt, heads, hello, at, ins, outs, scratch):
    s, z, t = lax.axis_index(SECTION), lax.axis_index(EXPERT), lax.axis_index(TENSOR)
    (x_ref, tabs, gains, dat_ref, dh1_ref, term_moe, q_ref, k_ref, v_ref, qr_ref, kr_ref) = ins[:11]
    wq, wk, wv, wo = ins[11:15]
    dx_ref, dqkv_ref, terms_ref = outs[:3]
    wq_s, wk_s, wv_s, wo_s, part, outgoing, came, s_sem, r_sem, w_sem, gs_sem, gr_sem = scratch[:12]
    x_s, scratch = scratch[12], scratch[13:]
    if layer == 0:
        whole, terms_near, terms_in, t_sem, near_send, near_recv = scratch
        terms_other, terms_out = ins[15], outs[3]
    block, model_width = dat_ref.shape
    rows = block // nt
    mine = rows_at(t * rows, rows)
    x_copy = pltpu.make_async_copy(
        x_ref.at[mine] if source is None else x_ref.at[source, mine], x_s, w_sem.at[4]
    )
    x_copy.start()
    loads = [
        pltpu.make_async_copy(src, dst, w_sem.at[i])
        for i, (src, dst) in enumerate(((wo, wo_s), (wq, wq_s), (wk, wk_s), (wv, wv_s)))
    ]
    for load in loads:
        load.start()
    hello(all_peers(s, z, t, nz, nt))
    if layer == 0:
        late = [at.moves[name] for name in (MOVE_DQKV_0, MOVE_DX_0, MOVE_TERMS_0)]
        late[0].src, late[1].src, late[2].src = dqkv_ref, whole, terms_ref
    at(BEGIN)

    size = tabs.shape[-1]
    g_attn, _, g_query, g_key = split_gains(gains[layer], model_width, size)
    scale = 1.0 / math.sqrt(size)
    cos, sin, bias = tabs[layer, 0], tabs[layer, 1], tabs[layer, 2]
    cos_all, sin_all = tiled(cos, heads), tiled(sin, heads)
    qr, kr, v = qr_ref[...], kr_ref[...], v_ref[...]
    scores = dot_nt(qr, kr) * scale + tiled(bias, heads)
    peak = jnp.max(scores, axis=-1, keepdims=True)
    weight = jnp.exp(scores - peak)
    probs = weight * (1.0 / jnp.sum(weight, axis=-1, keepdims=True))
    loads[0].wait()
    do = heads_to_rows(dot_nt(dat_ref[...], wo_s[...]).astype(BF16), heads, size)
    dv = dot_tn(probs.astype(BF16), do).astype(BF16)
    dp = dot_nt(do, v)
    ds = (probs * (dp - jnp.sum(probs * dp, axis=-1, keepdims=True))).astype(BF16)
    dqr = dot(ds, kr) * scale
    dkr = dot_tn(ds, qr) * scale
    dqn = dqr * cos_all - half_turn(dqr) * sin_all
    dkn = dkr * cos - half_turn(dkr) * sin
    q_unit, q_factor = unit_rows(heads_to_rows(q_ref[...], heads, size))
    k_unit, k_factor = unit_rows(k_ref[...])
    dq, term_query = norm_back(dqn, g_query, q_unit, q_factor)
    dk, term_key = norm_back(dkn, g_key, k_unit, k_factor)
    dq = rows_to_heads(dq.astype(BF16), heads, block)
    dk = dk.astype(BF16)
    dqkv_ref[:, : heads * size] = dq
    dqkv_ref[:, heads * size : (heads + 1) * size] = dk
    dqkv_ref[:, (heads + 1) * size :] = dv
    if layer == 0:
        late[0].start()
    at(DQKV)
    for load in loads[1:]:
        load.wait()
    part[...] = dot_nt(dq, wq_s[...]) + dot_nt(dk, wk_s[...]) + dot_nt(dv, wv_s[...])
    total = reduce_rows(t, nt, rows, part, outgoing, came, s_sem, r_sem, at)
    at(REDUCED)
    x_copy.wait()
    unit, factor = unit_rows(x_s[...].astype(F32))
    back, term_attn = norm_back(total, g_attn, unit, factor)
    dx = (dh1_ref[...] + back).astype(BF16)
    terms_ref[...] = jnp.zeros_like(terms_ref)
    write_terms(terms_ref, 0, term_moe[...])
    write_terms(terms_ref, 8, term_attn)
    terms_ref[16:17, :size] = term_query
    terms_ref[16:17, size : 2 * size] = term_key
    at(TERMS)
    if layer == 1:
        dx_ref[...] = dx
    else:
        late[2].start()
        whole[mine] = dx
        wait = spread_rows(t, nt, rows, whole, gs_sem, gr_sem)
        wait()
        late[1].start()
        late[2].arrive()

        def total_of(ref):
            out = ref[0, 0]
            for section in range(2):
                for origin in range(nz):
                    if section or origin:
                        out = out + ref[section, origin]
            return out

        @pl.when(s == 0)
        def _():
            copy = pltpu.make_async_copy(late[2].out, terms_in, t_sem.at[0])
            copy.start()
            copy.wait()

        @pl.when(s != 0)
        def _():
            copy = pltpu.make_async_copy(terms_other, terms_in, t_sem.at[0])
            copy.start()
            copy.wait()

        terms_near[0] = total_of(terms_in)

        def near(j):
            return remote(
                terms_near.at[0],
                terms_near.at[j],
                near_send.at[j],
                near_recv.at[j],
                tensor=partner(t, jnp.int32(j), nt),
            )

        for j in range(1, nt):
            near(j).start()
        sums = terms_near[0]
        for j in range(1, nt):
            near(j).wait_recv()
            sums = sums + terms_near[j]
        for j in range(1, nt):
            near(j).wait_send()
        terms_out[...] = sums
        at(TAIL)
        late[0].finish()
        late[1].finish()
        late[2].leave()
        dx_ref[...] = dx
    at(END)


class ExpertGrads:
    def __init__(self, nz, step):
        self.nz, self.step = nz, step

    def begin(self, ins, outs, scratch):
        s = lax.axis_index(SECTION)
        own, near = (ins[0:5], ins[5:10]), (ins[10:15], ins[15:20])
        left, right, _, in_sem, _ = scratch

        def loads(layer):
            out = []
            for i in range(5):
                target = left.at[i] if i < 3 else right.at[i - 3]
                for j, src in enumerate((own[layer][i], near[layer][i])):
                    half = target.at[pl.ds(j * self.nz, self.nz)]
                    out.append(pltpu.make_async_copy(src, half, in_sem.at[i, j]))
            return out

        for layer in range(2):

            @pl.when(s == layer)
            def _():
                copies = loads(layer)
                for i in (3, 0, 1, 4, 2):
                    copies[2 * i].start()
                    copies[2 * i + 1].start()

        self.waits, self.outs, self.scratch = loads(0), outs, scratch

    def work(self):
        left, right, stage, _, out_sem = self.scratch
        step, outs = self.step, self.outs
        width, cols = right.shape[-1], left.shape[-1]
        tokens = 2 * self.nz * right.shape[2]

        def need(i):
            self.waits[2 * i].wait()
            self.waits[2 * i + 1].wait()

        def stored(slot):
            return pltpu.make_async_copy(stage.at[slot], outs[0].at[pl.ds(0, step)], out_sem.at[slot])

        turn = 0
        for i, r in ((0, 0), (1, 0), (2, 1)):
            if i != 1:
                need(3 + r)
            need(i)
            for c in range(0, cols, step):
                slot = turn % 2
                if turn >= 2:
                    stored(slot).wait()
                lhs = left[i, :, :, c : c + step].reshape(tokens, step)
                stage[slot] = dot_tn(lhs, right[r].reshape(tokens, width))
                pltpu.make_async_copy(
                    stage.at[slot], outs[i].at[pl.ds(c, step)], out_sem.at[slot]
                ).start()
                turn += 1
        for slot in range(2):
            stored(slot).wait()


class AttendGrads:
    def __init__(self, width, q_cols, size):
        self.width, self.q_cols, self.size = width, q_cols, size

    def begin(self, ins, outs, scratch):
        s = lax.axis_index(SECTION)
        self.spaces, sems = scratch[:4], scratch[4]
        self.terms, self.outs = ins[10], outs

        def loads(layer):
            refs = ins[5 * layer : 5 * layer + 5]
            targets = list(self.spaces) + [outs[0]]
            return [
                pltpu.make_async_copy(r, d, sems.at[i]) for i, (r, d) in enumerate(zip(refs, targets))
            ]

        for layer in range(2):

            @pl.when(s == layer)
            def _():
                for load in loads(layer):
                    load.start()

        self.waits = loads(0)

    def work(self):
        (_, attn, moe, query, key, g_query, g_key, g_value, g_output) = self.outs
        terms, size, q_cols = self.terms, self.size, self.q_cols
        for i in range(self.width // TERM_COLS):
            cols = slice(i * TERM_COLS, (i + 1) * TERM_COLS)
            moe[:, cols] = terms[i : i + 1, :]
            attn[:, cols] = terms[8 + i : 9 + i, :]
        query[...] = terms[16:17, :size]
        key[...] = terms[16:17, size : 2 * size]
        for wait in self.waits:
            wait.wait()

        def flat(ref):
            return ref[...].reshape(-1, ref.shape[-1])

        a_s, o_s, t_s, d_s = self.spaces
        grad = dot_tn(flat(a_s), flat(d_s))
        g_query[...] = grad[:, :q_cols]
        g_key[...] = grad[:, q_cols : q_cols + size]
        g_value[...] = grad[:, q_cols + size :]
        g_output[...] = dot_tn(flat(o_s), flat(t_s))


def shape_of(shape, dtype):
    return jax.ShapeDtypeStruct(tuple(shape), dtype)


def like(value, lead=()):
    return shape_of(tuple(lead) + tuple(value.shape), value.dtype)


def call(body, name, number, ins, outs, scratch):
    def kernel(*refs):
        body(refs[: len(ins)], refs[len(ins) : len(ins) + len(outs)], refs[len(ins) + len(outs) :])

    return pl.pallas_call(
        kernel,
        out_shape=tuple(shape_of(o.shape, o.dtype) for o, _ in outs),
        in_specs=[spec for _, spec in ins],
        out_specs=tuple(spec for _, spec in outs),
        scratch_shapes=list(scratch),
        compiler_params=pltpu.CompilerParams(
            collective_id=number, has_side_effects=number is not None, vmem_limit_bytes=VMEM_LIMIT
        ),
        name=name,
    )(*[value for value, _ in ins])


class Slot:
    def __init__(self, shape):
        self.shape, self.dtype, self.value = tuple(shape.shape), shape.dtype, None


class At:
    def __init__(self, stage, plan, moves):
        self.stage, self.plan, self.moves = stage, plan, moves

    def __call__(self, point):
        for name, act in self.plan.get((self.stage, point), ()):
            act(self.moves[name])


USUAL = {
    SECOND: None,
    LOOPED: 1, OUT: 1, DQKV: 1,
    COLLECTED: 2, REDUCED: 2,
    SPREAD: 3, TERMS: 3,
}


class Group:
    def __init__(self, name, number, fused):
        self.name, self.number, self.fused = name, number, fused
        self.stages, self.moves, self.plan = [], {}, {}

    def stage(self, name, body, ins, outs, scratch):
        slots = [Slot(shape) for shape, _ in outs]
        self.stages.append((name, body, ins, list(zip(slots, [spec for _, spec in outs])), scratch))
        return slots

    def move(self, name, stage, move, ins, outs, plan, start=BEGIN, manual=False):
        slots = [Slot(shape) for shape in outs]
        self.moves[name] = (stage, move, ins, [(slot, ANY) for slot in slots])
        if not self.fused:
            plan = []
            if not manual:
                plan = [(stage, start, lambda m: m.start()), (stage, END, lambda m: m.finish())]
                for point, turn in USUAL.items():
                    if turn:
                        plan.append((stage, point, lambda m, turn=turn: m.poll(turn)))
        for at_stage, point, act in plan:
            self.plan.setdefault((at_stage, point), []).append((name, act))
        return slots

    def run(self):
        if self.fused:
            self.launch(self.name, self.number, self.stages, list(self.moves))
            return
        for i, stage in enumerate(self.stages):
            names = [name for name, entry in self.moves.items() if entry[0] == stage[0]]
            self.launch(self.name + str(i), self.number + i, [stage], names)

    def launch(self, name, number, stages, names):
        moves = [self.moves[n] for n in names]
        outs = [pair for stage in stages for pair in stage[3]] + [p for m in moves for p in m[3]]
        out_at = {id(slot): i for i, (slot, _) in enumerate(outs)}
        ins, in_at, scratch, scratch_at = [], {}, [], {}

        def place(pairs):
            where = []
            for value, spec in pairs:
                if id(value) in out_at:
                    where.append((True, out_at[id(value)]))
                    continue
                key = (id(value), id(spec))
                if key not in in_at:
                    in_at[key] = len(ins)
                    ins.append((value.value if isinstance(value, Slot) else value, spec))
                where.append((False, in_at[key]))
            return where

        def reserve(items):
            where = []
            for item in items:
                key, space = item if isinstance(item, tuple) else (None, item)
                if key is not None and key in scratch_at:
                    where.append(scratch_at[key])
                    continue
                scratch.append(space)
                where.append(len(scratch) - 1)
                if key is not None:
                    scratch_at[key] = len(scratch) - 1
            return where

        stage_at = [(place(st[2]), [out_at[id(o)] for o, _ in st[3]], reserve(st[4])) for st in stages]
        move_at = [
            (place(m[2]), [out_at[id(o)] for o, _ in m[3]], reserve(m[1].scratch())) for m in moves
        ]

        def body(in_refs, out_refs, scratch_refs):
            def pick(places):
                where, results, spaces = places
                refs = [(out_refs if made else in_refs)[i] for made, i in where]
                return refs, [out_refs[i] for i in results], [scratch_refs[i] for i in spaces]

            bound = {n: m[1].bind(*pick(at)) for n, m, at in zip(names, moves, move_at)}
            for i, stage in enumerate(stages):
                hello = greet if i == 0 else lambda peers: None
                stage[1](hello, At(stage[0], self.plan, bound), *pick(stage_at[i]))

        results = call(body, name, number, ins, outs, scratch)
        for (slot, _), value in zip(outs, results):
            slot.value = value


def vm(*values):
    return [(value, VM) for value in values]


def any_place(*values):
    return [(value, ANY) for value in values]


def on_device(
    boundary, seq_lengths, expert_ids, route_weights, attn_gain, moe_gain, query_gain, key_norm_gain,
    w_query, key_weight, value_weight, w_output, w_gate, w_up, w_down,
):
    nz, nt = lax.axis_size("expert"), lax.axis_size("tensor")
    micro, block, width = boundary.shape[1:]
    size = query_gain.shape[1]
    heads = w_query.shape[2] // size
    local_experts = w_gate.shape[1]
    hidden = local_experts * w_gate.shape[2]
    experts = local_experts * nz
    rows = block // nt
    q_cols = heads * size
    assert micro == 2 and key_weight.shape[2] == size == block and experts <= LANES
    dma = pltpu.SemaphoreType.DMA

    wg, wu, wd = (w[0].reshape(hidden, width) for w in (w_gate, w_up, w_down))
    wq, wk, wv, wo = w_query[0], key_weight[0], value_weight[0], w_output[0]
    gains = shape_of((1, 2 * width + 2 * size), F32)

    def attend_spaces(own):
        return [
            (SHARED_WQ, pltpu.VMEM((width, q_cols), BF16)),
            (SHARED_WK, pltpu.VMEM((width, size), BF16)),
            (SHARED_WV, pltpu.VMEM((width, size), BF16)),
            (SHARED_WO, pltpu.VMEM((q_cols, width), BF16)),
            (SHARED_PART, pltpu.VMEM((block, width), F32)),
            pltpu.VMEM((block, width), BF16),
            pltpu.VMEM((nt, rows, width), BF16),
            dma((nt,)),
            dma((nt,)),
        ]

    gathered = [
        shape_of((width, q_cols), BF16),
        shape_of((width, size), BF16),
        shape_of((width, size), BF16),
        shape_of((q_cols, width), BF16),
    ]
    attend_outs = vm(
        shape_of((rows, width), F32),
        shape_of((rows, width), BF16),
        shape_of((block, width), BF16),
        shape_of((block, q_cols), F32),
        shape_of((block, size), F32),
        shape_of((block, size), BF16),
        shape_of((heads * block, size), BF16),
        shape_of((block, size), BF16),
        shape_of((block, q_cols), BF16),
    )
    expert_scratch = [(SHARED_WG, pltpu.VMEM((hidden, width), BF16)), (SHARED_WU, pltpu.VMEM((hidden, width), BF16))]
    expert_scratch += [(SHARED_WD, pltpu.VMEM((hidden, width), BF16))]
    hid_scratch = [(n, pltpu.VMEM((nz, block, hidden), BF16)) for n in (SHARED_HID, SHARED_DG, SHARED_DU)]
    all_tokens = shape_of((nz, block, width), BF16)
    all_hidden = shape_of((nz, block, hidden), BF16)
    cols = width // nz
    sliced = [shape_of((2, nz, block, cols), BF16), shape_of((2, nz, rows, cols), BF16)]

    def start(move):
        move.start()

    def finish(move):
        move.finish()

    def poll(turn):
        return lambda move: move.poll(turn)

    def steps(arrays, k):
        return lambda move: [move.step(a, k) for a in arrays]

    def begins(*arrays):
        return lambda move: [move.begin(a) for a in arrays]

    def settles(*arrays):
        return lambda move: [move.settle(a) for a in arrays]

    def ends_of(move):
        for a in range(4):
            move.end(a)

    fused = nz <= 4
    fore = Group("forward", 0, fused)
    relay = Relay(0, (0, 0, 0, 1), nz)
    started = fore.stage(
        ATTEND_0,
        functools.partial(start_attend_kernel, nz, nt, heads, relay),
        [(seq_lengths[0, :, 0], SM)]
        + vm(expert_ids[0], route_weights[0], attn_gain, moe_gain, query_gain, key_norm_gain)
        + any_place(boundary[0], wq, wk, wv, wo, wg, wu, wd),
        any_place(
            shape_of((2, block, width), BF16),
            shape_of((2, 3, block, size), F32),
            shape_of((2, nz, block, LANES), F32),
            like(gains, (2,)),
            *gathered,
            *[shape_of((hidden, width), BF16)] * 3,
        )
        + attend_outs,
        [
            pltpu.VMEM((block, width), BF16),
            pltpu.VMEM((3, block, size), F32),
            pltpu.VMEM(gains.shape, F32),
            pltpu.VMEM(gains.shape, F32),
            pltpu.VMEM((2, 3, block, size), F32),
            pltpu.VMEM((2, block, LANES), F32),
            dma((4,)), dma((3,)), dma((5,)), dma((6,)), dma((6,)), dma((2, nz)), dma((2, nz)),
        ]
        + relay.scratch(4)
        + attend_spaces(0),
    )
    edges, tabs_all, gates_all, gains_all = started[:4]
    weights_0 = started[4:8]
    expert_weights = (wg, wu, wd) + tuple(started[8:11])
    h1_0, b_0, a_0, q_0, k_0, v_0, qr_0, kr_0, o_0 = started[11:]

    x_1, ball_0, gp_0, up_0 = fore.stage(
        EXPERTS_0,
        functools.partial(experts_kernel, 0, nz, nt, local_experts),
        vm(b_0, h1_0) + any_place(gates_all, *expert_weights),
        vm(shape_of((block, width), BF16))
        + any_place(
            all_tokens,
            shape_of((nz, block, hidden), F32),
            shape_of((nz, block, hidden), F32),
        ),
        expert_scratch
        + [pltpu.VMEM((nz, block, hidden), F32)] * 2
        + [pltpu.VMEM((nz, block, LANES), F32), dma((4,)), dma((3,))]
        + exchange_scratch(nz, nt, rows, block, width),
    )

    weights_1 = fore.move(
        MOVE_WEIGHTS_1, EXPERTS_0, Relay(1, (0, 0, 0, 1), nz), any_place(wq, wk, wv, wo), gathered,
        [
            (ATTEND_0, SHARDS, begins(0, 1, 2)),
            (ATTEND_0, SENT, steps((0, 1, 2), 1)),
            (ATTEND_0, SENT, begins(3)),
            (EXPERTS_0, ARRIVED, steps((0, 1, 2), 2)),
            (EXPERTS_0, ARRIVED, steps((3,), 1)),
            (EXPERTS_0, LOOPED, steps((0, 1, 2), 3)),
            (EXPERTS_0, LOOPED, steps((3,), 2)),
            (ATTEND_1, QKV, settles(0, 1, 2)),
            (ATTEND_1, OUT, steps((3,), 3)),
            (ATTEND_1, OUT, settles(3)),
            (ATTEND_1, END, ends_of),
        ],
    )

    (dy_rows,) = fore.move(
        MOVE_DY_ROWS, ATTEND_0, RowsFar(1, nz, nt), any_place(edges), [shape_of((nz, rows, width), BF16)],
        [(ATTEND_0, TABLES, start), (ATTEND_0, QKV, finish)],
        SHARDS,
    )
    (dyall_1,) = fore.move(
        MOVE_DY_ALL, EXPERTS_0, Spread(nz, nt), any_place(dy_rows), [all_tokens],
        [(ATTEND_0, QKV, start), (ATTEND_0, SHARDS, poll(1)), (EXPERTS_0, END, finish)],
    )

    h1_1, b_1, a_1, q_1, k_1, v_1, qr_1, kr_1, o_1 = fore.stage(
        ATTEND_1,
        functools.partial(attend_kernel, 1, nz, nt, heads),
        vm(x_1) + any_place(tabs_all, gains_all, *weights_1),
        attend_outs,
        [dma((6,)), pltpu.VMEM((3, block, size), F32), pltpu.VMEM(gains.shape, F32)] + attend_spaces(1),
    )
    fore.run()

    back = Group("backward", 8, fused)
    dat_1, dh1_1, tm_1, ball_1, yparts_1, hid_1, dg_1, du_1 = back.stage(
        BOTH_1,
        functools.partial(experts_both_kernel, 1, nz, nt, local_experts),
        vm(b_1, h1_1, gains_all) + any_place(edges, gates_all, dyall_1, *expert_weights),
        vm(
            shape_of((block, width), BF16),
            shape_of((rows, width), F32),
            shape_of((1, width), F32),
        )
        + any_place(all_tokens, all_tokens, all_hidden, all_hidden, all_hidden),
        expert_scratch
        + [pltpu.VMEM((2, block, width), BF16)] * 2
        + hid_scratch
        + [dma((5,)), dma((2,)), dma((2,)), dma((4,)), (SHARED_GATES, pltpu.VMEM((nz, block, LANES), F32))]
        + [pltpu.VMEM((rows, width), BF16)]
        + exchange_scratch(nz, nt, rows, block, width),
    )

    def attend_back(layer, x, source, dat, dh1, term_moe, kept, weights, others=None):
        outs = vm(
            shape_of((rows, width), BF16),
            shape_of((block, q_cols + 2 * size), BF16),
            shape_of((TERM_ROWS, TERM_COLS), F32),
        )
        scratch = attend_spaces(layer) + [dma((5,)), dma((nt,)), dma((nt,))]
        scratch += [pltpu.VMEM((rows, width), BF16)]
        ins = any_place(x) + vm(tabs_all, gains_all, dat, dh1, term_moe, *kept) + any_place(*weights)
        if others is not None:
            outs += vm(shape_of((TERM_ROWS, TERM_COLS), F32))
            scratch += [
                pltpu.VMEM((block, width), BF16),
                pltpu.VMEM((nt, TERM_ROWS, TERM_COLS), F32),
                pltpu.VMEM((2, nz, TERM_ROWS, TERM_COLS), F32),
                dma((1,)),
                dma((nt,)),
                dma((nt,)),
            ]
            ins += any_place(others)
        return back.stage(
            ATTEND_BACK_1 if layer else ATTEND_BACK_0,
            functools.partial(attend_back_kernel, layer, source, nz, nt, heads),
            ins,
            outs,
            scratch,
        )

    last = (ATTEND_BACK_0, END, finish)
    kept_1, kept_0 = (q_1, k_1, v_1, qr_1, kr_1), (q_0, k_0, v_0, qr_0, kr_0)
    dx_1, dqkv_1, terms_1 = attend_back(1, x_1, None, dat_1, dh1_1, tm_1, kept_1, weights_1)
    dat_0, dh1_0, tm_0, dyall_0, hid_0, dg_0, du_0 = back.stage(
        EXPERTS_BACK_0,
        functools.partial(experts_back_kernel, 0, nz, nt, local_experts),
        vm(dx_1, h1_0, gains_all) + any_place(gates_all, gp_0, up_0, *expert_weights),
        vm(
            shape_of((block, width), BF16),
            shape_of((rows, width), F32),
            shape_of((1, width), F32),
        )
        + any_place(all_tokens, all_hidden, all_hidden, all_hidden),
        expert_scratch
        + [pltpu.VMEM((2, block, hidden), F32)] * 2
        + hid_scratch
        + [dma((4,)), dma((2,)), dma((2,)), dma((4,)), (SHARED_GATES, pltpu.VMEM((nz, block, LANES), F32))]
        + exchange_scratch(nz, nt, rows, block, width),
    )

    def gather(name, stage, layer, value, begin, end=last):
        return back.move(
            name, stage, Gather(layer, nz), any_place(value), [like(value, (2, nz))],
            [begin + (start,), end], begin[1],
        )

    def line(name, stage, layer, value, begin, *points):
        plan = [begin + (start,)]
        plan += [point + (steps((0,), k + 1),) for k, point in enumerate(points)]
        plan += [(ATTEND_BACK_0, END, settles(0)), (ATTEND_BACK_0, END, lambda m: m.end(0))]
        return back.move(
            name, stage, Line(layer, nz), any_place(value), [like(value, (2, nz))], plan, begin[1]
        )

    def near(name, stage, layer, value):
        return back.move(
            name, stage, Near(layer), any_place(value), [like(value)], [(stage, BEGIN, start), last]
        )

    def columns(name, stage, layer, value, begin, middle):
        return back.move(
            name, stage, Slice(layer, nz, nt), any_place(value), sliced,
            [begin + (start,), middle + (poll(1),), last], begin[1] if begin[0] == stage else BEGIN,
        )

    (bnear_0,) = near(MOVE_B_0, BOTH_1, 0, ball_0)
    (oall_0,) = gather(MOVE_O_0, BOTH_1, 0, o_0, (BOTH_1, ARRIVED))
    aall_0, _ = columns(
        MOVE_A_0, BOTH_1, 0, a_0, (ATTEND_BACK_1, BEGIN), (EXPERTS_BACK_0, BEGIN)
    )
    aall_1, _ = columns(
        MOVE_A_1, BOTH_1, 1, a_1, (ATTEND_BACK_1, BEGIN), (EXPERTS_BACK_0, BEGIN)
    )
    (oall_1,) = gather(MOVE_O_1, ATTEND_BACK_1, 1, o_1, (ATTEND_BACK_1, BEGIN))
    near_1 = [
        near(NEAR_1 + i, ATTEND_BACK_1, 1, value)[0]
        for i, value in enumerate((dg_1, du_1, hid_1, ball_1, dyall_1))
    ]
    datall_1, _ = columns(
        MOVE_DAT_1, ATTEND_BACK_1, 1, dat_1, (BOTH_1, SPREAD), (ATTEND_BACK_1, DQKV)
    )
    (ysums_1,) = back.move(
        MOVE_Y_NEAR, ATTEND_BACK_1, SumNear(nz, nt, rows, block, width), any_place(yparts_1),
        [shape_of((nz, rows, width), BF16)],
        [
            (ATTEND_BACK_1, BEGIN, start),
            (EXPERTS_BACK_0, BEGIN, poll(1)),
            (EXPERTS_BACK_0, LOOPED, poll(2)),
            (EXPERTS_BACK_0, COLLECTED, finish),
        ],
    )
    (dqkvall_1,) = gather(MOVE_DQKV_1, EXPERTS_BACK_0, 1, dqkv_1, (EXPERTS_BACK_0, ARRIVED))
    (termsall_1,) = gather(
        MOVE_TERMS_1, EXPERTS_BACK_0, 1, terms_1, (EXPERTS_BACK_0, BEGIN),
        (ATTEND_BACK_0, BEGIN, finish),
    )
    (yrows_1,) = back.move(
        MOVE_Y_FAR, EXPERTS_BACK_0, SumFar(nz, rows, width), any_place(ysums_1) + vm(h1_1),
        [shape_of((rows, width), BF16)],
        [
            (EXPERTS_BACK_0, SPREAD, start),
            (ATTEND_BACK_0, SENT, poll(2)),
            (ATTEND_BACK_0, SENT, finish),
        ],
    )
    _, dqkv_0, terms_0, terms = attend_back(
        0, edges, 0, dat_0, dh1_0, tm_0, kept_0, weights_0, termsall_1
    )
    datall_0, _ = columns(
        MOVE_DAT_0, ATTEND_BACK_0, 0, dat_0, (EXPERTS_BACK_0, SPREAD), (ATTEND_BACK_0, DQKV)
    )
    near_0 = [bnear_0] + [
        near(NEAR_0 + i, ATTEND_BACK_0, 0, value)[0]
        for i, value in enumerate((dyall_0, dg_0, du_0, hid_0))
    ]
    (ends_1,) = back.move(
        MOVE_Y_SPREAD, ATTEND_BACK_0, SpreadNear(1, nt, block, width), any_place(yrows_1),
        [shape_of((2, block, width), BF16)],
        [(ATTEND_BACK_0, TERMS, start), (ATTEND_BACK_0, TAIL, poll(1)), last],
    )
    hand = [(MOVE_DQKV_0, Gather(0, nz), like(dqkv_0, (2, nz)))]
    hand += [(MOVE_DX_0, Near(0, True), shape_of((2, block, width), BF16))]
    hand += [(MOVE_TERMS_0, Gather(0, nz), like(terms_0, (2, nz)))]
    dqkvall_0, ends_0, _ = (
        back.move(name, ATTEND_BACK_0, move, [], [shape], [], manual=True)[0]
        for name, move, shape in hand
    )
    back.run()

    flat = shape_of((hidden, width), F32)
    experts_part = (
        ExpertGrads(nz, 256),
        any_place(
            *(
                slot.value
                for slot in (
                    dg_0, du_0, hid_0, ball_0, dyall_0,
                    dg_1, du_1, hid_1, ball_1, dyall_1,
                    *near_0[2:], *near_0[:2],
                    *near_1,
                )
            )
        ),
        any_place(flat, flat, flat),
        [
            pltpu.VMEM((3, 2 * nz, block, hidden), BF16),
            pltpu.VMEM((2, 2 * nz, block, width), BF16),
            pltpu.VMEM((2, 256, width), F32),
            dma((5, 2)),
            dma((2,)),
        ],
    )
    operands = (aall_0, oall_0, datall_0, dqkvall_0, ends_0, aall_1, oall_1, datall_1, dqkvall_1, ends_1)
    attend_part = (
        AttendGrads(width, q_cols, size),
        any_place(*(slot.value for slot in operands)) + vm(terms.value),
        vm(
            operands[4],
            shape_of((1, width), F32),
            shape_of((1, width), F32),
            shape_of((1, size), F32),
            shape_of((1, size), F32),
            shape_of(wq.shape, F32),
            shape_of(wk.shape, F32),
            shape_of(wv.shape, F32),
            shape_of(wo.shape, F32),
        ),
        [pltpu.VMEM(o.shape, o.dtype) for o in operands[:4]] + [dma((5,))],
    )

    def gradients(name, parts):
        def body(ins, outs, scratch):
            for work, part_ins, part_outs, part_scratch in parts:
                work.begin(ins[: len(part_ins)], outs[: len(part_outs)], scratch[: len(part_scratch)])
                ins, outs = ins[len(part_ins) :], outs[len(part_outs) :]
                scratch = scratch[len(part_scratch) :]
            for part in parts:
                part[0].work()

        joined = [sum((list(part[i]) for part in parts), []) for i in (1, 2, 3)]
        return call(body, name, None, *joined)

    if fused:
        results = gradients("grads", [experts_part, attend_part])
    else:
        results = gradients("expert_grads", [experts_part])
        results = list(results) + list(gradients("attend_grads", [attend_part]))
    grad_gate, grad_up, grad_down, ends = results[:4]
    return (
        ends[None],
        *results[4:8],
        *(grad[None] for grad in results[8:]),
        grad_gate.reshape(w_gate.shape),
        grad_up.reshape(w_gate.shape),
        grad_down.reshape(w_gate.shape),
    )


def solution(mesh):
    return jax.shard_map(
        on_device,
        mesh=mesh,
        in_specs=(
            P(SECTION, None, EXPERT, None),
            P(SECTION, None, EXPERT, None),
            P(SECTION, None, EXPERT, None),
            P(SECTION, None, EXPERT, None),
            P(SECTION, None),
            P(SECTION, None),
            P(SECTION, None),
            P(SECTION, None),
            P(SECTION, EXPERT, TENSOR),
            P(SECTION, EXPERT, TENSOR),
            P(SECTION, EXPERT, TENSOR),
            P(SECTION, TENSOR, EXPERT),
            P(SECTION, EXPERT, TENSOR, None),
            P(SECTION, EXPERT, TENSOR, None),
            P(SECTION, EXPERT, TENSOR, None),
        ),
        out_specs=(
            P(SECTION, None, EXPERT, None),
            P(SECTION, None),
            P(SECTION, None),
            P(SECTION, None),
            P(SECTION, None),
            P(SECTION, EXPERT, TENSOR),
            P(SECTION, EXPERT, TENSOR),
            P(SECTION, EXPERT, TENSOR),
            P(SECTION, TENSOR, EXPERT),
            P(SECTION, EXPERT, TENSOR, None),
            P(SECTION, EXPERT, TENSOR, None),
            P(SECTION, EXPERT, TENSOR, None),
        ),
        check_vma=False,
    )
```

```python
import functools
import math

import jax
import jax.numpy as jnp
from jax import lax
from jax.experimental import pallas as pl
from jax.experimental.pallas import tpu as pltpu
from jax.sharding import PartitionSpec as P

EPSILON = 1e-06
THETA = 1000000.0
LANES = 128
TERM_ROWS = 24
TERM_COLS = 256
MESH = pl.DeviceIdType.MESH
SECTION, EXPERT, TENSOR = "section", "expert", "tensor"
F32 = jnp.float32
BF16 = jnp.bfloat16
VMEM_LIMIT = 62 * 1024 * 1024

ANY = pl.BlockSpec(memory_space=pl.ANY)
VM = pl.BlockSpec(memory_space=pltpu.VMEM)
SM = pl.BlockSpec(memory_space=pltpu.SMEM)

(
    BEGIN, END, SPREAD, ARRIVED, SECOND, LOOPED, COLLECTED, TABLES, QKV, SHARDS, SENT, OUT, REDUCED, DQKV, TERMS, TAIL,
) = range(0, 16)
(
    ATTEND_0, EXPERTS_0, ATTEND_1, BOTH_1, ATTEND_BACK_1, EXPERTS_BACK_0, ATTEND_BACK_0,
) = range(0, 7)
(
    MOVE_WEIGHTS_1, MOVE_DY_ROWS, MOVE_DY_ALL, MOVE_B_0, MOVE_O_0, MOVE_A_0, MOVE_A_1, MOVE_O_1, MOVE_DAT_1, MOVE_Y_NEAR, MOVE_DQKV_1, MOVE_TERMS_1, MOVE_Y_FAR, MOVE_DAT_0, MOVE_Y_SPREAD, MOVE_DQKV_0, MOVE_DX_0, MOVE_TERMS_0,
) = range(0, 18)
NEAR_0, NEAR_1 = 40, 50
(
    SHARED_PART, SHARED_OWN, SHARED_GATES, SHARED_WG, SHARED_WU, SHARED_WD, SHARED_WQ, SHARED_WK, SHARED_WV, SHARED_WO, SHARED_HID, SHARED_DG, SHARED_DU,
) = range(0, 13)


def partner(index, k, count):
    out, bit = 0, 1
    while bit < count:
        out = out + bit * lax.rem(lax.div(index, bit) + lax.div(k, bit), 2)
        bit *= 2
    return out


def rows_at(start, size):
    return pl.ds(pl.multiple_of(start, size), size)


def remote(src, dst, send_sem, recv_sem, **where):
    return pltpu.make_async_remote_copy(
        src_ref=src,
        dst_ref=dst,
        send_sem=send_sem,
        recv_sem=recv_sem,
        device_id=where,
        device_id_type=MESH,
    )


def greet(peers):
    barrier = pltpu.get_barrier_semaphore()
    for where in peers:
        pl.semaphore_signal(barrier, inc=1, device_id=where, device_id_type=MESH)
    pl.semaphore_wait(barrier, len(peers))


def layer_peers(z, t, nz, nt):
    i32 = jnp.int32
    peers = [{"expert": partner(z, i32(k), nz)} for k in range(1, nz)]
    peers += [{TENSOR: partner(t, i32(k), nt)} for k in range(1, nt)]
    return peers


def dot(a, b):
    return lax.dot_general(a, b, (((1,), (0,)), ((), ())), preferred_element_type=F32)


def dot_nt(a, b):
    return lax.dot_general(a, b, (((1,), (1,)), ((), ())), preferred_element_type=F32)


def dot_tn(a, b):
    return lax.dot_general(a, b, (((0,), (0,)), ((), ())), preferred_element_type=F32)


def unit_rows(value):
    factor = lax.rsqrt(jnp.mean(value * value, axis=-1, keepdims=True) + EPSILON)
    return value * factor, factor


def norm_back(grad, gain, unit, factor):
    weighted = grad * gain
    inner = jnp.mean(weighted * unit, axis=-1, keepdims=True)
    return factor * (weighted - unit * inner), jnp.sum(grad * unit, axis=0, keepdims=True)


def expert_gates(gate_rows, first_expert, local_experts, width):
    rows = gate_rows.shape[0]
    lane = lax.broadcasted_iota(jnp.int32, gate_rows.shape, 1)
    column = lax.broadcasted_iota(jnp.int32, (rows, local_experts * width), 1)
    out = None
    for e in range(local_experts):
        one = jnp.sum(jnp.where(lane == first_expert + e, gate_rows, 0.0), axis=1, keepdims=True)
        wide = jnp.broadcast_to(one, column.shape)
        out = wide if out is None else jnp.where(column >= e * width, wide, out)
    return out


def write_terms(terms_ref, row, vector):
    for i in range(vector.shape[1] // TERM_COLS):
        terms_ref[row + i : row + i + 1, :] = vector[:, i * TERM_COLS : (i + 1) * TERM_COLS]


class Square:
    def __init__(self, nz, nt, rows, width):
        assert nt == 4
        self.z, self.t = lax.axis_index(EXPERT), lax.axis_index(TENSOR)
        self.nz, self.rows = nz, rows
        half = width // 2
        self.half, self.first, self.second = half, pl.ds(0, half), pl.ds(half, half)
        near_x, near_y, across = (partner(self.t, jnp.int32(j), nt) for j in (1, 2, 3))
        self.near = (near_x, near_y)
        self.mine, self.x_rows, self.y_rows, self.across_rows = (
            self.window(i) for i in (self.t, near_x, near_y, across)
        )
        self.y_pair = rows_at(lax.div(near_y, 2) * (2 * rows), 2 * rows)
        in_pair = lax.rem(self.t, 2)
        self.pair_mine, self.pair_x = self.window(in_pair), self.window(1 - in_pair)

    def window(self, index):
        return rows_at(index * self.rows, self.rows)


class RowGather:
    @staticmethod
    def scratch(nz):
        return [pltpu.SemaphoreType.DMA((2, nz)), pltpu.SemaphoreType.DMA((4, nz, 2))]

    def __init__(self, square, full, sems):
        self.sq, self.full = square, full
        self.far_sem, self.row_sem = sems

    def far_copy(self, k, source, src=None):
        sq = self.sq
        spot = self.full.at[source, sq.mine]
        return remote(
            spot if src is None else src,
            spot,
            self.far_sem.at[0, k],
            self.far_sem.at[1, k],
            expert=partner(sq.z, jnp.int32(k), sq.nz),
        )

    def row_copy(self, k, source, j, window, src=None):
        spot = self.full.at[source, window]
        return remote(
            spot if src is None else src,
            spot,
            self.row_sem.at[0, k, j],
            self.row_sem.at[1, k, j],
            tensor=self.sq.near[j],
        )

    def on_copy(self, k, source, j, window):
        spot = self.full.at[source, window, (self.sq.second, self.sq.first)[j]]
        return remote(
            spot, spot, self.row_sem.at[2, k, j], self.row_sem.at[3, k, j], tensor=self.sq.near[j]
        )

    def send(self, k, source, src=None):
        for j in range(2):
            self.row_copy(k, source, j, self.sq.mine, src).start()

    def hand_on(self, k, source):
        self.row_copy(k, source, 0, self.sq.x_rows).wait_recv()
        self.on_copy(k, source, 1, self.sq.x_rows).start()
        self.row_copy(k, source, 1, self.sq.y_rows).wait_recv()
        self.on_copy(k, source, 0, self.sq.y_rows).start()

    def arrive(self, k, source):
        for j in range(2):
            self.on_copy(k, source, j, self.sq.across_rows).wait_recv()

    def leave(self, k, source):
        for j in range(2):
            self.row_copy(k, source, j, self.sq.mine).wait_send()
            self.on_copy(k, source, j, (self.sq.y_rows, self.sq.x_rows)[j]).wait_send()


class RowSum:
    @staticmethod
    def scratch(nz, rows, block, width):
        half = width // 2
        dma = pltpu.SemaphoreType.DMA
        return [
            pltpu.VMEM((nz, block, width), BF16),
            pltpu.VMEM((nz, 2 * rows, half), BF16),
            pltpu.VMEM((nz, 2, rows, half), BF16),
            pltpu.VMEM((nz, 2, rows, half), BF16),
            pltpu.VMEM((nz, 2, rows, half), BF16),
            pltpu.VMEM((nz, rows, width), BF16),
            pltpu.VMEM((nz, rows, width), BF16),
            pltpu.VMEM((rows, width), F32),
            dma((2, nz)),
            dma((6, nz, 2)),
        ]

    count = 10

    def __init__(self, square, scratch, own=None):
        self.sq, self.own = square, own
        (self.outgoing, self.from_y, self.from_x, self.pairs, self.came_pairs) = scratch[:5]
        (self.passed, self.came_far, self.total, self.far_sem, self.part_sem) = scratch[5:]

    def part_copy(self, k, i):
        sq = self.sq
        window, cols = ((sq.y_pair, sq.first), (sq.across_rows, sq.second), (sq.x_rows, sq.second))[i]
        dst = (self.from_y.at[k], self.from_x.at[k, 1], self.from_x.at[k, 0])[i]
        group, slot = ((0, 0), (2, 1), (2, 0))[i]
        return remote(
            self.outgoing.at[k, window, cols],
            dst,
            self.part_sem.at[group, k, slot],
            self.part_sem.at[group + 1, k, slot],
            tensor=sq.near[0] if i else sq.near[1],
        )

    def pair_copy(self, k, j):
        return remote(
            self.pairs.at[k, j],
            self.came_pairs.at[k, j],
            self.part_sem.at[4, k, j],
            self.part_sem.at[5, k, j],
            tensor=self.sq.near[j],
        )

    def sum_copy(self, k):
        return remote(
            self.passed.at[k],
            self.came_far.at[k],
            self.far_sem.at[0, k],
            self.far_sem.at[1, k],
            expert=partner(self.sq.z, k, self.sq.nz),
        )

    def send(self, k):
        for i in range(3):
            self.part_copy(k, i).start()

    def pair_up(self, k):
        sq = self.sq
        self.part_copy(k, 0).wait_recv()
        kept = self.outgoing[k, sq.x_rows, sq.first].astype(F32)
        self.pairs[k, 0] = (kept + self.from_y[k, sq.pair_x].astype(F32)).astype(BF16)
        self.pair_copy(k, 0).start()
        self.part_copy(k, 1).wait_recv()
        kept = self.outgoing[k, sq.y_rows, sq.second].astype(F32)
        self.pairs[k, 1] = (kept + self.from_x[k, 1].astype(F32)).astype(BF16)
        self.pair_copy(k, 1).start()

    def collect(self, k):
        sq = self.sq
        self.part_copy(k, 2).wait_recv()
        self.pair_copy(k, 0).wait_recv()
        self.pair_copy(k, 1).wait_recv()
        own = self.outgoing[k, sq.mine].astype(F32) if self.own is None else self.own[k]
        left = own[:, : sq.half] + self.from_y[k, sq.pair_mine].astype(F32)
        right = own[:, sq.half :] + self.from_x[k, 0].astype(F32)
        return (
            left + self.came_pairs[k, 0].astype(F32),
            right + self.came_pairs[k, 1].astype(F32),
        )

    def collect_own(self):
        left, right = self.collect(jnp.int32(0))
        self.total[:, : self.sq.half] = left
        self.total[:, self.sq.half :] = right

    def collect_far(self, k):
        left, right = self.collect(k)
        self.passed[k, :, self.sq.first] = left.astype(BF16)
        self.passed[k, :, self.sq.second] = right.astype(BF16)
        self.sum_copy(k).start()

    def add_far(self):
        for k in range(1, self.sq.nz):
            self.sum_copy(jnp.int32(k)).wait_recv()
            self.total[...] += self.came_far[k].astype(F32)

    def leave(self, far=True):
        for k in range(self.sq.nz):
            if k and far:
                self.sum_copy(jnp.int32(k)).wait_send()
            for j in range(2):
                self.pair_copy(k, j).wait_send()
            for i in range(3):
                self.part_copy(k, i).wait_send()


def exchange_scratch(nz, nt, rows, block, width):
    return (
        [
            pltpu.VMEM((nz, block, width), BF16),
            (SHARED_PART, pltpu.VMEM((block, width), F32)),
            (SHARED_OWN, pltpu.VMEM((nz, rows, width), F32)),
            pltpu.VMEM((block, width), BF16),
            pltpu.SemaphoreType.DMA((2, nt)),
        ]
        + RowGather.scratch(nz)
        + RowSum.scratch(nz, rows, block, width)
    )


EXCHANGE_SCRATCH = 7 + RowSum.count


def exchange(nz, nt, own_rows, scratch, ready, work, at):
    full, part, own_part = scratch[:3]
    sq = Square(nz, nt, own_rows.shape[0], full.shape[-1])
    z = sq.z
    gather = RowGather(sq, full, scratch[5:7])
    sums = RowSum(sq, scratch[7 : 7 + RowSum.count], own_part)
    i32 = jnp.int32

    def produce(k, source):
        gather.arrive(k, source)
        part[...] = work(k, source, full[source])
        sums.outgoing[k] = part[...].astype(BF16)
        sums.send(k)
        own_part[k] = part[sq.mine]

    full[z, sq.mine] = own_rows
    for k in range(1, nz):
        gather.far_copy(k, z).start()
    gather.send(0, z)
    at(BEGIN)
    ready()
    for k in range(1, nz):
        source = partner(z, i32(k), nz)
        gather.far_copy(k, source).wait_recv()
        gather.send(k, source)
        if k == 1:
            gather.hand_on(0, z)
    at(ARRIVED)
    gather.hand_on(1, partner(z, i32(1), nz))

    def step(k, carry):
        @pl.when(k + 1 < nz)
        def _():
            gather.hand_on(k + 1, partner(z, k + 1, nz))

        turn = lax.rem(k, nz)
        produce(turn, partner(z, turn, nz))

        @pl.when(k >= 2)
        def _():
            sums.pair_up(k - 1)

        @pl.when(k >= 3)
        def _():
            sums.collect_far(k - 2)

        @pl.when(k == 2)
        def _():
            at(SECOND)

        return carry

    lax.fori_loop(1, nz + 1, step, 0)
    at(LOOPED)
    sums.collect_far(i32(nz - 1))
    sums.pair_up(i32(0))
    sums.collect_own()
    at(COLLECTED)
    sums.add_far()

    def finish():
        for k in range(nz):
            source = partner(z, i32(k), nz)
            if k:
                gather.far_copy(k, z).wait_send()
            gather.leave(k, source)
        sums.leave()

    return sums.total, finish


def spread_rows(t, nt, rows, block_ref, send_sem, recv_sem):
    i32 = jnp.int32
    mine = rows_at(t * rows, rows)
    for j in range(1, nt):
        remote(
            block_ref.at[mine],
            block_ref.at[mine],
            send_sem.at[j],
            recv_sem.at[j],
            tensor=partner(t, i32(j), nt),
        ).start()

    def wait():
        for j in range(1, nt):
            peer = partner(t, i32(j), nt)
            theirs = rows_at(peer * rows, rows)
            copy = remote(
                block_ref.at[theirs],
                block_ref.at[theirs],
                send_sem.at[j],
                recv_sem.at[j],
                tensor=peer,
            )
            copy.wait_send()
            copy.wait_recv()

    return wait


def reduce_rows(t, nt, rows, part, outgoing, came, send_sem, recv_sem, at):
    i32 = jnp.int32
    outgoing[...] = part[...].astype(BF16)

    def copy(j):
        peer = partner(t, i32(j), nt)
        return remote(
            outgoing.at[rows_at(peer * rows, rows)],
            came.at[j],
            send_sem.at[j],
            recv_sem.at[j],
            tensor=peer,
        )

    for j in range(1, nt):
        copy(j).start()
    at(SENT)
    total = part[rows_at(t * rows, rows)]
    for j in range(1, nt):
        copy(j).wait_recv()
        total = total + came[j].astype(F32)
    for j in range(1, nt):
        copy(j).wait_send()
    return total


def all_peers(s, z, t, nz, nt):
    i32 = jnp.int32
    peers = [{SECTION: 1 - s}]
    for k in range(1, nz):
        zz = partner(z, i32(k), nz)
        peers += [{EXPERT: zz}, {SECTION: 1 - s, EXPERT: zz}]
    return peers + [{TENSOR: partner(t, i32(j), nt)} for j in range(1, nt)]


class Relay:
    def __init__(self, layer, spots, nz):
        self.layer, self.spots, self.nz = layer, spots, nz

    def scratch(self, count=4):
        dma = pltpu.SemaphoreType.DMA
        return [dma((count,))] + [dma((count, self.nz))] * 6

    def bind(self, shards, outs, sems):
        self.s, self.z = lax.axis_index(SECTION), lax.axis_index(EXPERT)
        self.shards, self.outs, self.sems = shards, outs, sems
        self.source = self.hands = self.s == self.layer
        self.count = len(shards)
        return self

    def place(self, a, owner):
        dim = self.spots[a]
        size = self.shards[a].shape[dim]
        window = rows_at(owner * size, size)
        return self.outs[a].at[window] if dim == 0 else self.outs[a].at[:, window]

    def home(self, a):
        return pltpu.make_async_copy(self.shards[a], self.place(a, self.z), self.sems[0].at[a])

    def hop(self, a, owner, step, right, own=False):
        spot = self.place(a, owner)
        send, recv = self.sems[1:3] if right else self.sems[3:5]
        return remote(
            self.shards[a] if own else spot,
            spot,
            send.at[a, step],
            recv.at[a, step],
            expert=self.z + 1 if right else self.z - 1,
        )

    def hand(self, a, owner, own=False):
        spot = self.place(a, owner)
        return remote(
            self.shards[a] if own else spot,
            spot,
            self.sems[5].at[a, owner],
            self.sems[6].at[a, owner],
            section=1 - self.s,
        )

    def begin_side(self, a, right):
        @pl.when(self.source & ((self.z + 1 < self.nz) if right else (self.z >= 1)))
        def _():
            self.hop(a, self.z, 1, right, True).start()

    def begin_home(self, a):
        @pl.when(self.source)
        def _():
            self.home(a).start()

        @pl.when(self.hands)
        def _():
            self.hand(a, self.z, True).start()

    def begin(self, a):
        self.begin_side(a, True)
        self.begin_side(a, False)
        self.begin_home(a)

    def step(self, a, k):
        z, nz = self.z, self.nz

        @pl.when(self.source & (z >= k))
        def _():
            self.hop(a, z - k, k, True).wait_recv()

            @pl.when(z + 1 < nz)
            def _():
                self.hop(a, z - k, k + 1, True).start()

            @pl.when(self.hands)
            def _():
                self.hand(a, z - k).start()

        @pl.when(self.source & (z + k < nz))
        def _():
            self.hop(a, z + k, k, False).wait_recv()

            @pl.when(z >= 1)
            def _():
                self.hop(a, z + k, k + 1, False).start()

            @pl.when(self.hands)
            def _():
                self.hand(a, z + k).start()

    def settle(self, a):
        @pl.when(self.source)
        def _():
            self.home(a).wait()

        @pl.when(jnp.logical_not(self.source))
        def _():
            for owner in range(self.nz):
                self.hand(a, owner).wait_recv()

    def end(self, a):
        z, nz = self.z, self.nz

        @pl.when(self.hands)
        def _():
            for owner in range(nz):
                self.hand(a, owner).wait_send()

        @pl.when(self.source)
        def _():
            for step in range(1, nz):

                @pl.when((z >= step - 1) & (z + 1 < nz))
                def _():
                    self.hop(a, z - (step - 1), step, True).wait_send()

                @pl.when((z + step - 1 < nz) & (z >= 1))
                def _():
                    self.hop(a, z + (step - 1), step, False).wait_send()

    def start(self):
        for a in range(self.count):
            self.begin(a)

    def poll(self, turn):
        if turn < min(3, self.nz - 1):
            for a in range(self.count):
                self.step(a, turn)

    def finish(self):
        for k in range(min(3, self.nz - 1), self.nz):
            for a in range(self.count):
                self.step(a, k)
        for a in range(self.count):
            self.settle(a)
            self.end(a)


class Line(Relay):
    def __init__(self, layer, nz):
        super().__init__(layer, None, nz)

    def scratch(self):
        return super().scratch(1)

    def bind(self, ins, outs, sems):
        super().bind(ins, outs, sems)
        self.source, self.hands = self.s >= 0, self.s != self.layer
        return self

    def place(self, a, owner, section=None):
        return self.outs[a].at[self.s if section is None else section, owner]

    def settle(self, a):
        self.home(a).wait()

        @pl.when(self.s == self.layer)
        def _():
            for owner in range(self.nz):
                spot = self.place(a, owner, 1 - self.layer)
                remote(
                    spot, spot, self.sems[5].at[a, owner], self.sems[6].at[a, owner], section=1 - self.s
                ).wait_recv()


class Slice:
    def __init__(self, layer, nz, nt):
        self.layer, self.nz, self.nt = layer, nz, nt

    def scratch(self):
        dma = pltpu.SemaphoreType.DMA
        return [dma((2,)), dma((self.nz,)), dma((2, self.nz)), dma((2, self.nt))]

    def bind(self, ins, outs, sems):
        self.s, self.z, self.t = (lax.axis_index(a) for a in (SECTION, EXPERT, TENSOR))
        self.src, (self.out, self.rows_out), self.sems = ins[0], outs, sems
        rows, self.cols = self.rows_out.shape[2:]
        self.rows = rows
        self.mine = rows_at(self.t * rows, rows)
        self.receives = self.s == self.layer
        return self

    def far(self, k, local, section=None, origin=None):
        zz = partner(self.z, jnp.int32(k), self.nz)
        src = self.src.at[self.mine, rows_at(zz * self.cols, self.cols)]
        section = self.s if section is None else section
        spot = self.rows_out.at[section, self.z if origin is None else origin]
        if local:
            return pltpu.make_async_copy(src, spot, self.sems[0].at[0])
        return remote(
            src,
            spot,
            self.sems[1].at[k],
            self.sems[2].at[section, k],
            section=jnp.int32(self.layer),
            expert=zz,
        )

    def near(self, j, window):
        return remote(
            self.rows_out,
            self.out.at[:, :, window],
            self.sems[3].at[0, j],
            self.sems[3].at[1, j],
            tensor=partner(self.t, jnp.int32(j), self.nt),
        )

    def home(self):
        return pltpu.make_async_copy(self.rows_out, self.out.at[:, :, self.mine], self.sems[0].at[1])

    def start(self):
        for k in range(1, self.nz):
            self.far(k, False).start()

        @pl.when(self.receives)
        def _():
            self.far(0, True).start()

        @pl.when(jnp.logical_not(self.receives))
        def _():
            self.far(0, False).start()

    def poll(self, turn):
        if turn != 1:
            return

        @pl.when(self.receives)
        def _():
            self.far(0, True).wait()
            for section in range(2):
                for k in range(self.nz):
                    if k or section != self.layer:
                        zz = partner(self.z, jnp.int32(k), self.nz)
                        self.far(k, False, section, zz).wait_recv()
            self.home().start()
            for j in range(1, self.nt):
                self.near(j, self.mine).start()

    def finish(self):
        for k in range(1, self.nz):
            self.far(k, False).wait_send()

        @pl.when(jnp.logical_not(self.receives))
        def _():
            self.far(0, False).wait_send()

        @pl.when(self.receives)
        def _():
            self.home().wait()
            for j in range(1, self.nt):
                theirs = partner(self.t, jnp.int32(j), self.nt) * self.rows
                self.near(j, rows_at(theirs, self.rows)).wait_recv()
                self.near(j, self.mine).wait_send()


class Gather:
    def __init__(self, layer, nz):
        self.layer, self.nz = layer, nz

    def scratch(self):
        dma = pltpu.SemaphoreType.DMA
        return [dma((1,)), dma((self.nz,)), dma((2, self.nz))]

    def bind(self, ins, outs, sems):
        self.s, self.z = lax.axis_index(SECTION), lax.axis_index(EXPERT)
        self.src, self.out, self.sems = (ins or (None,))[0], outs[0], sems
        return self

    def copy(self, k, local, section=None, origin=None):
        zz = partner(self.z, jnp.int32(k), self.nz)
        src = self.src
        section = self.s if section is None else section
        spot = self.out.at[section, self.z if origin is None else origin]
        if local:
            return pltpu.make_async_copy(src, spot, self.sems[0].at[0])
        return remote(
            src,
            spot,
            self.sems[1].at[k],
            self.sems[2].at[section, k],
            section=jnp.int32(self.layer),
            expert=zz,
        )

    def start(self):
        for k in range(1, self.nz):
            self.copy(k, False).start()

        @pl.when(self.s == self.layer)
        def _():
            self.copy(0, True).start()

        @pl.when(self.s != self.layer)
        def _():
            self.copy(0, False).start()

    def poll(self, turn):
        pass

    def arrive(self):
        @pl.when(self.s == self.layer)
        def _():
            self.copy(0, True).wait()
            for section in range(2):
                for k in range(self.nz):
                    if k or section != self.layer:
                        zz = partner(self.z, jnp.int32(k), self.nz)
                        self.copy(k, False, section, zz).wait_recv()

    def leave(self):
        for k in range(1, self.nz):
            self.copy(k, False).wait_send()

        @pl.when(self.s != self.layer)
        def _():
            self.copy(0, False).wait_send()

    def finish(self):
        self.arrive()
        self.leave()


class Near:
    def __init__(self, layer, both=False):
        self.layer, self.both = layer, both

    def scratch(self):
        dma = pltpu.SemaphoreType.DMA
        return [dma((1,)), dma((1,)), dma((1,))]

    def bind(self, ins, outs, sems):
        self.s, self.sems = lax.axis_index(SECTION), sems
        self.src, self.out = (ins or (None,))[0], outs[0]
        return self

    def local(self):
        return pltpu.make_async_copy(self.src, self.out.at[self.layer], self.sems[0].at[0])

    def copy(self):
        return remote(
            self.src,
            self.out.at[1 - self.layer] if self.both else self.out,
            self.sems[1].at[0],
            self.sems[2].at[0],
            section=jnp.int32(self.layer),
        )

    def start(self):
        if self.both:

            @pl.when(self.s == self.layer)
            def _():
                self.local().start()

        @pl.when(self.s != self.layer)
        def _():
            self.copy().start()

    def poll(self, turn):
        pass

    def finish(self):
        @pl.when(self.s == self.layer)
        def _():
            if self.both:
                self.local().wait()
            remote(
                self.src,
                self.out.at[1 - self.layer] if self.both else self.out,
                self.sems[1].at[0],
                self.sems[2].at[0],
                section=1 - self.s,
            ).wait_recv()

        @pl.when(self.s != self.layer)
        def _():
            self.copy().wait_send()


class RowsFar:
    def __init__(self, slot, nz, nt):
        self.slot, self.nz, self.nt = slot, nz, nt

    def scratch(self):
        return [pltpu.SemaphoreType.DMA((1,)), pltpu.SemaphoreType.DMA((2, self.nz))]

    def bind(self, ins, outs, sems):
        self.z, self.t = lax.axis_index(EXPERT), lax.axis_index(TENSOR)
        self.src, self.out, self.sems = ins[0], outs[0], sems
        return self

    def copy(self, k, origin):
        rows = self.out.shape[1]
        src = self.src.at[self.slot, rows_at(self.t * rows, rows)]
        if k == 0:
            return pltpu.make_async_copy(src, self.out.at[origin], self.sems[0].at[0])
        return remote(
            src,
            self.out.at[origin],
            self.sems[1].at[0, k],
            self.sems[1].at[1, k],
            expert=partner(self.z, jnp.int32(k), self.nz),
        )

    def start(self):
        for k in range(self.nz):
            self.copy(k, self.z).start()

    def poll(self, turn):
        pass

    def finish(self):
        self.copy(0, self.z).wait()
        for k in range(1, self.nz):
            self.copy(k, self.z).wait_send()
            self.copy(k, partner(self.z, jnp.int32(k), self.nz)).wait_recv()


class Spread:
    def __init__(self, nz, nt):
        self.nz, self.nt = nz, nt

    def scratch(self):
        return [pltpu.SemaphoreType.DMA((1,))] + RowGather.scratch(self.nz)

    def bind(self, ins, outs, sems):
        self.src, self.out, self.sems = ins[0], outs[0], sems
        self.sq = Square(self.nz, self.nt, *self.src.shape[1:])
        self.gather = RowGather(self.sq, self.out, sems[1:])
        return self

    def local(self):
        return pltpu.make_async_copy(self.src, self.out.at[:, self.sq.mine], self.sems[0].at[0])

    def start(self):
        self.local().start()
        for k in range(self.nz):
            self.gather.send(k, k, self.src.at[k])

    def poll(self, turn):
        if turn == 1:
            for k in range(self.nz):
                self.gather.hand_on(k, k)

    def finish(self):
        self.local().wait()
        for k in range(self.nz):
            self.gather.arrive(k, k)
            self.gather.leave(k, k)


class SumNear:
    def __init__(self, nz, nt, rows, block, width):
        self.nz, self.nt = nz, nt
        self.shape = rows, block, width

    def scratch(self):
        rows, block, width = self.shape
        half = width // 2
        return [
            pltpu.SemaphoreType.DMA((2,)),
            pltpu.SemaphoreType.DMA((2, 5)),
            pltpu.VMEM((self.nz, block, width), BF16),
            pltpu.VMEM((self.nz, 2 * rows, half), BF16),
            pltpu.VMEM((2, self.nz, rows, half), BF16),
            pltpu.VMEM((2, self.nz, rows, half), BF16),
            pltpu.VMEM((2, self.nz, rows, half), BF16),
            pltpu.VMEM((self.nz, rows, width), BF16),
        ]

    def bind(self, ins, outs, scratch):
        self.src, self.out = ins[0], outs[0]
        self.sems, self.sem = scratch[:2]
        self.parts, self.from_y, self.from_x, self.pairs, self.came, self.result = scratch[2:]
        self.sq = Square(self.nz, self.nt, self.shape[0], self.shape[2])
        return self

    def load(self):
        return pltpu.make_async_copy(self.src, self.parts, self.sems.at[0])

    def save(self):
        return pltpu.make_async_copy(self.result, self.out, self.sems.at[1])

    def copy(self, i):
        sq = self.sq
        if i < 3:
            window, cols = ((sq.y_pair, sq.first), (sq.across_rows, sq.second), (sq.x_rows, sq.second))[i]
            src = self.src.at[:, window, cols]
            dst = (self.from_y, self.from_x.at[1], self.from_x.at[0])[i]
        else:
            src, dst = self.pairs.at[i - 3], self.came.at[i - 3]
        peer = sq.near[(1, 0, 0, 0, 1)[i]]
        return remote(src, dst, self.sem.at[0, i], self.sem.at[1, i], tensor=peer)

    def start(self):
        self.load().start()
        for i in range(3):
            self.copy(i).start()

    def poll(self, turn):
        sq = self.sq
        if turn == 1:
            self.load().wait()
            self.copy(0).wait_recv()
            kept = self.parts[:, sq.x_rows, sq.first].astype(F32)
            self.pairs[0] = (kept + self.from_y[:, sq.pair_x].astype(F32)).astype(BF16)
            self.copy(3).start()
            self.copy(1).wait_recv()
            kept = self.parts[:, sq.y_rows, sq.second].astype(F32)
            self.pairs[1] = (kept + self.from_x[1].astype(F32)).astype(BF16)
            self.copy(4).start()
        if turn == 2:
            for i in (2, 3, 4):
                self.copy(i).wait_recv()
            left = self.parts[:, sq.mine, sq.first].astype(F32)
            left = left + self.from_y[:, sq.pair_mine].astype(F32) + self.came[0].astype(F32)
            right = self.parts[:, sq.mine, sq.second].astype(F32)
            right = right + self.from_x[0].astype(F32) + self.came[1].astype(F32)
            self.result[:, :, sq.first] = left.astype(BF16)
            self.result[:, :, sq.second] = right.astype(BF16)
            self.save().start()

    def finish(self):
        self.save().wait()
        for i in range(5):
            self.copy(i).wait_send()


class SumFar:
    def __init__(self, nz, rows, width):
        self.nz, self.shape = nz, (rows, width)

    def scratch(self):
        dma = pltpu.SemaphoreType.DMA
        return [
            pltpu.VMEM((self.nz,) + self.shape, BF16),
            pltpu.VMEM(self.shape, BF16),
            dma((2,)),
            dma((2, self.nz)),
        ]

    def bind(self, ins, outs, scratch):
        self.z = lax.axis_index(EXPERT)
        self.src, self.rows_ref = ins
        self.out = outs[0]
        self.came, self.result, self.sems, self.far_sem = scratch
        return self

    def copy(self, k):
        if k == 0:
            return pltpu.make_async_copy(self.src.at[0], self.came.at[0], self.sems.at[0])
        return remote(
            self.src.at[k],
            self.came.at[k],
            self.far_sem.at[0, k],
            self.far_sem.at[1, k],
            expert=partner(self.z, jnp.int32(k), self.nz),
        )

    def save(self):
        return pltpu.make_async_copy(self.result, self.out, self.sems.at[1])

    def start(self):
        for k in range(self.nz):
            self.copy(k).start()

    def poll(self, turn):
        if turn == 2:
            self.copy(0).wait()
            total = self.rows_ref[...] + self.came[0].astype(F32)
            for k in range(1, self.nz):
                self.copy(k).wait_recv()
                total = total + self.came[k].astype(F32)
            self.result[...] = total.astype(BF16)
            self.save().start()

    def finish(self):
        self.save().wait()
        for k in range(1, self.nz):
            self.copy(k).wait_send()


class SpreadNear:
    def __init__(self, layer, nt, block, width):
        self.nt, self.shape, self.near = nt, (block, width), Near(layer, True)

    def scratch(self):
        dma = pltpu.SemaphoreType.DMA
        return [pltpu.VMEM(self.shape, BF16), dma((1,)), dma((2, self.nt))] + self.near.scratch()

    def bind(self, ins, outs, scratch):
        self.t = lax.axis_index(TENSOR)
        self.src = ins[0]
        self.whole, self.load_sem, self.spread_sem = scratch[:3]
        self.near.bind([self.whole], outs, scratch[3:])
        self.rows = self.src.shape[0]
        return self

    def start(self):
        load = pltpu.make_async_copy(
            self.src, self.whole.at[rows_at(self.t * self.rows, self.rows)], self.load_sem.at[0]
        )
        load.start()
        load.wait()
        self.wait = spread_rows(
            self.t, self.nt, self.rows, self.whole, self.spread_sem.at[0], self.spread_sem.at[1]
        )

    def poll(self, turn):
        if turn == 1:
            self.wait()
            self.near.start()

    def finish(self):
        self.near.finish()


def heads_to_rows(value, heads, size):
    return jnp.concatenate([value[:, h * size : (h + 1) * size] for h in range(heads)], axis=0)


def rows_to_heads(value, heads, block):
    return jnp.concatenate([value[h * block : (h + 1) * block] for h in range(heads)], axis=1)


def split_gains(row, width, size):
    return (
        row[:, :width],
        row[:, width : 2 * width],
        row[:, 2 * width : 2 * width + size],
        row[:, 2 * width + size :],
    )


def tiled(value, times):
    return jnp.concatenate([value] * times, axis=0)


def half_turn(value):
    return pltpu.roll(value, value.shape[-1] // 2, value.ndim - 1)


def attend_body(t, nt, heads, x_ref, tables, gains, outs, scratch, wait_qkv, wait_out, at):
    (h1_ref, b_ref, a_ref, q_ref, k_ref, v_ref, qr_ref, kr_ref, o_ref) = outs
    (wq_s, wk_s, wv_s, wo_s, part, outgoing, came, s_sem, r_sem) = scratch
    block, width = x_ref.shape
    rows = block // nt
    cos, sin, bias = tables
    size = cos.shape[-1]
    g_attn, g_moe, g_query, g_key = split_gains(gains, width, size)
    unit, _ = unit_rows(x_ref[...].astype(F32))
    a_ref[...] = (unit * g_attn).astype(BF16)
    wait_qkv()
    q = dot(a_ref[...], wq_s[...])
    q_ref[...] = q
    k = dot(a_ref[...], wk_s[...])
    k_ref[...] = k
    v = dot(a_ref[...], wv_s[...]).astype(BF16)
    v_ref[...] = v
    qn = unit_rows(heads_to_rows(q, heads, size))[0] * g_query
    kn = unit_rows(k)[0] * g_key
    qr = (qn * tiled(cos, heads) + half_turn(qn) * tiled(sin, heads)).astype(BF16)
    kr = (kn * cos + half_turn(kn) * sin).astype(BF16)
    qr_ref[...] = qr
    kr_ref[...] = kr
    scores = dot_nt(qr, kr) * (1.0 / math.sqrt(size)) + tiled(bias, heads)
    peak = jnp.max(scores, axis=-1, keepdims=True)
    weight = jnp.exp(scores - peak)
    probs = weight * (1.0 / jnp.sum(weight, axis=-1, keepdims=True))
    o = dot(probs.astype(BF16), v).astype(BF16)
    o_ref[...] = rows_to_heads(o, heads, block)
    wait_out()
    part[...] = dot(o_ref[...], wo_s[...])
    total = reduce_rows(t, nt, rows, part, outgoing, came, s_sem, r_sem, at)
    h1 = x_ref[rows_at(t * rows, rows)].astype(F32) + total
    h1_ref[...] = h1
    b_ref[...] = (unit_rows(h1)[0] * g_moe).astype(BF16)


def fill_tables(tabs, lengths, m):
    block, size = tabs.shape[2:]
    row = lax.broadcasted_iota(jnp.int32, (block, size), 0)
    lane = lax.broadcasted_iota(jnp.int32, (block, size), 1)
    begin, segment, segment_of_lane = (jnp.zeros((block, size), jnp.int32) for _ in range(3))
    end = jnp.int32(0)
    for n in range(lengths.shape[1]):
        end = end + lengths[m, n]
        begin = jnp.where(row >= end, end, begin)
        segment = segment + jnp.where(row >= end, 1, 0)
        segment_of_lane = segment_of_lane + jnp.where(lane >= end, 1, 0)
    half = size // 2
    position = jnp.where(lane >= half, lane - half, lane).astype(F32)
    inverse = jnp.exp(position * (-2.0 * math.log(THETA) / size))
    angle = (row - begin).astype(F32) * inverse
    sin = jnp.sin(angle)
    tabs[m, 0] = jnp.cos(angle)
    tabs[m, 1] = jnp.where(lane >= half, sin, -sin)
    tabs[m, 2] = jnp.where((lane <= row) & (segment == segment_of_lane), 0.0, -1e30)


def fill_gates(gates, ids, route_weights, m):
    expert_of, weight_of = ids[m], route_weights[m]
    lane = lax.broadcasted_iota(jnp.int32, gates.shape[1:], 1)
    out = jnp.zeros(gates.shape[1:], F32)
    for c in range(expert_of.shape[1]):
        out = out + jnp.where(lane == expert_of[:, c : c + 1], weight_of[:, c : c + 1], 0.0)
    gates[m] = out


def start_attend_kernel(nz, nt, heads, relay, hello, at, ins, outs, scratch):
    s, z, t = lax.axis_index(SECTION), lax.axis_index(EXPERT), lax.axis_index(TENSOR)
    lengths, ids, route_weights, g_attn, g_moe, g_query, g_key, boundary, wq, wk, wv, wo, wg, wu, wd = ins
    edges, tabs_out, gates_out, gains_out = outs[:4]
    gathered, (sg, su, sd), results = outs[4:8], outs[8:11], outs[11:]
    x_s, tabs_s, gains_s, gains, tabs, gates = scratch[:6]
    w_sem, in_sem, own_sem, sib_send, sib_recv, gate_send, gate_recv = scratch[6:13]
    relay.bind((wq, wk, wv, wo), gathered, scratch[13:20])
    attn_scratch = scratch[20:]
    column = 0
    for gain in (g_attn, g_moe, g_query, g_key):
        gains[:, column : column + gain.shape[1]] = gain[...]
        column += gain.shape[1]
    other = 1 - s
    i32 = jnp.int32

    own = [
        pltpu.make_async_copy(boundary.at[s], edges.at[s], own_sem.at[0]),
        pltpu.make_async_copy(tabs.at[s], tabs_out.at[s], own_sem.at[1]),
        pltpu.make_async_copy(gains, gains_out.at[s], own_sem.at[2]),
        pltpu.make_async_copy(gates.at[s], gates_out.at[s, z], own_sem.at[3]),
    ]
    own[0].start()
    own[2].start()
    hello(all_peers(s, z, t, nz, nt))

    def sibling(i, src, dst):
        return remote(src, dst, sib_send.at[i], sib_recv.at[i], section=other)

    pairs = [
        (boundary.at[other], edges.at[s], edges.at[other]),
        (tabs.at[other], tabs_out.at[s], tabs_out.at[other]),
        (gains, gains_out.at[s], gains_out.at[other]),
        (wg, sg, sg),
        (wu, su, su),
        (wd, sd, sd),
    ]
    for i in (0, 2):
        sibling(i, *pairs[i][:2]).start()
    for a in range(3):
        relay.begin(a)
    relay.begin_home(3)

    def gate_copy(d, k, arrival=False):
        zz = partner(z, i32(k), nz)
        section = s if d == 0 else other
        return remote(
            gates.at[section],
            gates_out.at[section, zz] if arrival else gates_out.at[s, z],
            gate_send.at[d, k],
            gate_recv.at[d, k],
            section=section,
            expert=zz,
        )

    for m in range(2):
        fill_tables(tabs, lengths, m)
    sibling(1, *pairs[1][:2]).start()
    own[1].start()
    for m in range(2):
        fill_gates(gates, ids, route_weights, m)
    own[3].start()
    turns = [(d, k) for d in range(2) for k in range(nz) if d or k]
    for d, k in turns:
        gate_copy(d, k).start()
    for i in range(3, 6):
        sibling(i, *pairs[i][:2]).start()

    for copy in own:
        copy.wait()
    for i in range(3):
        sibling(i, pairs[i][0], pairs[i][2]).wait_recv()
    at(TABLES)
    loads = [
        pltpu.make_async_copy(edges.at[0], x_s, in_sem.at[0]),
        pltpu.make_async_copy(tabs_out.at[0], tabs_s, in_sem.at[1]),
        pltpu.make_async_copy(gains_out.at[0], gains_s, in_sem.at[2]),
    ]
    for load in loads:
        load.start()
    for load in loads:
        load.wait()

    def bring(a):
        return pltpu.make_async_copy(gathered[a], attn_scratch[a], w_sem.at[a])

    def wait_qkv():
        for k in range(1, nz):
            for a in range(3):
                relay.step(a, k)

            @pl.when((z == k) | ((z == 0) & (k == 1)))
            def _():
                relay.begin_side(3, True)

            @pl.when((z == nz - 1 - k) | ((z == nz - 1) & (k == 1)))
            def _():
                relay.begin_side(3, False)

        for a in range(3):
            relay.settle(a)
            bring(a).start()
        for a in range(3):
            bring(a).wait()
        at(QKV)

    def wait_out():
        for k in range(1, nz):
            relay.step(3, k)
        at(SHARDS)
        relay.settle(3)
        bring(3).start()
        bring(3).wait()

    tables = (tabs_s[0], tabs_s[1], tabs_s[2])
    attend_body(t, nt, heads, x_s, tables, gains_s[...], results, attn_scratch, wait_qkv, wait_out, at)
    for i in range(6):
        sibling(i, *pairs[i][:2]).wait_send()
    for i in range(3, 6):
        sibling(i, pairs[i][0], pairs[i][2]).wait_recv()
    for d, k in turns:
        gate_copy(d, k).wait_send()
        gate_copy(d, k, True).wait_recv()
    for a in range(4):
        relay.end(a)
    at(END)


def attend_kernel(layer, nz, nt, heads, hello, at, ins, outs, scratch):
    s, z, t = lax.axis_index(SECTION), lax.axis_index(EXPERT), lax.axis_index(TENSOR)
    x_ref, tabs, gains, wq, wk, wv, wo = ins
    w_sem, tabs_s, gains_s, attn_scratch = scratch[0], scratch[1], scratch[2], scratch[3:]
    loads = [
        pltpu.make_async_copy(src, dst, w_sem.at[i])
        for i, (src, dst) in enumerate(zip((wq, wk, wv, wo), attn_scratch))
    ]
    small = [
        pltpu.make_async_copy(tabs.at[layer], tabs_s, w_sem.at[4]),
        pltpu.make_async_copy(gains.at[layer], gains_s, w_sem.at[5]),
    ]
    for load in small:
        load.start()
    hello(all_peers(s, z, t, nz, nt))
    at(BEGIN)
    for load in small:
        load.wait()

    def wait_qkv():
        at(QKV)
        for load in loads[:3]:
            load.start()
        for load in loads[:3]:
            load.wait()

    def wait_out():
        at(OUT)
        loads[3].start()
        loads[3].wait()

    tables = (tabs_s[0], tabs_s[1], tabs_s[2])
    attend_body(t, nt, heads, x_ref, tables, gains_s[...], outs, attn_scratch, wait_qkv, wait_out, at)
    at(END)


def load_experts(layer, s, own, sibling, scratch, sems):
    def copies(refs):
        return [pltpu.make_async_copy(r, d, sems.at[i]) for i, (r, d) in enumerate(zip(refs, scratch))]

    @pl.when(s == layer)
    def _():
        for copy in copies(own):
            copy.start()

    @pl.when(s != layer)
    def _():
        for copy in copies(sibling):
            copy.start()

    return copies(own)


def experts_kernel(layer, nz, nt, local_experts, hello, at, ins, outs, scratch):
    s, z, t = lax.axis_index(SECTION), lax.axis_index(EXPERT), lax.axis_index(TENSOR)
    b_ref, h1_ref, gates, wg, wu, wd, sg, su, sd = ins
    y_ref, b_out, g_out, u_out = outs
    wg_s, wu_s, wd_s, g_s, u_s, gates_s, w_sem, o_sem = scratch[:8]
    spaces = scratch[8:]
    rows = b_ref.shape[0]
    loads = load_experts(layer, s, (wg, wu, wd), (sg, su, sd), (wg_s, wu_s, wd_s), w_sem)
    loads.append(pltpu.make_async_copy(gates.at[layer], gates_s, w_sem.at[3]))
    loads[3].start()
    hello(all_peers(s, z, t, nz, nt))
    width = wg.shape[0] // local_experts

    def ready():
        for load in loads:
            load.wait()

    def work(k, origin, rows_in):
        gate_pre = dot_nt(rows_in, wg_s[...])
        up_pre = dot_nt(rows_in, wu_s[...])
        g_s[origin] = gate_pre
        u_s[origin] = up_pre
        weight = expert_gates(gates_s[origin], z * local_experts, local_experts, width)
        hidden = (gate_pre * jax.nn.sigmoid(gate_pre) * up_pre * weight).astype(BF16)
        return dot(hidden, wd_s[...])

    total, finish = exchange(nz, nt, b_ref[...], spaces, ready, work, at)
    full, whole, spread_sem = spaces[0], spaces[3], spaces[4]
    saves = [
        pltpu.make_async_copy(full, b_out, o_sem.at[0]),
        pltpu.make_async_copy(g_s, g_out, o_sem.at[1]),
        pltpu.make_async_copy(u_s, u_out, o_sem.at[2]),
    ]
    for save in saves:
        save.start()
    whole[rows_at(t * rows, rows)] = (h1_ref[...] + total[...]).astype(BF16)
    wait = spread_rows(t, nt, rows, whole, spread_sem.at[0], spread_sem.at[1])
    at(SPREAD)
    finish()
    wait()
    y_ref[...] = whole[...]
    for save in saves:
        save.wait()
    at(END)


def experts_back_kernel(layer, nz, nt, local_experts, hello, at, ins, outs, scratch):
    s, z, t = lax.axis_index(SECTION), lax.axis_index(EXPERT), lax.axis_index(TENSOR)
    dy_ref, h1_ref, gains, gates, g_in, u_in, wg, wu, wd, sg, su, sd = ins
    dat_ref, dh1_ref, term_ref, dy_out, hid_out, dg_out, du_out = outs
    wg_s, wu_s, wd_s, g_s, u_s, hid_s, dg_s, du_s, w_sem, g_sem, u_sem, o_sem = scratch[:12]
    gates_s, scratch = scratch[12], scratch[:12] + scratch[13:]
    spaces = scratch[12:]
    rows, model_width = dy_ref.shape
    loads = load_experts(layer, s, (wd, wg, wu), (sd, sg, su), (wd_s, wg_s, wu_s), w_sem)
    loads.append(pltpu.make_async_copy(gates.at[layer], gates_s, w_sem.at[3]))
    loads[3].start()

    def kept(k):
        origin, slot = partner(z, lax.rem(k + 1, nz), nz), lax.rem(k, 2)
        return (
            pltpu.make_async_copy(g_in.at[origin], g_s.at[slot], g_sem.at[slot]),
            pltpu.make_async_copy(u_in.at[origin], u_s.at[slot], u_sem.at[slot]),
        )

    for load in kept(jnp.int32(0)):
        load.start()
    hello(all_peers(s, z, t, nz, nt))
    width = wg.shape[0] // local_experts

    def ready():
        for load in loads:
            load.wait()

    def work(k, origin, rows_in):
        turn = lax.rem(k + nz - 1, nz)
        for load in kept(turn):
            load.wait()

        @pl.when(turn + 1 < nz)
        def _():
            for load in kept(turn + 1):
                load.start()

        slot = lax.rem(turn, 2)
        gate_pre, up_pre = g_s[slot], u_s[slot]
        weight = expert_gates(gates_s[origin], z * local_experts, local_experts, width)
        sigmoid = jax.nn.sigmoid(gate_pre)
        silu = gate_pre * sigmoid
        hid_s[origin] = (silu * up_pre * weight).astype(BF16)
        grad_hidden = dot_nt(rows_in, wd_s[...]) * weight
        dg_s[origin] = (grad_hidden * up_pre * sigmoid * (1.0 + gate_pre * (1.0 - sigmoid))).astype(BF16)
        du_s[origin] = (grad_hidden * silu).astype(BF16)
        return dot(dg_s[origin], wg_s[...]) + dot(du_s[origin], wu_s[...])

    total, finish = exchange(nz, nt, dy_ref[...], spaces, ready, work, at)
    full, whole, spread_sem = spaces[0], spaces[3], spaces[4]
    saves = [
        pltpu.make_async_copy(full, dy_out, o_sem.at[0]),
        pltpu.make_async_copy(hid_s, hid_out, o_sem.at[1]),
        pltpu.make_async_copy(dg_s, dg_out, o_sem.at[2]),
        pltpu.make_async_copy(du_s, du_out, o_sem.at[3]),
    ]
    for save in saves:
        save.start()
    unit, factor = unit_rows(h1_ref[...])
    g_moe = gains[layer, :, model_width : 2 * model_width]
    back, term = norm_back(total[...], g_moe, unit, factor)
    dh1 = dy_ref[...].astype(F32) + back
    dh1_ref[...] = dh1
    term_ref[...] = term
    mine = rows_at(t * rows, rows)
    whole[mine] = dh1.astype(BF16)
    dat_ref[mine] = dh1.astype(BF16)
    wait = spread_rows(t, nt, rows, whole, spread_sem.at[0], spread_sem.at[1])
    at(SPREAD)
    finish()
    wait()
    for j in range(1, nt):
        theirs = rows_at(partner(t, jnp.int32(j), nt) * rows, rows)
        dat_ref[theirs] = whole[theirs]
    for save in saves:
        save.wait()
    at(END)


def experts_both_kernel(layer, nz, nt, local_experts, hello, at, ins, outs, scratch):
    s, z, t = lax.axis_index(SECTION), lax.axis_index(EXPERT), lax.axis_index(TENSOR)
    b_ref, h1_ref, gains, edges, gates, dy_all, wg, wu, wd, sg, su, sd = ins
    dat_ref, dh1_ref, term_ref, b_out, y_out, hid_out, dg_out, du_out = outs
    wg_s, wu_s, wd_s, dy_s, y_s, hid_s, dg_s, du_s, w_sem, dy_sem, y_sem, o_sem = scratch[:12]
    gates_s, dy_ref, scratch = scratch[12], scratch[13], scratch[:12] + scratch[14:]
    spaces = scratch[12:]
    rows, model_width = b_ref.shape
    loads = load_experts(layer, s, (wg, wu, wd), (sg, su, sd), (wg_s, wu_s, wd_s), w_sem)
    loads.append(pltpu.make_async_copy(gates.at[layer], gates_s, w_sem.at[3]))
    loads[3].start()
    own_rows = edges.at[layer, rows_at(t * rows, rows)]
    loads.append(pltpu.make_async_copy(own_rows, dy_ref, w_sem.at[4]))
    loads[4].start()

    def cotangent(turn):
        origin, slot = partner(z, lax.rem(turn + 1, nz), nz), lax.rem(turn, 2)
        return pltpu.make_async_copy(dy_all.at[origin], dy_s.at[slot], dy_sem.at[slot])

    def store(turn):
        k, slot = lax.rem(turn + 1, nz), lax.rem(turn, 2)
        return pltpu.make_async_copy(y_s.at[slot], y_out.at[k], y_sem.at[slot])

    cotangent(jnp.int32(0)).start()
    hello(all_peers(s, z, t, nz, nt))
    width = wg.shape[0] // local_experts

    def ready():
        for load in loads:
            load.wait()

    def work(k, origin, rows_in):
        turn = lax.rem(k + nz - 1, nz)
        slot = lax.rem(turn, 2)
        cotangent(turn).wait()

        @pl.when(turn + 1 < nz)
        def _():
            cotangent(turn + 1).start()

        @pl.when(turn >= 2)
        def _():
            store(turn - 2).wait()

        gate_pre = dot_nt(rows_in, wg_s[...])
        up_pre = dot_nt(rows_in, wu_s[...])
        weight = expert_gates(gates_s[origin], z * local_experts, local_experts, width)
        sigmoid = jax.nn.sigmoid(gate_pre)
        silu = gate_pre * sigmoid
        hid_s[origin] = (silu * up_pre * weight).astype(BF16)
        grad_hidden = dot_nt(dy_s[slot], wd_s[...]) * weight
        dg_s[origin] = (grad_hidden * up_pre * sigmoid * (1.0 + gate_pre * (1.0 - sigmoid))).astype(BF16)
        du_s[origin] = (grad_hidden * silu).astype(BF16)
        y_s[slot] = dot(hid_s[origin], wd_s[...]).astype(BF16)
        store(turn).start()
        return dot(dg_s[origin], wg_s[...]) + dot(du_s[origin], wu_s[...])

    total, finish = exchange(nz, nt, b_ref[...], spaces, ready, work, at)
    full, whole, spread_sem = spaces[0], spaces[3], spaces[4]
    saves = [
        pltpu.make_async_copy(full, b_out, o_sem.at[0]),
        pltpu.make_async_copy(hid_s, hid_out, o_sem.at[1]),
        pltpu.make_async_copy(dg_s, dg_out, o_sem.at[2]),
        pltpu.make_async_copy(du_s, du_out, o_sem.at[3]),
    ]
    for save in saves:
        save.start()
    unit, factor = unit_rows(h1_ref[...])
    g_moe = gains[layer, :, model_width : 2 * model_width]
    back, term = norm_back(total[...], g_moe, unit, factor)
    dh1 = dy_ref[...].astype(F32) + back
    dh1_ref[...] = dh1
    term_ref[...] = term
    mine = rows_at(t * rows, rows)
    whole[mine] = dh1.astype(BF16)
    dat_ref[mine] = dh1.astype(BF16)
    wait = spread_rows(t, nt, rows, whole, spread_sem.at[0], spread_sem.at[1])
    at(SPREAD)
    finish()
    wait()
    for j in range(1, nt):
        theirs = rows_at(partner(t, jnp.int32(j), nt) * rows, rows)
        dat_ref[theirs] = whole[theirs]
    for save in saves:
        save.wait()
    store(jnp.int32(nz - 2)).wait()
    store(jnp.int32(nz - 1)).wait()
    at(END)


def attend_back_kernel(layer, source, nz, nt, heads, hello, at, ins, outs, scratch):
    s, z, t = lax.axis_index(SECTION), lax.axis_index(EXPERT), lax.axis_index(TENSOR)
    (x_ref, tabs, gains, dat_ref, dh1_ref, term_moe, q_ref, k_ref, v_ref, qr_ref, kr_ref) = ins[:11]
    wq, wk, wv, wo = ins[11:15]
    dx_ref, dqkv_ref, terms_ref = outs[:3]
    wq_s, wk_s, wv_s, wo_s, part, outgoing, came, s_sem, r_sem, w_sem, gs_sem, gr_sem = scratch[:12]
    x_s, scratch = scratch[12], scratch[13:]
    if layer == 0:
        whole, terms_near, terms_in, t_sem, near_send, near_recv = scratch
        terms_other, terms_out = ins[15], outs[3]
    block, model_width = dat_ref.shape
    rows = block // nt
    mine = rows_at(t * rows, rows)
    x_copy = pltpu.make_async_copy(
        x_ref.at[mine] if source is None else x_ref.at[source, mine], x_s, w_sem.at[4]
    )
    x_copy.start()
    loads = [
        pltpu.make_async_copy(src, dst, w_sem.at[i])
        for i, (src, dst) in enumerate(((wo, wo_s), (wq, wq_s), (wk, wk_s), (wv, wv_s)))
    ]
    for load in loads:
        load.start()
    hello(all_peers(s, z, t, nz, nt))
    if layer == 0:
        late = [at.moves[name] for name in (MOVE_DQKV_0, MOVE_DX_0, MOVE_TERMS_0)]
        late[0].src, late[1].src, late[2].src = dqkv_ref, whole, terms_ref
    at(BEGIN)

    size = tabs.shape[-1]
    g_attn, _, g_query, g_key = split_gains(gains[layer], model_width, size)
    scale = 1.0 / math.sqrt(size)
    cos, sin, bias = tabs[layer, 0], tabs[layer, 1], tabs[layer, 2]
    cos_all, sin_all = tiled(cos, heads), tiled(sin, heads)
    qr, kr, v = qr_ref[...], kr_ref[...], v_ref[...]
    scores = dot_nt(qr, kr) * scale + tiled(bias, heads)
    peak = jnp.max(scores, axis=-1, keepdims=True)
    weight = jnp.exp(scores - peak)
    probs = weight * (1.0 / jnp.sum(weight, axis=-1, keepdims=True))
    loads[0].wait()
    do = heads_to_rows(dot_nt(dat_ref[...], wo_s[...]).astype(BF16), heads, size)
    dv = dot_tn(probs.astype(BF16), do).astype(BF16)
    dp = dot_nt(do, v)
    ds = (probs * (dp - jnp.sum(probs * dp, axis=-1, keepdims=True))).astype(BF16)
    dqr = dot(ds, kr) * scale
    dkr = dot_tn(ds, qr) * scale
    dqn = dqr * cos_all - half_turn(dqr) * sin_all
    dkn = dkr * cos - half_turn(dkr) * sin
    q_unit, q_factor = unit_rows(heads_to_rows(q_ref[...], heads, size))
    k_unit, k_factor = unit_rows(k_ref[...])
    dq, term_query = norm_back(dqn, g_query, q_unit, q_factor)
    dk, term_key = norm_back(dkn, g_key, k_unit, k_factor)
    dq = rows_to_heads(dq.astype(BF16), heads, block)
    dk = dk.astype(BF16)
    dqkv_ref[:, : heads * size] = dq
    dqkv_ref[:, heads * size : (heads + 1) * size] = dk
    dqkv_ref[:, (heads + 1) * size :] = dv
    if layer == 0:
        late[0].start()
    at(DQKV)
    for load in loads[1:]:
        load.wait()
    part[...] = dot_nt(dq, wq_s[...]) + dot_nt(dk, wk_s[...]) + dot_nt(dv, wv_s[...])
    total = reduce_rows(t, nt, rows, part, outgoing, came, s_sem, r_sem, at)
    at(REDUCED)
    x_copy.wait()
    unit, factor = unit_rows(x_s[...].astype(F32))
    back, term_attn = norm_back(total, g_attn, unit, factor)
    dx = (dh1_ref[...] + back).astype(BF16)
    terms_ref[...] = jnp.zeros_like(terms_ref)
    write_terms(terms_ref, 0, term_moe[...])
    write_terms(terms_ref, 8, term_attn)
    terms_ref[16:17, :size] = term_query
    terms_ref[16:17, size : 2 * size] = term_key
    at(TERMS)
    if layer == 1:
        dx_ref[...] = dx
    else:
        late[2].start()
        whole[mine] = dx
        wait = spread_rows(t, nt, rows, whole, gs_sem, gr_sem)
        wait()
        late[1].start()
        late[2].arrive()

        def total_of(ref):
            out = ref[0, 0]
            for section in range(2):
                for origin in range(nz):
                    if section or origin:
                        out = out + ref[section, origin]
            return out

        @pl.when(s == 0)
        def _():
            copy = pltpu.make_async_copy(late[2].out, terms_in, t_sem.at[0])
            copy.start()
            copy.wait()

        @pl.when(s != 0)
        def _():
            copy = pltpu.make_async_copy(terms_other, terms_in, t_sem.at[0])
            copy.start()
            copy.wait()

        terms_near[0] = total_of(terms_in)

        def near(j):
            return remote(
                terms_near.at[0],
                terms_near.at[j],
                near_send.at[j],
                near_recv.at[j],
                tensor=partner(t, jnp.int32(j), nt),
            )

        for j in range(1, nt):
            near(j).start()
        sums = terms_near[0]
        for j in range(1, nt):
            near(j).wait_recv()
            sums = sums + terms_near[j]
        for j in range(1, nt):
            near(j).wait_send()
        terms_out[...] = sums
        at(TAIL)
        late[0].finish()
        late[1].finish()
        late[2].leave()
        dx_ref[...] = dx
    at(END)


class ExpertGrads:
    def __init__(self, nz, step):
        self.nz, self.step = nz, step

    def begin(self, ins, outs, scratch):
        s = lax.axis_index(SECTION)
        own, near = (ins[0:5], ins[5:10]), (ins[10:15], ins[15:20])
        left, right, _, in_sem, _ = scratch

        def loads(layer):
            out = []
            for i in range(5):
                target = left.at[i] if i < 3 else right.at[i - 3]
                for j, src in enumerate((own[layer][i], near[layer][i])):
                    half = target.at[pl.ds(j * self.nz, self.nz)]
                    out.append(pltpu.make_async_copy(src, half, in_sem.at[i, j]))
            return out

        for layer in range(2):

            @pl.when(s == layer)
            def _():
                copies = loads(layer)
                for i in (3, 0, 1, 4, 2):
                    copies[2 * i].start()
                    copies[2 * i + 1].start()

        self.waits, self.outs, self.scratch = loads(0), outs, scratch

    def work(self):
        left, right, stage, _, out_sem = self.scratch
        step, outs = self.step, self.outs
        width, cols = right.shape[-1], left.shape[-1]
        tokens = 2 * self.nz * right.shape[2]

        def need(i):
            self.waits[2 * i].wait()
            self.waits[2 * i + 1].wait()

        def stored(slot):
            return pltpu.make_async_copy(stage.at[slot], outs[0].at[pl.ds(0, step)], out_sem.at[slot])

        turn = 0
        for i, r in ((0, 0), (1, 0), (2, 1)):
            if i != 1:
                need(3 + r)
            need(i)
            for c in range(0, cols, step):
                slot = turn % 2
                if turn >= 2:
                    stored(slot).wait()
                lhs = left[i, :, :, c : c + step].reshape(tokens, step)
                stage[slot] = dot_tn(lhs, right[r].reshape(tokens, width))
                pltpu.make_async_copy(
                    stage.at[slot], outs[i].at[pl.ds(c, step)], out_sem.at[slot]
                ).start()
                turn += 1
        for slot in range(2):
            stored(slot).wait()


class AttendGrads:
    def __init__(self, width, q_cols, size):
        self.width, self.q_cols, self.size = width, q_cols, size

    def begin(self, ins, outs, scratch):
        s = lax.axis_index(SECTION)
        self.spaces, sems = scratch[:4], scratch[4]
        self.terms, self.outs = ins[10], outs

        def loads(layer):
            refs = ins[5 * layer : 5 * layer + 5]
            targets = list(self.spaces) + [outs[0]]
            return [
                pltpu.make_async_copy(r, d, sems.at[i]) for i, (r, d) in enumerate(zip(refs, targets))
            ]

        for layer in range(2):

            @pl.when(s == layer)
            def _():
                for load in loads(layer):
                    load.start()

        self.waits = loads(0)

    def work(self):
        (_, attn, moe, query, key, g_query, g_key, g_value, g_output) = self.outs
        terms, size, q_cols = self.terms, self.size, self.q_cols
        for i in range(self.width // TERM_COLS):
            cols = slice(i * TERM_COLS, (i + 1) * TERM_COLS)
            moe[:, cols] = terms[i : i + 1, :]
            attn[:, cols] = terms[8 + i : 9 + i, :]
        query[...] = terms[16:17, :size]
        key[...] = terms[16:17, size : 2 * size]
        for wait in self.waits:
            wait.wait()

        def flat(ref):
            return ref[...].reshape(-1, ref.shape[-1])

        a_s, o_s, t_s, d_s = self.spaces
        grad = dot_tn(flat(a_s), flat(d_s))
        g_query[...] = grad[:, :q_cols]
        g_key[...] = grad[:, q_cols : q_cols + size]
        g_value[...] = grad[:, q_cols + size :]
        g_output[...] = dot_tn(flat(o_s), flat(t_s))


def shape_of(shape, dtype):
    return jax.ShapeDtypeStruct(tuple(shape), dtype)


def like(value, lead=()):
    return shape_of(tuple(lead) + tuple(value.shape), value.dtype)


def call(body, name, number, ins, outs, scratch):
    def kernel(*refs):
        body(refs[: len(ins)], refs[len(ins) : len(ins) + len(outs)], refs[len(ins) + len(outs) :])

    return pl.pallas_call(
        kernel,
        out_shape=tuple(shape_of(o.shape, o.dtype) for o, _ in outs),
        in_specs=[spec for _, spec in ins],
        out_specs=tuple(spec for _, spec in outs),
        scratch_shapes=list(scratch),
        compiler_params=pltpu.CompilerParams(
            collective_id=number, has_side_effects=number is not None, vmem_limit_bytes=VMEM_LIMIT
        ),
        name=name,
    )(*[value for value, _ in ins])


class Slot:
    def __init__(self, shape):
        self.shape, self.dtype, self.value = tuple(shape.shape), shape.dtype, None


class At:
    def __init__(self, stage, plan, moves):
        self.stage, self.plan, self.moves = stage, plan, moves

    def __call__(self, point):
        for name, act in self.plan.get((self.stage, point), ()):
            act(self.moves[name])


USUAL = {
    SECOND: None,
    LOOPED: 1, OUT: 1, DQKV: 1,
    COLLECTED: 2, REDUCED: 2,
    SPREAD: 3, TERMS: 3,
}


class Group:
    def __init__(self, name, number, fused):
        self.name, self.number, self.fused = name, number, fused
        self.stages, self.moves, self.plan = [], {}, {}

    def stage(self, name, body, ins, outs, scratch):
        slots = [Slot(shape) for shape, _ in outs]
        self.stages.append((name, body, ins, list(zip(slots, [spec for _, spec in outs])), scratch))
        return slots

    def move(self, name, stage, move, ins, outs, plan, start=BEGIN, manual=False):
        slots = [Slot(shape) for shape in outs]
        self.moves[name] = (stage, move, ins, [(slot, ANY) for slot in slots])
        if not self.fused:
            plan = []
            if not manual:
                plan = [(stage, start, lambda m: m.start()), (stage, END, lambda m: m.finish())]
                for point, turn in USUAL.items():
                    if turn:
                        plan.append((stage, point, lambda m, turn=turn: m.poll(turn)))
        for at_stage, point, act in plan:
            self.plan.setdefault((at_stage, point), []).append((name, act))
        return slots

    def run(self):
        if self.fused:
            self.launch(self.name, self.number, self.stages, list(self.moves))
            return
        for i, stage in enumerate(self.stages):
            names = [name for name, entry in self.moves.items() if entry[0] == stage[0]]
            self.launch(self.name + str(i), self.number + i, [stage], names)

    def launch(self, name, number, stages, names):
        moves = [self.moves[n] for n in names]
        outs = [pair for stage in stages for pair in stage[3]] + [p for m in moves for p in m[3]]
        out_at = {id(slot): i for i, (slot, _) in enumerate(outs)}
        ins, in_at, scratch, scratch_at = [], {}, [], {}

        def place(pairs):
            where = []
            for value, spec in pairs:
                if id(value) in out_at:
                    where.append((True, out_at[id(value)]))
                    continue
                key = (id(value), id(spec))
                if key not in in_at:
                    in_at[key] = len(ins)
                    ins.append((value.value if isinstance(value, Slot) else value, spec))
                where.append((False, in_at[key]))
            return where

        def reserve(items):
            where = []
            for item in items:
                key, space = item if isinstance(item, tuple) else (None, item)
                if key is not None and key in scratch_at:
                    where.append(scratch_at[key])
                    continue
                scratch.append(space)
                where.append(len(scratch) - 1)
                if key is not None:
                    scratch_at[key] = len(scratch) - 1
            return where

        stage_at = [(place(st[2]), [out_at[id(o)] for o, _ in st[3]], reserve(st[4])) for st in stages]
        move_at = [
            (place(m[2]), [out_at[id(o)] for o, _ in m[3]], reserve(m[1].scratch())) for m in moves
        ]

        def body(in_refs, out_refs, scratch_refs):
            def pick(places):
                where, results, spaces = places
                refs = [(out_refs if made else in_refs)[i] for made, i in where]
                return refs, [out_refs[i] for i in results], [scratch_refs[i] for i in spaces]

            bound = {n: m[1].bind(*pick(at)) for n, m, at in zip(names, moves, move_at)}
            for i, stage in enumerate(stages):
                hello = greet if i == 0 else lambda peers: None
                stage[1](hello, At(stage[0], self.plan, bound), *pick(stage_at[i]))

        results = call(body, name, number, ins, outs, scratch)
        for (slot, _), value in zip(outs, results):
            slot.value = value


def vm(*values):
    return [(value, VM) for value in values]


def any_place(*values):
    return [(value, ANY) for value in values]


def on_device(
    boundary, seq_lengths, expert_ids, route_weights, attn_gain, moe_gain, query_gain, key_norm_gain,
    w_query, key_weight, value_weight, w_output, w_gate, w_up, w_down,
):
    nz, nt = lax.axis_size("expert"), lax.axis_size("tensor")
    micro, block, width = boundary.shape[1:]
    size = query_gain.shape[1]
    heads = w_query.shape[2] // size
    local_experts = w_gate.shape[1]
    hidden = local_experts * w_gate.shape[2]
    experts = local_experts * nz
    rows = block // nt
    q_cols = heads * size
    assert micro == 2 and key_weight.shape[2] == size == block and experts <= LANES
    dma = pltpu.SemaphoreType.DMA

    wg, wu, wd = (w[0].reshape(hidden, width) for w in (w_gate, w_up, w_down))
    wq, wk, wv, wo = w_query[0], key_weight[0], value_weight[0], w_output[0]
    gains = shape_of((1, 2 * width + 2 * size), F32)

    def attend_spaces(own):
        return [
            (SHARED_WQ, pltpu.VMEM((width, q_cols), BF16)),
            (SHARED_WK, pltpu.VMEM((width, size), BF16)),
            (SHARED_WV, pltpu.VMEM((width, size), BF16)),
            (SHARED_WO, pltpu.VMEM((q_cols, width), BF16)),
            (SHARED_PART, pltpu.VMEM((block, width), F32)),
            pltpu.VMEM((block, width), BF16),
            pltpu.VMEM((nt, rows, width), BF16),
            dma((nt,)),
            dma((nt,)),
        ]

    gathered = [
        shape_of((width, q_cols), BF16),
        shape_of((width, size), BF16),
        shape_of((width, size), BF16),
        shape_of((q_cols, width), BF16),
    ]
    attend_outs = vm(
        shape_of((rows, width), F32),
        shape_of((rows, width), BF16),
        shape_of((block, width), BF16),
        shape_of((block, q_cols), F32),
        shape_of((block, size), F32),
        shape_of((block, size), BF16),
        shape_of((heads * block, size), BF16),
        shape_of((block, size), BF16),
        shape_of((block, q_cols), BF16),
    )
    expert_scratch = [(SHARED_WG, pltpu.VMEM((hidden, width), BF16)), (SHARED_WU, pltpu.VMEM((hidden, width), BF16))]
    expert_scratch += [(SHARED_WD, pltpu.VMEM((hidden, width), BF16))]
    hid_scratch = [(n, pltpu.VMEM((nz, block, hidden), BF16)) for n in (SHARED_HID, SHARED_DG, SHARED_DU)]
    all_tokens = shape_of((nz, block, width), BF16)
    all_hidden = shape_of((nz, block, hidden), BF16)
    cols = width // nz
    sliced = [shape_of((2, nz, block, cols), BF16), shape_of((2, nz, rows, cols), BF16)]

    def start(move):
        move.start()

    def finish(move):
        move.finish()

    def poll(turn):
        return lambda move: move.poll(turn)

    def steps(arrays, k):
        return lambda move: [move.step(a, k) for a in arrays]

    def begins(*arrays):
        return lambda move: [move.begin(a) for a in arrays]

    def settles(*arrays):
        return lambda move: [move.settle(a) for a in arrays]

    def ends_of(move):
        for a in range(4):
            move.end(a)

    fused = nz <= 4
    fore = Group("forward", 0, fused)
    relay = Relay(0, (0, 0, 0, 1), nz)
    started = fore.stage(
        ATTEND_0,
        functools.partial(start_attend_kernel, nz, nt, heads, relay),
        [(seq_lengths[0, :, 0], SM)]
        + vm(expert_ids[0], route_weights[0], attn_gain, moe_gain, query_gain, key_norm_gain)
        + any_place(boundary[0], wq, wk, wv, wo, wg, wu, wd),
        any_place(
            shape_of((2, block, width), BF16),
            shape_of((2, 3, block, size), F32),
            shape_of((2, nz, block, LANES), F32),
            like(gains, (2,)),
            *gathered,
            *[shape_of((hidden, width), BF16)] * 3,
        )
        + attend_outs,
        [
            pltpu.VMEM((block, width), BF16),
            pltpu.VMEM((3, block, size), F32),
            pltpu.VMEM(gains.shape, F32),
            pltpu.VMEM(gains.shape, F32),
            pltpu.VMEM((2, 3, block, size), F32),
            pltpu.VMEM((2, block, LANES), F32),
            dma((4,)), dma((3,)), dma((5,)), dma((6,)), dma((6,)), dma((2, nz)), dma((2, nz)),
        ]
        + relay.scratch(4)
        + attend_spaces(0),
    )
    edges, tabs_all, gates_all, gains_all = started[:4]
    weights_0 = started[4:8]
    expert_weights = (wg, wu, wd) + tuple(started[8:11])
    h1_0, b_0, a_0, q_0, k_0, v_0, qr_0, kr_0, o_0 = started[11:]

    x_1, ball_0, gp_0, up_0 = fore.stage(
        EXPERTS_0,
        functools.partial(experts_kernel, 0, nz, nt, local_experts),
        vm(b_0, h1_0) + any_place(gates_all, *expert_weights),
        vm(shape_of((block, width), BF16))
        + any_place(
            all_tokens,
            shape_of((nz, block, hidden), F32),
            shape_of((nz, block, hidden), F32),
        ),
        expert_scratch
        + [pltpu.VMEM((nz, block, hidden), F32)] * 2
        + [pltpu.VMEM((nz, block, LANES), F32), dma((4,)), dma((3,))]
        + exchange_scratch(nz, nt, rows, block, width),
    )

    weights_1 = fore.move(
        MOVE_WEIGHTS_1, EXPERTS_0, Relay(1, (0, 0, 0, 1), nz), any_place(wq, wk, wv, wo), gathered,
        [
            (ATTEND_0, SHARDS, begins(0, 1, 2)),
            (ATTEND_0, SENT, steps((0, 1, 2), 1)),
            (ATTEND_0, SENT, begins(3)),
            (EXPERTS_0, ARRIVED, steps((0, 1, 2), 2)),
            (EXPERTS_0, ARRIVED, steps((3,), 1)),
            (EXPERTS_0, LOOPED, steps((0, 1, 2), 3)),
            (EXPERTS_0, LOOPED, steps((3,), 2)),
            (ATTEND_1, QKV, settles(0, 1, 2)),
            (ATTEND_1, OUT, steps((3,), 3)),
            (ATTEND_1, OUT, settles(3)),
            (ATTEND_1, END, ends_of),
        ],
    )

    (dy_rows,) = fore.move(
        MOVE_DY_ROWS, ATTEND_0, RowsFar(1, nz, nt), any_place(edges), [shape_of((nz, rows, width), BF16)],
        [(ATTEND_0, TABLES, start), (ATTEND_0, QKV, finish)],
        SHARDS,
    )
    (dyall_1,) = fore.move(
        MOVE_DY_ALL, EXPERTS_0, Spread(nz, nt), any_place(dy_rows), [all_tokens],
        [(ATTEND_0, QKV, start), (ATTEND_0, SHARDS, poll(1)), (EXPERTS_0, END, finish)],
    )

    h1_1, b_1, a_1, q_1, k_1, v_1, qr_1, kr_1, o_1 = fore.stage(
        ATTEND_1,
        functools.partial(attend_kernel, 1, nz, nt, heads),
        vm(x_1) + any_place(tabs_all, gains_all, *weights_1),
        attend_outs,
        [dma((6,)), pltpu.VMEM((3, block, size), F32), pltpu.VMEM(gains.shape, F32)] + attend_spaces(1),
    )
    fore.run()

    back = Group("backward", 8, fused)
    dat_1, dh1_1, tm_1, ball_1, yparts_1, hid_1, dg_1, du_1 = back.stage(
        BOTH_1,
        functools.partial(experts_both_kernel, 1, nz, nt, local_experts),
        vm(b_1, h1_1, gains_all) + any_place(edges, gates_all, dyall_1, *expert_weights),
        vm(
            shape_of((block, width), BF16),
            shape_of((rows, width), F32),
            shape_of((1, width), F32),
        )
        + any_place(all_tokens, all_tokens, all_hidden, all_hidden, all_hidden),
        expert_scratch
        + [pltpu.VMEM((2, block, width), BF16)] * 2
        + hid_scratch
        + [dma((5,)), dma((2,)), dma((2,)), dma((4,)), (SHARED_GATES, pltpu.VMEM((nz, block, LANES), F32))]
        + [pltpu.VMEM((rows, width), BF16)]
        + exchange_scratch(nz, nt, rows, block, width),
    )

    def attend_back(layer, x, source, dat, dh1, term_moe, kept, weights, others=None):
        outs = vm(
            shape_of((rows, width), BF16),
            shape_of((block, q_cols + 2 * size), BF16),
            shape_of((TERM_ROWS, TERM_COLS), F32),
        )
        scratch = attend_spaces(layer) + [dma((5,)), dma((nt,)), dma((nt,))]
        scratch += [pltpu.VMEM((rows, width), BF16)]
        ins = any_place(x) + vm(tabs_all, gains_all, dat, dh1, term_moe, *kept) + any_place(*weights)
        if others is not None:
            outs += vm(shape_of((TERM_ROWS, TERM_COLS), F32))
            scratch += [
                pltpu.VMEM((block, width), BF16),
                pltpu.VMEM((nt, TERM_ROWS, TERM_COLS), F32),
                pltpu.VMEM((2, nz, TERM_ROWS, TERM_COLS), F32),
                dma((1,)),
                dma((nt,)),
                dma((nt,)),
            ]
            ins += any_place(others)
        return back.stage(
            ATTEND_BACK_1 if layer else ATTEND_BACK_0,
            functools.partial(attend_back_kernel, layer, source, nz, nt, heads),
            ins,
            outs,
            scratch,
        )

    last = (ATTEND_BACK_0, END, finish)
    kept_1, kept_0 = (q_1, k_1, v_1, qr_1, kr_1), (q_0, k_0, v_0, qr_0, kr_0)
    dx_1, dqkv_1, terms_1 = attend_back(1, x_1, None, dat_1, dh1_1, tm_1, kept_1, weights_1)
    dat_0, dh1_0, tm_0, dyall_0, hid_0, dg_0, du_0 = back.stage(
        EXPERTS_BACK_0,
        functools.partial(experts_back_kernel, 0, nz, nt, local_experts),
        vm(dx_1, h1_0, gains_all) + any_place(gates_all, gp_0, up_0, *expert_weights),
        vm(
            shape_of((block, width), BF16),
            shape_of((rows, width), F32),
            shape_of((1, width), F32),
        )
        + any_place(all_tokens, all_hidden, all_hidden, all_hidden),
        expert_scratch
        + [pltpu.VMEM((2, block, hidden), F32)] * 2
        + hid_scratch
        + [dma((4,)), dma((2,)), dma((2,)), dma((4,)), (SHARED_GATES, pltpu.VMEM((nz, block, LANES), F32))]
        + exchange_scratch(nz, nt, rows, block, width),
    )

    def gather(name, stage, layer, value, begin, end=last):
        return back.move(
            name, stage, Gather(layer, nz), any_place(value), [like(value, (2, nz))],
            [begin + (start,), end], begin[1] if begin[0] == stage else BEGIN,
        )

    def line(name, stage, layer, value, begin, *points):
        plan = [begin + (start,)]
        plan += [point + (steps((0,), k + 1),) for k, point in enumerate(points)]
        plan += [(ATTEND_BACK_0, END, settles(0)), (ATTEND_BACK_0, END, lambda m: m.end(0))]
        return back.move(
            name, stage, Line(layer, nz), any_place(value), [like(value, (2, nz))], plan, begin[1]
        )

    def near(name, stage, layer, value):
        return back.move(
            name, stage, Near(layer), any_place(value), [like(value)], [(stage, BEGIN, start), last]
        )

    def columns(name, stage, layer, value, begin, middle):
        return back.move(
            name, stage, Slice(layer, nz, nt), any_place(value), sliced,
            [begin + (start,), middle + (poll(1),), last], begin[1] if begin[0] == stage else BEGIN,
        )

    (bnear_0,) = near(MOVE_B_0, BOTH_1, 0, ball_0)
    (oall_0,) = gather(MOVE_O_0, BOTH_1, 0, o_0, (BOTH_1, ARRIVED))
    aall_0, _ = columns(
        MOVE_A_0, BOTH_1, 0, a_0, (BOTH_1, ARRIVED), (BOTH_1, SPREAD)
    )
    aall_1, _ = columns(
        MOVE_A_1, BOTH_1, 1, a_1, (BOTH_1, ARRIVED), (BOTH_1, SPREAD)
    )
    (oall_1,) = gather(MOVE_O_1, ATTEND_BACK_1, 1, o_1, (EXPERTS_BACK_0, BEGIN))
    near_1 = [
        near(NEAR_1 + i, ATTEND_BACK_1, 1, value)[0]
        for i, value in enumerate((dg_1, du_1, hid_1, ball_1, dyall_1))
    ]
    datall_1, _ = columns(
        MOVE_DAT_1, ATTEND_BACK_1, 1, dat_1, (BOTH_1, SPREAD), (ATTEND_BACK_1, DQKV)
    )
    (ysums_1,) = back.move(
        MOVE_Y_NEAR, ATTEND_BACK_1, SumNear(nz, nt, rows, block, width), any_place(yparts_1),
        [shape_of((nz, rows, width), BF16)],
        [
            (ATTEND_BACK_1, BEGIN, start),
            (EXPERTS_BACK_0, BEGIN, poll(1)),
            (EXPERTS_BACK_0, LOOPED, poll(2)),
            (EXPERTS_BACK_0, COLLECTED, finish),
        ],
    )
    (dqkvall_1,) = gather(MOVE_DQKV_1, EXPERTS_BACK_0, 1, dqkv_1, (ATTEND_BACK_1, DQKV))
    (termsall_1,) = gather(
        MOVE_TERMS_1, EXPERTS_BACK_0, 1, terms_1, (EXPERTS_BACK_0, BEGIN),
        (ATTEND_BACK_0, BEGIN, finish),
    )
    (yrows_1,) = back.move(
        MOVE_Y_FAR, EXPERTS_BACK_0, SumFar(nz, rows, width), any_place(ysums_1) + vm(h1_1),
        [shape_of((rows, width), BF16)],
        [
            (EXPERTS_BACK_0, SPREAD, start),
            (ATTEND_BACK_0, SENT, poll(2)),
            (ATTEND_BACK_0, SENT, finish),
        ],
    )
    _, dqkv_0, terms_0, terms = attend_back(
        0, edges, 0, dat_0, dh1_0, tm_0, kept_0, weights_0, termsall_1
    )
    datall_0, _ = columns(
        MOVE_DAT_0, ATTEND_BACK_0, 0, dat_0, (EXPERTS_BACK_0, SPREAD), (ATTEND_BACK_0, DQKV)
    )
    near_0 = [bnear_0] + [
        near(NEAR_0 + i, ATTEND_BACK_0, 0, value)[0]
        for i, value in enumerate((dyall_0, dg_0, du_0, hid_0))
    ]
    (ends_1,) = back.move(
        MOVE_Y_SPREAD, ATTEND_BACK_0, SpreadNear(1, nt, block, width), any_place(yrows_1),
        [shape_of((2, block, width), BF16)],
        [(ATTEND_BACK_0, TERMS, start), (ATTEND_BACK_0, TAIL, poll(1)), last],
    )
    hand = [(MOVE_DQKV_0, Gather(0, nz), like(dqkv_0, (2, nz)))]
    hand += [(MOVE_DX_0, Near(0, True), shape_of((2, block, width), BF16))]
    hand += [(MOVE_TERMS_0, Gather(0, nz), like(terms_0, (2, nz)))]
    dqkvall_0, ends_0, _ = (
        back.move(name, ATTEND_BACK_0, move, [], [shape], [], manual=True)[0]
        for name, move, shape in hand
    )
    back.run()

    flat = shape_of((hidden, width), F32)
    experts_part = (
        ExpertGrads(nz, 256),
        any_place(
            *(
                slot.value
                for slot in (
                    dg_0, du_0, hid_0, ball_0, dyall_0,
                    dg_1, du_1, hid_1, ball_1, dyall_1,
                    *near_0[2:], *near_0[:2],
                    *near_1,
                )
            )
        ),
        any_place(flat, flat, flat),
        [
            pltpu.VMEM((3, 2 * nz, block, hidden), BF16),
            pltpu.VMEM((2, 2 * nz, block, width), BF16),
            pltpu.VMEM((2, 256, width), F32),
            dma((5, 2)),
            dma((2,)),
        ],
    )
    operands = (aall_0, oall_0, datall_0, dqkvall_0, ends_0, aall_1, oall_1, datall_1, dqkvall_1, ends_1)
    attend_part = (
        AttendGrads(width, q_cols, size),
        any_place(*(slot.value for slot in operands)) + vm(terms.value),
        vm(
            operands[4],
            shape_of((1, width), F32),
            shape_of((1, width), F32),
            shape_of((1, size), F32),
            shape_of((1, size), F32),
            shape_of(wq.shape, F32),
            shape_of(wk.shape, F32),
            shape_of(wv.shape, F32),
            shape_of(wo.shape, F32),
        ),
        [pltpu.VMEM(o.shape, o.dtype) for o in operands[:4]] + [dma((5,))],
    )

    def gradients(name, parts):
        def body(ins, outs, scratch):
            for work, part_ins, part_outs, part_scratch in parts:
                work.begin(ins[: len(part_ins)], outs[: len(part_outs)], scratch[: len(part_scratch)])
                ins, outs = ins[len(part_ins) :], outs[len(part_outs) :]
                scratch = scratch[len(part_scratch) :]
            for part in parts:
                part[0].work()

        joined = [sum((list(part[i]) for part in parts), []) for i in (1, 2, 3)]
        return call(body, name, None, *joined)

    if fused:
        results = gradients("grads", [experts_part, attend_part])
    else:
        results = gradients("expert_grads", [experts_part])
        results = list(results) + list(gradients("attend_grads", [attend_part]))
    grad_gate, grad_up, grad_down, ends = results[:4]
    return (
        ends[None],
        *results[4:8],
        *(grad[None] for grad in results[8:]),
        grad_gate.reshape(w_gate.shape),
        grad_up.reshape(w_gate.shape),
        grad_down.reshape(w_gate.shape),
    )


def solution(mesh):
    return jax.shard_map(
        on_device,
        mesh=mesh,
        in_specs=(
            P(SECTION, None, EXPERT, None),
            P(SECTION, None, EXPERT, None),
            P(SECTION, None, EXPERT, None),
            P(SECTION, None, EXPERT, None),
            P(SECTION, None),
            P(SECTION, None),
            P(SECTION, None),
            P(SECTION, None),
            P(SECTION, EXPERT, TENSOR),
            P(SECTION, EXPERT, TENSOR),
            P(SECTION, EXPERT, TENSOR),
            P(SECTION, TENSOR, EXPERT),
            P(SECTION, EXPERT, TENSOR, None),
            P(SECTION, EXPERT, TENSOR, None),
            P(SECTION, EXPERT, TENSOR, None),
        ),
        out_specs=(
            P(SECTION, None, EXPERT, None),
            P(SECTION, None),
            P(SECTION, None),
            P(SECTION, None),
            P(SECTION, None),
            P(SECTION, EXPERT, TENSOR),
            P(SECTION, EXPERT, TENSOR),
            P(SECTION, EXPERT, TENSOR),
            P(SECTION, TENSOR, EXPERT),
            P(SECTION, EXPERT, TENSOR, None),
            P(SECTION, EXPERT, TENSOR, None),
            P(SECTION, EXPERT, TENSOR, None),
        ),
        check_vma=False,
    )
```
